32 devices in a mesh: seq: 8 (over z, y), wt: 4 (over x, core).
Axes of the slice: x: 2, y: 2, z: 4, core: 2. Of those that a mesh axis runs over, the one named last changes fastest.
Arguments:
- hidden_in: bfloat16 [4, 2048, 2048], P('wt', 'seq'), may hold values from -6 to 6
- doc_starts: int32 [4, 2048], P('wt', 'seq'), may hold values from 0 to 1, as said below
- norm_gain: bfloat16 [2048], P('wt'), may hold values from 0.5 to 1.5
- in_weight: bfloat16 [2048, 8192], P('wt'), may hold values from -0.125 to 0.125
- conv_weight: bfloat16 [4096, 4], P('wt'), may hold values from -3 to 3
- conv_bias: bfloat16 [4096], P('wt'), may hold values from -3 to 3
- x_weight: bfloat16 [4096, 160], P('wt'), may hold values from -0.09375 to 0.09375
- dt_weight: bfloat16 [4096, 128], P('wt'), may hold values from -0.5 to 0.5
- dt_bias: bfloat16 [4096], P('wt'), may hold values from -11 to -2
- a_log: bfloat16 [4096, 16], P('wt'), may hold values from -5 to 2.796875
- d_skip: bfloat16 [4096], P('wt'), may hold values from 0.5 to 1.5
- out_weight: bfloat16 [4096, 2048], P('wt'), may hold values from -0.09375 to 0.09375
- grad_output: bfloat16 [4, 2048, 2048], P('wt', 'seq'), may hold values from -6 to 6
Outputs:
- output: float32 [4, 2048, 2048], P('wt', 'seq')
- input_grad: float32 [4, 2048, 2048], P('wt', 'seq')
- norm_gain_grad: float32 [2048], P(('seq', 'wt'))
- in_weight_grad: float32 [2048, 8192], P(('seq', 'wt'))
- conv_weight_grad: float32 [4096, 4], P(('seq', 'wt'))
- conv_bias_grad: float32 [4096], P(('seq', 'wt'))
- x_weight_grad: float32 [4096, 160], P(('seq', 'wt'))
- dt_weight_grad: float32 [4096, 128], P(('seq', 'wt'))
- dt_bias_grad: float32 [4096], P(('seq', 'wt'))
- a_log_grad: float32 [4096, 16], P(('seq', 'wt'))
- d_skip_grad: float32 [4096], P(('seq', 'wt'))
- out_weight_grad: float32 [4096, 2048], P(('seq', 'wt'))
The draws below stay inside these ranges and needn't reach their ends.
Inputs may be any that keep to these rules, and one draw needn't show every extreme that they name: `doc_starts`: each stream's first position begins a document; in each stream one document begins within the first 256 positions and ends within the last 256.
All inputs are finite; a program needn't handle non-finite values.
Results may differ from the reference program's by a relative error of at most 0.0095.
Values may be sent and summed in bfloat16 or wider, within the bound.
A program may use at most 640 MiB of HBM per device.

```python
import math
import jax
import jax.numpy as jnp
from jax import lax

D = 2048
DI = 4096
N = 16
R = 128
KC = 4
TOK_DEV = 256
LEN = 2048
STREAMS = 4


def draw_doc_starts(key, part):
    key = jax.random.fold_in(key, 11)
    key_first, key_last, key_flags = jax.random.split(key, 3)
    position = jnp.arange(LEN, dtype=jnp.int32)[None, :]
    long_start = jax.random.randint(key_first, (STREAMS, 1), 1, TOK_DEV)
    long_end = jax.random.randint(key_last, (STREAMS, 1), LEN - TOK_DEV + 1, LEN)
    random_flags = jax.random.randint(key_flags, (STREAMS, LEN), 0, 24) == 0
    covered = (position > long_start) & (position < long_end)
    start_flags = jnp.where(covered, False, random_flags)
    start_flags = start_flags | (position == long_start) | (position == long_end) | (position == 0)
    return start_flags.astype(jnp.int32)


def block_levels(stream_key, extent, cuts, low, largest):
    factor_of = 1.0
    for dim, shards_of in cuts:
        draws = jax.random.uniform(jax.random.fold_in(jax.random.fold_in(stream_key, 6), dim), (shards_of,), jnp.float32, low / len(cuts), largest / len(cuts))
        factor_of = factor_of * jnp.repeat(jnp.exp(draws), extent[dim] // shards_of).reshape((-1,) + (1,) * (len(extent) - 1 - dim))
    return factor_of


def noise(own_key, dims, spread, bound, shards=(), kind=jnp.bfloat16):
    level = block_levels(own_key, dims, shards, -0.22, 0.18) if shards else 1.0
    entries = jax.random.normal(own_key, dims, jnp.float32) * spread * level
    return jnp.minimum(jnp.maximum(entries, -bound), bound).astype(kind)


def setup_inputs(seed: int = 0) -> dict:
    seeds = jax.random.split(jax.random.key(seed), 14)
    hidden_in = noise(seeds[0], (STREAMS, LEN, D), 1.0, 6.0, ((0, 4), (1, 8)))
    doc_starts = draw_doc_starts(jax.random.fold_in(seeds[13], 71), 0)
    norm_gain = jnp.clip(1.0 + 0.1 * jax.random.normal(seeds[2], (D,), jnp.float32), 0.5, 1.5).astype(jnp.bfloat16)
    in_weight = noise(seeds[3], (D, 2 * DI), D ** -0.5, 0.125, ((0, 4),))
    conv_weight = noise(seeds[4], (DI, KC), KC ** -0.5, 3.0, ((0, 4),))
    conv_bias = noise(seeds[5], (DI,), 0.5, 3.0, ((0, 4),))
    x_weight = noise(seeds[6], (DI, R + 2 * N), DI ** -0.5, 0.09375, ((0, 4),))
    dt_weight = noise(seeds[7], (DI, R), R ** -0.5, 0.5, ((0, 4),))
    dt_bias = jnp.clip(-11.0 + 9.0 * jax.random.uniform(seeds[8], (DI,), jnp.float32) ** block_levels(seeds[8], (DI,), ((0, 4),), -0.2, 0.2), -11.0, -2.0).astype(jnp.bfloat16)
    a_log = jnp.clip(-5.0 + 7.796875 * jax.random.uniform(seeds[9], (DI, N), jnp.float32) ** block_levels(seeds[9], (DI, N), ((0, 4),), -0.2, 0.2), -5.0, 2.796875).astype(jnp.bfloat16)
    d_skip = jnp.clip(0.5 + 1.0 * jax.random.uniform(seeds[10], (DI,), jnp.float32) ** block_levels(seeds[10], (DI,), ((0, 4),), -0.2, 0.2), 0.5, 1.5).astype(jnp.bfloat16)
    out_weight = noise(seeds[11], (DI, D), DI ** -0.5, 0.09375, ((0, 4),))
    grad_output = noise(seeds[12], (STREAMS, LEN, D), 1.0, 6.0, ((0, 4), (1, 8)))
    return dict(hidden_in=hidden_in, doc_starts=doc_starts, norm_gain=norm_gain, in_weight=in_weight, conv_weight=conv_weight, conv_bias=conv_bias, x_weight=x_weight, dt_weight=dt_weight, dt_bias=dt_bias, a_log=a_log, d_skip=d_skip, out_weight=out_weight, grad_output=grad_output)


EPS = 1e-05

@jax.custom_vjp
def low(v):
    return lax.optimization_barrier(v.astype(jnp.bfloat16)).astype(jnp.float32)

@jax.custom_vjp
def low_back(v):
    return v

def low_keep(v):
    return (low(v), None)

def low_pass(kept, grad):
    return (grad,)

def back_keep(v):
    return (v, None)

def back_low(kept, grad):
    return (low(grad),)
low.defvjp(low_keep, low_pass)
low_back.defvjp(back_keep, back_low)

def matmul_hi(left_op, right_op):
    return jnp.dot(left_op, right_op, precision=lax.Precision.HIGHEST, preferred_element_type=jnp.float32)

def combine_pairs(earlier, later):
    return (earlier[0] * later[0], later[0] * earlier[1] + later[1])

def selective(inputs, deltas, b_rows, c_rows, keep_rows, a_neg):
    n_rows = inputs.shape[0]
    span_len = math.gcd(n_rows, 256)

    def to_pieces(values):
        return values.reshape((n_rows // span_len, span_len) + values.shape[1:])

    def scan_block(carried, pieces):
        u_blk, d_blk, b_blk, c_blk, k_blk = pieces
        decays = k_blk[:, None, None] * jnp.exp(d_blk[:, None, :] * a_neg[None])
        driving = (d_blk * u_blk)[:, None, :] * b_blk[:, :, None]
        cum_decay, cum_drive = lax.associative_scan(combine_pairs, (decays, driving), axis=0)
        states = cum_decay * carried[None] + cum_drive
        return (states[-1], jnp.einsum('knc,kn->kc', states, c_blk))
    initial = jnp.zeros(a_neg.shape, jnp.float32)
    _, outputs = lax.scan(jax.checkpoint(scan_block), initial, (to_pieces(inputs), to_pieces(deltas), to_pieces(b_rows), to_pieces(c_rows), to_pieces(keep_rows)))
    return outputs.reshape(n_rows, inputs.shape[1])

def mamba_layer(rows_in, starts, norm_gain, in_weight, conv_weight, conv_bias, x_weight, dt_weight, dt_bias, a_log, d_skip, out_weight):
    n_rows = rows_in.shape[0]
    inner_width = dt_weight.shape[0]
    dt_rank = dt_weight.shape[1]
    n_state = a_log.shape[1]
    conv_taps = conv_weight.shape[1]
    inv_rms = lax.rsqrt(lax.optimization_barrier(jnp.mean(rows_in * rows_in, axis=1, keepdims=True)) + EPS)
    normed = low(rows_in * inv_rms * norm_gain)
    projected = low_back(low(matmul_hi(normed, in_weight)))
    conv_in = projected[:, :inner_width]
    gate_in = projected[:, inner_width:]
    padded = jnp.concatenate([jnp.zeros((conv_taps - 1, inner_width), jnp.float32), conv_in], 0)
    conv_out = conv_bias + padded[0:n_rows] * conv_weight[:, 0]
    for offset in range(1, conv_taps):
        conv_out = conv_out + padded[offset:offset + n_rows] * conv_weight[:, offset]
    inputs = low(jax.nn.silu(conv_out))
    x_mixed = matmul_hi(inputs, x_weight)
    dt_low = low_back(low(x_mixed[:, :dt_rank]))
    bc_rows = low_back(low(x_mixed[:, dt_rank:]))
    dt_raw = low_back(low(matmul_hi(dt_low, dt_weight.T)))
    deltas = jax.nn.softplus(dt_raw + dt_bias)
    a_neg = -jnp.exp(a_log).T
    scan_in = low_back(inputs)
    keep_rows = 1.0 - starts.astype(jnp.float32)
    scanned = selective(scan_in, deltas, bc_rows[:, :n_state], bc_rows[:, n_state:], keep_rows, a_neg)
    scanned = low_back(low(scanned + d_skip * scan_in))
    gated = low(scanned * jax.nn.silu(gate_in))
    return rows_in + matmul_hi(gated, out_weight)

def reference(hidden_in, doc_starts, norm_gain, in_weight, conv_weight, conv_bias, x_weight, dt_weight, dt_bias, a_log, d_skip, out_weight, grad_output):
    params = (norm_gain.astype(jnp.float32), in_weight.astype(jnp.float32), conv_weight.astype(jnp.float32), conv_bias.astype(jnp.float32), x_weight.astype(jnp.float32), dt_weight.astype(jnp.float32), dt_bias.astype(jnp.float32), a_log.astype(jnp.float32), d_skip.astype(jnp.float32), out_weight.astype(jnp.float32))

    def per_stream(totals, pieces):
        rows_in, starts, cotangent = pieces

        def forward(rows_f, *weights):
            return mamba_layer(rows_f, starts, *weights)
        output, pullback = jax.vjp(forward, rows_in.astype(jnp.float32), *params)
        gradients = pullback(cotangent.astype(jnp.float32))
        summed = tuple((first_term + second_term for first_term, second_term in zip(totals, gradients[1:])))
        return (summed, (output, gradients[0]))
    zero_grads = tuple((jnp.zeros(item.shape, jnp.float32) for item in params))
    totals, (outputs, input_grads) = lax.scan(per_stream, zero_grads, (hidden_in, doc_starts, grad_output))
    return (outputs, input_grads, totals[0], totals[1], totals[2], totals[3], totals[4], totals[5], totals[6], totals[7], totals[8], totals[9])
```

```python
import functools
import math

import jax
import jax.numpy as jnp
from jax import lax
from jax.experimental import pallas as pl
from jax.experimental.pallas import tpu as pltpu
from jax.sharding import PartitionSpec as P

EPS = 1e-05
LOG2E = 1.4426950408889634
RESET = 1e30
SUB = 8
LANE = 128
NBLK = 4
F32 = jnp.float32
BF16 = jnp.bfloat16
MESH = pl.DeviceIdType.MESH


def softplus(v):
    return jnp.maximum(v, 0.0) + jnp.log1p(jnp.exp(-jnp.abs(v)))


def wide(tile, width):
    return jnp.concatenate([tile] * (width // LANE), axis=1)


def fold(values):
    total = values[:, :LANE]
    for k in range(1, values.shape[1] // LANE):
        total = total + values[:, k * LANE : (k + 1) * LANE]
    return total


def chunk_prefix(decay, drive, reverse):
    chunk = lax.broadcasted_iota(jnp.int32, drive.shape, 0)
    for shift in (1, 2, 4):
        if reverse:
            other_decay = pltpu.roll(decay, SUB - shift, 0)
            other_drive = pltpu.roll(drive, SUB - shift, 0)
            inside = chunk < SUB - shift
        else:
            other_decay = pltpu.roll(decay, shift, 0)
            other_drive = pltpu.roll(drive, shift, 0)
            inside = chunk >= shift
        drive = jnp.where(inside, decay * other_drive + drive, drive)
        decay = jnp.where(inside, decay * other_decay, decay)
    return decay, drive


def spread_rows(bcs_ref, spread_ref, bcb):
    bcb[...] = jnp.dot(bcs_ref[...], spread_ref[...], preferred_element_type=F32)


def ends_kernel(
    n_state, bcs_ref, spread_ref, raw_ref, u_ref, g_ref, bias_ref, a_ref,
    end_ref, lead_ref, total_ref, bcb, dec_in, drive_in, g_in,
):
    n_rows, width = raw_ref.shape
    steps = n_rows // SUB

    @pl.when(pl.program_id(1) == 0)
    def _():
        spread_rows(bcs_ref, spread_ref, bcb)

    start_at = 2 * n_state * LANE

    def prepare(j, total):
        rows = pl.ds(pl.multiple_of(j * 16, 16), 16)
        delta = softplus(raw_ref[rows, :].astype(F32) + bias_ref[...])
        starts = wide(bcb[rows, start_at : start_at + LANE], width)
        held = jnp.where(starts > 0.5, RESET, delta)
        dec_in[rows, :] = held
        drive_in[rows, :] = delta * u_ref[rows, :].astype(F32)
        g_in[rows, :] = g_ref[rows, :].astype(F32)
        return total + held[:SUB] + held[SUB:]

    total = lax.fori_loop(0, steps // 2, prepare, jnp.zeros((SUB, width), F32))
    total_ref[0] = total
    for first in range(0, n_state, NBLK):
        states = range(first, first + NBLK)

        def step(j, carry):
            rows = pl.ds(pl.multiple_of(j * SUB, SUB), SUB)
            back = pl.ds(pl.multiple_of((steps - 1 - j) * SUB, SUB), SUB)
            held, drive = dec_in[rows, :], drive_in[rows, :]
            held_back, g_back = dec_in[back, :], g_in[back, :]
            running, passed = [], []
            for n, h, p in zip(states, carry[0], carry[1]):
                b = wide(bcb[rows, n * LANE : (n + 1) * LANE], width)
                c = wide(bcb[back, (n_state + n) * LANE : (n_state + n + 1) * LANE], width)
                running.append(jnp.exp2(held * a_ref[n]) * h + drive * b)
                passed.append(jnp.exp2(held_back * a_ref[n]) * (g_back * c + p))
            return tuple(running), tuple(passed)

        zero = tuple(jnp.zeros((SUB, width), F32) for _ in states)
        running, passed = lax.fori_loop(0, steps, step, (zero, zero))
        for n, h, p in zip(states, running, passed):
            decay = jnp.exp2(total * a_ref[n])
            end_ref[0, n] = chunk_prefix(decay, h, False)[1]
            lead_ref[0, n] = chunk_prefix(decay, p, True)[1]


def scan_kernel(
    n_state, bcs_ref, spread_ref, gather_ref, raw_ref, u_ref, g_ref, gate_ref, dgated_ref,
    bias_ref, skip_ref, a_ref, end_ref, lead_ref, total_ref, head_ref, tail_ref,
    gated_ref, dgate_ref, dscan_ref, draw_ref, dbc_ref, da_ref, sums_ref,
    bcb, acc, dec_in, delta_in, drive_in, g_in, y_sum, b_sum, d_sum, kept, decays,
):
    n_rows, width = raw_ref.shape
    steps = n_rows // SUB
    part = pl.program_id(1)
    start_at = 2 * n_state * LANE
    columns = pl.ds(pl.multiple_of(part * width, width), width)

    @pl.when(part == 0)
    def _():
        spread_rows(bcs_ref, spread_ref, bcb)
        acc[...] = jnp.zeros_like(acc)

    @pl.when(pl.program_id(0) == 0)
    def _():
        da_ref[:, :, columns] = jnp.zeros((n_state, SUB, width), F32)
        sums_ref[:, :, columns] = jnp.zeros((2, SUB, width), F32)

    def prepare(j, carry):
        rows = pl.ds(pl.multiple_of(j * 16, 16), 16)
        delta = softplus(raw_ref[rows, :].astype(F32) + bias_ref[...])
        starts = wide(bcb[rows, start_at : start_at + LANE], width)
        delta_in[rows, :] = delta
        dec_in[rows, :] = jnp.where(starts > 0.5, RESET, delta)
        drive_in[rows, :] = delta * u_ref[rows, :].astype(F32)
        g_in[rows, :] = g_ref[rows, :].astype(F32)
        return carry

    lax.fori_loop(0, steps // 2, prepare, 0)
    chunk = lax.broadcasted_iota(jnp.int32, (SUB, width), 0)
    total = total_ref[0]
    before, after = total, total
    for shift in (1, 2, 4):
        before = jnp.where(chunk >= shift, before + pltpu.roll(before, shift, 0), before)
        after = jnp.where(chunk < SUB - shift, after + pltpu.roll(after, SUB - shift, 0), after)
    before, after = pltpu.roll(before, 1, 0), pltpu.roll(after, SUB - 1, 0)

    for first in range(0, n_state, NBLK):
        states = range(first, first + NBLK)
        entry, incoming = [], []
        for n in states:
            head, tail = head_ref[0, n : n + 1, :], tail_ref[0, n : n + 1, :]
            inner = pltpu.roll(end_ref[0, n], 1, 0) + jnp.exp2(before * a_ref[n]) * head
            outer = pltpu.roll(lead_ref[0, n], SUB - 1, 0) + jnp.exp2(after * a_ref[n]) * tail
            entry.append(jnp.where(chunk == 0, head, inner))
            incoming.append(jnp.where(chunk == SUB - 1, tail, outer))

        def forward(j, carry):
            rows = pl.ds(pl.multiple_of(j * SUB, SUB), SUB)
            held, drive, g = dec_in[rows, :], drive_in[rows, :], g_in[rows, :]
            running = []
            y = y_sum[rows, :] if first else None
            for k, (n, h) in enumerate(zip(states, carry)):
                b = wide(bcb[rows, n * LANE : (n + 1) * LANE], width)
                c_at = slice((n_state + n) * LANE, (n_state + n + 1) * LANE)
                c = wide(bcb[rows, c_at], width)
                decay = jnp.exp2(held * a_ref[n])
                kept[k, rows, :] = h
                decays[k, rows, :] = decay
                h = decay * h + drive * b
                y = c * h if y is None else y + c * h
                acc[rows, c_at] += fold(h * g)
                running.append(h)
            y_sum[rows, :] = y
            return tuple(running)

        lax.fori_loop(0, steps, forward, tuple(entry))

        def backward(j, carry):
            rows = pl.ds(pl.multiple_of((steps - 1 - j) * SUB, SUB), SUB)
            delta, drive, g = delta_in[rows, :], drive_in[rows, :], g_in[rows, :]
            through = b_sum[rows, :] if first else None
            pulled = d_sum[rows, :] if first else None
            passed, da = [], []
            for k, (n, p, da_n) in enumerate(zip(states, carry[0], carry[1])):
                b_at = slice(n * LANE, (n + 1) * LANE)
                b = wide(bcb[rows, b_at], width)
                c = wide(bcb[rows, (n_state + n) * LANE : (n_state + n + 1) * LANE], width)
                adjoint = g * c + p
                p = decays[k, rows, :] * adjoint
                weighed = p * kept[k, rows, :]
                pulled = weighed * a_ref[n] if pulled is None else pulled + weighed * a_ref[n]
                through = adjoint * b if through is None else through + adjoint * b
                acc[rows, b_at] += fold(adjoint * drive)
                passed.append(p)
                da.append(da_n + weighed * delta)
            b_sum[rows, :] = through
            d_sum[rows, :] = pulled
            return tuple(passed), tuple(da)

        zero = tuple(jnp.zeros((SUB, width), F32) for _ in states)
        _, da = lax.fori_loop(0, steps, backward, (tuple(incoming), zero))
        for n, da_n in zip(states, da):
            da_ref[n, :, columns] += da_n

    def finish(j, carry):
        bias_sum, skip_sum = carry
        rows = pl.ds(pl.multiple_of(j * 16, 16), 16)
        u, g, delta = u_ref[rows, :].astype(F32), g_in[rows, :], delta_in[rows, :]
        gate, d_gated = gate_ref[rows, :].astype(F32), dgated_ref[rows, :]
        scanned = (y_sum[rows, :] + skip_ref[...] * u).astype(BF16).astype(F32)
        sig = jax.nn.sigmoid(gate)
        gated_ref[rows, :] = (scanned * gate * sig).astype(BF16)
        d_gate = d_gated * scanned * sig * (1.0 + gate * (1.0 - sig))
        dgate_ref[rows, :] = d_gate.astype(BF16)
        through = b_sum[rows, :]
        dscan_ref[rows, :] = (delta * through + skip_ref[...] * g).astype(BF16)
        slope = jax.nn.sigmoid(raw_ref[rows, :].astype(F32) + bias_ref[...])
        d_pre = (d_sum[rows, :] * (1.0 / LOG2E) + u * through) * slope
        draw_ref[rows, :] = d_pre.astype(BF16)
        gu = g * u
        return bias_sum + d_pre[:SUB] + d_pre[SUB:], skip_sum + gu[:SUB] + gu[SUB:]

    zero = jnp.zeros((SUB, width), F32)
    bias_sum, skip_sum = lax.fori_loop(0, steps // 2, finish, (zero, zero))
    sums_ref[0, :, columns] += bias_sum
    sums_ref[1, :, columns] += skip_sum

    @pl.when(part == pl.num_programs(1) - 1)
    def _():
        dbc_ref[...] = jnp.dot(
            acc[...], gather_ref[...], precision=lax.Precision.HIGHEST, preferred_element_type=F32
        )


def spread_matrix(n_state):
    count = 2 * n_state + 1
    column = jnp.arange(count * LANE, dtype=jnp.int32)[None, :] // LANE
    return (jnp.arange(LANE, dtype=jnp.int32)[:, None] == column).astype(BF16)


def scan_specs(n_streams, n_rows, n_chan, n_state, width):
    row = pl.BlockSpec((n_rows, width), lambda b, c: (b, c))
    thin = pl.BlockSpec((n_rows, LANE), lambda b, c: (b, 0))
    chan = pl.BlockSpec((1, width), lambda b, c: (0, c))
    rate = pl.BlockSpec((n_state, SUB, width), lambda b, c: (0, 0, c))
    edge = pl.BlockSpec((1, n_state, SUB, width), lambda b, c: (b, 0, 0, c))
    total = pl.BlockSpec((1, SUB, width), lambda b, c: (b, 0, c))
    head = pl.BlockSpec((1, n_state, width), lambda b, c: (b, 0, c))
    return row, thin, chan, rate, edge, total, head


def whole(shape):
    return pl.BlockSpec(shape, lambda b, c: (0,) * len(shape))


def chunk_ends(bcs, raw, u, g, bias, rates, n_streams):
    n_rows, n_chan = raw.shape[0] // n_streams, raw.shape[1]
    n_state = rates.shape[0]
    width = min(512, n_chan)
    row, thin, chan, rate, edge, total, _ = scan_specs(n_streams, n_rows, n_chan, n_state, width)
    count = (2 * n_state + 1) * LANE
    return pl.pallas_call(
        functools.partial(ends_kernel, n_state),
        grid=(n_streams, n_chan // width),
        in_specs=[thin, whole((LANE, count)), row, row, row, chan, rate],
        out_specs=[edge, edge, total],
        out_shape=[
            jax.ShapeDtypeStruct((n_streams, n_state, SUB, n_chan), F32),
            jax.ShapeDtypeStruct((n_streams, n_state, SUB, n_chan), F32),
            jax.ShapeDtypeStruct((n_streams, SUB, n_chan), F32),
        ],
        scratch_shapes=[pltpu.VMEM((n_rows, count), F32)]
        + [pltpu.VMEM((n_rows, width), F32)] * 3,
        compiler_params=pltpu.CompilerParams(vmem_limit_bytes=48 * 2**20),
        name="chunk_ends",
    )(bcs, spread_matrix(n_state), raw, u, g, bias, rates)


def scan_all(
    bcs, raw, u, g, gate, d_gated, bias, skip, rates, ends, leads, totals, heads, tails, n_streams
):
    n_rows, n_chan = raw.shape[0] // n_streams, raw.shape[1]
    n_state = rates.shape[0]
    width = min(512, n_chan)
    row, thin, chan, rate, edge, total, head = scan_specs(
        n_streams, n_rows, n_chan, n_state, width
    )
    count = (2 * n_state + 1) * LANE
    spread = spread_matrix(n_state)
    gather = spread[:, : 2 * n_state * LANE].T.astype(F32)
    rows = jax.ShapeDtypeStruct(raw.shape, BF16)
    return pl.pallas_call(
        functools.partial(scan_kernel, n_state),
        grid=(n_streams, n_chan // width),
        in_specs=[
            thin, whole((LANE, count)), whole(gather.shape), row, row, row, row, row,
            chan, chan, rate, edge, edge, total, head, head,
        ],
        out_specs=[
            row, row, row, row, thin, whole((n_state, SUB, n_chan)), whole((2, SUB, n_chan)),
        ],
        out_shape=[
            rows, rows, rows, rows,
            jax.ShapeDtypeStruct((raw.shape[0], LANE), F32),
            jax.ShapeDtypeStruct((n_state, SUB, n_chan), F32),
            jax.ShapeDtypeStruct((2, SUB, n_chan), F32),
        ],
        scratch_shapes=[
            pltpu.VMEM((n_rows, count), F32),
            pltpu.VMEM((n_rows, 2 * n_state * LANE), F32),
        ]
        + [pltpu.VMEM((n_rows, width), F32)] * 7
        + [pltpu.VMEM((NBLK, n_rows, width), F32)] * 2,
        compiler_params=pltpu.CompilerParams(vmem_limit_bytes=56 * 2**20),
        name="scan_all",
    )(
        bcs, spread, gather, raw, u, g, gate, d_gated, bias, skip, rates,
        ends, leads, totals, heads, tails,
    )


def flip(index, bit):
    return index + (1 - 2 * ((index // 2**bit) % 2)) * 2**bit


def bit_of(index, bit):
    return (index // 2**bit) % 2


def pick(left, bit, value):
    return tuple(value if b == bit else slice(None) for b in left)


def over_blocks(count, rows, body):
    tile = math.gcd(rows, 32)
    per_block = rows // tile

    def one(i, carry):
        block, row = i // per_block, (i % per_block) * tile
        index = tuple((block // 2 ** (count - 1 - k)) % 2 for k in range(count))
        body(index, pl.ds(pl.multiple_of(row, tile), tile))
        return carry

    lax.fori_loop(0, 2**count * per_block, one, 0)


class Halving:
    def __init__(self, source, dims, order, columns, own, landing, final, sems, me, peer):
        self.source, self.order, self.columns = source, order, columns
        self.own, self.landing, self.final = own, landing, final
        self.load_sem, self.send_sems, self.recv_sems = sems
        self.me, self.peer = me, peer
        self.bits = dims
        self.copies = []

    def left(self, stage):
        return [b for b in self.bits if b not in self.order[:stage]]

    def load(self):
        bit = self.order[0]
        mine = self.source.at[
            pick(self.bits, bit, bit_of(self.me, bit)) + (slice(None), self.columns)
        ]
        self.loading = pltpu.make_async_copy(mine, self.own, self.load_sem)
        self.loading.start()

    def send(self, stage):
        bit = self.order[stage]
        other = pick(self.left(stage), bit, 1 - bit_of(self.me, bit))
        if stage == 0:
            block = self.source.at[other + (slice(None), self.columns)]
        else:
            block = self.landing[stage - 1].at[other]
        copy = pltpu.make_async_remote_copy(
            src_ref=block,
            dst_ref=self.landing[stage],
            send_sem=self.send_sems[stage],
            recv_sem=self.recv_sems[stage],
            device_id=self.peer(bit),
            device_id_type=MESH,
        )
        copy.start()
        self.copies.append(copy)

    def add(self, stage):
        if stage == 0:
            self.loading.wait()
        self.copies[stage].wait_recv()
        bit = self.order[stage]
        mine = bit_of(self.me, bit)
        left, after = self.left(stage), self.left(stage + 1)
        landed = self.landing[stage]

        def body(index, rows):
            if stage == 0:
                kept = self.own[index + (rows, slice(None))]
            else:
                at = iter(index)
                full = tuple(mine if b == bit else next(at) for b in left)
                kept = self.landing[stage - 1][full + (rows, slice(None))]
            total = kept.astype(F32) + landed[index + (rows, slice(None))].astype(F32)
            if after:
                landed[index + (rows, slice(None))] = total.astype(BF16)
            else:
                self.final(rows, total)

        over_blocks(len(after), landed.shape[-2], body)

    def finish(self):
        for copy in self.copies:
            copy.wait_send()


def reduce_kernel(
    plan, n_seq, n_wt, n_chan,
    feat_ref, chan_ref, out_ref, norm_ref, w_ref,
    feat_out, chan_out, out_out, norm_out, gain_out,
    *scratch,
):
    scratch = list(scratch)
    take = lambda count: [scratch.pop(0) for _ in range(count)]
    seq, wt = lax.axis_index("seq"), lax.axis_index("wt")
    seq_bits, wt_bits = n_seq.bit_length() - 1, n_wt.bit_length() - 1
    seq_peer = lambda bit: (flip(seq, bit), wt)
    wt_peer = lambda bit: (seq, flip(wt, bit))
    flat = n_seq * wt + (seq % 2) * (n_seq // 2) + seq // 2
    owner = (flat // n_wt, flat % n_wt)
    here = n_wt * seq + wt
    block = here % n_seq
    giver = ((block % (n_seq // 2)) * 2 + block // (n_seq // 2), here // n_seq)
    elsewhere = flat != here

    barrier = pltpu.get_barrier_semaphore()
    partners = [seq_peer(b) for b in range(seq_bits)]
    partners += [(seq, lax.rem(wt + k, n_wt)) for k in range(1, n_wt)]
    for partner in partners:
        pl.semaphore_signal(barrier, inc=1, device_id=partner, device_id_type=MESH)

    @pl.when(elsewhere)
    def _():
        for partner in (owner, giver):
            pl.semaphore_signal(barrier, inc=1, device_id=partner, device_id_type=MESH)

    pl.semaphore_wait(barrier, len(partners) + 2 * elsewhere.astype(jnp.int32))

    fin_feat, fin_chan, w_rows, gain_sum = take(4)
    load_sems, send_sems, recv_sems, wide_sems, own_sems, out_sems = take(6)
    weights = pltpu.make_async_copy(
        w_ref.at[pl.ds(pl.multiple_of(seq * w_rows.shape[0], w_rows.shape[0]), w_rows.shape[0])],
        w_rows, own_sems.at[0],
    )
    weights.start()

    jobs = []
    slot = 0
    for name, at, width, order in plan:
        seq_wise = name in ("feat", "chan")
        me, peer = (seq, seq_peer) if seq_wise else (wt, wt_peer)
        source = {"feat": feat_ref, "chan": chan_ref, "out": out_ref, "norm": norm_ref}[name]
        bits = len(order)
        dims = sorted(order, reverse=True)
        if name == "chan":
            dims = [0] + dims[:-1]
        own, landing = take(1)[0], take(bits)

        def final(rows, total, name=name, at=at, width=width):
            columns = slice(at, at + width)
            if name == "feat":
                fin_feat[rows, columns] = total
            elif name == "chan":
                fin_chan[rows, columns] = total.astype(BF16)
            elif name == "out":
                out_out[rows, columns] = total
            else:
                norm_out[rows, columns] = total

        sems = (
            load_sems.at[slot],
            [send_sems.at[slot, k] for k in range(bits)],
            [recv_sems.at[slot, k] for k in range(bits)],
        )
        slot += 1
        jobs.append(
            Halving(source, dims, order, slice(at, at + width), own, landing, final, sems, me, peer)
        )

    rows_own = feat_out.shape[0]
    count = [0]
    sent = []

    def to_wt(block_of, place_of):
        k = count[0]
        count[0] += 1
        for step in range(1, n_wt):
            peer = lax.rem(wt + step, n_wt)
            copy = pltpu.make_async_remote_copy(
                src_ref=block_of(peer), dst_ref=place_of(),
                send_sem=wide_sems.at[0, k, step], recv_sem=wide_sems.at[1, k, step],
                device_id=(seq, peer), device_id_type=MESH,
            )
            copy.start()
            sent.append(copy)
        copy = pltpu.make_async_copy(block_of(wt), place_of(), wide_sems.at[0, k, 0])
        copy.start()
        sent.append(copy)

    def own_rows(w):
        return pl.ds(pl.multiple_of(w * rows_own, 8), rows_own)

    def feat_done(at, width):
        tile = math.gcd(w_rows.shape[0], 32)

        def body(i, carry):
            rows = pl.ds(pl.multiple_of(i * tile, tile), tile)
            product = w_rows[rows, at : at + width].astype(F32) * fin_feat[rows, at : at + width]
            gain_sum[rows, :] += fold(product)
            return carry

        lax.fori_loop(0, w_rows.shape[0] // tile, body, 0)
        half, inside = at // n_chan, at % n_chan
        start = pl.multiple_of((half * n_wt + wt) * n_chan + inside, LANE)
        to_wt(
            lambda w: fin_feat.at[own_rows(w), at : at + width],
            lambda: feat_out.at[:, pl.ds(start, width)],
        )

    def chan_done(at, width, k):
        block, place = fin_chan.at[:, at : at + width], chan_out.at[:, at : at + width]

        @pl.when(elsewhere)
        def _():
            pltpu.make_async_remote_copy(
                src_ref=block, dst_ref=place, send_sem=out_sems.at[0, k],
                recv_sem=out_sems.at[1, k], device_id=owner, device_id_type=MESH,
            ).start()

        @pl.when(jnp.logical_not(elsewhere))
        def _():
            pltpu.make_async_copy(block, place, out_sems.at[0, k]).start()

    def chan_wait(at, width, k):
        block, place = fin_chan.at[:, at : at + width], chan_out.at[:, at : at + width]

        @pl.when(elsewhere)
        def _():
            pltpu.make_async_remote_copy(
                src_ref=block, dst_ref=place, send_sem=out_sems.at[0, k],
                recv_sem=out_sems.at[1, k], device_id=owner, device_id_type=MESH,
            ).wait()

        @pl.when(jnp.logical_not(elsewhere))
        def _():
            pltpu.make_async_copy(block, place, out_sems.at[0, k]).wait()

    gain_sum[...] = jnp.zeros_like(gain_sum)
    wt_jobs = [(j, p) for j, p in zip(jobs, plan) if p[0] in ("out", "norm")]
    groups = {}
    for job, item in zip(jobs, plan):
        if item[0] in ("feat", "chan"):
            groups.setdefault((item[0], item[1] // 512), []).append((job, item))
    groups = list(groups.items())
    for job in jobs:
        job.load()
    for job, _ in wt_jobs:
        job.send(0)
    weights.wait()
    chans = []
    total_slots = max(len(groups) + seq_bits, wt_bits + 1)
    for t in range(total_slots):
        if t < len(groups):
            for job, _ in groups[t][1]:
                job.send(0)
        if 1 <= t < wt_bits:
            for job, _ in wt_jobs:
                job.add(t - 1)
                job.send(t)
        for stage in range(seq_bits):
            g = t - 1 - stage
            if 0 <= g < len(groups):
                (name, _), members = groups[g]
                for job, item in members:
                    job.add(stage)
                    if stage + 1 < seq_bits:
                        job.send(stage + 1)
                if stage + 1 == seq_bits:
                    start = members[0][1][1]
                    width = sum(item[2] for _, item in members)
                    if name == "feat":
                        feat_done(start, width)
                    else:
                        chan_done(start, width, len(chans))
                        chans.append((start, width))
    for job, _ in wt_jobs:
        job.add(wt_bits - 1)
    to_wt(lambda w: gain_sum.at[own_rows(w)], lambda: gain_out.at[wt])
    for copy in sent:
        copy.wait()
    for k, (at, width) in enumerate(chans):
        chan_wait(at, width, k)
    for job in jobs:
        job.finish()


def reduce_plan(feat_cols, chan_cols, out_cols, n_seq, n_wt):
    seq_bits, wt_bits = n_seq.bit_length() - 1, n_wt.bit_length() - 1
    first = tuple(range(seq_bits))
    second = (1, 0) + first[2:]
    plan = []
    for name, columns in (("chan", chan_cols), ("feat", feat_cols)):
        for at in range(0, columns, 512):
            width = min(512, columns - at)
            plan.append((name, at, width - LANE, first))
            plan.append((name, at + width - LANE, LANE, second))
    for name in ("out", "norm"):
        for at in range(0, out_cols, 1024):
            plan.append((name, at, 1024, tuple(range(wt_bits))))
    return plan


def reduce_all(feat, chan, out, norm, w_in):
    n_seq, n_wt = lax.axis_size("seq"), lax.axis_size("wt")
    seq_bits, wt_bits = n_seq.bit_length() - 1, n_wt.bit_length() - 1
    sizes = {}
    for name, block, bits in (
        ("feat", feat, seq_bits), ("chan", chan, seq_bits), ("out", out, wt_bits), ("norm", norm, wt_bits),
    ):
        sizes[name] = block.shape[0] >> bits

    def by_bits(block, bits):
        return block.reshape((2,) * bits + (block.shape[0] >> bits, block.shape[1]))

    plan = reduce_plan(feat.shape[1], chan.shape[1], out.shape[1], n_seq, n_wt)
    n_feat = feat.shape[0]
    n_chan = feat.shape[1] // 2
    feat_rows = n_feat // (n_seq * n_wt)
    groups = -(-feat.shape[1] // 512) + 1
    scratch = [
        pltpu.VMEM((sizes["feat"], feat.shape[1]), F32),
        pltpu.VMEM((sizes["chan"], chan.shape[1]), BF16),
        pltpu.VMEM((sizes["feat"], feat.shape[1]), BF16),
        pltpu.VMEM((sizes["feat"], LANE), F32),
        pltpu.SemaphoreType.DMA((len(plan),)),
        pltpu.SemaphoreType.DMA((len(plan), max(seq_bits, wt_bits))),
        pltpu.SemaphoreType.DMA((len(plan), max(seq_bits, wt_bits))),
        pltpu.SemaphoreType.DMA((2, groups, n_wt)),
        pltpu.SemaphoreType.DMA((1,)),
        pltpu.SemaphoreType.DMA((2, -(-chan.shape[1] // 512))),
    ]
    for name, _, width, order in plan:
        bits = len(order)
        scratch.append(pltpu.VMEM((2,) * (bits - 1) + (sizes[name], width), BF16))
        for stage in range(bits):
            scratch.append(pltpu.VMEM((2,) * (bits - 1 - stage) + (sizes[name], width), BF16))
    hbm = pl.BlockSpec(memory_space=pl.ANY)
    vmem = pl.BlockSpec(memory_space=pltpu.VMEM)
    return pl.pallas_call(
        functools.partial(reduce_kernel, plan, n_seq, n_wt, n_chan),
        in_specs=[hbm] * 5,
        out_specs=[hbm, hbm, vmem, vmem, hbm],
        out_shape=[
            jax.ShapeDtypeStruct((feat_rows, n_wt * feat.shape[1]), F32),
            jax.ShapeDtypeStruct((sizes["chan"], chan.shape[1]), BF16),
            jax.ShapeDtypeStruct((sizes["out"], out.shape[1]), F32),
            jax.ShapeDtypeStruct((sizes["norm"], norm.shape[1]), F32),
            jax.ShapeDtypeStruct((n_wt, feat_rows, LANE), F32),
        ],
        scratch_shapes=scratch,
        compiler_params=pltpu.CompilerParams(
            collective_id=1, has_side_effects=True, vmem_limit_bytes=56 * 2**20
        ),
        name="reduce_all",
    )(
        by_bits(feat, seq_bits), by_bits(chan, seq_bits), by_bits(out, wt_bits),
        by_bits(norm, wt_bits), w_in,
    )


def turn(index, mask, bits):
    for bit in range(bits):
        if mask >> bit & 1:
            index = flip(index, bit)
    return index


class Copies:
    def __init__(self, send_sems, recv_sems):
        self.send_sems, self.recv_sems = send_sems, recv_sems
        self.count, self.open = 0, []

    def remote(self, src, dst, peer):
        k, self.count = self.count, self.count + 1
        copy = pltpu.make_async_remote_copy(
            src_ref=src, dst_ref=dst, send_sem=self.send_sems.at[k],
            recv_sem=self.recv_sems.at[k], device_id=peer, device_id_type=MESH,
        )
        copy.start()
        self.open.append(copy)
        return copy

    def local(self, src, dst):
        k, self.count = self.count, self.count + 1
        copy = pltpu.make_async_copy(src, dst, self.send_sems.at[k])
        copy.start()
        return copy

    def finish(self):
        for copy in self.open:
            copy.wait_send()


class Gather:
    def __init__(self, copies, slots, seq, wt, bits):
        self.copies, self.slots, self.seq, self.wt, self.bits = copies, slots, seq, wt, bits
        self.arriving = {}

    def send(self, mask, src):
        slot = self.slots.at[turn(self.wt, mask, self.bits)]
        low = self.bits if mask == 0 else (mask & -mask).bit_length() - 1
        for bit in reversed(range(low)):
            peer = (self.seq, flip(self.wt, bit))
            self.arriving[mask | 1 << bit] = self.copies.remote(src, slot, peer)

    def arrive(self, mask):
        self.arriving[mask].wait_recv()
        self.send(mask, self.slots.at[turn(self.wt, mask, self.bits)])


def start_kernel(
    n_seq, n_wt,
    hidden_ref, grad_ref, gain_ref, starts_ref, win_ref, wout_ref, wconv_ref, bconv_ref, wx_ref,
    wdt_ref,
    normed_out, win_out, conv_out, gate_out, u_out, raw_out, low_out, bcs_out, dgated_out,
    dscan_out, grad_out, gain_out,
    rows_s, grads_s, gain_s, starts_s, normed_s, win_s, wout_s, conv_s, gate_s, u_s, raw_s, low_s,
    bcs_s, dgated_s, dscan_s, mix_s, fin_s, half_s, land_s, rim_s, rim_in,
    send_sems, recv_sems,
):
    seq, wt = lax.axis_index("seq"), lax.axis_index("wt")
    bits = n_wt.bit_length() - 1
    n_rows, n_feat = hidden_ref.shape
    n_chan, shard = wout_ref.shape[0], win_ref.shape[0]
    taps = wconv_ref.shape[0]
    rim = (taps - 1) * SUB
    all_rows = n_wt * n_rows
    near_y, near_z = (flip(seq, 0), wt), (flip(seq, 1), wt)
    wt_peers = [(seq, turn(wt, mask, bits)) for mask in range(1, n_wt)]
    ahead, behind = (lax.rem(seq + 1, n_seq), wt), (lax.rem(seq + n_seq - 1, n_seq), wt)

    barrier = pltpu.get_barrier_semaphore()
    partners = wt_peers + [near_y, near_z, ahead, behind]
    for partner in partners:
        pl.semaphore_signal(barrier, inc=1, device_id=partner, device_id_type=MESH)
    pl.semaphore_wait(barrier, len(partners))

    copies = Copies(send_sems, recv_sems)
    part = shard // 4
    quarter = seq % 4

    def win_part(owner, which, at, rows, half):
        start = pl.multiple_of(owner * shard + which * part + at, 16)
        return win_s.at[pl.ds(start, rows), half * n_chan : (half + 1) * n_chan]

    def send_far(half):
        found = {}
        rows = pl.ds(pl.multiple_of(quarter * part, 16), part)
        for mask in range(2, n_wt):
            to = turn(wt, mask, bits)
            columns = pl.ds(pl.multiple_of((half * n_wt + to) * n_chan, LANE), n_chan)
            found[mask] = copies.remote(
                win_ref.at[rows, columns], win_part(wt, quarter, 0, part, half), (seq, to)
            )
        return found

    def send_near(half):
        to = flip(wt, 0)
        place = win_s.at[
            pl.ds(pl.multiple_of(wt * shard, 16), shard), half * n_chan : (half + 1) * n_chan
        ]
        columns = pl.ds(pl.multiple_of((half * n_wt + to) * n_chan, LANE), n_chan)
        own = pl.ds(pl.multiple_of((half * n_wt + wt) * n_chan, LANE), n_chan)
        return (
            copies.remote(win_ref.at[:, columns], place, (seq, to)),
            copies.local(win_ref.at[:, own], place),
        )

    def share_first(half, found):
        passed = {}
        for mask, copy in found.items():
            copy.wait_recv()
            block = win_part(turn(wt, mask, bits), quarter, 0, part, half)
            passed[mask] = (
                copies.remote(block, block, near_y), copies.remote(block, block, near_z)
            )
        return passed

    def share_second(half, passed):
        last = []
        for mask, (by_y, by_z) in passed.items():
            owner = turn(wt, mask, bits)
            by_z.wait_recv()
            block = win_part(owner, flip(quarter, 1), 0, part // 2, half)
            last.append(copies.remote(block, block, near_y))
            by_y.wait_recv()
            block = win_part(owner, flip(quarter, 0), part // 2, part // 2, half)
            last.append(copies.remote(block, block, near_z))
        return last

    def normalise(mask):
        at = turn(wt, mask, bits)
        gain = jnp.concatenate(
            [gain_s[k].astype(F32)[0:1] for k in range(n_wt)], axis=1
        )

        def body(i, carry):
            rows = pl.ds(pl.multiple_of(i * 16, 16), 16)
            x = rows_s[at, rows, :].astype(F32)
            inv = lax.rsqrt(jnp.mean(x * x, axis=1, keepdims=True) + EPS)
            place = pl.ds(pl.multiple_of(at * n_rows + i * 16, 16), 16)
            normed_s[place, :] = (x * inv * gain).astype(BF16)
            return carry

        lax.fori_loop(0, n_rows // 16, body, 0)

    far = send_far(0)
    rows = Gather(copies, rows_s, seq, wt, bits)
    gains = Gather(copies, gain_s, seq, wt, bits)
    starts = Gather(copies, starts_s, seq, wt, bits)
    own_copies = [
        copies.local(gain_ref, gain_s.at[wt]),
        copies.local(starts_ref, starts_s.at[wt]),
        copies.local(hidden_ref, rows_s.at[wt]),
    ]
    gains.send(0, gain_ref)
    rows.send(0, hidden_ref)
    near = send_near(0)
    starts.send(0, starts_ref)
    wout_copy = copies.local(wout_ref, wout_s)
    for mask in range(n_wt - 1, 0, -1):
        if mask in gains.arriving:
            gains.arrive(mask)
    for mask in range(1, n_wt):
        if mask not in (1, 2):
            gains.arriving[mask].wait_recv()
    for copy in own_copies:
        copy.wait()
    normalise(0)
    rows.arrive(1)
    normalise(1)
    passed = share_first(0, far)
    far = send_far(1)
    last = share_second(0, passed)
    near_gate = send_near(1)
    for mask in range(2, n_wt):
        rows.arrive(mask)
        if mask == 2:
            grads = Gather(copies, grads_s, seq, wt, bits)
            grad_copy = copies.local(grad_ref, grads_s.at[wt])
            grads.send(0, grad_ref)
        normalise(mask)
    results = [copies.local(normed_s, normed_out), copies.local(gain_s, gain_out)]
    near[0].wait_recv()
    near[1].wait()
    for copy in last:
        copy.wait_recv()

    n_block, m_block = 256, 512

    def tiles(body):
        m_count = all_rows // m_block

        def one(i, carry):
            m = pl.multiple_of((i % m_count) * m_block, m_block)
            n = pl.multiple_of((i // m_count) * n_block, n_block)
            body(m, n)
            return carry

        lax.fori_loop(0, m_count * (n_chan // n_block), one, 0)

    def conv_tile(m, n):
        value = jnp.dot(
            normed_s[pl.ds(m, m_block), :], win_s[:, pl.ds(n, n_block)], preferred_element_type=F32
        )
        value = value.astype(BF16).astype(F32)
        for k in range(m_block // n_rows):
            conv_s[m // n_rows + k, rim:, pl.ds(n, n_block)] = value[k * n_rows : (k + 1) * n_rows]

    tiles(conv_tile)

    rim_s[...] = jnp.zeros_like(rim_s)
    for b in range(n_wt):
        for k in range(taps - 1):
            at = rim + n_rows - (taps - 1 - k) * SUB
            rim_s[b * (taps - 1) + k, :] = conv_s[b, at + SUB - 1, :]
    rim_s2 = rim_s[...].astype(BF16)
    rim_in[0] = rim_s2

    @pl.when(seq == 0)
    def _():
        rim_in[1] = jnp.zeros_like(rim_s2)

    k_rim, copies.count = copies.count, copies.count + 1
    rim_copy = pltpu.make_async_remote_copy(
        src_ref=rim_in.at[0], dst_ref=rim_in.at[1], send_sem=send_sems.at[k_rim],
        recv_sem=recv_sems.at[k_rim], device_id=ahead, device_id_type=MESH,
    )

    @pl.when(seq < n_seq - 1)
    def _():
        rim_copy.start()

    passed = share_first(1, far)

    def convolve(b, j):
        rows = pl.ds(pl.multiple_of(j * 16, 16), 16)
        total = bconv_ref[...] + conv_s[b, rows, :] * wconv_ref[0:1, :]
        for k in range(1, taps):
            at = pl.ds(pl.multiple_of(j * 16 + k * SUB, SUB), 16)
            total = total + conv_s[b, at, :] * wconv_ref[k : k + 1, :]
        place = pl.ds(pl.multiple_of(b * n_rows + j * 16, 16), 16)
        u_s[place, :] = (total * jax.nn.sigmoid(total)).astype(BF16)

    head = -(-(taps - 1) // 2)
    pairs = n_rows // 16

    def convolve_tail(i, carry):
        convolve(i // (pairs - head), head + i % (pairs - head))
        return carry

    lax.fori_loop(0, n_wt * (pairs - head), convolve_tail, 0)

    @pl.when(seq > 0)
    def _():
        rim_copy.wait_recv()

    rim_rows = rim_in[1].astype(F32)
    first = lax.broadcasted_iota(jnp.int32, (SUB, n_chan), 0) == 0
    for b in range(n_wt):
        for k in range(taps - 1):
            at = rim + n_rows - (taps - 1 - k) * SUB
            moved = pltpu.roll(conv_s[b, at : at + SUB, :], 1, 0)
            row = rim_rows[b * (taps - 1) + k : b * (taps - 1) + k + 1, :]
            conv_s[b, k * SUB : (k + 1) * SUB, :] = jnp.where(first, row, moved)
    lax.fori_loop(0, n_wt * head, lambda i, c: (convolve(i // head, i % head), c)[1], 0)
    results += [copies.local(conv_s, conv_out), copies.local(u_s, u_out)]

    packed = jnp.zeros((n_rows, LANE), F32)
    for b in range(n_wt):
        block = u_s[b * n_rows : (b + 1) * n_rows, :]
        mix_s[b * n_rows : (b + 1) * n_rows, :] = jnp.dot(
            block, wx_ref[:, :LANE], preferred_element_type=F32
        )
        packed = packed + jnp.dot(
            block, wx_ref[:, (b + 1) * LANE : (b + 2) * LANE], preferred_element_type=F32
        )
    mix_s[all_rows:, :] = packed
    size = mix_s.shape[0] // 2
    mine = bit_of(wt, 0)
    kept = pl.ds(pl.multiple_of(mine * size, 16), size)
    given = pl.ds(pl.multiple_of((1 - mine) * size, 16), size)
    copy = copies.remote(mix_s.at[given], land_s.at[0], (seq, flip(wt, 0)))
    last = share_second(1, passed)
    grads.arrive(1)
    starts.arrive(2)
    copy.wait_recv()
    half_s[0] = mix_s[kept, :] + land_s[0]
    for bit in range(1, bits):
        copy = copies.remote(half_s.at[bit - 1], land_s.at[bit], (seq, flip(wt, bit)))
        copy.wait_recv()
        half_s[bit] = half_s[bit - 1] + land_s[bit]
    fin_s[kept, :] = half_s[bits - 1]
    copy = copies.remote(half_s.at[bits - 1], fin_s.at[kept], (seq, flip(wt, 0)))
    copy.wait_recv()

    low_s[...] = fin_s[:all_rows, :].astype(BF16)
    starts.arriving[1].wait_recv()
    starts.arriving[3].wait_recv()
    lane = lax.broadcasted_iota(jnp.int32, (n_rows, LANE), 1)
    width = LANE // n_wt
    for b in range(n_wt):
        moved = fin_s[all_rows:, :]
        if b:
            moved = pltpu.roll(moved, LANE - b * width, 1)
        bcs_s[b * n_rows : (b + 1) * n_rows, :] = (
            jnp.where(lane < width, moved, 0.0).astype(BF16) + starts_s[b]
        )

    def raw_tile(m, n):
        value = lax.dot_general(
            low_s[pl.ds(m, m_block), :], wdt_ref[pl.ds(n, n_block), :], (((1,), (1,)), ((), ())),
            preferred_element_type=F32,
        )
        raw_s[pl.ds(m, m_block), pl.ds(n, n_block)] = value.astype(BF16)

    tiles(raw_tile)
    results += [
        copies.local(low_s, low_out), copies.local(bcs_s, bcs_out), copies.local(raw_s, raw_out)
    ]

    near_gate[0].wait_recv()
    near_gate[1].wait()
    for copy in last:
        copy.wait_recv()
    results.append(copies.local(win_s, win_out))

    def gate_tile(m, n):
        value = jnp.dot(
            normed_s[pl.ds(m, m_block), :], win_s[:, pl.ds(n_chan + n, n_block)],
            preferred_element_type=F32,
        )
        gate_s[pl.ds(m, m_block), pl.ds(n, n_block)] = value.astype(BF16)

    tiles(gate_tile)
    results.append(copies.local(gate_s, gate_out))
    grad_copy.wait()
    for mask in range(2, n_wt):
        grads.arrive(mask)
    wout_copy.wait()
    results.append(copies.local(grads_s, grad_out))

    def back_tile(m, n):
        b = m // n_rows
        for k in range(m_block // n_rows):
            at = pl.ds(pl.multiple_of(m + k * n_rows, n_rows), n_rows)
            d_gated = lax.dot_general(
                grads_s[b + k], wout_s[pl.ds(n, n_block), :], (((1,), (1,)), ((), ())),
                preferred_element_type=F32,
            )
            gate = gate_s[at, pl.ds(n, n_block)].astype(F32)
            dgated_s[at, pl.ds(n, n_block)] = d_gated
            dscan_s[at, pl.ds(n, n_block)] = (d_gated * gate * jax.nn.sigmoid(gate)).astype(BF16)

    tiles(back_tile)
    results += [copies.local(dgated_s, dgated_out), copies.local(dscan_s, dscan_out)]
    for copy in results:
        copy.wait()

    @pl.when(seq < n_seq - 1)
    def _():
        rim_copy.wait_send()

    copies.finish()


def start_all(hidden, grad, gain, starts, w_in, w_out, w_conv, b_conv, w_x, w_dt):
    n_seq, n_wt = lax.axis_size("seq"), lax.axis_size("wt")
    n_rows, n_feat = hidden.shape
    n_chan, taps = w_out.shape[0], w_conv.shape[0]
    rows, rim = n_wt * n_rows, (taps - 1) * SUB
    shapes = [
        ((rows, n_feat), BF16), ((n_feat, 2 * n_chan), BF16), ((n_wt, rim + n_rows, n_chan), F32),
        ((rows, n_chan), BF16), ((rows, n_chan), BF16), ((rows, n_chan), BF16), ((rows, LANE), BF16),
        ((rows, LANE), BF16), ((rows, n_chan), F32), ((rows, n_chan), BF16),
        ((n_wt, n_rows, n_feat), BF16), ((n_wt,) + gain.shape, BF16),
    ]
    normed, win, conv, gate, u, raw, low, bcs, dgated, dscan, grads, gains = shapes
    size = (rows + n_rows) // 2
    bits = n_wt.bit_length() - 1
    scratch = [
        grads, grads, gains, ((n_wt, n_rows, LANE), BF16), normed, win, (w_out.shape, BF16), conv,
        gate, u, raw, low, bcs, dgated, dscan, ((2 * size, LANE), F32), ((2 * size, LANE), F32),
        ((bits, size, LANE), F32), ((bits, size, LANE), F32), ((16, n_chan), F32),
        ((2, 16, n_chan), BF16),
    ]
    hbm = pl.BlockSpec(memory_space=pl.ANY)
    vmem = pl.BlockSpec(memory_space=pltpu.VMEM)
    return pl.pallas_call(
        functools.partial(start_kernel, n_seq, n_wt),
        in_specs=[hbm] * 6 + [vmem] * 4,
        out_specs=[hbm] * len(shapes),
        out_shape=[jax.ShapeDtypeStruct(*item) for item in shapes],
        scratch_shapes=[pltpu.VMEM(*item) for item in scratch]
        + [pltpu.SemaphoreType.DMA((80,))] * 2,
        compiler_params=pltpu.CompilerParams(
            collective_id=2, has_side_effects=True, vmem_limit_bytes=60 * 2**20
        ),
        name="start_all",
    )(hidden, grad, gain, starts, w_in, w_out, w_conv, b_conv, w_x, w_dt)


def dot(left, right, left_dim=1, right_dim=0):
    return lax.dot_general(
        left, right, (((left_dim,), (right_dim,)), ((), ())), preferred_element_type=F32
    )


def shift_seq(block, distance):
    count = lax.axis_size("seq")
    route = [(i - distance, i) for i in range(count) if 0 <= i - distance < count]
    return lax.ppermute(block, "seq", route)


def to_chunks(rows):
    n_rows, width = rows.shape
    return rows.reshape(SUB, n_rows // SUB, width).swapaxes(0, 1).reshape(n_rows, width)


def from_chunks(rows, n_streams):
    n_rows, width = rows.shape[0] // n_streams, rows.shape[1]
    parts = rows.reshape(n_streams, n_rows // SUB, SUB, width)
    return parts.swapaxes(1, 2).reshape(n_streams * n_rows, width)


def per_device(
    hidden_in, doc_starts, norm_gain, in_weight, conv_weight, conv_bias, x_weight,
    dt_weight, dt_bias, a_log, d_skip, out_weight, grad_output,
):
    n_wt, n_seq = lax.axis_size("wt"), lax.axis_size("seq")
    seq_at = lax.axis_index("seq")
    n_chan = out_weight.shape[0]
    taps = conv_weight.shape[1]
    dt_rank = dt_weight.shape[1]
    n_state = a_log.shape[1]
    rows_own = hidden_in[0]
    n_rows, n_feat = rows_own.shape
    steps = n_rows // SUB

    w_conv = conv_weight.astype(F32)
    starts = jnp.pad(
        to_chunks(doc_starts[0].astype(BF16)[:, None]), ((0, 0), (2 * n_state, LANE - 2 * n_state - 1))
    )
    w_x = [x_weight[:, :dt_rank]]
    for b in range(n_wt):
        w_x.append(
            jnp.pad(
                x_weight[:, dt_rank:],
                ((0, 0), (2 * n_state * b, LANE - 2 * n_state * (b + 1))),
            )
        )
    (
        normed, w_in, padded, gate_in, inputs, dt_raw, dt_low, bcs, d_gated, d_scanned, grad_all, gain,
    ) = start_all(
        to_chunks(rows_own), to_chunks(grad_output[0]),
        jnp.broadcast_to(norm_gain[None], (16, norm_gain.shape[0])), starts, in_weight, out_weight,
        w_conv.T, conv_bias.astype(F32)[None], jnp.concatenate(w_x, 1), dt_weight,
    )
    gain = gain[:, 0].reshape(n_feat).astype(F32)
    grad_all = grad_all.reshape(n_wt * n_rows, n_feat)
    padded = padded.reshape(n_wt, steps + taps - 1, SUB, n_chan)
    conv_out = conv_bias.astype(F32) + padded[:, 0:steps] * w_conv[:, 0]
    for k in range(1, taps):
        conv_out = conv_out + padded[:, k : k + steps] * w_conv[:, k]

    a_neg = -jnp.exp(a_log.astype(F32)).T
    rates = jnp.broadcast_to((a_neg * LOG2E)[:, None, :], (n_state, SUB, n_chan))
    bias = dt_bias.astype(F32)[None]
    skip = d_skip.astype(F32)[None]
    ends, leads, totals = chunk_ends(bcs, dt_raw, inputs, d_scanned, bias, rates, n_wt)

    edges = jnp.stack([ends[:, :, SUB - 1], leads[:, :, 0]])
    span = jnp.sum(totals, 1)
    edges_all = lax.all_gather(edges, "seq")
    span_all = lax.all_gather(span, "seq")
    head = jnp.zeros(edges.shape[1:], F32)
    tail = jnp.zeros(edges.shape[1:], F32)
    for i in range(n_seq):
        k = n_seq - 1 - i
        decay = jnp.exp2(span_all[i][:, None, :] * (a_neg * LOG2E))
        head = jnp.where(i < seq_at, decay * head + edges_all[i, 0], head)
        decay = jnp.exp2(span_all[k][:, None, :] * (a_neg * LOG2E))
        tail = jnp.where(k > seq_at, decay * tail + edges_all[k, 1], tail)

    gated, d_gate, d_scan_in, d_raw, d_bc, d_rate, sums = scan_all(
        bcs, dt_raw, inputs, d_scanned, gate_in, d_gated, bias, skip, rates,
        ends, leads, totals, head, tail, n_wt,
    )

    partial_out = dot(from_chunks(gated, n_wt), out_weight).astype(BF16)
    d_wout = dot(gated, grad_all, 0, 0)

    d_mixed = jnp.concatenate([dot(d_raw, dt_weight), d_bc[:, : 2 * n_state]], 1)
    d_mixed = lax.psum(d_mixed, "wt").astype(BF16)
    d_wdt = dot(d_raw, dt_low, 0, 0)
    d_wx = dot(inputs, d_mixed, 0, 0)
    d_inputs = dot(d_mixed, x_weight, 1, 1) + d_scan_in.astype(F32)
    sig = jax.nn.sigmoid(conv_out)
    d_conv = d_inputs.reshape(conv_out.shape) * sig * (1.0 + conv_out * (1.0 - sig))
    d_bconv = jnp.sum(d_conv, (0, 1, 2))
    d_wconv = jnp.stack(
        [jnp.sum(d_conv * padded[:, k : k + steps], (0, 1, 2)) for k in range(taps)], 1
    )
    lead_rows = d_conv[:, : taps - 1]
    rim_grad = shift_seq(lead_rows[:, :, 0].astype(BF16), -1).astype(F32)
    suffix = jnp.concatenate([lead_rows[:, :, 1:], rim_grad[:, :, None]], 2)
    behind = jnp.concatenate([d_conv, suffix], 1)
    d_conv_in = behind[:, 0:steps] * w_conv[:, taps - 1]
    for k in range(taps - 1):
        shift = taps - 1 - k
        d_conv_in = d_conv_in + behind[:, shift : shift + steps] * w_conv[:, k]
    d_conv_in = d_conv_in.reshape(n_wt * n_rows, n_chan).astype(BF16)
    d_proj = jnp.concatenate([d_conv_in, d_gate], 1)
    d_win = dot(normed, d_proj, 0, 0)
    partial_normed = dot(from_chunks(d_proj, n_wt), w_in, 1, 1).astype(BF16)

    chan_parts = [
        d_wout, d_wx, d_wdt, (jnp.sum(d_rate, 1) * a_neg).T, d_wconv,
        d_bconv[:, None], jnp.sum(sums, 1).T,
    ]
    cols = sum(piece.shape[1] for piece in chan_parts)
    chan_parts.append(jnp.zeros((n_chan, -cols % LANE), F32))
    chan_grads = jnp.concatenate(chan_parts, 1).astype(BF16)
    feat_grads, chan_grads, out_sum, d_normed, gain_parts = reduce_all(
        d_win.astype(BF16), chan_grads, partial_out, partial_normed, w_in
    )
    chan_grads = chan_grads.astype(F32)
    cuts, at = [], 0
    for piece in chan_parts:
        cuts.append(chan_grads[:, at : at + piece.shape[1]])
        at += piece.shape[1]
    own = n_feat // (n_seq * n_wt)
    own_at = own * (n_wt * seq_at + lax.axis_index("wt"))
    gain_grad = jnp.sum(gain_parts, (0, 2)) / lax.dynamic_slice_in_dim(gain, own_at, own, 0)
    x = rows_own.astype(F32)
    output = x + out_sum
    inv_rms = lax.rsqrt(jnp.mean(x * x, axis=1, keepdims=True) + EPS)
    scaled = d_normed * gain
    cubed = inv_rms * inv_rms * inv_rms
    d_rows = inv_rms * scaled - x * cubed * jnp.mean(scaled * x, axis=1, keepdims=True)
    input_grad = grad_output[0].astype(F32) + d_rows
    return (
        output[None],
        input_grad[None],
        gain_grad,
        feat_grads,
        cuts[4],
        cuts[5][:, 0],
        cuts[1],
        cuts[2],
        cuts[6][:, 0],
        cuts[3],
        cuts[6][:, 1],
        cuts[0],
    )


def solution(mesh):
    placed = (
        P("wt", "seq", None),
        P("wt", "seq"),
        P("wt"),
        P("wt", None),
        P("wt", None),
        P("wt"),
        P("wt", None),
        P("wt", None),
        P("wt"),
        P("wt", None),
        P("wt"),
        P("wt", None),
        P("wt", "seq", None),
    )
    every = ("seq", "wt")
    return jax.shard_map(
        per_device,
        mesh=mesh,
        in_specs=placed,
        out_specs=(
            P("wt", "seq", None),
            P("wt", "seq", None),
            P(every),
            P(every, None),
            P(every, None),
            P(every),
            P(every, None),
            P(every, None),
            P(every),
            P(every, None),
            P(every),
            P(every, None),
        ),
        check_vma=False,
    )
```

```python
import functools
import math

import jax
import jax.numpy as jnp
from jax import lax
from jax.experimental import pallas as pl
from jax.experimental.pallas import tpu as pltpu
from jax.sharding import PartitionSpec as P

EPS = 1e-05
LOG2E = 1.4426950408889634
RESET = 1e30
SUB = 8
LANE = 128
NBLK = 4
F32 = jnp.float32
BF16 = jnp.bfloat16
MESH = pl.DeviceIdType.MESH


def softplus(v):
    return jnp.maximum(v, 0.0) + jnp.log1p(jnp.exp(-jnp.abs(v)))


def wide(tile, width):
    return jnp.concatenate([tile] * (width // LANE), axis=1)


def fold(values):
    total = values[:, :LANE]
    for k in range(1, values.shape[1] // LANE):
        total = total + values[:, k * LANE : (k + 1) * LANE]
    return total


def chunk_prefix(decay, drive, reverse):
    chunk = lax.broadcasted_iota(jnp.int32, drive.shape, 0)
    for shift in (1, 2, 4):
        if reverse:
            other_decay = pltpu.roll(decay, SUB - shift, 0)
            other_drive = pltpu.roll(drive, SUB - shift, 0)
            inside = chunk < SUB - shift
        else:
            other_decay = pltpu.roll(decay, shift, 0)
            other_drive = pltpu.roll(drive, shift, 0)
            inside = chunk >= shift
        drive = jnp.where(inside, decay * other_drive + drive, drive)
        decay = jnp.where(inside, decay * other_decay, decay)
    return decay, drive


def spread_rows(bcs_ref, spread_ref, bcb):
    bcb[...] = jnp.dot(bcs_ref[...], spread_ref[...], preferred_element_type=F32)


def ends_kernel(
    n_state, bcs_ref, spread_ref, raw_ref, u_ref, g_ref, bias_ref, a_ref,
    end_ref, lead_ref, total_ref, first_ref, last_ref, span_ref, bcb, dec_in, drive_in, g_in,
):
    n_rows, width = raw_ref.shape
    steps = n_rows // SUB

    @pl.when(pl.program_id(1) == 0)
    def _():
        spread_rows(bcs_ref, spread_ref, bcb)

    start_at = 2 * n_state * LANE

    def prepare(j, total):
        rows = pl.ds(pl.multiple_of(j * 16, 16), 16)
        delta = softplus(raw_ref[rows, :].astype(F32) + bias_ref[...])
        starts = wide(bcb[rows, start_at : start_at + LANE], width)
        held = jnp.where(starts > 0.5, RESET, delta)
        dec_in[rows, :] = held
        drive_in[rows, :] = delta * u_ref[rows, :].astype(F32)
        g_in[rows, :] = g_ref[rows, :].astype(F32)
        return total + held[:SUB] + held[SUB:]

    total = lax.fori_loop(0, steps // 2, prepare, jnp.zeros((SUB, width), F32))
    total_ref[0] = total
    span_ref[0] = jnp.sum(total, 0, keepdims=True)
    for first in range(0, n_state, NBLK):
        states = range(first, first + NBLK)

        def step(j, carry):
            rows = pl.ds(pl.multiple_of(j * SUB, SUB), SUB)
            back = pl.ds(pl.multiple_of((steps - 1 - j) * SUB, SUB), SUB)
            held, drive = dec_in[rows, :], drive_in[rows, :]
            held_back, g_back = dec_in[back, :], g_in[back, :]
            running, passed = [], []
            for n, h, p in zip(states, carry[0], carry[1]):
                b = wide(bcb[rows, n * LANE : (n + 1) * LANE], width)
                c = wide(bcb[back, (n_state + n) * LANE : (n_state + n + 1) * LANE], width)
                running.append(jnp.exp2(held * a_ref[n]) * h + drive * b)
                passed.append(jnp.exp2(held_back * a_ref[n]) * (g_back * c + p))
            return tuple(running), tuple(passed)

        zero = tuple(jnp.zeros((SUB, width), F32) for _ in states)
        running, passed = lax.fori_loop(0, steps, step, (zero, zero))
        for n, h, p in zip(states, running, passed):
            decay = jnp.exp2(total * a_ref[n])
            end = chunk_prefix(decay, h, False)[1]
            lead = chunk_prefix(decay, p, True)[1]
            end_ref[0, n], lead_ref[0, n] = end, lead
            last_ref[0, n : n + 1, :], first_ref[0, n : n + 1, :] = end[SUB - 1 :], lead[:1]


def scan_kernel(
    n_state, bcs_ref, spread_ref, gather_ref, raw_ref, u_ref, g_ref, gate_ref, dgated_ref,
    bias_ref, skip_ref, a_ref, end_ref, lead_ref, total_ref, head_ref, tail_ref,
    gated_ref, gated_t_ref, dgate_ref, dscan_ref, draw_ref, dbc_ref, da_ref, sums_ref,
    bcb, acc, dec_in, delta_in, drive_in, g_in, y_sum, b_sum, d_sum, kept, decays,
):
    n_rows, width = raw_ref.shape
    steps = n_rows // SUB
    part = pl.program_id(1)
    start_at = 2 * n_state * LANE
    columns = pl.ds(pl.multiple_of(part * width, width), width)

    @pl.when(part == 0)
    def _():
        spread_rows(bcs_ref, spread_ref, bcb)
        acc[...] = jnp.zeros_like(acc)

    @pl.when(pl.program_id(0) == 0)
    def _():
        da_ref[:, :, columns] = jnp.zeros((n_state, SUB, width), F32)
        sums_ref[:, :, columns] = jnp.zeros((2, SUB, width), F32)

    def prepare(j, carry):
        rows = pl.ds(pl.multiple_of(j * 16, 16), 16)
        delta = softplus(raw_ref[rows, :].astype(F32) + bias_ref[...])
        starts = wide(bcb[rows, start_at : start_at + LANE], width)
        delta_in[rows, :] = delta
        dec_in[rows, :] = jnp.where(starts > 0.5, RESET, delta)
        drive_in[rows, :] = delta * u_ref[rows, :].astype(F32)
        g_in[rows, :] = g_ref[rows, :].astype(F32)
        return carry

    lax.fori_loop(0, steps // 2, prepare, 0)
    chunk = lax.broadcasted_iota(jnp.int32, (SUB, width), 0)
    total = total_ref[0]
    before, after = total, total
    for shift in (1, 2, 4):
        before = jnp.where(chunk >= shift, before + pltpu.roll(before, shift, 0), before)
        after = jnp.where(chunk < SUB - shift, after + pltpu.roll(after, SUB - shift, 0), after)
    before, after = pltpu.roll(before, 1, 0), pltpu.roll(after, SUB - 1, 0)

    for first in range(0, n_state, NBLK):
        states = range(first, first + NBLK)
        entry, incoming = [], []
        for n in states:
            head, tail = head_ref[0, n : n + 1, :], tail_ref[0, n : n + 1, :]
            inner = pltpu.roll(end_ref[0, n], 1, 0) + jnp.exp2(before * a_ref[n]) * head
            outer = pltpu.roll(lead_ref[0, n], SUB - 1, 0) + jnp.exp2(after * a_ref[n]) * tail
            entry.append(jnp.where(chunk == 0, head, inner))
            incoming.append(jnp.where(chunk == SUB - 1, tail, outer))

        def forward(j, carry):
            rows = pl.ds(pl.multiple_of(j * SUB, SUB), SUB)
            held, drive, g = dec_in[rows, :], drive_in[rows, :], g_in[rows, :]
            running = []
            y = y_sum[rows, :] if first else None
            for k, (n, h) in enumerate(zip(states, carry)):
                b = wide(bcb[rows, n * LANE : (n + 1) * LANE], width)
                c_at = slice((n_state + n) * LANE, (n_state + n + 1) * LANE)
                c = wide(bcb[rows, c_at], width)
                decay = jnp.exp2(held * a_ref[n])
                kept[k, rows, :] = h
                decays[k, rows, :] = decay
                h = decay * h + drive * b
                y = c * h if y is None else y + c * h
                acc[rows, c_at] += fold(h * g)
                running.append(h)
            y_sum[rows, :] = y
            return tuple(running)

        lax.fori_loop(0, steps, forward, tuple(entry))

        def backward(j, carry):
            rows = pl.ds(pl.multiple_of((steps - 1 - j) * SUB, SUB), SUB)
            delta, drive, g = delta_in[rows, :], drive_in[rows, :], g_in[rows, :]
            through = b_sum[rows, :] if first else None
            pulled = d_sum[rows, :] if first else None
            passed, da = [], []
            for k, (n, p, da_n) in enumerate(zip(states, carry[0], carry[1])):
                b_at = slice(n * LANE, (n + 1) * LANE)
                b = wide(bcb[rows, b_at], width)
                c = wide(bcb[rows, (n_state + n) * LANE : (n_state + n + 1) * LANE], width)
                adjoint = g * c + p
                p = decays[k, rows, :] * adjoint
                weighed = p * kept[k, rows, :]
                pulled = weighed * a_ref[n] if pulled is None else pulled + weighed * a_ref[n]
                through = adjoint * b if through is None else through + adjoint * b
                acc[rows, b_at] += fold(adjoint * drive)
                passed.append(p)
                da.append(da_n + weighed * delta)
            b_sum[rows, :] = through
            d_sum[rows, :] = pulled
            return tuple(passed), tuple(da)

        zero = tuple(jnp.zeros((SUB, width), F32) for _ in states)
        _, da = lax.fori_loop(0, steps, backward, (tuple(incoming), zero))
        for n, da_n in zip(states, da):
            da_ref[n, :, columns] += da_n

    def finish(j, carry):
        bias_sum, skip_sum = carry
        rows = pl.ds(pl.multiple_of(j * 16, 16), 16)
        u, g, delta = u_ref[rows, :].astype(F32), g_in[rows, :], delta_in[rows, :]
        gate, d_gated = gate_ref[rows, :].astype(F32), dgated_ref[rows, :]
        scanned = (y_sum[rows, :] + skip_ref[...] * u).astype(BF16).astype(F32)
        sig = jax.nn.sigmoid(gate)
        gated_ref[rows, :] = (scanned * gate * sig).astype(BF16)
        d_gate = d_gated * scanned * sig * (1.0 + gate * (1.0 - sig))
        dgate_ref[rows, :] = d_gate.astype(BF16)
        through = b_sum[rows, :]
        dscan_ref[rows, :] = (delta * through + skip_ref[...] * g).astype(BF16)
        slope = jax.nn.sigmoid(raw_ref[rows, :].astype(F32) + bias_ref[...])
        d_pre = (d_sum[rows, :] * (1.0 / LOG2E) + u * through) * slope
        draw_ref[rows, :] = d_pre.astype(BF16)
        gu = g * u
        return bias_sum + d_pre[:SUB] + d_pre[SUB:], skip_sum + gu[:SUB] + gu[SUB:]

    zero = jnp.zeros((SUB, width), F32)
    bias_sum, skip_sum = lax.fori_loop(0, steps // 2, finish, (zero, zero))
    gated_t_ref[...] = gated_ref[...].T
    sums_ref[0, :, columns] += bias_sum
    sums_ref[1, :, columns] += skip_sum

    @pl.when(part == pl.num_programs(1) - 1)
    def _():
        dbc_ref[...] = jnp.dot(
            acc[...], gather_ref[...], precision=lax.Precision.HIGHEST, preferred_element_type=F32
        )


def spread_matrix(n_state):
    count = 2 * n_state + 1
    column = jnp.arange(count * LANE, dtype=jnp.int32)[None, :] // LANE
    return (jnp.arange(LANE, dtype=jnp.int32)[:, None] == column).astype(BF16)


def scan_specs(n_streams, n_rows, n_chan, n_state, width):
    row = pl.BlockSpec((n_rows, width), lambda b, c: (b, c))
    thin = pl.BlockSpec((n_rows, LANE), lambda b, c: (b, 0))
    chan = pl.BlockSpec((1, width), lambda b, c: (0, c))
    rate = pl.BlockSpec((n_state, SUB, width), lambda b, c: (0, 0, c))
    edge = pl.BlockSpec((1, n_state, SUB, width), lambda b, c: (b, 0, 0, c))
    total = pl.BlockSpec((1, SUB, width), lambda b, c: (b, 0, c))
    head = pl.BlockSpec((1, n_state, width), lambda b, c: (b, 0, c))
    return row, thin, chan, rate, edge, total, head


def whole(shape):
    return pl.BlockSpec(shape, lambda b, c: (0,) * len(shape))


def chunk_ends(bcs, raw, u, g, bias, rates, n_streams):
    n_rows, n_chan = raw.shape[0] // n_streams, raw.shape[1]
    n_state = rates.shape[0]
    width = min(512, n_chan)
    row, thin, chan, rate, edge, total, head = scan_specs(
        n_streams, n_rows, n_chan, n_state, width
    )
    count = (2 * n_state + 1) * LANE
    return pl.pallas_call(
        functools.partial(ends_kernel, n_state),
        grid=(n_streams, n_chan // width),
        in_specs=[thin, whole((LANE, count)), row, row, row, chan, rate],
        out_specs=[
            edge, edge, total, head, head, pl.BlockSpec((1, 1, width), lambda b, c: (b, 0, c)),
        ],
        out_shape=[
            jax.ShapeDtypeStruct((n_streams, n_state, SUB, n_chan), F32),
            jax.ShapeDtypeStruct((n_streams, n_state, SUB, n_chan), F32),
            jax.ShapeDtypeStruct((n_streams, SUB, n_chan), F32),
            jax.ShapeDtypeStruct((n_streams, n_state, n_chan), F32),
            jax.ShapeDtypeStruct((n_streams, n_state, n_chan), F32),
            jax.ShapeDtypeStruct((n_streams, 1, n_chan), F32),
        ],
        scratch_shapes=[pltpu.VMEM((n_rows, count), F32)]
        + [pltpu.VMEM((n_rows, width), F32)] * 3,
        compiler_params=pltpu.CompilerParams(vmem_limit_bytes=48 * 2**20),
        name="chunk_ends",
    )(bcs, spread_matrix(n_state), raw, u, g, bias, rates)


def join_kernel(
    n_seq, first_ref, last_ref, span_ref, rate_ref, head_ref, tail_ref,
    run_s, span_s, gap_s, send_s, land_s, span_send, span_land, send_sems, recv_sems,
):
    seq, wt = lax.axis_index("seq"), lax.axis_index("wt")
    rounds = n_seq.bit_length() - 1
    n_streams = first_ref.shape[0]
    barrier = pltpu.get_barrier_semaphore()
    count = 0
    for r in range(rounds):
        d = 2**r
        for inside, other in ((seq + d < n_seq, seq + d), (seq >= d, seq - d)):

            @pl.when(inside)
            def _():
                pl.semaphore_signal(
                    barrier, inc=1, device_id=(lax.rem(other + n_seq, n_seq), wt),
                    device_id_type=MESH,
                )

            count = count + inside.astype(jnp.int32)
    pl.semaphore_wait(barrier, count)

    rate = rate_ref[...]
    head_ref[...] = jnp.zeros_like(head_ref)
    tail_ref[...] = jnp.zeros_like(tail_ref)
    gap_s[...] = jnp.zeros_like(gap_s)
    run_s[0], run_s[1] = last_ref[...], first_ref[...]
    for b in range(n_streams):
        span_s[b : b + 1, :] = span_ref[b]
        span_s[n_streams + b : n_streams + b + 1, :] = span_ref[b]
    started = []
    for r in range(rounds):
        d = 2**r
        send_s[r] = run_s[...].astype(BF16)
        span_send[r] = span_s[...]
        up, down = (seq + d < n_seq, lax.rem(seq + d, n_seq)), (seq >= d, lax.rem(seq + n_seq - d, n_seq))
        for way, (inside, other) in enumerate((up, down)):
            copies = [
                pltpu.make_async_remote_copy(
                    src_ref=src, dst_ref=dst, send_sem=send_sems.at[r, way, k],
                    recv_sem=recv_sems.at[r, way, k], device_id=(other, wt), device_id_type=MESH,
                )
                for k, (src, dst) in enumerate(
                    ((send_s.at[r, way], land_s.at[r, way]), (span_send.at[r], span_land.at[r, way]))
                )
            ]

            @pl.when(inside)
            def _():
                for copy in copies:
                    copy.start()

            started.append((inside, copies))
        for way, inside in ((0, down[0]), (1, up[0])):
            copies = started[-2 + way][1]
            out = (head_ref, tail_ref)[way]

            @pl.when(inside)
            def _():
                for copy in copies:
                    copy.wait_recv()
                for b in range(n_streams):
                    k = way * n_streams + b
                    landed = land_s[r, way, b].astype(F32)
                    span = span_land[r, way, k : k + 1, :]
                    gap, own = gap_s[k : k + 1, :], span_s[k : k + 1, :]
                    out[b] = out[b] + jnp.exp2(rate * gap) * landed
                    run_s[way, b] = run_s[way, b] + jnp.exp2(rate * own) * landed
                    gap_s[k : k + 1, :] = gap + span
                    span_s[k : k + 1, :] = own + span

    for inside, copies in started:

        @pl.when(inside)
        def _():
            for copy in copies:
                copy.wait_send()


def join_edges(first, last, span, rate):
    n_seq = lax.axis_size("seq")
    rounds = n_seq.bit_length() - 1
    n_streams, n_state, n_chan = first.shape
    vmem = pl.BlockSpec(memory_space=pltpu.VMEM)
    edges = (rounds, 2) + first.shape
    spans = (2 * n_streams, n_chan)
    return pl.pallas_call(
        functools.partial(join_kernel, n_seq),
        in_specs=[vmem] * 4,
        out_specs=[vmem] * 2,
        out_shape=[jax.ShapeDtypeStruct(first.shape, F32)] * 2,
        scratch_shapes=[
            pltpu.VMEM((2,) + first.shape, F32),
            pltpu.VMEM(spans, F32),
            pltpu.VMEM(spans, F32),
            pltpu.VMEM(edges, BF16),
            pltpu.VMEM(edges, BF16),
            pltpu.VMEM((rounds,) + spans, F32),
            pltpu.VMEM((rounds, 2) + spans, F32),
            pltpu.SemaphoreType.DMA((rounds, 2, 2)),
            pltpu.SemaphoreType.DMA((rounds, 2, 2)),
        ],
        compiler_params=pltpu.CompilerParams(
            collective_id=3, has_side_effects=True, vmem_limit_bytes=32 * 2**20
        ),
        name="join_edges",
    )(first, last, span, rate)


def scan_all(
    bcs, raw, u, g, gate, d_gated, bias, skip, rates, ends, leads, totals, heads, tails, n_streams
):
    n_rows, n_chan = raw.shape[0] // n_streams, raw.shape[1]
    n_state = rates.shape[0]
    width = min(512, n_chan)
    row, thin, chan, rate, edge, total, head = scan_specs(
        n_streams, n_rows, n_chan, n_state, width
    )
    count = (2 * n_state + 1) * LANE
    spread = spread_matrix(n_state)
    gather = spread[:, : 2 * n_state * LANE].T.astype(F32)
    rows = jax.ShapeDtypeStruct(raw.shape, BF16)
    return pl.pallas_call(
        functools.partial(scan_kernel, n_state),
        grid=(n_streams, n_chan // width),
        in_specs=[
            thin, whole((LANE, count)), whole(gather.shape), row, row, row, row, row,
            chan, chan, rate, edge, edge, total, head, head,
        ],
        out_specs=[
            row, pl.BlockSpec((width, n_rows), lambda b, c: (c, b)), row, row, row, thin,
            whole((n_state, SUB, n_chan)), whole((2, SUB, n_chan)),
        ],
        out_shape=[
            rows, jax.ShapeDtypeStruct(raw.shape[::-1], BF16), rows, rows, rows,
            jax.ShapeDtypeStruct((raw.shape[0], LANE), F32),
            jax.ShapeDtypeStruct((n_state, SUB, n_chan), F32),
            jax.ShapeDtypeStruct((2, SUB, n_chan), F32),
        ],
        scratch_shapes=[
            pltpu.VMEM((n_rows, count), F32),
            pltpu.VMEM((n_rows, 2 * n_state * LANE), F32),
        ]
        + [pltpu.VMEM((n_rows, width), F32)] * 7
        + [pltpu.VMEM((NBLK, n_rows, width), F32)] * 2,
        compiler_params=pltpu.CompilerParams(vmem_limit_bytes=56 * 2**20),
        name="scan_all",
    )(
        bcs, spread, gather, raw, u, g, gate, d_gated, bias, skip, rates,
        ends, leads, totals, heads, tails,
    )


def flip(index, bit):
    return index + (1 - 2 * ((index // 2**bit) % 2)) * 2**bit


def bit_of(index, bit):
    return (index // 2**bit) % 2


def pick(left, bit, value):
    return tuple(value if b == bit else slice(None) for b in left)


def over_blocks(count, rows, body):
    tile = math.gcd(rows, 32)
    per_block = rows // tile

    def one(i, carry):
        block, row = i // per_block, (i % per_block) * tile
        index = tuple((block // 2 ** (count - 1 - k)) % 2 for k in range(count))
        body(index, pl.ds(pl.multiple_of(row, tile), tile))
        return carry

    lax.fori_loop(0, 2**count * per_block, one, 0)


class Halving:
    def __init__(self, copies, source, dims, order, columns, landing, final, me, peer):
        self.copies, self.source, self.dims, self.order = copies, source, dims, order
        self.columns, self.landing, self.final = columns, landing, final
        self.me, self.peer = me, peer
        self.moves = []

    def left(self, stage):
        return [b for b in self.dims if b not in self.order[:stage]]

    def send(self, stage):
        bit = self.order[stage]
        other = pick(self.left(stage), bit, 1 - bit_of(self.me, bit))
        if stage == 0:
            block = self.source.at[other + (slice(None), self.columns)]
        else:
            block = self.landing[stage - 1].at[other]
        self.moves.append(self.copies.remote(block, self.landing[stage], self.peer(bit)))

    def add(self, stage):
        self.moves[stage].wait_recv()
        mine = bit_of(self.me, self.order[stage])
        left, after = self.left(stage), self.left(stage + 1)
        landed = self.landing[stage]

        def body(index, rows):
            at = iter(index)
            full = tuple(mine if b == self.order[stage] else next(at) for b in left)
            if stage == 0:
                kept = self.source[full + (rows, self.columns)]
            else:
                kept = self.landing[stage - 1][full + (rows, slice(None))]
            total = kept.astype(F32) + landed[index + (rows, slice(None))].astype(F32)
            if after:
                landed[index + (rows, slice(None))] = total.astype(BF16)
            else:
                self.final(rows, total)

        over_blocks(len(after), landed.shape[-2], body)


class Group:
    def __init__(self, members, done=None):
        self.members, self.done, self.stage = members, done, 0

    def launch(self):
        for job in self.members:
            job.send(0)

    def step(self):
        stages = len(self.members[0].order)
        if self.stage == stages:
            return False
        for job in self.members:
            job.add(self.stage)
            if self.stage + 1 < stages:
                job.send(self.stage + 1)
        self.stage += 1
        if self.stage == stages and self.done:
            self.done()
        return True

    def release(self):
        for job in self.members:
            job.moves[0].wait_send()
            job.copies.drop(job.moves[0])


def finish_kernel(
    n_seq, n_wt, n_state,
    gated_t_ref, dgate_ref, dscan_ref, draw_ref, u_ref, conv_ref, grad_ref, normed_t_ref, win_ref,
    dbc_ref, low_ref, wxd_ref, wxb_ref, wdt_ref, wconv_ref, bconv_ref, da_ref, a_ref, sums_ref,
    feat_out, chan_out, norm_out, gain_out,
    *scratch,
):
    scratch = list(scratch)
    take = lambda count: [scratch.pop(0) for _ in range(count)]
    seq, wt = lax.axis_index("seq"), lax.axis_index("wt")
    seq_bits, wt_bits = n_seq.bit_length() - 1, n_wt.bit_length() - 1
    seq_peer = lambda bit: (flip(seq, bit), wt)
    wt_peer = lambda bit: (seq, flip(wt, bit))
    flat = n_seq * wt + (seq % 2) * (n_seq // 2) + seq // 2
    owner = (flat // n_wt, flat % n_wt)
    here = n_wt * seq + wt
    block = here % n_seq
    giver = ((block % (n_seq // 2)) * 2 + block // (n_seq // 2), here // n_seq)
    elsewhere = flat != here
    ahead, behind = (lax.rem(seq + 1, n_seq), wt), (lax.rem(seq + n_seq - 1, n_seq), wt)

    barrier = pltpu.get_barrier_semaphore()
    partners = [seq_peer(b) for b in range(seq_bits)]
    partners += [(seq, turn(wt, mask, wt_bits)) for mask in range(1, n_wt)]
    partners += [ahead, behind]
    for partner in partners:
        pl.semaphore_signal(barrier, inc=1, device_id=partner, device_id_type=MESH)

    @pl.when(elsewhere)
    def _():
        for partner in (owner, giver):
            pl.semaphore_signal(barrier, inc=1, device_id=partner, device_id_type=MESH)

    (
        gated_t, dgate, dscan, draw, normed_t, grads, win_rows, conv, d_conv, mix, half, land, fin,
        ddt, dbc, pack, rim_f, rim_s, fin_feat, fin_chan, w_rows, gain_sum, small, send_sems,
        recv_sems,
    ) = take(25)
    wout_parts, feat_parts, norm_parts = take(4), take(2), take(2)
    copies = Copies(send_sems, recv_sems)
    n_chan, all_rows = gated_t.shape
    n_feat = normed_t.shape[0]
    n_rows = all_rows // n_wt
    taps = wconv_ref.shape[0]
    steps = n_rows // SUB
    rim = (taps - 1) * SUB
    cols = 512

    def load(src, dst):
        return copies.local(src, dst)

    def grad_block(k):
        return load(grad_ref.at[:, :, k * cols : (k + 1) * cols], grads.at[k % 2])

    coming = {
        "gated": load(gated_t_ref, gated_t),
        0: grad_block(0),
        1: grad_block(1),
        "draw": load(draw_ref, draw),
        "normed": load(normed_t_ref, normed_t),
        "dgate": load(dgate_ref, dgate),
        "conv": load(conv_ref.at[:, :, :cols], conv),
        "dscan": load(dscan_ref.at[:, :cols], dscan),
        "w_rows": load(
            win_ref.at[pl.ds(pl.multiple_of(seq * w_rows.shape[0], 16), w_rows.shape[0])], w_rows
        ),
        "win": load(win_ref.at[:256], win_rows.at[0]),
    }
    pl.semaphore_wait(barrier, len(partners) + 2 * elsewhere.astype(jnp.int32))

    def seq_group(source, name, at, done):
        width = source.shape[-1]
        first = tuple(range(seq_bits))
        second = (1, 0) + first[2:]
        dims = list(reversed(first))
        if name == "chan":
            dims = [0] + dims[:-1]
        members = []
        for start, size, order in ((0, width - LANE, first), (width - LANE, LANE, second)):

            def final(rows, total, start=start, size=size):
                columns = slice(at + start, at + start + size)
                if name == "chan":
                    fin_chan[rows, columns] = total.astype(BF16)
                else:
                    fin_feat[rows, columns] = total

            members.append(
                Halving(
                    copies, source, dims, order, slice(start, start + size), take(seq_bits), final,
                    seq, seq_peer,
                )
            )
        return Group(members, done)

    rows_own = feat_out.shape[0]

    def own_rows(w):
        return pl.ds(pl.multiple_of(w * rows_own, 8), rows_own)

    delivered = []

    def to_wt(block_of, place):
        for mask in range(1, n_wt):
            peer = turn(wt, mask, wt_bits)
            delivered.append(copies.remote(block_of(peer), place, (seq, peer)).wait_recv)
        delivered.append(copies.local(block_of(wt), place).wait)

    def feat_done(at):
        tile = math.gcd(w_rows.shape[0], 32)

        def body(i, carry):
            rows = pl.ds(pl.multiple_of(i * tile, tile), tile)
            product = w_rows[rows, at : at + cols].astype(F32) * fin_feat[rows, at : at + cols]
            gain_sum[rows, :] += fold(product)
            return carry

        lax.fori_loop(0, w_rows.shape[0] // tile, body, 0)
        start = pl.multiple_of(((at // n_chan) * n_wt + wt) * n_chan + at % n_chan, LANE)
        to_wt(
            lambda w: fin_feat.at[own_rows(w), at : at + cols],
            feat_out.at[:, pl.ds(start, cols)],
        )

    moved = []

    def chan_done(at, width):
        k, copies.count = copies.count, copies.count + 1
        place, target = fin_chan.at[:, at : at + width], chan_out.at[:, at : at + width]
        away = pltpu.make_async_remote_copy(
            src_ref=place, dst_ref=target, send_sem=send_sems.at[k], recv_sem=recv_sems.at[k],
            device_id=owner, device_id_type=MESH,
        )
        home = pltpu.make_async_copy(place, target, send_sems.at[k])
        moved.append((away, home))

        @pl.when(elsewhere)
        def _():
            away.start()

        @pl.when(jnp.logical_not(elsewhere))
        def _():
            home.start()

    def fill(target, at, value):
        rows = target.shape[-2]
        lead = len(target.shape) - 2
        inner = (value.shape[0] // rows).bit_length() - 1
        index = tuple((at // 2 ** (lead - 1 - k)) % 2 for k in range(lead - inner))
        target[index] = value.reshape((2,) * inner + (rows, value.shape[1])).astype(BF16)

    def by_tiles(target, rows, value_of):
        tile = min(512, rows)

        def one(i, carry):
            m = pl.multiple_of(i * tile, tile)
            fill(target, i * (tile // target.shape[-2]), value_of(pl.ds(m, tile)))
            return carry

        lax.fori_loop(0, rows // tile, one, 0)

    wout_groups = []
    for k in range(4):
        done = functools.partial(chan_done, k * cols, cols)
        wout_groups.append(seq_group(wout_parts[k], "chan", k * cols, done))

    def wout(k):
        coming[k].wait()
        right = grads[k % 2].reshape(all_rows, cols)
        by_tiles(
            wout_parts[k], n_chan,
            lambda m: jnp.dot(gated_t[m, :], right, preferred_element_type=F32),
        )
        wout_groups[k].launch()
        if k + 2 < 4:
            coming[k + 2] = grad_block(k + 2)

    gain_sum[...] = jnp.zeros_like(gain_sum)
    coming["gated"].wait()
    wout(0)
    wout(1)

    coming["draw"].wait()
    for b in range(n_wt):
        at = slice(b * n_rows, (b + 1) * n_rows)
        mix[at, :] = jnp.dot(draw[at, :], wdt_ref[...], preferred_element_type=F32)
    width = LANE // n_wt
    packed = dbc_ref[:n_rows, :]
    for b in range(1, n_wt):
        packed = packed + pltpu.roll(dbc_ref[b * n_rows : (b + 1) * n_rows, :], b * width, 1)
    mix[all_rows:, :] = packed
    mixed = WtSum(copies, mix, half, land, fin, seq, wt, wt_bits)
    mixed.begin()
    wout(2)
    for bit in range(1, wt_bits):
        mixed.middle(bit)
    wout(3)
    wout_groups[0].step()
    pack[LANE : 2 * LANE, :] = lax.dot_general(
        low_ref[...], draw[...], (((0,), (0,)), ((), ())), preferred_element_type=F32
    )
    mixed.end_send()

    coming["normed"].wait()
    coming["dgate"].wait()
    feat_groups = [None] * 4
    for k in (2, 3):
        done = functools.partial(feat_done, k * cols)
        feat_groups[k] = seq_group(feat_parts[k - 2], "feat", k * cols, done)

    def feat(k, right):
        part = feat_parts[k % 2]
        by_tiles(
            part, n_feat, lambda m: jnp.dot(normed_t[m, :], right, preferred_element_type=F32)
        )
        feat_groups[k].launch()

    feat(2, dgate[:, :cols])
    wout_groups[1].step()
    wout_groups[0].step()
    mixed.copy.wait_recv()
    ddt[...] = fin[:all_rows, :].astype(BF16)
    lane = lax.broadcasted_iota(jnp.int32, (n_rows, LANE), 1)
    for b in range(n_wt):
        part = fin[all_rows:, :]
        if b:
            part = pltpu.roll(part, LANE - b * width, 1)
        dbc[b * n_rows : (b + 1) * n_rows, :] = jnp.where(lane < width, part, 0.0).astype(BF16)
    coming["u"] = load(u_ref, gated_t)

    def sums_of(total):
        return jnp.sum(total, 0, keepdims=True)

    pack[2 * LANE :, :] = jnp.zeros((LANE, n_chan), F32)
    tail_at = 2 * LANE + 2 * n_state
    for n in range(n_state):
        pack[tail_at + n : tail_at + n + 1, :] = sums_of(da_ref[n]) * a_ref[n : n + 1, :]
    tail_at += n_state
    for k in range(2):
        at = tail_at + taps + 1 + k
        pack[at : at + 1, :] = sums_of(sums_ref[k])

    chunk = lax.broadcasted_iota(jnp.int32, (SUB, cols), 0)
    rim_moves = []

    def conv_first(h):
        at = slice(h * cols, (h + 1) * cols)
        for b in range(n_wt):
            rows = slice(b * n_rows, (b + 1) * n_rows)
            d_in = lax.dot_general(
                ddt[rows, :], wxd_ref[at, :], (((1,), (1,)), ((), ())), preferred_element_type=F32
            )
            d_in = d_in + lax.dot_general(
                dbc[rows, :], wxb_ref[at, :], (((1,), (1,)), ((), ())), preferred_element_type=F32
            )
            d_conv[b, :n_rows, :] = d_in
        coming["conv"].wait()
        coming["dscan"].wait()

        def one(i, carry):
            b, j = i // (n_rows // 16), i % (n_rows // 16)
            rows = pl.ds(pl.multiple_of(j * 16, 16), 16)
            taken = [
                conv[b, pl.ds(pl.multiple_of(j * 16 + k * SUB, SUB), 16), :] for k in range(taps)
            ]
            out = bconv_ref[:, at]
            for k in range(taps):
                out = out + taken[k] * wconv_ref[k : k + 1, at]
            sig = jax.nn.sigmoid(out)
            from_scan = dscan[pl.ds(pl.multiple_of(i * 16, 16), 16), :].astype(F32)
            value = (d_conv[b, rows, :] + from_scan) * sig * (1.0 + out * (1.0 - sig))
            d_conv[b, rows, :] = value
            found = [value] + [value * piece for piece in taken]
            return tuple(c + f[:SUB] + f[SUB:] for c, f in zip(carry, found))

        zero = jnp.zeros((SUB, cols), F32)
        totals = lax.fori_loop(0, all_rows // 16, one, (zero,) * (taps + 1))
        pack[tail_at + taps : tail_at + taps + 1, at] = sums_of(totals[0])
        for k in range(taps):
            pack[tail_at + k : tail_at + k + 1, at] = sums_of(totals[k + 1])

        rim_f[...] = jnp.zeros_like(rim_f)
        for b in range(n_wt):
            for k in range(taps - 1):
                rim_f[b * (taps - 1) + k, :] = d_conv[b, k * SUB, :]
        rim_s[h, 0] = rim_f[...].astype(BF16)

        @pl.when(seq == n_seq - 1)
        def _():
            rim_s[h, 1] = jnp.zeros((16, cols), BF16)

        k, copies.count = copies.count, copies.count + 1
        move = pltpu.make_async_remote_copy(
            src_ref=rim_s.at[h, 0], dst_ref=rim_s.at[h, 1], send_sem=send_sems.at[k],
            recv_sem=recv_sems.at[k], device_id=behind, device_id_type=MESH,
        )
        rim_moves.append(move)

        @pl.when(seq > 0)
        def _():
            move.start()

        if h == 0:
            coming["conv"] = load(conv_ref.at[:, :, cols : 2 * cols], conv)
            coming["dscan"] = load(dscan_ref.at[:, cols : 2 * cols], dscan)

    def conv_second(h):
        at = slice(h * cols, (h + 1) * cols)

        @pl.when(seq < n_seq - 1)
        def _():
            rim_moves[h].wait_recv()

        landed = rim_s[h, 1].astype(F32)
        for b in range(n_wt):
            for k in range(taps - 1):
                turned = pltpu.roll(d_conv[b, k * SUB : (k + 1) * SUB, :], SUB - 1, 0)
                row = landed[b * (taps - 1) + k : b * (taps - 1) + k + 1, :]
                place = slice(n_rows + k * SUB, n_rows + (k + 1) * SUB)
                d_conv[b, place, :] = jnp.where(chunk == SUB - 1, row, turned)

        def one(i, carry):
            b, j = i // (n_rows // 16), i % (n_rows // 16)
            total = jnp.zeros((16, cols), F32)
            for k in range(taps):
                start = pl.multiple_of(j * 16 + (taps - 1 - k) * SUB, SUB)
                total = total + d_conv[b, pl.ds(start, 16), :] * wconv_ref[k : k + 1, at]
            draw[pl.ds(pl.multiple_of(i * 16, 16), 16), at] = total.astype(BF16)
            return carry

        lax.fori_loop(0, all_rows // 16, one, 0)

    conv_first(0)
    wout_groups[2].step()
    wout_groups[1].step()
    wout_groups[0].step()
    feat(3, dgate[:, cols:])
    conv_second(0)
    wout_groups[3].step()
    wout_groups[2].step()
    wout_groups[1].step()
    conv_first(1)
    coming["u"].wait()
    pack[:LANE, :] = lax.dot_general(
        ddt[...], gated_t[...], (((0,), (0,)), ((), ())), preferred_element_type=F32
    )
    for_b = lax.dot_general(
        dbc[...], gated_t[...], (((0,), (0,)), ((), ())), preferred_element_type=F32
    )
    pack[2 * LANE : 2 * LANE + 2 * n_state, :] = for_b[: 2 * n_state, :]
    conv_second(1)
    small_at = 4 * cols
    small_group = seq_group(
        small, "chan", small_at, functools.partial(chan_done, small_at, small.shape[-1])
    )
    for k in range(2):
        done = functools.partial(feat_done, k * cols)
        feat_groups[k] = seq_group(feat_parts[k], "feat", k * cols, done)
    tile = min(512, n_chan)
    for m in range(0, n_chan, tile):
        fill(small, m // small.shape[-2], pack[:, m : m + tile].T)
    small_group.launch()
    feat_groups[2].step()
    wout_groups[3].step()
    wout_groups[2].step()

    norm_groups = []
    per = cols // 256
    for k in range(n_feat // cols):

        def final(rows, total, k=k):
            norm_out[rows, k * cols : (k + 1) * cols] = total

        order = tuple(range(wt_bits))
        job = Halving(
            copies, norm_parts[k % 2], list(reversed(order)), order, slice(0, cols), take(wt_bits),
            final, wt, wt_peer,
        )
        norm_groups.append(Group([job]))

    def norm(k):
        if k >= 2:
            norm_groups[k - 2].release()
        for part in range(per):
            i = k * per + part
            coming["win"].wait()
            if i + 1 < per * len(norm_groups):
                coming["win"] = load(
                    win_ref.at[(i + 1) * 256 : (i + 2) * 256], win_rows.at[(i + 1) % 2]
                )
            rows_w = win_rows[i % 2]
            for b in range(n_wt):
                at = slice(b * n_rows, (b + 1) * n_rows)
                value = lax.dot_general(
                    draw[at, :], rows_w[:, :n_chan], (((1,), (1,)), ((), ())),
                    preferred_element_type=F32,
                )
                value = value + lax.dot_general(
                    dgate[at, :], rows_w[:, n_chan:], (((1,), (1,)), ((), ())),
                    preferred_element_type=F32,
                )
                index = tuple((b >> (wt_bits - 1 - q)) & 1 for q in range(wt_bits))
                norm_parts[k % 2][index + (slice(None), slice(part * 256, (part + 1) * 256))] = (
                    value.astype(BF16)
                )
        norm_groups[k].launch()

    coming["w_rows"].wait()
    norm(0)
    feat_groups[3].step()
    feat_groups[2].step()
    wout_groups[3].step()
    feat_groups[2].release()
    feat(0, draw[:, :cols])
    norm(1)
    norm_groups[0].step()
    small_group.step()
    feat_groups[3].step()
    feat_groups[2].step()
    feat_groups[3].release()
    feat(1, draw[:, cols:])
    norm(2)
    norm_groups[1].step()
    norm(3)
    rest = wout_groups + [feat_groups[2], feat_groups[3], small_group, feat_groups[0], feat_groups[1]]
    for group in norm_groups[2:]:
        group.step()
    going = True
    while going:
        going = False
        for group in rest:
            going = group.step() or going
    going = True
    while going:
        going = False
        for group in norm_groups:
            going = group.step() or going
    to_wt(lambda w: gain_sum.at[own_rows(w)], gain_out.at[wt])
    for wait in delivered:
        wait()
    for away, home in moved:

        @pl.when(elsewhere)
        def _():
            away.wait()

        @pl.when(jnp.logical_not(elsewhere))
        def _():
            home.wait()

    for move in rim_moves:

        @pl.when(seq > 0)
        def _():
            move.wait_send()

    copies.finish()


def finish_all(
    gated_t, d_gate, d_scan_in, d_raw, inputs, conv, grads, normed_t, w_in,
    d_bc, dt_low, wx_dt, wx_bc, w_dt, w_conv, b_conv, d_rate, a_neg, sums,
):
    n_seq, n_wt = lax.axis_size("seq"), lax.axis_size("wt")
    seq_bits, wt_bits = n_seq.bit_length() - 1, n_wt.bit_length() - 1
    n_chan, all_rows = gated_t.shape
    n_feat, n_rows = normed_t.shape[0], all_rows // n_wt
    n_state, taps = a_neg.shape[0], w_conv.shape[0]
    cols = 512
    chan_rows, feat_rows = n_chan // n_seq, n_feat // n_seq
    size = (all_rows + n_rows) // 2
    chan_cols = 4 * cols + 3 * LANE
    square = ((all_rows, n_chan), BF16)
    scratch = [
        ((n_chan, all_rows), BF16), square, ((all_rows, cols), BF16), square,
        (normed_t.shape, BF16), ((2, n_wt, n_rows, cols), BF16), ((2, 256, 2 * n_chan), BF16),
        ((n_wt, conv.shape[1], cols), F32), ((n_wt, conv.shape[1], cols), F32),
        ((2 * size, LANE), F32), ((wt_bits, size, LANE), F32), ((wt_bits, size, LANE), F32),
        ((2 * size, LANE), F32), ((all_rows, LANE), BF16), ((all_rows, LANE), BF16),
        ((3 * LANE, n_chan), F32), ((16, cols), F32), ((2, 2, 16, cols), BF16),
        ((feat_rows, 2 * n_chan), F32), ((chan_rows, chan_cols), BF16),
        ((feat_rows, 2 * n_chan), BF16), ((feat_rows, LANE), F32),
        ((2,) * seq_bits + (chan_rows, 3 * LANE), BF16),
    ]
    scratch = [pltpu.VMEM(*item) for item in scratch]
    scratch += [pltpu.SemaphoreType.DMA((180,))] * 2
    blocks = (2,) * seq_bits
    scratch += [pltpu.VMEM(blocks + (chan_rows, cols), BF16)] * 4
    scratch += [pltpu.VMEM(blocks + (feat_rows, cols), BF16)] * 2
    scratch += [pltpu.VMEM((2,) * wt_bits + (n_rows, cols), BF16)] * 2

    def landings(bits, rows, widths):
        for width in widths:
            for stage in range(bits):
                scratch.append(pltpu.VMEM((2,) * (bits - 1 - stage) + (rows, width), BF16))

    pair = (cols - LANE, LANE)
    landings(seq_bits, chan_rows, pair * 4)
    landings(seq_bits, feat_rows, pair * 2)
    landings(seq_bits, chan_rows, (2 * LANE, LANE))
    landings(seq_bits, feat_rows, pair * 2)
    landings(wt_bits, n_rows, (cols,) * (n_feat // cols))
    hbm = pl.BlockSpec(memory_space=pl.ANY)
    vmem = pl.BlockSpec(memory_space=pltpu.VMEM)
    return pl.pallas_call(
        functools.partial(finish_kernel, n_seq, n_wt, n_state),
        in_specs=[hbm] * 9 + [vmem] * 10,
        out_specs=[hbm, hbm, vmem, hbm],
        out_shape=[
            jax.ShapeDtypeStruct((feat_rows // n_wt, 2 * n_chan * n_wt), F32),
            jax.ShapeDtypeStruct((chan_rows, chan_cols), BF16),
            jax.ShapeDtypeStruct((n_rows, n_feat), F32),
            jax.ShapeDtypeStruct((n_wt, feat_rows // n_wt, LANE), F32),
        ],
        scratch_shapes=scratch,
        compiler_params=pltpu.CompilerParams(
            collective_id=1, has_side_effects=True, vmem_limit_bytes=63 * 2**20
        ),
        name="finish_all",
    )(
        gated_t, d_gate, d_scan_in, d_raw, inputs, conv, grads, normed_t, w_in,
        d_bc, dt_low, wx_dt, wx_bc, w_dt, w_conv, b_conv, d_rate, a_neg, sums,
    )


def turn(index, mask, bits):
    for bit in range(bits):
        if mask >> bit & 1:
            index = flip(index, bit)
    return index


class Copies:
    def __init__(self, send_sems, recv_sems):
        self.send_sems, self.recv_sems = send_sems, recv_sems
        self.count, self.open = 0, []

    def remote(self, src, dst, peer):
        k, self.count = self.count, self.count + 1
        copy = pltpu.make_async_remote_copy(
            src_ref=src, dst_ref=dst, send_sem=self.send_sems.at[k],
            recv_sem=self.recv_sems.at[k], device_id=peer, device_id_type=MESH,
        )
        copy.start()
        self.open.append(copy)
        return copy

    def local(self, src, dst):
        k, self.count = self.count, self.count + 1
        copy = pltpu.make_async_copy(src, dst, self.send_sems.at[k])
        copy.start()
        return copy

    def drop(self, copy):
        self.open = [other for other in self.open if other is not copy]

    def finish(self):
        for copy in self.open:
            copy.wait_send()


class WtSum:
    def __init__(self, copies, mix, half, land, total, seq, wt, bits):
        self.copies, self.mix, self.half, self.land, self.total = copies, mix, half, land, total
        self.seq, self.wt, self.bits = seq, wt, bits
        size = mix.shape[0] // 2
        mine = bit_of(wt, 0)
        self.kept = pl.ds(pl.multiple_of(mine * size, 16), size)
        self.given = pl.ds(pl.multiple_of((1 - mine) * size, 16), size)

    def begin(self):
        peer = (self.seq, flip(self.wt, 0))
        self.copy = self.copies.remote(self.mix.at[self.given], self.land.at[0], peer)

    def middle(self, bit):
        self.copy.wait_recv()
        kept = self.mix[self.kept, :] if bit == 1 else self.half[bit - 2]
        self.half[bit - 1] = kept + self.land[bit - 1]
        peer = (self.seq, flip(self.wt, bit))
        self.copy = self.copies.remote(self.half.at[bit - 1], self.land.at[bit], peer)

    def end(self):
        self.end_send()
        self.copy.wait_recv()

    def end_send(self):
        bits = self.bits
        self.copy.wait_recv()
        kept = self.mix[self.kept, :] if bits == 1 else self.half[bits - 2]
        self.half[bits - 1] = kept + self.land[bits - 1]
        self.total[self.kept, :] = self.half[bits - 1]
        peer = (self.seq, flip(self.wt, 0))
        self.copy = self.copies.remote(self.half.at[bits - 1], self.total.at[self.kept], peer)


class Gather:
    def __init__(self, copies, slots, seq, wt, bits):
        self.copies, self.slots, self.seq, self.wt, self.bits = copies, slots, seq, wt, bits
        self.arriving = {}

    def send(self, mask, src):
        slot = self.slots.at[turn(self.wt, mask, self.bits)]
        low = self.bits if mask == 0 else (mask & -mask).bit_length() - 1
        for bit in reversed(range(low)):
            peer = (self.seq, flip(self.wt, bit))
            self.arriving[mask | 1 << bit] = self.copies.remote(src, slot, peer)

    def arrive(self, mask):
        self.arriving[mask].wait_recv()
        self.send(mask, self.slots.at[turn(self.wt, mask, self.bits)])


def start_kernel(
    n_seq, n_wt,
    hidden_ref, grad_ref, gain_ref, starts_ref, win_ref, wout_ref, wconv_ref, bconv_ref, wx_ref,
    wdt_ref,
    normed_out, win_out, conv_out, gate_out, u_out, raw_out, low_out, bcs_out, dgated_out,
    dscan_out, grad_out, gain_out,
    rows_s, grads_s, gain_s, starts_s, normed_s, win_s, wout_s, conv_s, gate_s, u_s, raw_s, low_s,
    bcs_s, dgated_s, dscan_s, mix_s, fin_s, half_s, land_s, rim_s, rim_in, normed_t,
    send_sems, recv_sems,
):
    seq, wt = lax.axis_index("seq"), lax.axis_index("wt")
    bits = n_wt.bit_length() - 1
    n_rows, n_feat = hidden_ref.shape
    n_chan, shard = wout_ref.shape[0], win_ref.shape[0]
    taps = wconv_ref.shape[0]
    rim = (taps - 1) * SUB
    all_rows = n_wt * n_rows
    near_y, near_z = (flip(seq, 0), wt), (flip(seq, 1), wt)
    wt_peers = [(seq, turn(wt, mask, bits)) for mask in range(1, n_wt)]
    ahead, behind = (lax.rem(seq + 1, n_seq), wt), (lax.rem(seq + n_seq - 1, n_seq), wt)

    barrier = pltpu.get_barrier_semaphore()
    partners = wt_peers + [near_y, near_z, ahead, behind]
    for partner in partners:
        pl.semaphore_signal(barrier, inc=1, device_id=partner, device_id_type=MESH)
    pl.semaphore_wait(barrier, len(partners))

    copies = Copies(send_sems, recv_sems)
    part = shard // 4
    quarter = seq % 4

    def win_part(owner, which, at, rows, half):
        start = pl.multiple_of(owner * shard + which * part + at, 16)
        return win_s.at[pl.ds(start, rows), half * n_chan : (half + 1) * n_chan]

    def send_far(half):
        found = {}
        rows = pl.ds(pl.multiple_of(quarter * part, 16), part)
        for mask in range(2, n_wt):
            to = turn(wt, mask, bits)
            columns = pl.ds(pl.multiple_of((half * n_wt + to) * n_chan, LANE), n_chan)
            found[mask] = copies.remote(
                win_ref.at[rows, columns], win_part(wt, quarter, 0, part, half), (seq, to)
            )
        return found

    def send_near(half):
        to = flip(wt, 0)
        place = win_s.at[
            pl.ds(pl.multiple_of(wt * shard, 16), shard), half * n_chan : (half + 1) * n_chan
        ]
        columns = pl.ds(pl.multiple_of((half * n_wt + to) * n_chan, LANE), n_chan)
        own = pl.ds(pl.multiple_of((half * n_wt + wt) * n_chan, LANE), n_chan)
        return (
            copies.remote(win_ref.at[:, columns], place, (seq, to)),
            copies.local(win_ref.at[:, own], place),
        )

    def share_first(half, found):
        passed = {}
        for mask, copy in found.items():
            copy.wait_recv()
            block = win_part(turn(wt, mask, bits), quarter, 0, part, half)
            passed[mask] = (
                copies.remote(block, block, near_y), copies.remote(block, block, near_z)
            )
        return passed

    def share_second(half, passed):
        last = []
        for mask, (by_y, by_z) in passed.items():
            owner = turn(wt, mask, bits)
            by_z.wait_recv()
            block = win_part(owner, flip(quarter, 1), 0, part // 2, half)
            last.append(copies.remote(block, block, near_y))
            by_y.wait_recv()
            block = win_part(owner, flip(quarter, 0), part // 2, part // 2, half)
            last.append(copies.remote(block, block, near_z))
        return last

    def normalise(mask):
        at = turn(wt, mask, bits)
        gain = jnp.concatenate(
            [gain_s[k].astype(F32)[0:1] for k in range(n_wt)], axis=1
        )

        def body(i, carry):
            rows = pl.ds(pl.multiple_of(i * 16, 16), 16)
            x = rows_s[at, rows, :].astype(F32)
            inv = lax.rsqrt(jnp.mean(x * x, axis=1, keepdims=True) + EPS)
            place = pl.ds(pl.multiple_of(at * n_rows + i * 16, 16), 16)
            normed_s[place, :] = (x * inv * gain).astype(BF16)
            return carry

        lax.fori_loop(0, n_rows // 16, body, 0)

    far = send_far(0)
    rows = Gather(copies, rows_s, seq, wt, bits)
    gains = Gather(copies, gain_s, seq, wt, bits)
    starts = Gather(copies, starts_s, seq, wt, bits)
    own_copies = [
        copies.local(gain_ref, gain_s.at[wt]),
        copies.local(starts_ref, starts_s.at[wt]),
        copies.local(hidden_ref, rows_s.at[wt]),
    ]
    gains.send(0, gain_ref)
    rows.send(0, hidden_ref)
    near = send_near(0)
    starts.send(0, starts_ref)
    wout_copy = copies.local(wout_ref, wout_s)
    for mask in range(n_wt - 1, 0, -1):
        if mask in gains.arriving:
            gains.arrive(mask)
    for mask in range(1, n_wt):
        if mask not in (1, 2):
            gains.arriving[mask].wait_recv()
    for copy in own_copies:
        copy.wait()
    normalise(0)
    rows.arrive(1)
    normalise(1)
    passed = share_first(0, far)
    far = send_far(1)
    last = share_second(0, passed)
    near_gate = send_near(1)
    for mask in range(2, n_wt):
        rows.arrive(mask)
        if mask == 2:
            grads = Gather(copies, grads_s, seq, wt, bits)
            grad_copy = copies.local(grad_ref, grads_s.at[wt])
            grads.send(0, grad_ref)
        normalise(mask)
    results = [copies.local(gain_s, gain_out)]
    near[0].wait_recv()
    near[1].wait()
    for copy in last:
        copy.wait_recv()

    n_block, m_block = 256, 512

    def tiles(body):
        m_count = all_rows // m_block

        def one(i, carry):
            m = pl.multiple_of((i % m_count) * m_block, m_block)
            n = pl.multiple_of((i // m_count) * n_block, n_block)
            body(m, n)
            return carry

        lax.fori_loop(0, m_count * (n_chan // n_block), one, 0)

    def conv_tile(m, n):
        value = jnp.dot(
            normed_s[pl.ds(m, m_block), :], win_s[:, pl.ds(n, n_block)], preferred_element_type=F32
        )
        value = value.astype(BF16).astype(F32)
        for k in range(m_block // n_rows):
            conv_s[m // n_rows + k, rim:, pl.ds(n, n_block)] = value[k * n_rows : (k + 1) * n_rows]

    tiles(conv_tile)

    rim_s[...] = jnp.zeros_like(rim_s)
    for b in range(n_wt):
        for k in range(taps - 1):
            at = rim + n_rows - (taps - 1 - k) * SUB
            rim_s[b * (taps - 1) + k, :] = conv_s[b, at + SUB - 1, :]
    rim_s2 = rim_s[...].astype(BF16)
    rim_in[0] = rim_s2

    @pl.when(seq == 0)
    def _():
        rim_in[1] = jnp.zeros_like(rim_s2)

    k_rim, copies.count = copies.count, copies.count + 1
    rim_copy = pltpu.make_async_remote_copy(
        src_ref=rim_in.at[0], dst_ref=rim_in.at[1], send_sem=send_sems.at[k_rim],
        recv_sem=recv_sems.at[k_rim], device_id=ahead, device_id_type=MESH,
    )

    @pl.when(seq < n_seq - 1)
    def _():
        rim_copy.start()

    passed = share_first(1, far)

    def convolve(b, j):
        rows = pl.ds(pl.multiple_of(j * 16, 16), 16)
        total = bconv_ref[...] + conv_s[b, rows, :] * wconv_ref[0:1, :]
        for k in range(1, taps):
            at = pl.ds(pl.multiple_of(j * 16 + k * SUB, SUB), 16)
            total = total + conv_s[b, at, :] * wconv_ref[k : k + 1, :]
        place = pl.ds(pl.multiple_of(b * n_rows + j * 16, 16), 16)
        u_s[place, :] = (total * jax.nn.sigmoid(total)).astype(BF16)

    head = -(-(taps - 1) // 2)
    pairs = n_rows // 16

    def convolve_tail(i, carry):
        convolve(i // (pairs - head), head + i % (pairs - head))
        return carry

    lax.fori_loop(0, n_wt * (pairs - head), convolve_tail, 0)

    @pl.when(seq > 0)
    def _():
        rim_copy.wait_recv()

    rim_rows = rim_in[1].astype(F32)
    first = lax.broadcasted_iota(jnp.int32, (SUB, n_chan), 0) == 0
    for b in range(n_wt):
        for k in range(taps - 1):
            at = rim + n_rows - (taps - 1 - k) * SUB
            moved = pltpu.roll(conv_s[b, at : at + SUB, :], 1, 0)
            row = rim_rows[b * (taps - 1) + k : b * (taps - 1) + k + 1, :]
            conv_s[b, k * SUB : (k + 1) * SUB, :] = jnp.where(first, row, moved)
    lax.fori_loop(0, n_wt * head, lambda i, c: (convolve(i // head, i % head), c)[1], 0)
    results += [copies.local(conv_s, conv_out), copies.local(u_s, u_out)]

    packed = jnp.zeros((n_rows, LANE), F32)
    for b in range(n_wt):
        block = u_s[b * n_rows : (b + 1) * n_rows, :]
        mix_s[b * n_rows : (b + 1) * n_rows, :] = jnp.dot(
            block, wx_ref[:, :LANE], preferred_element_type=F32
        )
        packed = packed + jnp.dot(
            block, wx_ref[:, (b + 1) * LANE : (b + 2) * LANE], preferred_element_type=F32
        )
    mix_s[all_rows:, :] = packed
    mixed = WtSum(copies, mix_s, half_s, land_s, fin_s, seq, wt, bits)
    mixed.begin()
    last = share_second(1, passed)
    grads.arrive(1)
    starts.arrive(2)
    for bit in range(1, bits):
        mixed.middle(bit)
    mixed.end()

    low_s[...] = fin_s[:all_rows, :].astype(BF16)
    starts.arriving[1].wait_recv()
    starts.arriving[3].wait_recv()
    lane = lax.broadcasted_iota(jnp.int32, (n_rows, LANE), 1)
    width = LANE // n_wt
    for b in range(n_wt):
        moved = fin_s[all_rows:, :]
        if b:
            moved = pltpu.roll(moved, LANE - b * width, 1)
        bcs_s[b * n_rows : (b + 1) * n_rows, :] = (
            jnp.where(lane < width, moved, 0.0).astype(BF16) + starts_s[b]
        )

    def raw_tile(m, n):
        value = lax.dot_general(
            low_s[pl.ds(m, m_block), :], wdt_ref[pl.ds(n, n_block), :], (((1,), (1,)), ((), ())),
            preferred_element_type=F32,
        )
        raw_s[pl.ds(m, m_block), pl.ds(n, n_block)] = value.astype(BF16)

    tiles(raw_tile)
    results += [
        copies.local(low_s, low_out), copies.local(bcs_s, bcs_out), copies.local(raw_s, raw_out)
    ]

    for b in range(n_wt):
        at = slice(b * n_rows, (b + 1) * n_rows)
        normed_t[:, at] = normed_s[at, :].T
    results.append(copies.local(normed_t, normed_out))
    near_gate[0].wait_recv()
    near_gate[1].wait()
    for copy in last:
        copy.wait_recv()
    results.append(copies.local(win_s, win_out))

    def gate_tile(m, n):
        value = jnp.dot(
            normed_s[pl.ds(m, m_block), :], win_s[:, pl.ds(n_chan + n, n_block)],
            preferred_element_type=F32,
        )
        gate_s[pl.ds(m, m_block), pl.ds(n, n_block)] = value.astype(BF16)

    tiles(gate_tile)
    results.append(copies.local(gate_s, gate_out))
    grad_copy.wait()
    for mask in range(2, n_wt):
        grads.arrive(mask)
    wout_copy.wait()
    results.append(copies.local(grads_s, grad_out))

    def back_tile(m, n):
        b = m // n_rows
        for k in range(m_block // n_rows):
            at = pl.ds(pl.multiple_of(m + k * n_rows, n_rows), n_rows)
            d_gated = lax.dot_general(
                grads_s[b + k], wout_s[pl.ds(n, n_block), :], (((1,), (1,)), ((), ())),
                preferred_element_type=F32,
            )
            gate = gate_s[at, pl.ds(n, n_block)].astype(F32)
            dgated_s[at, pl.ds(n, n_block)] = d_gated
            dscan_s[at, pl.ds(n, n_block)] = (d_gated * gate * jax.nn.sigmoid(gate)).astype(BF16)

    tiles(back_tile)
    results += [copies.local(dgated_s, dgated_out), copies.local(dscan_s, dscan_out)]
    for copy in results:
        copy.wait()

    @pl.when(seq < n_seq - 1)
    def _():
        rim_copy.wait_send()

    copies.finish()


def start_all(hidden, grad, gain, starts, w_in, w_out, w_conv, b_conv, w_x, w_dt):
    n_seq, n_wt = lax.axis_size("seq"), lax.axis_size("wt")
    n_rows, n_feat = hidden.shape
    n_chan, taps = w_out.shape[0], w_conv.shape[0]
    rows, rim = n_wt * n_rows, (taps - 1) * SUB
    shapes = [
        ((n_feat, rows), BF16), ((n_feat, 2 * n_chan), BF16), ((n_wt, rim + n_rows, n_chan), F32),
        ((rows, n_chan), BF16), ((rows, n_chan), BF16), ((rows, n_chan), BF16), ((rows, LANE), BF16),
        ((rows, LANE), BF16), ((rows, n_chan), F32), ((rows, n_chan), BF16),
        ((n_wt, n_rows, n_feat), BF16), ((n_wt,) + gain.shape, BF16),
    ]
    normed, win, conv, gate, u, raw, low, bcs, dgated, dscan, grads, gains = shapes
    size = (rows + n_rows) // 2
    bits = n_wt.bit_length() - 1
    scratch = [
        grads, grads, gains, ((n_wt, n_rows, LANE), BF16), ((rows, n_feat), BF16), win, (w_out.shape, BF16), conv,
        gate, u, raw, low, bcs, dgated, dscan, ((2 * size, LANE), F32), ((2 * size, LANE), F32),
        ((bits, size, LANE), F32), ((bits, size, LANE), F32), ((16, n_chan), F32),
        ((2, 16, n_chan), BF16), normed,
    ]
    hbm = pl.BlockSpec(memory_space=pl.ANY)
    vmem = pl.BlockSpec(memory_space=pltpu.VMEM)
    return pl.pallas_call(
        functools.partial(start_kernel, n_seq, n_wt),
        in_specs=[hbm] * 6 + [vmem] * 4,
        out_specs=[hbm] * len(shapes),
        out_shape=[jax.ShapeDtypeStruct(*item) for item in shapes],
        scratch_shapes=[pltpu.VMEM(*item) for item in scratch]
        + [pltpu.SemaphoreType.DMA((80,))] * 2,
        compiler_params=pltpu.CompilerParams(
            collective_id=2, has_side_effects=True, vmem_limit_bytes=60 * 2**20
        ),
        name="start_all",
    )(hidden, grad, gain, starts, w_in, w_out, w_conv, b_conv, w_x, w_dt)


def dot(left, right, left_dim=1, right_dim=0):
    return lax.dot_general(
        left, right, (((left_dim,), (right_dim,)), ((), ())), preferred_element_type=F32
    )


def to_chunks(rows):
    n_rows, width = rows.shape
    return rows.reshape(SUB, n_rows // SUB, width).swapaxes(0, 1).reshape(n_rows, width)


def from_chunks(rows, n_streams):
    n_rows, width = rows.shape[0] // n_streams, rows.shape[1]
    parts = rows.reshape(n_streams, n_rows // SUB, SUB, width)
    return parts.swapaxes(1, 2).reshape(n_streams * n_rows, width)


def per_device(
    hidden_in, doc_starts, norm_gain, in_weight, conv_weight, conv_bias, x_weight,
    dt_weight, dt_bias, a_log, d_skip, out_weight, grad_output,
):
    n_wt, n_seq = lax.axis_size("wt"), lax.axis_size("seq")
    seq_at = lax.axis_index("seq")
    n_chan = out_weight.shape[0]
    taps = conv_weight.shape[1]
    dt_rank = dt_weight.shape[1]
    n_state = a_log.shape[1]
    rows_own = hidden_in[0]
    n_rows, n_feat = rows_own.shape
    steps = n_rows // SUB

    w_conv = conv_weight.astype(F32)
    starts = jnp.pad(
        to_chunks(doc_starts[0].astype(BF16)[:, None]), ((0, 0), (2 * n_state, LANE - 2 * n_state - 1))
    )
    w_x = [x_weight[:, :dt_rank]]
    for b in range(n_wt):
        w_x.append(
            jnp.pad(
                x_weight[:, dt_rank:],
                ((0, 0), (2 * n_state * b, LANE - 2 * n_state * (b + 1))),
            )
        )
    (
        normed_t, w_in, padded, gate_in, inputs, dt_raw, dt_low, bcs, d_gated, d_scanned, grad_all, gain,
    ) = start_all(
        to_chunks(rows_own), to_chunks(grad_output[0]),
        jnp.broadcast_to(norm_gain[None], (16, norm_gain.shape[0])), starts, in_weight, out_weight,
        w_conv.T, conv_bias.astype(F32)[None], jnp.concatenate(w_x, 1), dt_weight,
    )
    gain = gain[:, 0].reshape(n_feat).astype(F32)

    a_neg = -jnp.exp(a_log.astype(F32)).T
    rates = jnp.broadcast_to((a_neg * LOG2E)[:, None, :], (n_state, SUB, n_chan))
    bias = dt_bias.astype(F32)[None]
    skip = d_skip.astype(F32)[None]
    ends, leads, totals, first, last, span = chunk_ends(
        bcs, dt_raw, inputs, d_scanned, bias, rates, n_wt
    )
    head, tail = join_edges(first, last, span, a_neg * LOG2E)
    gated, gated_t, d_gate, d_scan_in, d_raw, d_bc, d_rate, sums = scan_all(
        bcs, dt_raw, inputs, d_scanned, gate_in, d_gated, bias, skip, rates,
        ends, leads, totals, head, tail, n_wt,
    )


    out_sum = lax.psum_scatter(
        dot(gated, out_weight).astype(BF16), "wt", scatter_dimension=0, tiled=True
    )
    feat_grads, chan_grads, d_normed, gain_parts = finish_all(
        gated_t, d_gate, d_scan_in, d_raw, inputs, padded, grad_all, normed_t, w_in,
        d_bc, dt_low, x_weight[:, :dt_rank],
        jnp.pad(x_weight[:, dt_rank:], ((0, 0), (0, LANE - 2 * n_state))), dt_weight,
        w_conv.T, conv_bias.astype(F32)[None], d_rate, a_neg, sums,
    )
    chan_grads = chan_grads.astype(F32)
    widths = (n_feat, dt_rank, dt_rank, 2 * n_state, n_state, taps, 1, 1, 1)
    cuts, at = [], 0
    for piece in widths:
        cuts.append(chan_grads[:, at : at + piece])
        at += piece
    d_wout, d_wx, d_wdt, d_wbc, d_loga, d_wconv, d_bconv, d_bdt, d_skips = cuts
    own = n_feat // (n_seq * n_wt)
    own_at = own * (n_wt * seq_at + lax.axis_index("wt"))
    gain_grad = jnp.sum(gain_parts, (0, 2)) / lax.dynamic_slice_in_dim(gain, own_at, own, 0)
    x = rows_own.astype(F32)
    output = x + from_chunks(out_sum, 1).astype(F32)
    d_normed = from_chunks(d_normed, 1)
    inv_rms = lax.rsqrt(jnp.mean(x * x, axis=1, keepdims=True) + EPS)
    scaled = d_normed * gain
    cubed = inv_rms * inv_rms * inv_rms
    d_rows = inv_rms * scaled - x * cubed * jnp.mean(scaled * x, axis=1, keepdims=True)
    input_grad = grad_output[0].astype(F32) + d_rows
    return (
        output[None],
        input_grad[None],
        gain_grad,
        feat_grads,
        d_wconv,
        d_bconv[:, 0],
        jnp.concatenate([d_wx, d_wbc], 1),
        d_wdt,
        d_bdt[:, 0],
        d_loga,
        d_skips[:, 0],
        d_wout,
    )


def solution(mesh):
    placed = (
        P("wt", "seq", None),
        P("wt", "seq"),
        P("wt"),
        P("wt", None),
        P("wt", None),
        P("wt"),
        P("wt", None),
        P("wt", None),
        P("wt"),
        P("wt", None),
        P("wt"),
        P("wt", None),
        P("wt", "seq", None),
    )
    every = ("seq", "wt")
    return jax.shard_map(
        per_device,
        mesh=mesh,
        in_specs=placed,
        out_specs=(
            P("wt", "seq", None),
            P("wt", "seq", None),
            P(every),
            P(every, None),
            P(every, None),
            P(every),
            P(every, None),
            P(every, None),
            P(every),
            P(every, None),
            P(every),
            P(every, None),
        ),
        check_vma=False,
    )
```

```python
import functools
import math

import jax
import jax.numpy as jnp
import ml_dtypes
import numpy as np
from jax import lax
from jax.experimental import pallas as pl
from jax.experimental.pallas import tpu as pltpu
from jax.sharding import PartitionSpec as P

EPS = 1e-05
LOG2E = 1.4426950408889634
RESET = 1e30
SUB = 8
LANE = 128
NBLK = 4
F32 = jnp.float32
BF16 = jnp.bfloat16
MESH = pl.DeviceIdType.MESH


def softplus(v):
    return jnp.maximum(v, 0.0) + jnp.log1p(jnp.exp(-jnp.abs(v)))


def wide(tile, width):
    return jnp.concatenate([tile] * (width // LANE), axis=1)


def fold(values):
    total = values[:, :LANE]
    for k in range(1, values.shape[1] // LANE):
        total = total + values[:, k * LANE : (k + 1) * LANE]
    return total


def chunk_prefix(decay, drive, reverse):
    chunk = lax.broadcasted_iota(jnp.int32, drive.shape, 0)
    for shift in (1, 2, 4):
        if reverse:
            other_decay = pltpu.roll(decay, SUB - shift, 0)
            other_drive = pltpu.roll(drive, SUB - shift, 0)
            inside = chunk < SUB - shift
        else:
            other_decay = pltpu.roll(decay, shift, 0)
            other_drive = pltpu.roll(drive, shift, 0)
            inside = chunk >= shift
        drive = jnp.where(inside, decay * other_drive + drive, drive)
        decay = jnp.where(inside, decay * other_decay, decay)
    return decay, drive


def spread_rows(bcs_ref, spread_ref, bcb):
    bcb[...] = jnp.dot(bcs_ref[...], spread_ref[...], preferred_element_type=F32)


def turn(index, mask, bits):
    for bit in range(bits):
        if mask >> bit & 1:
            index = flip(index, bit)
    return index


class Copies:
    def __init__(self, send_sems, recv_sems):
        self.send_sems, self.recv_sems = send_sems, recv_sems
        self.count, self.open = 0, []

    def remote(self, src, dst, peer):
        k, self.count = self.count, self.count + 1
        copy = pltpu.make_async_remote_copy(
            src_ref=src, dst_ref=dst, send_sem=self.send_sems.at[k],
            recv_sem=self.recv_sems.at[k], device_id=peer, device_id_type=MESH,
        )
        copy.start()
        self.open.append(copy)
        return copy

    def later(self, src_of, dst, peer):
        k, self.count = self.count, self.count + 1

        def make():
            return pltpu.make_async_remote_copy(
                src_ref=src_of(), dst_ref=dst, send_sem=self.send_sems.at[k],
                recv_sem=self.recv_sems.at[k], device_id=peer, device_id_type=MESH,
            )

        self.open.append(make)
        return make

    def local(self, src, dst):
        k, self.count = self.count, self.count + 1
        copy = pltpu.make_async_copy(src, dst, self.send_sems.at[k])
        copy.start()
        return copy

    def drop(self, copy):
        self.open = [other for other in self.open if other is not copy]

    def finish(self):
        for copy in self.open:
            (copy() if callable(copy) else copy).wait_send()


class WtSum:
    def __init__(self, copies, mix, half, land, total, seq, wt, bits):
        self.copies, self.mix, self.half, self.land, self.total = copies, mix, half, land, total
        self.seq, self.wt, self.bits = seq, wt, bits
        size = mix.shape[0] // 2
        mine = bit_of(wt, 0)
        self.kept = pl.ds(pl.multiple_of(mine * size, 16), size)
        self.given = pl.ds(pl.multiple_of((1 - mine) * size, 16), size)

    def begin(self):
        peer = (self.seq, flip(self.wt, 0))
        self.copy = self.copies.remote(self.mix.at[self.given], self.land.at[0], peer)

    def middle(self, bit):
        self.copy.wait_recv()
        kept = self.mix[self.kept, :] if bit == 1 else self.half[bit - 2]
        self.half[bit - 1] = kept + self.land[bit - 1]
        peer = (self.seq, flip(self.wt, bit))
        self.copy = self.copies.remote(self.half.at[bit - 1], self.land.at[bit], peer)

    def end(self):
        self.end_send()
        self.copy.wait_recv()

    def end_send(self):
        bits = self.bits
        self.copy.wait_recv()
        kept = self.mix[self.kept, :] if bits == 1 else self.half[bits - 2]
        self.half[bits - 1] = kept + self.land[bits - 1]
        self.total[self.kept, :] = self.half[bits - 1]
        peer = (self.seq, flip(self.wt, 0))
        self.copy = self.copies.remote(self.half.at[bits - 1], self.total.at[self.kept], peer)


def flip(index, bit):
    return index + (1 - 2 * ((index // 2**bit) % 2)) * 2**bit


def bit_of(index, bit):
    return (index // 2**bit) % 2


def pick(left, bit, value):
    return tuple(value if b == bit else slice(None) for b in left)


def over_blocks(count, rows, body):
    tile = math.gcd(rows, 32)
    per_block = rows // tile

    def one(i, carry):
        block, row = i // per_block, (i % per_block) * tile
        index = tuple((block // 2 ** (count - 1 - k)) % 2 for k in range(count))
        body(index, pl.ds(pl.multiple_of(row, tile), tile))
        return carry

    lax.fori_loop(0, 2**count * per_block, one, 0)


class Halving:
    def __init__(self, copies, source, dims, order, columns, landing, final, me, peer):
        self.copies, self.source, self.dims, self.order = copies, source, dims, order
        self.columns, self.landing, self.final = columns, landing, final
        self.mine = {bit: bit_of(me, bit) for bit in order}
        self.theirs = {bit: 1 - value for bit, value in self.mine.items()}
        self.peers = {bit: peer(bit) for bit in order}
        self.moves = []

    def left(self, stage):
        return [b for b in self.dims if b not in self.order[:stage]]

    def send(self, stage):
        bit = self.order[stage]
        other = pick(self.left(stage), bit, self.theirs[bit])

        def block():
            if stage == 0:
                return self.source.at[other + (slice(None), self.columns)]
            return self.landing[stage - 1].at[other]

        self.moves.append(self.copies.later(block, self.landing[stage], self.peers[bit]))
        self.moves[-1]().start()

    def add(self, stage):
        self.moves[stage]().wait_recv()
        mine = self.mine[self.order[stage]]
        left, after = self.left(stage), self.left(stage + 1)
        landed = self.landing[stage]

        def body(index, rows):
            at = iter(index)
            full = tuple(mine if b == self.order[stage] else next(at) for b in left)
            if stage == 0:
                kept = self.source[full + (rows, self.columns)]
            else:
                kept = self.landing[stage - 1][full + (rows, slice(None))]
            total = kept.astype(F32) + landed[index + (rows, slice(None))].astype(F32)
            if after:
                landed[index + (rows, slice(None))] = total.astype(BF16)
            else:
                self.final(rows, total)

        over_blocks(len(after), landed.shape[-2], body)


class Group:
    def __init__(self, members, done=None):
        self.members, self.done, self.stage = members, done, 0

    def launch(self):
        for job in self.members:
            job.send(0)

    def step(self):
        stages = len(self.members[0].order)
        if self.stage == stages:
            return False
        for job in self.members:
            job.add(self.stage)
            if self.stage + 1 < stages:
                job.send(self.stage + 1)
        self.stage += 1
        if self.stage == stages and self.done:
            self.done()
        return True

    def release(self):
        for job in self.members:
            job.moves[0]().wait_send()
            job.copies.drop(job.moves[0])


def fill(target, at, value):
    rows, lead = target.shape[-2], len(target.shape) - 2
    inner = (value.shape[0] // rows).bit_length() - 1
    index = tuple((at // 2 ** (lead - 1 - k)) % 2 for k in range(lead - inner))
    target[index] = value.reshape((2,) * inner + (rows, value.shape[1])).astype(BF16)


def by_tiles(target, rows, value_of):
    tile = min(512, rows)

    def one(i, carry):
        m = pl.multiple_of(i * tile, tile)
        fill(target, i * (tile // target.shape[-2]), value_of(pl.ds(m, tile)))
        return carry

    lax.fori_loop(0, rows // tile, one, 0)


def seq_orders(width, seq_bits):
    first = tuple(range(seq_bits))
    return ((0, width - LANE, first), (width - LANE, LANE, (1, 0) + first[2:]))


def seq_group(copies, source, name, take, final, seq, peer, done=None):
    seq_bits = len(source.shape) - 2
    dims = list(reversed(range(seq_bits)))
    if name == "chan":
        dims = [0] + dims[:-1]
    members = []
    for start, size, order in seq_orders(source.shape[-1], seq_bits):
        members.append(
            Halving(
                copies, source, dims, order, slice(start, start + size), take(seq_bits),
                functools.partial(final, start), seq, peer,
            )
        )
    return Group(members, done)


def landings(bits, rows, widths):
    return [
        pltpu.VMEM((2,) * (bits - 1 - stage) + (rows, width), BF16)
        for width in widths
        for stage in range(bits)
    ]


def seq_landings(seq_bits, rows, widths):
    found = []
    for width in widths:
        found += landings(seq_bits, rows, [size for _, size, _ in seq_orders(width, seq_bits)])
    return found


def parts_of(n_chan, n_seq):
    return 2 if n_chan // n_seq >= 32 else 1


WIDE = 1024
EARLY = 256


def ends_kernel(
    n_state, bcs_ref, spread_ref, raw_ref, u_ref, g_ref, bias_ref, a_ref,
    end_ref, lead_ref, total_ref, first_ref, last_ref, span_ref, bcb, dec_in, drive_in, g_in,
):
    n_rows, width = raw_ref.shape
    steps = n_rows // SUB

    @pl.when(pl.program_id(1) == 0)
    def _():
        spread_rows(bcs_ref, spread_ref, bcb)

    start_at = 2 * n_state * LANE

    def prepare(j, total):
        rows = pl.ds(pl.multiple_of(j * 16, 16), 16)
        delta = softplus(raw_ref[rows, :].astype(F32) + bias_ref[...])
        starts = wide(bcb[rows, start_at : start_at + LANE], width)
        held = jnp.where(starts > 0.5, RESET, delta)
        dec_in[rows, :] = held
        drive_in[rows, :] = delta * u_ref[rows, :].astype(F32)
        g_in[rows, :] = g_ref[rows, :].astype(F32)
        return total + held[:SUB] + held[SUB:]

    total = lax.fori_loop(0, steps // 2, prepare, jnp.zeros((SUB, width), F32))
    total_ref[0] = total
    span_ref[0] = jnp.sum(total, 0, keepdims=True)
    for first in range(0, n_state, 2):
        states = range(first, first + 2)

        def step(j, carry):
            rows = pl.ds(pl.multiple_of(j * SUB, SUB), SUB)
            held, drive, g = dec_in[rows, :], drive_in[rows, :], g_in[rows, :]
            running, products, passed = [], [], []
            for n, h, whole, p in zip(states, *carry):
                b = wide(bcb[rows, n * LANE : (n + 1) * LANE], width)
                c = wide(bcb[rows, (n_state + n) * LANE : (n_state + n + 1) * LANE], width)
                decay = jnp.exp2(held * a_ref[n])
                whole = whole * decay
                running.append(decay * h + drive * b)
                products.append(whole)
                passed.append(p + whole * (g * c))
            return tuple(running), tuple(products), tuple(passed)

        zero = tuple(jnp.zeros((SUB, width), F32) for _ in states)
        one = tuple(jnp.ones((SUB, width), F32) for _ in states)
        carry = lax.fori_loop(0, steps, step, (zero, one, zero), unroll=4)
        for n, h, decay, p in zip(states, *carry):
            end = chunk_prefix(decay, h, False)[1]
            lead = chunk_prefix(decay, p, True)[1]
            end_ref[0, n], lead_ref[0, n] = end, lead
            last_ref[0, n : n + 1, :], first_ref[0, n : n + 1, :] = end[SUB - 1 :], lead[:1]


def early_sums(n_seq, part, stream, width, grad_ref, normed_t_ref, wout_ref, feat_ref, scratch):
    gated_s, dgate_s, grads, normed_t, feat_part = scratch[:5]
    seq_bits = n_seq.bit_length() - 1
    count = grads.shape[1] // WIDE
    wout_parts, scratch = scratch[5 : 5 + count], scratch[5 + count :]
    load_sems, send_sems, recv_sems = scratch[:3]
    scratch = scratch[3:]
    take = lambda k: [scratch.pop(0) for _ in range(k)]
    seq, wt = lax.axis_index("seq"), lax.axis_index("wt")
    copies = Copies(send_sems, recv_sems)
    peer = lambda bit: (flip(seq, bit), wt)

    def loads():
        return [
            pltpu.make_async_copy(grad_ref, grads, load_sems.at[0]),
            pltpu.make_async_copy(normed_t_ref, normed_t, load_sems.at[1]),
        ]

    def wout_final(at, start, rows, total):
        wout_ref[rows, at + start : at + start + total.shape[1]] = total.astype(BF16)

    def feat_final(start, rows, total):
        feat_ref[rows, start : start + total.shape[1]] = total

    wouts = [
        seq_group(
            copies, wout_parts[k], "chan", take, functools.partial(wout_final, k * WIDE), seq, peer
        )
        for k in range(count)
    ]
    feat = seq_group(copies, feat_part, "feat", take, feat_final, seq, peer)
    groups = wouts + [feat]

    @pl.when((part == 0) & (stream == 0))
    def _():
        barrier = pltpu.get_barrier_semaphore()
        for bit in range(seq_bits):
            pl.semaphore_signal(barrier, inc=1, device_id=peer(bit), device_id_type=MESH)
        pl.semaphore_wait(barrier, seq_bits)
        for copy in loads():
            copy.start()

    @pl.when((part == 1) & (stream == 0))
    def _():
        for copy in loads():
            copy.wait()
        for k in range(count):
            for inner in range(0, WIDE, 512):
                at = k * WIDE + inner
                value = jnp.dot(
                    gated_s[...], grads[:, at : at + 512], preferred_element_type=F32
                )
                rows, lead = wout_parts[k].shape[-2], len(wout_parts[k].shape) - 2
                wout_parts[k][(slice(None),) * (lead + 1) + (slice(inner, inner + 512),)] = (
                    value.reshape((2,) * lead + (rows, 512)).astype(BF16)
                )
            wouts[k].launch()

    @pl.when((part == 1) & (stream == 1))
    def _():
        wouts[0].step()
        by_tiles(
            feat_part, normed_t.shape[0],
            lambda m: jnp.dot(normed_t[m, :], dgate_s[:, :EARLY], preferred_element_type=F32),
        )
        feat.launch()

    @pl.when((part == 1) & (stream == 2))
    def _():
        for group in reversed(wouts):
            group.step()

    @pl.when((part == 1) & (stream == 3))
    def _():
        feat.step()
        for group in reversed(wouts):
            group.step()

    def rest():
        going = True
        while going:
            going = False
            for group in reversed(groups):
                going = group.step() or going
        copies.finish()

    return rest


def scan_kernel(
    n_state, n_seq, parts, bcs_ref, spread_ref, gather_ref, raw_ref, u_ref, g_ref, gate_ref, dgated_ref,
    bias_ref, skip_ref, a_ref, end_ref, lead_ref, total_ref, head_ref, tail_ref, grad_ref,
    normed_t_ref,
    gated_ref, gated_t_ref, dgate_ref, dscan_ref, draw_ref, dbc_ref, da_ref, sums_ref, wout_ref,
    feat_ref,
    bcb, acc_all, dec_in, delta_in, drive_in, g_in, y_sum, b_sum, d_sum, kept, decays, *scratch,
):
    n_rows, width = raw_ref.shape
    steps = n_rows // SUB
    part, stream = pl.program_id(0), pl.program_id(1)
    n_streams = pl.num_programs(1)
    acc = acc_all.at[stream]
    if parts > 1:
        early_rest = early_sums(
            n_seq, part, stream, width, grad_ref, normed_t_ref, wout_ref, feat_ref, list(scratch)
        )
    start_at = 2 * n_state * LANE
    columns = pl.ds(pl.multiple_of(part * width, width), width)
    spread_rows(bcs_ref, spread_ref, bcb)

    @pl.when(part == 0)
    def _():
        acc_all[stream] = jnp.zeros(acc_all.shape[1:], F32)

    @pl.when(stream == 0)
    def _():
        da_ref[:, :, columns] = jnp.zeros((n_state, SUB, width), F32)
        sums_ref[:, :, columns] = jnp.zeros((2, SUB, width), F32)

    def prepare(j, carry):
        rows = pl.ds(pl.multiple_of(j * 16, 16), 16)
        delta = softplus(raw_ref[rows, :].astype(F32) + bias_ref[...])
        starts = wide(bcb[rows, start_at : start_at + LANE], width)
        delta_in[rows, :] = delta
        dec_in[rows, :] = jnp.where(starts > 0.5, RESET, delta)
        drive_in[rows, :] = delta * u_ref[rows, :].astype(F32)
        g_in[rows, :] = g_ref[rows, :].astype(F32)
        return carry

    lax.fori_loop(0, steps // 2, prepare, 0)
    chunk = lax.broadcasted_iota(jnp.int32, (SUB, width), 0)
    total = total_ref[0]
    before, after = total, total
    for shift in (1, 2, 4):
        before = jnp.where(chunk >= shift, before + pltpu.roll(before, shift, 0), before)
        after = jnp.where(chunk < SUB - shift, after + pltpu.roll(after, SUB - shift, 0), after)
    before, after = pltpu.roll(before, 1, 0), pltpu.roll(after, SUB - 1, 0)

    for first in range(0, n_state, NBLK):
        states = range(first, first + NBLK)
        entry, incoming = [], []
        for n in states:
            head, tail = head_ref[0, n : n + 1, :], tail_ref[0, n : n + 1, :]
            inner = pltpu.roll(end_ref[0, n], 1, 0) + jnp.exp2(before * a_ref[n]) * head
            outer = pltpu.roll(lead_ref[0, n], SUB - 1, 0) + jnp.exp2(after * a_ref[n]) * tail
            entry.append(jnp.where(chunk == 0, head, inner))
            incoming.append(jnp.where(chunk == SUB - 1, tail, outer))

        def forward(j, carry):
            rows = pl.ds(pl.multiple_of(j * SUB, SUB), SUB)
            held, drive, g = dec_in[rows, :], drive_in[rows, :], g_in[rows, :]
            running = []
            y = y_sum[rows, :] if first else None
            for k, (n, h) in enumerate(zip(states, carry)):
                b = wide(bcb[rows, n * LANE : (n + 1) * LANE], width)
                c_at = slice((n_state + n) * LANE, (n_state + n + 1) * LANE)
                c = wide(bcb[rows, c_at], width)
                decay = jnp.exp2(held * a_ref[n])
                kept[k, rows, :] = h
                decays[k, rows, :] = decay
                h = decay * h + drive * b
                y = c * h if y is None else y + c * h
                acc[rows, c_at] += fold(h * g)
                running.append(h)
            y_sum[rows, :] = y
            return tuple(running)

        lax.fori_loop(0, steps, forward, tuple(entry), unroll=4)

        def backward(j, carry):
            rows = pl.ds(pl.multiple_of((steps - 1 - j) * SUB, SUB), SUB)
            delta, drive, g = delta_in[rows, :], drive_in[rows, :], g_in[rows, :]
            through = b_sum[rows, :] if first else None
            pulled = d_sum[rows, :] if first else None
            passed, da = [], []
            for k, (n, p, da_n) in enumerate(zip(states, carry[0], carry[1])):
                b_at = slice(n * LANE, (n + 1) * LANE)
                b = wide(bcb[rows, b_at], width)
                c = wide(bcb[rows, (n_state + n) * LANE : (n_state + n + 1) * LANE], width)
                adjoint = g * c + p
                p = decays[k, rows, :] * adjoint
                weighed = p * kept[k, rows, :]
                pulled = weighed * a_ref[n] if pulled is None else pulled + weighed * a_ref[n]
                through = adjoint * b if through is None else through + adjoint * b
                acc[rows, b_at] += fold(adjoint * drive)
                passed.append(p)
                da.append(da_n + weighed * delta)
            b_sum[rows, :] = through
            d_sum[rows, :] = pulled
            return tuple(passed), tuple(da)

        zero = tuple(jnp.zeros((SUB, width), F32) for _ in states)
        _, da = lax.fori_loop(0, steps, backward, (tuple(incoming), zero), unroll=4)
        for n, da_n in zip(states, da):
            da_ref[n, :, columns] += da_n

    def finish(j, carry):
        bias_sum, skip_sum = carry
        rows = pl.ds(pl.multiple_of(j * 16, 16), 16)
        u, g, delta = u_ref[rows, :].astype(F32), g_in[rows, :], delta_in[rows, :]
        gate, d_gated = gate_ref[rows, :].astype(F32), dgated_ref[rows, :]
        scanned = (y_sum[rows, :] + skip_ref[...] * u).astype(BF16).astype(F32)
        sig = jax.nn.sigmoid(gate)
        gated_ref[rows, :] = (scanned * gate * sig).astype(BF16)
        d_gate = d_gated * scanned * sig * (1.0 + gate * (1.0 - sig))
        dgate_ref[rows, :] = d_gate.astype(BF16)
        through = b_sum[rows, :]
        dscan_ref[rows, :] = (delta * through + skip_ref[...] * g).astype(BF16)
        slope = jax.nn.sigmoid(raw_ref[rows, :].astype(F32) + bias_ref[...])
        d_pre = (d_sum[rows, :] * (1.0 / LOG2E) + u * through) * slope
        draw_ref[rows, :] = d_pre.astype(BF16)
        gu = g * u
        return bias_sum + d_pre[:SUB] + d_pre[SUB:], skip_sum + gu[:SUB] + gu[SUB:]

    zero = jnp.zeros((SUB, width), F32)
    bias_sum, skip_sum = lax.fori_loop(0, steps // 2, finish, (zero, zero))
    gated_t_ref[...] = gated_ref[...].T
    if parts > 1:
        gated_s, dgate_s = scratch[:2]

        @pl.when(part == 0)
        def _():
            at = pl.ds(pl.multiple_of(stream * n_rows, n_rows), n_rows)
            gated_s[:, at] = gated_t_ref[...]
            dgate_s[at, :] = dgate_ref[...]

    sums_ref[0, :, columns] += bias_sum
    sums_ref[1, :, columns] += skip_sum

    last = part == pl.num_programs(0) - 1

    @pl.when(last)
    def _():
        at = pl.ds(pl.multiple_of(stream * n_rows, n_rows), n_rows)
        dbc_ref[at, :] = jnp.dot(
            acc[...], gather_ref[...], precision=lax.Precision.HIGHEST, preferred_element_type=F32
        )

    if parts > 1:

        @pl.when(last & (stream == n_streams - 1))
        def _():
            early_rest()


def spread_matrix(n_state):
    count = 2 * n_state + 1
    column = np.arange(count * LANE)[None, :] // LANE
    return jnp.asarray((np.arange(LANE)[:, None] == column).astype(ml_dtypes.bfloat16))


def gather_matrix(n_state):
    row = np.arange(2 * n_state * LANE)[:, None] // LANE
    return jnp.asarray((np.arange(LANE)[None, :] == row).astype(np.float32))


def scan_specs(n_streams, n_rows, n_chan, n_state, width):
    row = pl.BlockSpec((n_rows, width), lambda b, c: (b, c))
    thin = pl.BlockSpec((n_rows, LANE), lambda b, c: (b, 0))
    chan = pl.BlockSpec((1, width), lambda b, c: (0, c))
    rate = pl.BlockSpec((n_state, SUB, width), lambda b, c: (0, 0, c))
    edge = pl.BlockSpec((1, n_state, SUB, width), lambda b, c: (b, 0, 0, c))
    total = pl.BlockSpec((1, SUB, width), lambda b, c: (b, 0, c))
    head = pl.BlockSpec((1, n_state, width), lambda b, c: (b, 0, c))
    return row, thin, chan, rate, edge, total, head


def whole(shape):
    return pl.BlockSpec(shape, lambda b, c: (0,) * len(shape))


def chunk_ends(bcs, raw, u, g, bias, rates, n_streams):
    n_rows, n_chan = raw.shape[0] // n_streams, raw.shape[1]
    n_state = rates.shape[0]
    width = min(512, n_chan)
    row, thin, chan, rate, edge, total, head = scan_specs(
        n_streams, n_rows, n_chan, n_state, width
    )
    count = (2 * n_state + 1) * LANE
    return pl.pallas_call(
        functools.partial(ends_kernel, n_state),
        grid=(n_streams, n_chan // width),
        in_specs=[thin, whole((LANE, count)), row, row, row, chan, rate],
        out_specs=[
            edge, edge, total, head, head, pl.BlockSpec((1, 1, width), lambda b, c: (b, 0, c)),
        ],
        out_shape=[
            jax.ShapeDtypeStruct((n_streams, n_state, SUB, n_chan), F32),
            jax.ShapeDtypeStruct((n_streams, n_state, SUB, n_chan), F32),
            jax.ShapeDtypeStruct((n_streams, SUB, n_chan), F32),
            jax.ShapeDtypeStruct((n_streams, n_state, n_chan), F32),
            jax.ShapeDtypeStruct((n_streams, n_state, n_chan), F32),
            jax.ShapeDtypeStruct((n_streams, 1, n_chan), F32),
        ],
        scratch_shapes=[pltpu.VMEM((n_rows, count), F32)]
        + [pltpu.VMEM((n_rows, width), F32)] * 3,
        compiler_params=pltpu.CompilerParams(vmem_limit_bytes=48 * 2**20),
        name="chunk_ends",
    )(bcs, spread_matrix(n_state), raw, u, g, bias, rates)


def join_kernel(
    n_seq, first_ref, last_ref, span_ref, rate_ref, head_ref, tail_ref,
    run_s, span_s, gap_s, send_s, land_s, span_send, span_land, send_sems, recv_sems,
):
    seq, wt = lax.axis_index("seq"), lax.axis_index("wt")
    rounds = n_seq.bit_length() - 1
    n_streams = first_ref.shape[0]
    barrier = pltpu.get_barrier_semaphore()
    count = 0
    for r in range(rounds):
        d = 2**r
        for inside, other in ((seq + d < n_seq, seq + d), (seq >= d, seq - d)):

            @pl.when(inside)
            def _():
                pl.semaphore_signal(
                    barrier, inc=1, device_id=(lax.rem(other + n_seq, n_seq), wt),
                    device_id_type=MESH,
                )

            count = count + inside.astype(jnp.int32)
    pl.semaphore_wait(barrier, count)

    rate = rate_ref[...]
    head_ref[...] = jnp.zeros_like(head_ref)
    tail_ref[...] = jnp.zeros_like(tail_ref)
    gap_s[...] = jnp.zeros_like(gap_s)
    run_s[0], run_s[1] = last_ref[...], first_ref[...]
    for b in range(n_streams):
        span_s[b : b + 1, :] = span_ref[b]
        span_s[n_streams + b : n_streams + b + 1, :] = span_ref[b]
    started = []
    for r in range(rounds):
        d = 2**r
        send_s[r] = run_s[...].astype(BF16)
        span_send[r] = span_s[...]
        up, down = (seq + d < n_seq, lax.rem(seq + d, n_seq)), (seq >= d, lax.rem(seq + n_seq - d, n_seq))
        for way, (inside, other) in enumerate((up, down)):
            copies = [
                pltpu.make_async_remote_copy(
                    src_ref=src, dst_ref=dst, send_sem=send_sems.at[r, way, k],
                    recv_sem=recv_sems.at[r, way, k], device_id=(other, wt), device_id_type=MESH,
                )
                for k, (src, dst) in enumerate(
                    ((send_s.at[r, way], land_s.at[r, way]), (span_send.at[r], span_land.at[r, way]))
                )
            ]

            @pl.when(inside)
            def _():
                for copy in copies:
                    copy.start()

            started.append((inside, copies))
        for way, inside in ((0, down[0]), (1, up[0])):
            copies = started[-2 + way][1]
            out = (head_ref, tail_ref)[way]

            @pl.when(inside)
            def _():
                for copy in copies:
                    copy.wait_recv()
                for b in range(n_streams):
                    k = way * n_streams + b
                    landed = land_s[r, way, b].astype(F32)
                    span = span_land[r, way, k : k + 1, :]
                    gap, own = gap_s[k : k + 1, :], span_s[k : k + 1, :]
                    out[b] = out[b] + jnp.exp2(rate * gap) * landed
                    run_s[way, b] = run_s[way, b] + jnp.exp2(rate * own) * landed
                    gap_s[k : k + 1, :] = gap + span
                    span_s[k : k + 1, :] = own + span

    for inside, copies in started:

        @pl.when(inside)
        def _():
            for copy in copies:
                copy.wait_send()


def join_edges(first, last, span, rate):
    n_seq = lax.axis_size("seq")
    rounds = n_seq.bit_length() - 1
    n_streams, n_state, n_chan = first.shape
    vmem = pl.BlockSpec(memory_space=pltpu.VMEM)
    edges = (rounds, 2) + first.shape
    spans = (2 * n_streams, n_chan)
    return pl.pallas_call(
        functools.partial(join_kernel, n_seq),
        in_specs=[vmem] * 4,
        out_specs=[vmem] * 2,
        out_shape=[jax.ShapeDtypeStruct(first.shape, F32)] * 2,
        scratch_shapes=[
            pltpu.VMEM((2,) + first.shape, F32),
            pltpu.VMEM(spans, F32),
            pltpu.VMEM(spans, F32),
            pltpu.VMEM(edges, BF16),
            pltpu.VMEM(edges, BF16),
            pltpu.VMEM((rounds,) + spans, F32),
            pltpu.VMEM((rounds, 2) + spans, F32),
            pltpu.SemaphoreType.DMA((rounds, 2, 2)),
            pltpu.SemaphoreType.DMA((rounds, 2, 2)),
        ],
        compiler_params=pltpu.CompilerParams(
            collective_id=3, has_side_effects=True, vmem_limit_bytes=32 * 2**20
        ),
        name="join_edges",
    )(first, last, span, rate)


def scan_all(
    bcs, raw, u, g, gate, d_gated, bias, skip, rates, ends, leads, totals, heads, tails, grads,
    normed_t,
):
    n_seq, n_streams = lax.axis_size("seq"), lax.axis_size("wt")
    n_rows, n_chan = raw.shape[0] // n_streams, raw.shape[1]
    n_state, n_feat = rates.shape[0], normed_t.shape[0]
    width = min(512, n_chan)
    parts = parts_of(n_chan, n_seq)
    seq_bits = n_seq.bit_length() - 1

    def swapped(spec):
        return pl.BlockSpec(spec.block_shape, lambda c, b: spec.index_map(b, c))

    row, thin, chan, rate, edge, total, head = map(
        swapped, scan_specs(n_streams, n_rows, n_chan, n_state, width)
    )
    count = (2 * n_state + 1) * LANE
    spread = spread_matrix(n_state)
    gather = gather_matrix(n_state)
    rows = jax.ShapeDtypeStruct(raw.shape, BF16)
    hbm = pl.BlockSpec(memory_space=pl.ANY)
    wout_rows, feat_rows = max(n_chan // parts // n_seq, 16), n_feat // n_seq
    scratch = [
        pltpu.VMEM((n_rows, count), F32),
        pltpu.VMEM((n_streams, n_rows, 2 * n_state * LANE), F32),
    ]
    scratch += [pltpu.VMEM((n_rows, width), F32)] * 7
    scratch += [pltpu.VMEM((NBLK, n_rows, width), F32)] * 2
    params = {}
    if parts > 1:
        blocks = (2,) * seq_bits
        n_wide = n_feat // WIDE
        scratch += [
            pltpu.VMEM((width, raw.shape[0]), BF16),
            pltpu.VMEM((raw.shape[0], width), BF16),
            pltpu.VMEM((raw.shape[0], n_feat), BF16),
            pltpu.VMEM(normed_t.shape, BF16),
            pltpu.VMEM(blocks + (feat_rows, EARLY), BF16),
        ]
        scratch += [pltpu.VMEM(blocks + (wout_rows, WIDE), BF16)] * n_wide
        scratch += [pltpu.SemaphoreType.DMA((2,))]
        scratch += [pltpu.SemaphoreType.DMA((2 * seq_bits * (n_wide + 1),))] * 2
        scratch += seq_landings(seq_bits, wout_rows, [WIDE] * n_wide)
        scratch += seq_landings(seq_bits, feat_rows, [EARLY])
        params = dict(collective_id=4, has_side_effects=True)
    return pl.pallas_call(
        functools.partial(scan_kernel, n_state, n_seq, parts),
        grid=(n_chan // width, n_streams),
        in_specs=[
            thin, whole((LANE, count)), whole(gather.shape), row, row, row, row, row,
            chan, chan, rate, edge, edge, total, head, head, hbm, hbm,
        ],
        out_specs=[
            row, pl.BlockSpec((width, n_rows), lambda c, b: (c, b)), row, row, row,
            whole((raw.shape[0], LANE)), whole((n_state, SUB, n_chan)), whole((2, SUB, n_chan)),
            whole((wout_rows, n_feat)), whole((feat_rows, EARLY)),
        ],
        out_shape=[
            rows, jax.ShapeDtypeStruct(raw.shape[::-1], BF16), rows, rows, rows,
            jax.ShapeDtypeStruct((raw.shape[0], LANE), F32),
            jax.ShapeDtypeStruct((n_state, SUB, n_chan), F32),
            jax.ShapeDtypeStruct((2, SUB, n_chan), F32),
            jax.ShapeDtypeStruct((wout_rows, n_feat), BF16),
            jax.ShapeDtypeStruct((feat_rows, EARLY), F32),
        ],
        scratch_shapes=scratch,
        compiler_params=pltpu.CompilerParams(vmem_limit_bytes=63 * 2**20, **params),
        name="scan_all",
    )(
        bcs, spread, gather, raw, u, g, gate, d_gated, bias, skip, rates,
        ends, leads, totals, heads, tails, grads, normed_t,
    )


def finish_kernel(
    n_seq, n_wt, n_state,
    gated_t_ref, dgate_ref, dscan_ref, draw_ref, u_ref, conv_ref, grad_ref, normed_t_ref, win_ref,
    wout_ref, feat_ref,
    dbc_ref, low_ref, wx_ref, wdt_ref, wconv_ref, bconv_ref, da_ref, a_ref, sums_ref,
    feat_out, wout_out, small_out, norm_out, gain_out,
    *scratch,
):
    scratch = list(scratch)
    take = lambda count: [scratch.pop(0) for _ in range(count)]
    seq, wt = lax.axis_index("seq"), lax.axis_index("wt")
    seq_bits, wt_bits = n_seq.bit_length() - 1, n_wt.bit_length() - 1
    seq_peer = lambda bit: (flip(seq, bit), wt)
    wt_peer = lambda bit: (seq, flip(wt, bit))
    n_chan, all_rows = gated_t_ref.shape
    parts = parts_of(n_chan, n_seq)
    ready = parts - 1
    half_seq = n_seq // 2
    here = n_wt * seq + wt
    mine = (seq % 2) * half_seq + seq // 2

    def summed_at(j):
        return (j % half_seq) * 2 + j // half_seq

    def device(flat):
        return flat // n_wt, flat % n_wt

    flat = n_seq * wt + mine
    owner, giver_block = device(flat), here % n_seq
    giver = (summed_at(giver_block), here // n_seq)
    elsewhere = flat != here
    per = n_seq // parts
    part_flat = [n_seq * wt + q * per + mine // parts for q in range(parts)]
    part_owner = [device(value) for value in part_flat]
    piece = mine % parts
    piece_giver = [
        (summed_at((giver_block % per) * parts + k), here // n_seq) for k in range(parts)
    ]
    piece_here = [n_wt * s + w == here for s, w in piece_giver]
    ahead, behind = (lax.rem(seq + 1, n_seq), wt), (lax.rem(seq + n_seq - 1, n_seq), wt)

    barrier = pltpu.get_barrier_semaphore()
    partners = [seq_peer(b) for b in range(seq_bits)]
    partners += [(seq, turn(wt, mask, wt_bits)) for mask in range(1, n_wt)]
    partners += [ahead, behind]
    for partner in partners:
        pl.semaphore_signal(barrier, inc=1, device_id=partner, device_id_type=MESH)

    arrivals = len(partners) + 2 * elsewhere.astype(jnp.int32)

    @pl.when(elsewhere)
    def _():
        for partner in (owner, giver):
            pl.semaphore_signal(barrier, inc=1, device_id=partner, device_id_type=MESH)

    if parts > 1:
        others = [(value != here, to) for value, to in zip(part_flat, part_owner)]
        others += [(jnp.logical_not(own), to) for own, to in zip(piece_here, piece_giver)]
        for away, to in others:
            arrivals = arrivals + away.astype(jnp.int32)

            @pl.when(away)
            def _():
                pl.semaphore_signal(barrier, inc=1, device_id=to, device_id_type=MESH)

    (
        gated_t, dgate, dscan, draw, normed_t, grads, win_rows, conv, d_conv, mix, half, land, fin,
        u_all, ddt, dbc, pack, rim_f, rim_s, fin_feat, fin_wout, fin_small, w_rows, gain_sum, small,
        piece_sems, send_sems, recv_sems,
    ) = take(28)
    n_wide = normed_t.shape[0] // WIDE
    wout_parts, feat_parts, norm_parts = take(n_wide), take(2), take(2)
    copies = Copies(send_sems, recv_sems)
    part_chan = gated_t.shape[0]
    n_feat = normed_t.shape[0]
    n_rows = all_rows // n_wt
    taps = wconv_ref.shape[0]
    steps = n_rows // SUB
    rim = (taps - 1) * SUB
    cols = 512

    def load(src, dst):
        return copies.local(src, dst)

    def grad_block(k):
        return load(grad_ref.at[:, :, k * cols : (k + 1) * cols], grads.at[k % 2])

    coming = {
        "gated": load(gated_t_ref.at[ready * part_chan :], gated_t),
        0: grad_block(0),
        1: grad_block(1),
        "draw": load(draw_ref, draw),
        "normed": load(normed_t_ref, normed_t),
        "dgate": load(dgate_ref, dgate),
        "conv": load(conv_ref.at[:, :, :cols], conv),
        "dscan": load(dscan_ref.at[:, :cols], dscan),
        "w_rows": load(
            win_ref.at[pl.ds(pl.multiple_of(seq * w_rows.shape[0], 16), w_rows.shape[0])], w_rows
        ),
        "win": load(win_ref.at[:256], win_rows.at[0]),
    }
    if ready:
        coming["wout"] = load(wout_ref, fin_wout.at[0])
        coming["feat"] = load(feat_ref, fin_feat.at[:, n_chan : n_chan + EARLY])
    pl.semaphore_wait(barrier, arrivals)

    rows_own = feat_out.shape[0]

    def own_rows(w):
        return pl.ds(pl.multiple_of(w * rows_own, 8), rows_own)

    delivered = []

    def to_wt(block_of, place):
        for mask in range(1, n_wt):
            peer = turn(wt, mask, wt_bits)
            delivered.append(copies.remote(block_of(peer), place, (seq, peer)).wait_recv)
        delivered.append(copies.local(block_of(wt), place).wait)

    def feat_done(at, cols):
        tile = math.gcd(w_rows.shape[0], 32)

        def body(i, carry):
            rows = pl.ds(pl.multiple_of(i * tile, tile), tile)
            product = w_rows[rows, at : at + cols].astype(F32) * fin_feat[rows, at : at + cols]
            gain_sum[rows, :] += fold(product)
            return carry

        lax.fori_loop(0, w_rows.shape[0] // tile, body, 0)
        start = pl.multiple_of(((at // n_chan) * n_wt + wt) * n_chan + at % n_chan, LANE)
        to_wt(
            lambda w: fin_feat.at[own_rows(w), at : at + cols],
            feat_out.at[:, pl.ds(start, cols)],
        )

    moved = []

    def small_done():
        k, copies.count = copies.count, copies.count + 1
        away = pltpu.make_async_remote_copy(
            src_ref=fin_small, dst_ref=small_out, send_sem=send_sems.at[k],
            recv_sem=recv_sems.at[k], device_id=owner, device_id_type=MESH,
        )
        home = pltpu.make_async_copy(fin_small, small_out, send_sems.at[k])

        @pl.when(elsewhere)
        def _():
            away.start()

        @pl.when(jnp.logical_not(elsewhere))
        def _():
            home.start()

        def wait():
            @pl.when(elsewhere)
            def _():
                away.wait()

            @pl.when(jnp.logical_not(elsewhere))
            def _():
                home.wait()

        moved.append(wait)

    def wout_done(q, at, width, slot):
        place = fin_wout.at[q, :, at : at + width]
        target = wout_out.at[piece, :, at : at + width]
        away = pltpu.make_async_remote_copy(
            src_ref=place, dst_ref=target, send_sem=piece_sems.at[0, q, slot],
            recv_sem=piece_sems.at[1, piece, slot], device_id=part_owner[q], device_id_type=MESH,
        )
        home = pltpu.make_async_copy(place, target, piece_sems.at[0, q, slot])
        remote = part_flat[q] != here

        @pl.when(remote)
        def _():
            away.start()

        @pl.when(jnp.logical_not(remote))
        def _():
            home.start()

        def wait():
            @pl.when(remote)
            def _():
                away.wait_send()

            @pl.when(jnp.logical_not(remote))
            def _():
                home.wait()

        moved.append(wait)

    def wout_arrive(k, at, width, slot):
        target = wout_out.at[k, :, at : at + width]
        copy = pltpu.make_async_remote_copy(
            src_ref=target, dst_ref=target, send_sem=piece_sems.at[0, k, slot],
            recv_sem=piece_sems.at[1, k, slot], device_id=piece_giver[k], device_id_type=MESH,
        )

        @pl.when(jnp.logical_not(piece_here[k]))
        def _():
            copy.wait_recv()

    def wout_final(at, start, rows, total):
        columns = slice(at + start, at + start + total.shape[1])
        fin_wout[ready, rows, columns] = total.astype(BF16)

    def feat_final(at, start, rows, total):
        fin_feat[rows, at + start : at + start + total.shape[1]] = total

    def small_final(start, rows, total):
        fin_small[rows, start : start + total.shape[1]] = total.astype(BF16)

    wout_groups = [
        seq_group(
            copies, wout_parts[k], "chan", take, functools.partial(wout_final, k * WIDE), seq,
            seq_peer, functools.partial(wout_done, ready, k * WIDE, WIDE, k),
        )
        for k in range(n_wide)
    ]

    def wout(k):
        for inner in range(WIDE // cols):
            block = k * (WIDE // cols) + inner
            coming[block].wait()
            right = grads[block % 2].reshape(all_rows, cols)
            lanes = slice(inner * cols, (inner + 1) * cols)
            tile = min(512, part_chan)
            rows, lead = wout_parts[k].shape[-2], len(wout_parts[k].shape) - 2
            within = (tile // rows).bit_length() - 1
            for m in range(0, part_chan, tile):
                value = jnp.dot(gated_t[m : m + tile, :], right, preferred_element_type=F32)
                index = tuple(
                    (m // rows >> (lead - 1 - q)) & 1 for q in range(lead - within)
                )
                wout_parts[k][index + (slice(None),) * (within + 1) + (lanes,)] = (
                    value.reshape((2,) * within + (rows, cols)).astype(BF16)
                )
            if block + 2 < n_feat // cols:
                coming[block + 2] = grad_block(block + 2)
        wout_groups[k].launch()

    gain_sum[...] = jnp.zeros_like(gain_sum)
    coming["gated"].wait()
    wout(0)
    coming["w_rows"].wait()
    if ready:
        coming["wout"].wait()
        for k in range(n_wide):
            wout_done(0, k * WIDE, WIDE, k)
        coming["feat"].wait()
        feat_done(n_chan, EARLY)

    coming["draw"].wait()
    for b in range(n_wt):
        at = slice(b * n_rows, (b + 1) * n_rows)
        mix[at, :] = jnp.dot(draw[at, :], wdt_ref[...], preferred_element_type=F32)
    width = LANE // n_wt
    packed = dbc_ref[:n_rows, :]
    for b in range(1, n_wt):
        packed = packed + pltpu.roll(dbc_ref[b * n_rows : (b + 1) * n_rows, :], b * width, 1)
    mix[all_rows:, :] = packed
    mixed = WtSum(copies, mix, half, land, fin, seq, wt, wt_bits)
    mixed.begin()
    wout(1)
    for bit in range(1, wt_bits):
        mixed.middle(bit)
    pack[LANE : 2 * LANE, :] = lax.dot_general(
        low_ref[...], draw[...], (((0,), (0,)), ((), ())), preferred_element_type=F32
    )
    mixed.end_send()

    coming["normed"].wait()
    coming["dgate"].wait()
    late = EARLY if ready else 0
    bounds = [(0, cols), (cols, cols), (n_chan + late, cols - late), (n_chan + cols, cols)]
    feat_groups = [None] * 4

    def feat(k, right):
        at, width = bounds[k]
        part = feat_parts[k % 2]
        if width < cols:
            part = part.at[(slice(None),) * (len(part.shape) - 1) + (slice(0, width),)]
        feat_groups[k] = seq_group(
            copies, part, "feat", take, functools.partial(feat_final, at), seq, seq_peer,
            functools.partial(feat_done, at, width),
        )
        by_tiles(
            part, n_feat, lambda m: jnp.dot(normed_t[m, :], right, preferred_element_type=F32)
        )
        feat_groups[k].launch()

    feat(2, dgate[:, late:cols])
    wout_groups[0].step()
    mixed.copy.wait_recv()
    ddt[...] = fin[:all_rows, :].astype(BF16)
    lane = lax.broadcasted_iota(jnp.int32, (n_rows, LANE), 1)
    for b in range(n_wt):
        part = fin[all_rows:, :]
        if b:
            part = pltpu.roll(part, LANE - b * width, 1)
        dbc[b * n_rows : (b + 1) * n_rows, :] = jnp.where(lane < width, part, 0.0).astype(BF16)
    coming["u"] = load(u_ref, u_all)

    def sums_of(total):
        return jnp.sum(total, 0, keepdims=True)

    pack[2 * LANE :, :] = jnp.zeros((LANE, n_chan), F32)
    tail_at = 2 * LANE + 2 * n_state
    for n in range(n_state):
        pack[tail_at + n : tail_at + n + 1, :] = sums_of(da_ref[n]) * a_ref[n : n + 1, :]
    tail_at += n_state
    for k in range(2):
        at = tail_at + taps + 1 + k
        pack[at : at + 1, :] = sums_of(sums_ref[k])

    chunk = lax.broadcasted_iota(jnp.int32, (SUB, cols), 0)
    rim_moves = []

    def conv_first(h):
        at = slice(h * cols, (h + 1) * cols)
        for b in range(n_wt):
            rows = slice(b * n_rows, (b + 1) * n_rows)
            d_in = lax.dot_general(
                ddt[rows, :], wx_ref[at, :LANE], (((1,), (1,)), ((), ())), preferred_element_type=F32
            )
            d_in = d_in + lax.dot_general(
                dbc[rows, : 2 * n_state], wx_ref[at, LANE:], (((1,), (1,)), ((), ())),
                preferred_element_type=F32,
            )
            d_conv[b, :n_rows, :] = d_in
        coming["conv"].wait()
        coming["dscan"].wait()

        def one(i, carry):
            b, j = i // (n_rows // 16), i % (n_rows // 16)
            rows = pl.ds(pl.multiple_of(j * 16, 16), 16)
            taken = [
                conv[b, pl.ds(pl.multiple_of(j * 16 + k * SUB, SUB), 16), :] for k in range(taps)
            ]
            out = bconv_ref[:, at]
            for k in range(taps):
                out = out + taken[k] * wconv_ref[k : k + 1, at]
            sig = jax.nn.sigmoid(out)
            from_scan = dscan[pl.ds(pl.multiple_of(i * 16, 16), 16), :].astype(F32)
            value = (d_conv[b, rows, :] + from_scan) * sig * (1.0 + out * (1.0 - sig))
            d_conv[b, rows, :] = value
            found = [value] + [value * piece for piece in taken]
            return tuple(c + f[:SUB] + f[SUB:] for c, f in zip(carry, found))

        zero = jnp.zeros((SUB, cols), F32)
        totals = lax.fori_loop(0, all_rows // 16, one, (zero,) * (taps + 1))
        pack[tail_at + taps : tail_at + taps + 1, at] = sums_of(totals[0])
        for k in range(taps):
            pack[tail_at + k : tail_at + k + 1, at] = sums_of(totals[k + 1])

        rim_f[...] = jnp.zeros_like(rim_f)
        for b in range(n_wt):
            for k in range(taps - 1):
                rim_f[b * (taps - 1) + k, :] = d_conv[b, k * SUB, :]
        rim_s[h, 0] = rim_f[...].astype(BF16)

        @pl.when(seq == n_seq - 1)
        def _():
            rim_s[h, 1] = jnp.zeros((16, cols), BF16)

        k, copies.count = copies.count, copies.count + 1
        move = pltpu.make_async_remote_copy(
            src_ref=rim_s.at[h, 0], dst_ref=rim_s.at[h, 1], send_sem=send_sems.at[k],
            recv_sem=recv_sems.at[k], device_id=behind, device_id_type=MESH,
        )
        rim_moves.append(move)

        @pl.when(seq > 0)
        def _():
            move.start()

        if h == 0:
            coming["conv"] = load(conv_ref.at[:, :, cols : 2 * cols], conv)
            coming["dscan"] = load(dscan_ref.at[:, cols : 2 * cols], dscan)

    def conv_second(h):
        at = slice(h * cols, (h + 1) * cols)

        @pl.when(seq < n_seq - 1)
        def _():
            rim_moves[h].wait_recv()

        landed = rim_s[h, 1].astype(F32)
        for b in range(n_wt):
            for k in range(taps - 1):
                turned = pltpu.roll(d_conv[b, k * SUB : (k + 1) * SUB, :], SUB - 1, 0)
                row = landed[b * (taps - 1) + k : b * (taps - 1) + k + 1, :]
                place = slice(n_rows + k * SUB, n_rows + (k + 1) * SUB)
                d_conv[b, place, :] = jnp.where(chunk == SUB - 1, row, turned)

        def one(i, carry):
            b, j = i // (n_rows // 16), i % (n_rows // 16)
            total = jnp.zeros((16, cols), F32)
            for k in range(taps):
                start = pl.multiple_of(j * 16 + (taps - 1 - k) * SUB, SUB)
                total = total + d_conv[b, pl.ds(start, 16), :] * wconv_ref[k : k + 1, at]
            draw[pl.ds(pl.multiple_of(i * 16, 16), 16), at] = total.astype(BF16)
            return carry

        lax.fori_loop(0, all_rows // 16, one, 0)

    conv_first(0)
    wout_groups[1].step()
    wout_groups[0].step()
    feat(3, dgate[:, cols:])
    conv_second(0)
    feat_groups[2].step()
    wout_groups[1].step()
    wout_groups[0].step()
    conv_first(1)
    coming["u"].wait()
    pack[:LANE, :] = lax.dot_general(
        ddt[...], u_all[...], (((0,), (0,)), ((), ())), preferred_element_type=F32
    )
    for_b = lax.dot_general(
        dbc[...], u_all[...], (((0,), (0,)), ((), ())), preferred_element_type=F32
    )
    pack[2 * LANE : 2 * LANE + 2 * n_state, :] = for_b[: 2 * n_state, :]
    conv_second(1)
    small_group = seq_group(
        copies, small, "chan", take, small_final, seq, seq_peer, small_done
    )
    tile = min(512, n_chan)
    for m in range(0, n_chan, tile):
        fill(small, m // small.shape[-2], pack[:, m : m + tile].T)
    small_group.launch()
    feat_groups[3].step()
    feat_groups[2].step()
    wout_groups[1].step()
    feat_groups[2].release()
    feat(0, draw[:, :cols])
    small_group.step()
    feat_groups[3].step()
    feat_groups[2].step()
    feat_groups[3].release()
    feat(1, draw[:, cols:])

    norm_groups = []
    per = cols // 256
    for k in range(n_feat // cols):

        def final(rows, total, k=k):
            norm_out[rows, k * cols : (k + 1) * cols] = total

        order = tuple(range(wt_bits))
        job = Halving(
            copies, norm_parts[k % 2], list(reversed(order)), order, slice(0, cols), take(wt_bits),
            final, wt, wt_peer,
        )
        norm_groups.append(Group([job]))

    def norm(k):
        if k >= 2:
            norm_groups[k - 2].release()
        for part in range(per):
            i = k * per + part
            coming["win"].wait()
            if i + 1 < per * len(norm_groups):
                coming["win"] = load(
                    win_ref.at[(i + 1) * 256 : (i + 2) * 256], win_rows.at[(i + 1) % 2]
                )
            rows_w = win_rows[i % 2]
            for b in range(n_wt):
                at = slice(b * n_rows, (b + 1) * n_rows)
                value = lax.dot_general(
                    draw[at, :], rows_w[:, :n_chan], (((1,), (1,)), ((), ())),
                    preferred_element_type=F32,
                )
                value = value + lax.dot_general(
                    dgate[at, :], rows_w[:, n_chan:], (((1,), (1,)), ((), ())),
                    preferred_element_type=F32,
                )
                index = tuple((b >> (wt_bits - 1 - q)) & 1 for q in range(wt_bits))
                norm_parts[k % 2][index + (slice(None), slice(part * 256, (part + 1) * 256))] = (
                    value.astype(BF16)
                )
        norm_groups[k].launch()

    norm(0)
    small_group.step()
    feat_groups[3].step()
    norm(1)
    feat_groups[0].step()
    norm_groups[0].step()
    norm(2)
    small_group.step()
    norm_groups[1].step()
    feat_groups[1].step()
    feat_groups[0].step()
    norm(3)
    rest = wout_groups + [feat_groups[2], feat_groups[3], small_group, feat_groups[0], feat_groups[1]]
    for group in norm_groups[2:]:
        group.step()
    going = True
    while going:
        going = False
        for group in rest:
            going = group.step() or going
    going = True
    while going:
        going = False
        for group in norm_groups:
            going = group.step() or going
    to_wt(lambda w: gain_sum.at[own_rows(w)], gain_out.at[wt])
    for wait in delivered:
        wait()
    for wait in moved:
        wait()
    for k in range(parts):
        for slot in range(n_wide):
            wout_arrive(k, slot * WIDE, WIDE, slot)
    for move in rim_moves:

        @pl.when(seq > 0)
        def _():
            move.wait_send()

    copies.finish()


def finish_all(
    gated_t, d_gate, d_scan_in, d_raw, inputs, conv, grads, normed_t, w_in, wout, feat,
    d_bc, dt_low, w_x, w_dt, w_conv, b_conv, d_rate, a_neg, sums,
):
    n_seq, n_wt = lax.axis_size("seq"), lax.axis_size("wt")
    seq_bits, wt_bits = n_seq.bit_length() - 1, n_wt.bit_length() - 1
    n_chan, all_rows = gated_t.shape
    n_feat, n_rows = normed_t.shape[0], all_rows // n_wt
    n_state, taps = a_neg.shape[0], w_conv.shape[0]
    cols = 512
    parts = parts_of(n_chan, n_seq)
    part_chan = n_chan // parts
    chan_rows, feat_rows, wout_rows = n_chan // n_seq, n_feat // n_seq, part_chan // n_seq
    size = (all_rows + n_rows) // 2
    small_cols, n_wide = 3 * LANE, n_feat // WIDE
    square = ((all_rows, n_chan), BF16)
    blocks = (2,) * seq_bits
    scratch = [
        ((part_chan, all_rows), BF16), square, ((all_rows, cols), BF16), square,
        (normed_t.shape, BF16), ((2, n_wt, n_rows, cols), BF16), ((2, 256, 2 * n_chan), BF16),
        ((n_wt, conv.shape[1], cols), F32), ((n_wt, conv.shape[1], cols), F32),
        ((2 * size, LANE), F32), ((wt_bits, size, LANE), F32), ((wt_bits, size, LANE), F32),
        ((2 * size, LANE), F32), square, ((all_rows, LANE), BF16), ((all_rows, LANE), BF16),
        ((small_cols, n_chan), F32), ((16, cols), F32), ((2, 2, 16, cols), BF16),
        ((feat_rows, 2 * n_chan), F32), ((parts, wout_rows, n_feat), BF16),
        ((chan_rows, small_cols), BF16), ((feat_rows, 2 * n_chan), BF16), ((feat_rows, LANE), F32),
        (blocks + (chan_rows, small_cols), BF16),
    ]
    scratch = [pltpu.VMEM(*item) for item in scratch]
    scratch += [pltpu.SemaphoreType.DMA((2, parts, n_wide))]
    scratch += [pltpu.SemaphoreType.DMA((180,))] * 2
    scratch += [pltpu.VMEM(blocks + (wout_rows, WIDE), BF16)] * n_wide
    scratch += [pltpu.VMEM(blocks + (feat_rows, cols), BF16)] * 2
    scratch += [pltpu.VMEM((2,) * wt_bits + (n_rows, cols), BF16)] * 2
    late = EARLY if parts > 1 else 0
    scratch += seq_landings(seq_bits, wout_rows, [WIDE] * n_wide)
    scratch += seq_landings(seq_bits, feat_rows, [cols - late, cols])
    scratch += seq_landings(seq_bits, chan_rows, [small_cols])
    scratch += seq_landings(seq_bits, feat_rows, [cols, cols])
    scratch += landings(wt_bits, n_rows, (cols,) * (n_feat // cols))
    hbm = pl.BlockSpec(memory_space=pl.ANY)
    vmem = pl.BlockSpec(memory_space=pltpu.VMEM)
    return pl.pallas_call(
        functools.partial(finish_kernel, n_seq, n_wt, n_state),
        in_specs=[hbm] * 11 + [vmem] * 9,
        out_specs=[hbm, hbm, hbm, vmem, hbm],
        out_shape=[
            jax.ShapeDtypeStruct((feat_rows // n_wt, 2 * n_chan * n_wt), F32),
            jax.ShapeDtypeStruct((parts, wout_rows, n_feat), BF16),
            jax.ShapeDtypeStruct((chan_rows, small_cols), BF16),
            jax.ShapeDtypeStruct((n_rows, n_feat), F32),
            jax.ShapeDtypeStruct((n_wt, feat_rows // n_wt, LANE), F32),
        ],
        scratch_shapes=scratch,
        compiler_params=pltpu.CompilerParams(
            collective_id=1, has_side_effects=True, vmem_limit_bytes=63 * 2**20
        ),
        name="finish_all",
    )(
        gated_t, d_gate, d_scan_in, d_raw, inputs, conv, grads, normed_t, w_in, wout, feat,
        d_bc, dt_low, w_x, w_dt, w_conv, b_conv, d_rate, a_neg, sums,
    )


class Gather:
    def __init__(self, copies, slots, seq, wt, bits):
        self.copies, self.slots, self.seq, self.wt, self.bits = copies, slots, seq, wt, bits
        self.arriving = {}

    def send(self, mask, src):
        slot = self.slots.at[turn(self.wt, mask, self.bits)]
        low = self.bits if mask == 0 else (mask & -mask).bit_length() - 1
        for bit in reversed(range(low)):
            peer = (self.seq, flip(self.wt, bit))
            self.arriving[mask | 1 << bit] = self.copies.remote(src, slot, peer)

    def arrive(self, mask):
        self.arriving[mask].wait_recv()
        self.send(mask, self.slots.at[turn(self.wt, mask, self.bits)])


def start_kernel(
    n_seq, n_wt,
    hidden_ref, grad_ref, gain_ref, starts_ref, win_ref, wout_ref, wconv_ref, bconv_ref, wx_ref,
    wdt_ref,
    normed_out, win_out, conv_out, gate_out, u_out, raw_out, low_out, bcs_out, dgated_out,
    dscan_out, grad_out, gain_out,
    rows_s, grads_s, gain_s, starts_s, normed_s, win_s, wout_s, conv_s, gate_s, u_s, raw_s, low_s,
    bcs_s, dgated_s, dscan_s, mix_s, fin_s, half_s, land_s, rim_s, rim_in, normed_t,
    send_sems, recv_sems,
):
    seq, wt = lax.axis_index("seq"), lax.axis_index("wt")
    bits = n_wt.bit_length() - 1
    n_rows, n_feat = hidden_ref.shape
    n_chan, shard = wout_ref.shape[0], win_ref.shape[0]
    taps = wconv_ref.shape[0]
    rim = (taps - 1) * SUB
    all_rows = n_wt * n_rows
    near_y, near_z = (flip(seq, 0), wt), (flip(seq, 1), wt)
    wt_peers = [(seq, turn(wt, mask, bits)) for mask in range(1, n_wt)]
    ahead, behind = (lax.rem(seq + 1, n_seq), wt), (lax.rem(seq + n_seq - 1, n_seq), wt)

    barrier = pltpu.get_barrier_semaphore()
    partners = wt_peers + [near_y, near_z, ahead, behind]
    for partner in partners:
        pl.semaphore_signal(barrier, inc=1, device_id=partner, device_id_type=MESH)
    pl.semaphore_wait(barrier, len(partners))

    copies = Copies(send_sems, recv_sems)
    part = shard // 4
    quarter = seq % 4

    def win_part(owner, which, at, rows, half):
        start = pl.multiple_of(owner * shard + which * part + at, 16)
        return win_s.at[pl.ds(start, rows), half * n_chan : (half + 1) * n_chan]

    def send_far(half):
        found = {}
        rows = pl.ds(pl.multiple_of(quarter * part, 16), part)
        for mask in range(2, n_wt):
            to = turn(wt, mask, bits)
            columns = pl.ds(pl.multiple_of((half * n_wt + to) * n_chan, LANE), n_chan)
            found[mask] = copies.remote(
                win_ref.at[rows, columns], win_part(wt, quarter, 0, part, half), (seq, to)
            )
        return found

    def send_near(half):
        to = flip(wt, 0)
        place = win_s.at[
            pl.ds(pl.multiple_of(wt * shard, 16), shard), half * n_chan : (half + 1) * n_chan
        ]
        columns = pl.ds(pl.multiple_of((half * n_wt + to) * n_chan, LANE), n_chan)
        own = pl.ds(pl.multiple_of((half * n_wt + wt) * n_chan, LANE), n_chan)
        return (
            copies.remote(win_ref.at[:, columns], place, (seq, to)),
            copies.local(win_ref.at[:, own], place),
        )

    def share_first(half, found):
        passed = {}
        for mask, copy in found.items():
            copy.wait_recv()
            block = win_part(turn(wt, mask, bits), quarter, 0, part, half)
            passed[mask] = (
                copies.remote(block, block, near_y), copies.remote(block, block, near_z)
            )
        return passed

    def share_second(half, passed):
        last = []
        for mask, (by_y, by_z) in passed.items():
            owner = turn(wt, mask, bits)
            by_z.wait_recv()
            block = win_part(owner, flip(quarter, 1), 0, part // 2, half)
            last.append(copies.remote(block, block, near_y))
            by_y.wait_recv()
            block = win_part(owner, flip(quarter, 0), part // 2, part // 2, half)
            last.append(copies.remote(block, block, near_z))
        return last

    def normalise(mask):
        at = turn(wt, mask, bits)
        gain = jnp.concatenate(
            [gain_s[k].astype(F32)[0:1] for k in range(n_wt)], axis=1
        )

        def body(i, carry):
            rows = pl.ds(pl.multiple_of(i * 16, 16), 16)
            x = rows_s[at, rows, :].astype(F32)
            inv = lax.rsqrt(jnp.mean(x * x, axis=1, keepdims=True) + EPS)
            place = pl.ds(pl.multiple_of(at * n_rows + i * 16, 16), 16)
            normed_s[place, :] = (x * inv * gain).astype(BF16)
            return carry

        lax.fori_loop(0, n_rows // 16, body, 0)

    far = send_far(0)
    rows = Gather(copies, rows_s, seq, wt, bits)
    gains = Gather(copies, gain_s, seq, wt, bits)
    starts = Gather(copies, starts_s, seq, wt, bits)
    own_copies = [
        copies.local(gain_ref, gain_s.at[wt]),
        copies.local(starts_ref, starts_s.at[wt]),
        copies.local(hidden_ref, rows_s.at[wt]),
    ]
    gains.send(0, gain_ref)
    rows.send(0, hidden_ref)
    near = send_near(0)
    starts.send(0, starts_ref)
    wout_copy = copies.local(wout_ref, wout_s)
    for mask in range(n_wt - 1, 0, -1):
        if mask in gains.arriving:
            gains.arrive(mask)
    for mask in range(1, n_wt):
        if mask not in (1, 2):
            gains.arriving[mask].wait_recv()
    for copy in own_copies:
        copy.wait()
    normalise(0)
    rows.arrive(1)
    normalise(1)
    passed = share_first(0, far)
    far = send_far(1)
    last = share_second(0, passed)
    near_gate = send_near(1)
    for mask in range(2, n_wt):
        rows.arrive(mask)
        if mask == 2:
            grads = Gather(copies, grads_s, seq, wt, bits)
            grad_copy = copies.local(grad_ref, grads_s.at[wt])
            grads.send(0, grad_ref)
        normalise(mask)
    results = [copies.local(gain_s, gain_out)]
    near[0].wait_recv()
    near[1].wait()
    for copy in last:
        copy.wait_recv()

    n_block, m_block = 256, 512

    def tiles(body):
        m_count = all_rows // m_block

        def one(i, carry):
            m = pl.multiple_of((i % m_count) * m_block, m_block)
            n = pl.multiple_of((i // m_count) * n_block, n_block)
            body(m, n)
            return carry

        lax.fori_loop(0, m_count * (n_chan // n_block), one, 0)

    def conv_tile(m, n):
        value = jnp.dot(
            normed_s[pl.ds(m, m_block), :], win_s[:, pl.ds(n, n_block)], preferred_element_type=F32
        )
        value = value.astype(BF16).astype(F32)
        for k in range(m_block // n_rows):
            conv_s[m // n_rows + k, rim:, pl.ds(n, n_block)] = value[k * n_rows : (k + 1) * n_rows]

    tiles(conv_tile)

    rim_s[...] = jnp.zeros_like(rim_s)
    for b in range(n_wt):
        for k in range(taps - 1):
            at = rim + n_rows - (taps - 1 - k) * SUB
            rim_s[b * (taps - 1) + k, :] = conv_s[b, at + SUB - 1, :]
    rim_s2 = rim_s[...].astype(BF16)
    rim_in[0] = rim_s2

    @pl.when(seq == 0)
    def _():
        rim_in[1] = jnp.zeros_like(rim_s2)

    k_rim, copies.count = copies.count, copies.count + 1
    rim_copy = pltpu.make_async_remote_copy(
        src_ref=rim_in.at[0], dst_ref=rim_in.at[1], send_sem=send_sems.at[k_rim],
        recv_sem=recv_sems.at[k_rim], device_id=ahead, device_id_type=MESH,
    )

    @pl.when(seq < n_seq - 1)
    def _():
        rim_copy.start()

    passed = share_first(1, far)

    def convolve(b, j):
        rows = pl.ds(pl.multiple_of(j * 16, 16), 16)
        total = bconv_ref[...] + conv_s[b, rows, :] * wconv_ref[0:1, :]
        for k in range(1, taps):
            at = pl.ds(pl.multiple_of(j * 16 + k * SUB, SUB), 16)
            total = total + conv_s[b, at, :] * wconv_ref[k : k + 1, :]
        place = pl.ds(pl.multiple_of(b * n_rows + j * 16, 16), 16)
        u_s[place, :] = (total * jax.nn.sigmoid(total)).astype(BF16)

    head = -(-(taps - 1) // 2)
    pairs = n_rows // 16

    def convolve_tail(i, carry):
        convolve(i // (pairs - head), head + i % (pairs - head))
        return carry

    lax.fori_loop(0, n_wt * (pairs - head), convolve_tail, 0)

    @pl.when(seq > 0)
    def _():
        rim_copy.wait_recv()

    rim_rows = rim_in[1].astype(F32)
    first = lax.broadcasted_iota(jnp.int32, (SUB, n_chan), 0) == 0
    for b in range(n_wt):
        for k in range(taps - 1):
            at = rim + n_rows - (taps - 1 - k) * SUB
            moved = pltpu.roll(conv_s[b, at : at + SUB, :], 1, 0)
            row = rim_rows[b * (taps - 1) + k : b * (taps - 1) + k + 1, :]
            conv_s[b, k * SUB : (k + 1) * SUB, :] = jnp.where(first, row, moved)
    lax.fori_loop(0, n_wt * head, lambda i, c: (convolve(i // head, i % head), c)[1], 0)
    results += [copies.local(conv_s, conv_out), copies.local(u_s, u_out)]

    packed = []
    for b in range(n_wt):
        block = u_s[b * n_rows : (b + 1) * n_rows, :]
        mix_s[b * n_rows : (b + 1) * n_rows, :] = jnp.dot(
            block, wx_ref[:, :LANE], preferred_element_type=F32
        )
        packed.append(jnp.dot(block, wx_ref[:, LANE:], preferred_element_type=F32))
    mix_s[all_rows:, :] = jnp.concatenate(packed, axis=1)
    mixed = WtSum(copies, mix_s, half_s, land_s, fin_s, seq, wt, bits)
    mixed.begin()
    last = share_second(1, passed)
    grads.arrive(1)
    starts.arrive(2)
    for bit in range(1, bits):
        mixed.middle(bit)
    mixed.end()

    low_s[...] = fin_s[:all_rows, :].astype(BF16)
    starts.arriving[1].wait_recv()
    starts.arriving[3].wait_recv()
    lane = lax.broadcasted_iota(jnp.int32, (n_rows, LANE), 1)
    width = LANE // n_wt
    for b in range(n_wt):
        moved = fin_s[all_rows:, :]
        if b:
            moved = pltpu.roll(moved, LANE - b * width, 1)
        bcs_s[b * n_rows : (b + 1) * n_rows, :] = (
            jnp.where(lane < width, moved, 0.0).astype(BF16) + starts_s[b]
        )

    def raw_tile(m, n):
        value = lax.dot_general(
            low_s[pl.ds(m, m_block), :], wdt_ref[pl.ds(n, n_block), :], (((1,), (1,)), ((), ())),
            preferred_element_type=F32,
        )
        raw_s[pl.ds(m, m_block), pl.ds(n, n_block)] = value.astype(BF16)

    tiles(raw_tile)
    results += [
        copies.local(low_s, low_out), copies.local(bcs_s, bcs_out), copies.local(raw_s, raw_out)
    ]

    for b in range(n_wt):
        at = slice(b * n_rows, (b + 1) * n_rows)
        normed_t[:, at] = normed_s[at, :].T
    results.append(copies.local(normed_t, normed_out))
    near_gate[0].wait_recv()
    near_gate[1].wait()
    for copy in last:
        copy.wait_recv()
    results.append(copies.local(win_s, win_out))

    def gate_tile(m, n):
        value = jnp.dot(
            normed_s[pl.ds(m, m_block), :], win_s[:, pl.ds(n_chan + n, n_block)],
            preferred_element_type=F32,
        )
        gate_s[pl.ds(m, m_block), pl.ds(n, n_block)] = value.astype(BF16)

    tiles(gate_tile)
    results.append(copies.local(gate_s, gate_out))
    grad_copy.wait()
    for mask in range(2, n_wt):
        grads.arrive(mask)
    wout_copy.wait()
    results.append(copies.local(grads_s, grad_out))

    def back_tile(m, n):
        b = m // n_rows
        for k in range(m_block // n_rows):
            at = pl.ds(pl.multiple_of(m + k * n_rows, n_rows), n_rows)
            d_gated = lax.dot_general(
                grads_s[b + k], wout_s[pl.ds(n, n_block), :], (((1,), (1,)), ((), ())),
                preferred_element_type=F32,
            )
            gate = gate_s[at, pl.ds(n, n_block)].astype(F32)
            dgated_s[at, pl.ds(n, n_block)] = d_gated
            dscan_s[at, pl.ds(n, n_block)] = (d_gated * gate * jax.nn.sigmoid(gate)).astype(BF16)

    tiles(back_tile)
    results += [copies.local(dgated_s, dgated_out), copies.local(dscan_s, dscan_out)]
    for copy in results:
        copy.wait()

    @pl.when(seq < n_seq - 1)
    def _():
        rim_copy.wait_send()

    copies.finish()


def start_all(hidden, grad, gain, starts, w_in, w_out, w_conv, b_conv, w_x, w_dt):
    n_seq, n_wt = lax.axis_size("seq"), lax.axis_size("wt")
    n_rows, n_feat = hidden.shape
    n_chan, taps = w_out.shape[0], w_conv.shape[0]
    rows, rim = n_wt * n_rows, (taps - 1) * SUB
    shapes = [
        ((n_feat, rows), BF16), ((n_feat, 2 * n_chan), BF16), ((n_wt, rim + n_rows, n_chan), F32),
        ((rows, n_chan), BF16), ((rows, n_chan), BF16), ((rows, n_chan), BF16), ((rows, LANE), BF16),
        ((rows, LANE), BF16), ((rows, n_chan), F32), ((rows, n_chan), BF16),
        ((n_wt, n_rows, n_feat), BF16), ((n_wt,) + gain.shape, BF16),
    ]
    normed, win, conv, gate, u, raw, low, bcs, dgated, dscan, grads, gains = shapes
    size = (rows + n_rows) // 2
    bits = n_wt.bit_length() - 1
    scratch = [
        grads, grads, gains, ((n_wt, n_rows, LANE), BF16), ((rows, n_feat), BF16), win, (w_out.shape, BF16), conv,
        gate, u, raw, low, bcs, dgated, dscan, ((2 * size, LANE), F32), ((2 * size, LANE), F32),
        ((bits, size, LANE), F32), ((bits, size, LANE), F32), ((16, n_chan), F32),
        ((2, 16, n_chan), BF16), normed,
    ]
    hbm = pl.BlockSpec(memory_space=pl.ANY)
    vmem = pl.BlockSpec(memory_space=pltpu.VMEM)
    return pl.pallas_call(
        functools.partial(start_kernel, n_seq, n_wt),
        in_specs=[hbm] * 6 + [vmem] * 4,
        out_specs=[hbm] * len(shapes),
        out_shape=[jax.ShapeDtypeStruct(*item) for item in shapes],
        scratch_shapes=[pltpu.VMEM(*item) for item in scratch]
        + [pltpu.SemaphoreType.DMA((80,))] * 2,
        compiler_params=pltpu.CompilerParams(
            collective_id=2, has_side_effects=True, vmem_limit_bytes=60 * 2**20
        ),
        name="start_all",
    )(hidden, grad, gain, starts, w_in, w_out, w_conv, b_conv, w_x, w_dt)


def dot(left, right, left_dim=1, right_dim=0):
    return lax.dot_general(
        left, right, (((left_dim,), (right_dim,)), ((), ())), preferred_element_type=F32
    )


def to_chunks(rows):
    n_rows, width = rows.shape
    return rows.reshape(SUB, n_rows // SUB, width).swapaxes(0, 1).reshape(n_rows, width)


def from_chunks(rows, n_streams):
    n_rows, width = rows.shape[0] // n_streams, rows.shape[1]
    parts = rows.reshape(n_streams, n_rows // SUB, SUB, width)
    return parts.swapaxes(1, 2).reshape(n_streams * n_rows, width)


def per_device(
    hidden_in, doc_starts, norm_gain, in_weight, conv_weight, conv_bias, x_weight,
    dt_weight, dt_bias, a_log, d_skip, out_weight, grad_output,
):
    n_wt, n_seq = lax.axis_size("wt"), lax.axis_size("seq")
    seq_at = lax.axis_index("seq")
    n_chan = out_weight.shape[0]
    taps = conv_weight.shape[1]
    dt_rank = dt_weight.shape[1]
    n_state = a_log.shape[1]
    rows_own = hidden_in[0]
    n_rows, n_feat = rows_own.shape
    steps = n_rows // SUB

    w_conv = conv_weight.astype(F32)
    starts = jnp.pad(
        to_chunks(doc_starts[0].astype(BF16)[:, None]), ((0, 0), (2 * n_state, LANE - 2 * n_state - 1))
    )
    (
        normed_t, w_in, padded, gate_in, inputs, dt_raw, dt_low, bcs, d_gated, d_scanned, grad_all, gain,
    ) = start_all(
        to_chunks(rows_own), to_chunks(grad_output[0]),
        jnp.broadcast_to(norm_gain[None], (16, norm_gain.shape[0])), starts, in_weight, out_weight,
        w_conv.T, conv_bias.astype(F32)[None], x_weight, dt_weight,
    )
    gain = gain[:, 0].reshape(n_feat).astype(F32)

    a_neg = -jnp.exp(a_log.astype(F32)).T
    rates = jnp.broadcast_to((a_neg * LOG2E)[:, None, :], (n_state, SUB, n_chan))
    bias = dt_bias.astype(F32)[None]
    skip = d_skip.astype(F32)[None]
    ends, leads, totals, first, last, span = chunk_ends(
        bcs, dt_raw, inputs, d_scanned, bias, rates, n_wt
    )
    head, tail = join_edges(first, last, span, a_neg * LOG2E)
    gated, gated_t, d_gate, d_scan_in, d_raw, d_bc, d_rate, sums, wout, feat = scan_all(
        bcs, dt_raw, inputs, d_scanned, gate_in, d_gated, bias, skip, rates,
        ends, leads, totals, head, tail, grad_all.reshape(n_wt * n_rows, n_feat), normed_t,
    )


    out_sum = lax.psum_scatter(
        dot(gated, out_weight).astype(BF16), "wt", scatter_dimension=0, tiled=True
    )
    feat_grads, d_wout, small, d_normed, gain_parts = finish_all(
        gated_t, d_gate, d_scan_in, d_raw, inputs, padded, grad_all, normed_t, w_in, wout, feat,
        d_bc, dt_low, x_weight, dt_weight, w_conv.T, conv_bias.astype(F32)[None], d_rate, a_neg,
        sums,
    )
    d_wout = d_wout.reshape(-1, n_feat).astype(F32)
    small = small.astype(F32)
    widths = (dt_rank, dt_rank, 2 * n_state, n_state, taps, 1, 1, 1)
    cuts, at = [], 0
    for piece in widths:
        cuts.append(small[:, at : at + piece])
        at += piece
    d_wx, d_wdt, d_wbc, d_loga, d_wconv, d_bconv, d_bdt, d_skips = cuts
    own = n_feat // (n_seq * n_wt)
    own_at = own * (n_wt * seq_at + lax.axis_index("wt"))
    gain_grad = jnp.sum(gain_parts, (0, 2)) / lax.dynamic_slice_in_dim(gain, own_at, own, 0)
    x = rows_own.astype(F32)
    output = x + from_chunks(out_sum, 1).astype(F32)
    d_normed = from_chunks(d_normed, 1)
    inv_rms = lax.rsqrt(jnp.mean(x * x, axis=1, keepdims=True) + EPS)
    scaled = d_normed * gain
    cubed = inv_rms * inv_rms * inv_rms
    d_rows = inv_rms * scaled - x * cubed * jnp.mean(scaled * x, axis=1, keepdims=True)
    input_grad = grad_output[0].astype(F32) + d_rows
    return (
        output[None],
        input_grad[None],
        gain_grad,
        feat_grads,
        d_wconv,
        d_bconv[:, 0],
        jnp.concatenate([d_wx, d_wbc], 1),
        d_wdt,
        d_bdt[:, 0],
        d_loga,
        d_skips[:, 0],
        d_wout,
    )


def solution(mesh):
    placed = (
        P("wt", "seq", None),
        P("wt", "seq"),
        P("wt"),
        P("wt", None),
        P("wt", None),
        P("wt"),
        P("wt", None),
        P("wt", None),
        P("wt"),
        P("wt", None),
        P("wt"),
        P("wt", None),
        P("wt", "seq", None),
    )
    every = ("seq", "wt")
    return jax.shard_map(
        per_device,
        mesh=mesh,
        in_specs=placed,
        out_specs=(
            P("wt", "seq", None),
            P("wt", "seq", None),
            P(every),
            P(every, None),
            P(every, None),
            P(every),
            P(every, None),
            P(every, None),
            P(every),
            P(every, None),
            P(every),
            P(every, None),
        ),
        check_vma=False,
    )
```

```python
import functools
import math

import jax
import jax.numpy as jnp
import ml_dtypes
import numpy as np
from jax import lax
from jax.experimental import pallas as pl
from jax.experimental.pallas import tpu as pltpu
from jax.sharding import PartitionSpec as P

EPS = 1e-05
LOG2E = 1.4426950408889634
RESET = 1e30
SUB = 8
LANE = 128
NBLK = 4
F32 = jnp.float32
BF16 = jnp.bfloat16
MESH = pl.DeviceIdType.MESH


def softplus(v):
    return jnp.maximum(v, 0.0) + jnp.log1p(jnp.exp(-jnp.abs(v)))


def wide(tile, width):
    return jnp.concatenate([tile] * (width // LANE), axis=1)


def fold(values):
    total = values[:, :LANE]
    for k in range(1, values.shape[1] // LANE):
        total = total + values[:, k * LANE : (k + 1) * LANE]
    return total


def chunk_prefix(decay, drive, reverse):
    chunk = lax.broadcasted_iota(jnp.int32, drive.shape, 0)
    for shift in (1, 2, 4):
        if reverse:
            other_decay = pltpu.roll(decay, SUB - shift, 0)
            other_drive = pltpu.roll(drive, SUB - shift, 0)
            inside = chunk < SUB - shift
        else:
            other_decay = pltpu.roll(decay, shift, 0)
            other_drive = pltpu.roll(drive, shift, 0)
            inside = chunk >= shift
        drive = jnp.where(inside, decay * other_drive + drive, drive)
        decay = jnp.where(inside, decay * other_decay, decay)
    return decay, drive


def spread_rows(bcs_ref, spread_ref, bcb):
    bcb[...] = jnp.dot(bcs_ref[...], spread_ref[...], preferred_element_type=F32)


def turn(index, mask, bits):
    for bit in range(bits):
        if mask >> bit & 1:
            index = flip(index, bit)
    return index


class Copies:
    def __init__(self, send_sems, recv_sems):
        self.send_sems, self.recv_sems = send_sems, recv_sems
        self.count, self.open = 0, []

    def remote(self, src, dst, peer):
        k, self.count = self.count, self.count + 1
        copy = pltpu.make_async_remote_copy(
            src_ref=src, dst_ref=dst, send_sem=self.send_sems.at[k],
            recv_sem=self.recv_sems.at[k], device_id=peer, device_id_type=MESH,
        )
        copy.start()
        self.open.append(copy)
        return copy

    def later(self, src_of, dst, peer):
        k, self.count = self.count, self.count + 1

        def make():
            return pltpu.make_async_remote_copy(
                src_ref=src_of(), dst_ref=dst, send_sem=self.send_sems.at[k],
                recv_sem=self.recv_sems.at[k], device_id=peer, device_id_type=MESH,
            )

        self.open.append(make)
        return make

    def local(self, src, dst):
        k, self.count = self.count, self.count + 1
        copy = pltpu.make_async_copy(src, dst, self.send_sems.at[k])
        copy.start()
        return copy

    def drop(self, copy):
        self.open = [other for other in self.open if other is not copy]

    def finish(self):
        for copy in self.open:
            (copy() if callable(copy) else copy).wait_send()


class WtSum:
    def __init__(self, copies, mix, first, half, land, total, seq, wt, bits):
        self.copies, self.mix, self.first, self.total = copies, mix, first, total
        self.half, self.land = half, land
        self.seq, self.wt, self.bits = seq, wt, bits
        size = mix.shape[0] // 2
        mine = bit_of(wt, 0)
        self.kept = pl.ds(pl.multiple_of(mine * size, 16), size)
        self.given = pl.ds(pl.multiple_of((1 - mine) * size, 16), size)

    def begin(self):
        peer = (self.seq, flip(self.wt, 0))
        self.copy = self.copies.remote(self.mix.at[self.given], self.first, peer)

    def so_far(self, bit):
        self.copy.wait_recv()
        if bit == 1:
            return self.mix[self.kept, :] + self.first[...]
        return self.half[bit - 2].astype(F32) + self.land[bit - 2].astype(F32)

    def middle(self, bit):
        self.half[bit - 1] = self.so_far(bit).astype(BF16)
        peer = (self.seq, flip(self.wt, bit))
        self.copy = self.copies.remote(self.half.at[bit - 1], self.land.at[bit - 1], peer)

    def end(self):
        self.end_send()
        self.copy.wait_recv()

    def end_send(self):
        self.total[self.kept, :] = self.so_far(self.bits)
        peer = (self.seq, flip(self.wt, 0))
        part = self.total.at[self.kept]
        self.copy = self.copies.remote(part, part, peer)


def flip(index, bit):
    return index + (1 - 2 * ((index // 2**bit) % 2)) * 2**bit


def bit_of(index, bit):
    return (index // 2**bit) % 2


def pick(left, bit, value):
    return tuple(value if b == bit else slice(None) for b in left)


def over_blocks(count, rows, body):
    tile = math.gcd(rows, 32)
    per_block = rows // tile

    def one(i, carry):
        block, row = i // per_block, (i % per_block) * tile
        index = tuple((block // 2 ** (count - 1 - k)) % 2 for k in range(count))
        body(index, pl.ds(pl.multiple_of(row, tile), tile))
        return carry

    lax.fori_loop(0, 2**count * per_block, one, 0)


class Halving:
    def __init__(self, copies, source, dims, order, columns, landing, final, me, peer):
        self.copies, self.source, self.dims, self.order = copies, source, dims, order
        self.columns, self.landing, self.final = columns, landing, final
        self.mine = {bit: bit_of(me, bit) for bit in order}
        self.theirs = {bit: 1 - value for bit, value in self.mine.items()}
        self.moves = [
            copies.later(functools.partial(self.block, stage), landing[stage], peer(bit))
            for stage, bit in enumerate(order)
        ]

    def left(self, stage):
        return [b for b in self.dims if b not in self.order[:stage]]

    def block(self, stage):
        bit = self.order[stage]
        other = pick(self.left(stage), bit, self.theirs[bit])
        if stage == 0:
            return self.source.at[other + (slice(None), self.columns)]
        return self.landing[stage - 1].at[other]

    def send(self, stage):
        self.moves[stage]().start()

    def add(self, stage):
        self.moves[stage]().wait_recv()
        mine = self.mine[self.order[stage]]
        left, after = self.left(stage), self.left(stage + 1)
        landed = self.landing[stage]

        def body(index, rows):
            at = iter(index)
            full = tuple(mine if b == self.order[stage] else next(at) for b in left)
            if stage == 0:
                kept = self.source[full + (rows, self.columns)]
            else:
                kept = self.landing[stage - 1][full + (rows, slice(None))]
            total = kept.astype(F32) + landed[index + (rows, slice(None))].astype(F32)
            if after:
                landed[index + (rows, slice(None))] = total.astype(BF16)
            else:
                self.final(rows, total)

        over_blocks(len(after), landed.shape[-2], body)


class Group:
    def __init__(self, members, done=None):
        self.members, self.done, self.stage = members, done, 0

    def launch(self):
        for job in self.members:
            job.send(0)

    def act(self, member, stage):
        job = self.members[member]
        if stage:
            job.add(stage - 1)
        if stage < len(job.order):
            job.send(stage)
        else:
            self.stage += 1
            if self.stage == len(self.members) and self.done:
                self.done()

    def advance(self, stage):
        stages = len(self.members[0].order)
        for job in self.members:
            job.add(stage)
            if stage + 1 < stages:
                job.send(stage + 1)
        if stage + 1 == stages and self.done:
            self.done()

    def release(self):
        for job in self.members:
            job.moves[0]().wait_send()
            job.copies.drop(job.moves[0])


def fill(target, at, value):
    rows, lead = target.shape[-2], len(target.shape) - 2
    inner = (value.shape[0] // rows).bit_length() - 1
    index = tuple((at // 2 ** (lead - 1 - k)) % 2 for k in range(lead - inner))
    target[index] = value.reshape((2,) * inner + (rows, value.shape[1])).astype(BF16)


def by_tiles(target, rows, value_of):
    tile = min(512, rows)

    def one(i, carry):
        m = pl.multiple_of(i * tile, tile)
        fill(target, i * (tile // target.shape[-2]), value_of(pl.ds(m, tile)))
        return carry

    lax.fori_loop(0, rows // tile, one, 0)


def seq_orders(width, seq_bits, low=None):
    low = width - LANE if low is None else low
    first = tuple(range(seq_bits))
    orders = ((0, low, first), (low, width - low, (1, 0) + first[2:]))
    return [item for item in orders if item[1]]


def timetable(groups, loads=()):
    rate, delay, turn_time, ahead = 23.3, 4.0, 1.0, 8.0
    jobs, free, clock, found = [], {}, 0.0, []
    for g, (ready, axis, size, members) in enumerate(groups):
        for m, (columns, order) in enumerate(members):
            jobs.append([ready, ready, g, m, 0, columns * size, axis, order])
    for ready, axis, bit, size in loads:
        jobs.append([ready, ready, -1, 0, 0, 2 * size, axis, (bit,)])
    while jobs:
        best = None
        for job in jobs:
            ready, made, g, m, stage, size, axis, order = job
            issue = max(clock, ready)
            if stage < len(order):
                bit = order[stage]
                link = (axis, min(bit, 1))
                issue = max(issue, free.get(link, 0.0) - ahead)
            key = (issue, -stage, made, g, m)
            if best is None or key < best[0]:
                best = (key, job)
        (issue, *_), job = best
        ready, made, g, m, stage, size, axis, order = job
        if g >= 0:
            found.append((issue, g, m, stage))
        clock = issue + (turn_time if stage else 0.1)
        if stage == len(order):
            jobs.remove(job)
            continue
        bit = order[stage]
        link = (axis, min(bit, 1))
        took = size / 2 ** (stage + 1) * rate
        if axis == "wt" and bit == 0:
            took = took / 6
        start = max(clock, free.get(link, 0.0))
        free[link] = end = start + took
        if bit > 1:
            start = max(start, free.get((axis, bit), 0.0))
            free[axis, bit] = end = start + 2 * took
        job[0], job[4] = end + delay, stage + 1
    return found


def seq_group(copies, source, name, take, final, seq, peer, done=None, low=None):
    seq_bits = len(source.shape) - 2
    dims = list(reversed(range(seq_bits)))
    if name == "chan":
        dims = [0] + dims[:-1]
    members = []
    for start, size, order in seq_orders(source.shape[-1], seq_bits, low):
        members.append(
            Halving(
                copies, source, dims, order, slice(start, start + size), take(seq_bits),
                functools.partial(final, start), seq, peer,
            )
        )
    return Group(members, done)


def landings(bits, rows, widths):
    return [
        pltpu.VMEM((2,) * (bits - 1 - stage) + (rows, width), BF16)
        for width in widths
        for stage in range(bits)
    ]


def seq_landings(seq_bits, rows, widths, low=None):
    found = []
    for width in widths:
        sizes = [size for _, size, _ in seq_orders(width, seq_bits, low)]
        found += landings(seq_bits, rows, sizes)
    return found


def wout_lows(n_wide, late):
    return [WIDE // 2 if late else 3 * WIDE // 4] + [7 * WIDE // 8 if late else WIDE // 2] * (n_wide - 1)


def feat_plan(n_chan, parts):
    half = n_chan // 2
    plan = [
        (n_chan + half, half, 3 * half // 4), (0, half, half), (half, half // 2, half // 2),
        (half + half // 2, half // 2, half // 4),
    ]
    return plan if parts > 1 else [(n_chan, half, None)] + plan


def feat_type(n_feat, n_seq, n_wt):
    return BF16 if n_feat // (n_seq * n_wt) % 16 == 0 else F32


def parts_of(n_chan, n_seq):
    return 2 if n_chan // n_seq >= 32 else 1


WIDE = 1024
EARLY = 512


def join_rounds(
    n_seq, n_streams, seq, wt, rate, head_ref, tail_ref, run_s, span_in, span_s, gap_s, send_s,
    land_s, span_send, span_land, send_sems, recv_sems,
):
    head_ref[...] = jnp.zeros_like(head_ref)
    tail_ref[...] = jnp.zeros_like(tail_ref)
    gap_s[...] = jnp.zeros_like(gap_s)
    for k in range(2 * n_streams):
        span_s[k : k + 1, :] = span_in[k % n_streams]
    started = []
    for r in range(n_seq.bit_length() - 1):
        d = 2**r
        if r > 1:
            for inside, copies in started[2 * r - 4 : 2 * r - 2]:

                @pl.when(inside)
                def _():
                    copies[0].wait_send()

        send_s[r % 2] = run_s[...].astype(BF16)
        span_send[r] = span_s[...]
        up = (seq + d < n_seq, lax.rem(seq + d, n_seq))
        down = (seq >= d, lax.rem(seq + n_seq - d, n_seq))
        for way, (inside, other) in enumerate((up, down)):
            copies = [
                pltpu.make_async_remote_copy(
                    src_ref=src, dst_ref=dst, send_sem=send_sems.at[r, way, k],
                    recv_sem=recv_sems.at[r, way, k], device_id=(other, wt), device_id_type=MESH,
                )
                for k, (src, dst) in enumerate(
                    ((send_s.at[r % 2, way], land_s.at[r, way]), (span_send.at[r], span_land.at[r, way]))
                )
            ]

            @pl.when(inside)
            def _():
                for copy in copies:
                    copy.start()

            started.append((inside, copies))
        for way, inside in ((0, down[0]), (1, up[0])):
            copies = started[-2 + way][1]
            out = (head_ref, tail_ref)[way]

            @pl.when(inside)
            def _():
                for copy in copies:
                    copy.wait_recv()
                for b in range(n_streams):
                    k = way * n_streams + b
                    landed = land_s[r, way, b].astype(F32)
                    span = span_land[r, way, k : k + 1, :]
                    gap, own = gap_s[k : k + 1, :], span_s[k : k + 1, :]
                    out[b] = out[b] + jnp.exp2(rate * gap) * landed
                    run_s[way, b] = run_s[way, b] + jnp.exp2(rate * own) * landed
                    gap_s[k : k + 1, :] = gap + span
                    span_s[k : k + 1, :] = own + span

    for at, (inside, copies) in enumerate(started):

        @pl.when(inside)
        def _():
            for copy in copies[at < len(started) - 4 :]:
                copy.wait_send()


def early_sums(n_seq, part, stream, width, grad_ref, normed_t_ref, wout_ref, feat_ref, scratch):
    gated_s, dgate_s, grads, normed_t = scratch[:4]
    feat_parts, scratch = scratch[4:6], scratch[6:]
    seq_bits = n_seq.bit_length() - 1
    count = grads.shape[1] // WIDE
    wout_parts, scratch = scratch[:count], scratch[count:]
    load_sems, send_sems, recv_sems = scratch[:3]
    scratch = scratch[3:]
    take = lambda k: [scratch.pop(0) for _ in range(k)]
    seq, wt = lax.axis_index("seq"), lax.axis_index("wt")
    copies = Copies(send_sems, recv_sems)
    peer = lambda bit: (flip(seq, bit), wt)

    def loads():
        return [
            pltpu.make_async_copy(grad_ref, grads, load_sems.at[0]),
            pltpu.make_async_copy(normed_t_ref, normed_t, load_sems.at[1]),
        ]

    def wout_final(at, start, rows, total):
        wout_ref[rows, at + start : at + start + total.shape[1]] = total.astype(BF16)

    def feat_final(at, start, rows, total):
        columns = slice(at + start, at + start + total.shape[1])
        feat_ref[rows, columns] = total.astype(feat_ref.dtype)

    lows = wout_lows(count, False)
    wouts = [
        seq_group(
            copies, wout_parts[k], "chan", take, functools.partial(wout_final, k * WIDE), seq, peer,
            low=lows[k],
        )
        for k in range(count)
    ]
    width = EARLY // 2
    feats = [
        seq_group(
            copies, feat_parts[k], "feat", take, functools.partial(feat_final, k * width), seq, peer
        )
        for k in range(2)
    ]
    groups = wouts + feats

    @pl.when((part == 0) & (stream == 0))
    def _():
        barrier = pltpu.get_barrier_semaphore()
        for bit in range(seq_bits):
            pl.semaphore_signal(barrier, inc=1, device_id=peer(bit), device_id_type=MESH)
        pl.semaphore_wait(barrier, seq_bits)
        for copy in loads():
            copy.start()

    def begin():
        for copy in loads():
            copy.wait()
        for k in range(count):
            for inner in range(0, WIDE, 512):
                at = k * WIDE + inner
                value = jnp.dot(
                    gated_s[...], grads[:, at : at + 512], preferred_element_type=F32
                )
                rows, lead = wout_parts[k].shape[-2], len(wout_parts[k].shape) - 2
                wout_parts[k][(slice(None),) * (lead + 1) + (slice(inner, inner + 512),)] = (
                    value.reshape((2,) * lead + (rows, 512)).astype(BF16)
                )

    def begin_feat():
        for k in range(2):
            at = slice(k * width, (k + 1) * width)
            by_tiles(
                feat_parts[k], normed_t.shape[0],
                lambda m: jnp.dot(normed_t[m, :], dgate_s[:, at], preferred_element_type=F32),
            )

    entries = []
    for which, group in enumerate(groups):
        rows = math.prod(group.members[0].source.shape[:-1])
        members = [(one.columns.stop - one.columns.start, one.order) for one in group.members]
        ready = 2.0 if which < count else 8.0
        entries.append((ready, "seq", rows * 2 / 2**20, members))
    times = [3.5, 9.0] + [9.0 + 2.9 * k for k in range(1, 15)]
    moments, last = {}, []
    for at, which, member, stage in timetable(entries):
        turns = [k for k, time in enumerate(times) if time >= at]
        moments.setdefault(turns[0] if turns else 16, []).append((which, member, stage))

    def moment(turn):
        if turn < 2:

            @pl.when((part == 1) & (stream == 0))
            def _():
                (begin, begin_feat)[turn]()

        for at in range(4):
            if at * 4 + turn in moments:

                @pl.when((part == 1) & (stream == at))
                def _():
                    for which, member, stage in moments[at * 4 + turn]:
                        groups[which].act(member, stage)

    def rest():
        for which, member, stage in moments.get(16, []):
            groups[which].act(member, stage)
        copies.finish()

    return moment, rest


def scan_kernel(
    n_state, n_seq, parts, bcs_ref, spread_ref, gather_ref, raw_ref, u_ref, g_ref, gate_ref, dgated_ref,
    bias_ref, skip_ref, a_ref, end_ref, lead_ref, total_ref, head_ref, tail_ref, grad_ref,
    normed_t_ref,
    gated_ref, gated_t_ref, dgate_ref, dscan_ref, draw_ref, dbc_ref, da_ref, sums_ref, wout_ref,
    feat_ref,
    bcb, acc_all, dec_in, delta_in, drive_in, g_in, y_sum, b_sum, d_sum, kept, decays, da_sum, row_sum, *scratch,
):
    n_rows, width = raw_ref.shape
    steps = n_rows // SUB
    part, stream = pl.program_id(0), pl.program_id(1)
    n_streams = pl.num_programs(1)
    acc = acc_all.at[stream]
    if parts > 1:
        early_moment, early_rest = early_sums(
            n_seq, part, stream, width, grad_ref, normed_t_ref, wout_ref, feat_ref, list(scratch)
        )
    start_at = 2 * n_state * LANE
    columns = pl.ds(pl.multiple_of(part * width, width), width)
    spread_rows(bcs_ref, spread_ref, bcb)

    @pl.when(part == 0)
    def _():
        acc_all[stream] = jnp.zeros(acc_all.shape[1:], F32)

    @pl.when(stream == 0)
    def _():
        da_sum[...] = jnp.zeros_like(da_sum)
        row_sum[...] = jnp.zeros_like(row_sum)

    def prepare(j, carry):
        rows = pl.ds(pl.multiple_of(j * 16, 16), 16)
        delta = softplus(raw_ref[rows, :].astype(F32) + bias_ref[...])
        starts = wide(bcb[rows, start_at : start_at + LANE], width)
        delta_in[rows, :] = delta
        dec_in[rows, :] = jnp.where(starts > 0.5, RESET, delta)
        drive_in[rows, :] = delta * u_ref[rows, :].astype(F32)
        g_in[rows, :] = g_ref[rows, :].astype(F32)
        return carry

    lax.fori_loop(0, steps // 2, prepare, 0)
    chunk = lax.broadcasted_iota(jnp.int32, (SUB, width), 0)
    total = total_ref[0]
    before, after = total, total
    for shift in (1, 2, 4):
        before = jnp.where(chunk >= shift, before + pltpu.roll(before, shift, 0), before)
        after = jnp.where(chunk < SUB - shift, after + pltpu.roll(after, SUB - shift, 0), after)
    before, after = pltpu.roll(before, 1, 0), pltpu.roll(after, SUB - 1, 0)

    for first in range(0, n_state, NBLK):
        if parts > 1:
            early_moment(first // NBLK)
        states = range(first, first + NBLK)
        entry, incoming = [], []
        for n in states:
            head, tail = head_ref[0, n : n + 1, :], tail_ref[0, n : n + 1, :]
            inner = pltpu.roll(end_ref[0, n], 1, 0) + jnp.exp2(before * a_ref[n : n + 1, :]) * head
            outer = pltpu.roll(lead_ref[0, n], SUB - 1, 0) + jnp.exp2(after * a_ref[n : n + 1, :]) * tail
            entry.append(jnp.where(chunk == 0, head, inner))
            incoming.append(jnp.where(chunk == SUB - 1, tail, outer))

        def forward(j, carry):
            rows = pl.ds(pl.multiple_of(j * SUB, SUB), SUB)
            held, drive, g = dec_in[rows, :], drive_in[rows, :], g_in[rows, :]
            running = []
            y = y_sum[rows, :] if first else None
            for k, (n, h) in enumerate(zip(states, carry)):
                b = wide(bcb[rows, n * LANE : (n + 1) * LANE], width)
                c_at = slice((n_state + n) * LANE, (n_state + n + 1) * LANE)
                c = wide(bcb[rows, c_at], width)
                decay = jnp.exp2(held * a_ref[n : n + 1, :])
                kept[k, rows, :] = h
                decays[k, rows, :] = decay
                h = decay * h + drive * b
                y = c * h if y is None else y + c * h
                acc[rows, c_at] += fold(h * g)
                running.append(h)
            y_sum[rows, :] = y
            return tuple(running)

        lax.fori_loop(0, steps, forward, tuple(entry), unroll=4)

        def backward(j, carry):
            rows = pl.ds(pl.multiple_of((steps - 1 - j) * SUB, SUB), SUB)
            delta, drive, g = delta_in[rows, :], drive_in[rows, :], g_in[rows, :]
            through = b_sum[rows, :] if first else None
            pulled = d_sum[rows, :] if first else None
            passed, da = [], []
            for k, (n, p, da_n) in enumerate(zip(states, carry[0], carry[1])):
                b_at = slice(n * LANE, (n + 1) * LANE)
                b = wide(bcb[rows, b_at], width)
                c = wide(bcb[rows, (n_state + n) * LANE : (n_state + n + 1) * LANE], width)
                adjoint = g * c + p
                p = decays[k, rows, :] * adjoint
                weighed = p * kept[k, rows, :]
                pulled = weighed * a_ref[n : n + 1, :] if pulled is None else pulled + weighed * a_ref[n : n + 1, :]
                through = adjoint * b if through is None else through + adjoint * b
                acc[rows, b_at] += fold(adjoint * drive)
                passed.append(p)
                da.append(da_n + weighed * delta)
            b_sum[rows, :] = through
            d_sum[rows, :] = pulled
            return tuple(passed), tuple(da)

        zero = tuple(jnp.zeros((SUB, width), F32) for _ in states)
        _, da = lax.fori_loop(0, steps, backward, (tuple(incoming), zero), unroll=4)
        for n, da_n in zip(states, da):
            da_sum[n] += da_n

    def finish(j, carry):
        bias_sum, skip_sum = carry
        rows = pl.ds(pl.multiple_of(j * 16, 16), 16)
        u, g, delta = u_ref[rows, :].astype(F32), g_in[rows, :], delta_in[rows, :]
        gate, d_gated = gate_ref[rows, :].astype(F32), dgated_ref[rows, :]
        scanned = (y_sum[rows, :] + skip_ref[...] * u).astype(BF16).astype(F32)
        sig = jax.nn.sigmoid(gate)
        gated_ref[rows, :] = (scanned * gate * sig).astype(BF16)
        d_gate = d_gated * scanned * sig * (1.0 + gate * (1.0 - sig))
        dgate_ref[rows, :] = d_gate.astype(BF16)
        through = b_sum[rows, :]
        dscan_ref[rows, :] = (delta * through + skip_ref[...] * g).astype(BF16)
        slope = jax.nn.sigmoid(raw_ref[rows, :].astype(F32) + bias_ref[...])
        d_pre = (d_sum[rows, :] * (1.0 / LOG2E) + u * through) * slope
        draw_ref[rows, :] = d_pre.astype(BF16)
        gu = g * u
        return bias_sum + d_pre[:SUB] + d_pre[SUB:], skip_sum + gu[:SUB] + gu[SUB:]

    zero = jnp.zeros((SUB, width), F32)
    bias_sum, skip_sum = lax.fori_loop(0, steps // 2, finish, (zero, zero))
    gated_t_ref[...] = gated_ref[...].T
    if parts > 1:
        gated_s, dgate_s = scratch[:2]

        @pl.when(part == 0)
        def _():
            at = pl.ds(pl.multiple_of(stream * n_rows, n_rows), n_rows)
            gated_s[:, at] = gated_t_ref[...]
            dgate_s[at, :] = dgate_ref[...]

    row_sum[0] += bias_sum
    row_sum[1] += skip_sum

    @pl.when(stream == n_streams - 1)
    def _():
        for n in range(n_state):
            da_ref[n : n + 1, columns] = jnp.sum(da_sum[n], 0, keepdims=True)
        for k in range(2):
            sums_ref[k : k + 1, columns] = jnp.sum(row_sum[k], 0, keepdims=True)


    last = part == pl.num_programs(0) - 1

    @pl.when(last)
    def _():
        found = jnp.dot(
            acc[...], gather_ref[...], precision=lax.Precision.HIGHEST, preferred_element_type=F32
        )

        @pl.when(stream == 0)
        def _():
            dbc_ref[...] = found

        @pl.when(stream > 0)
        def _():
            dbc_ref[...] += pltpu.roll(found, stream * 2 * n_state, 1)

    if parts > 1:

        @pl.when(last & (stream == n_streams - 1))
        def _():
            early_rest()


def spread_matrix(n_state):
    count = 2 * n_state + 1
    column = np.arange(count * LANE)[None, :] // LANE
    return jnp.asarray((np.arange(LANE)[:, None] == column).astype(ml_dtypes.bfloat16))


def gather_matrix(n_state):
    row = np.arange(2 * n_state * LANE)[:, None] // LANE
    return jnp.asarray((np.arange(LANE)[None, :] == row).astype(np.float32))


def scan_specs(n_streams, n_rows, n_chan, n_state, width):
    row = pl.BlockSpec((n_rows, width), lambda b, c: (b, c))
    thin = pl.BlockSpec((n_rows, LANE), lambda b, c: (b, 0))
    chan = pl.BlockSpec((1, width), lambda b, c: (0, c))
    rate = pl.BlockSpec((n_state, width), lambda b, c: (0, c))
    edge = pl.BlockSpec((1, n_state, SUB, width), lambda b, c: (b, 0, 0, c))
    total = pl.BlockSpec((1, SUB, width), lambda b, c: (b, 0, c))
    head = pl.BlockSpec((1, n_state, width), lambda b, c: (b, 0, c))
    return row, thin, chan, rate, edge, total, head


def whole(shape):
    return pl.BlockSpec(shape, lambda b, c: (0,) * len(shape))


def scan_all(
    bcs, raw, u, g, gate, d_gated, bias, skip, rates, ends, leads, totals, heads, tails, grads,
    normed_t,
):
    n_seq, n_streams = lax.axis_size("seq"), lax.axis_size("wt")
    n_rows, n_chan = raw.shape[0] // n_streams, raw.shape[1]
    n_state, n_feat = rates.shape[0], normed_t.shape[0]
    width = min(512, n_chan)
    parts = parts_of(n_chan, n_seq)
    seq_bits = n_seq.bit_length() - 1

    def swapped(spec):
        return pl.BlockSpec(spec.block_shape, lambda c, b: spec.index_map(b, c))

    row, thin, chan, rate, edge, total, head = map(
        swapped, scan_specs(n_streams, n_rows, n_chan, n_state, width)
    )
    count = (2 * n_state + 1) * LANE
    spread = spread_matrix(n_state)
    gather = gather_matrix(n_state)
    rows = jax.ShapeDtypeStruct(raw.shape, BF16)
    hbm = pl.BlockSpec(memory_space=pl.ANY)
    wout_rows, feat_rows = max(n_chan // parts // n_seq, 16), n_feat // n_seq
    scratch = [
        pltpu.VMEM((n_rows, count), F32),
        pltpu.VMEM((n_streams, n_rows, 2 * n_state * LANE), F32),
    ]
    scratch += [pltpu.VMEM((n_rows, width), F32)] * 7
    scratch += [pltpu.VMEM((NBLK, n_rows, width), F32)] * 2
    scratch += [pltpu.VMEM((n_state, SUB, width), F32), pltpu.VMEM((2, SUB, width), F32)]
    params = {}
    if parts > 1:
        blocks = (2,) * seq_bits
        n_wide = n_feat // WIDE
        scratch += [
            pltpu.VMEM((width, raw.shape[0]), BF16),
            pltpu.VMEM((raw.shape[0], width), BF16),
            pltpu.VMEM((raw.shape[0], n_feat), BF16),
            pltpu.VMEM(normed_t.shape, BF16),
        ]
        scratch += [pltpu.VMEM(blocks + (feat_rows, EARLY // 2), BF16)] * 2
        scratch += [pltpu.VMEM(blocks + (wout_rows, WIDE), BF16)] * n_wide
        scratch += [pltpu.SemaphoreType.DMA((2,))]
        scratch += [pltpu.SemaphoreType.DMA((2 * seq_bits * (n_wide + 2),))] * 2
        for low in wout_lows(n_wide, False):
            scratch += seq_landings(seq_bits, wout_rows, [WIDE], low)
        scratch += seq_landings(seq_bits, feat_rows, [EARLY // 2] * 2)
        params = dict(collective_id=4, has_side_effects=True)
    return pl.pallas_call(
        functools.partial(scan_kernel, n_state, n_seq, parts),
        grid=(n_chan // width, n_streams),
        in_specs=[
            thin, whole((LANE, count)), whole(gather.shape), row, row, row, row, row,
            chan, chan, rate, edge, edge, total, head, head, hbm, hbm,
        ],
        out_specs=[
            row, pl.BlockSpec((width, n_rows), lambda c, b: (c, b)), row, row, row,
            whole((n_rows, LANE)), whole((n_state, n_chan)), whole((2, n_chan)),
            whole((wout_rows, n_feat)), whole((feat_rows, EARLY)),
        ],
        out_shape=[
            rows, jax.ShapeDtypeStruct(raw.shape[::-1], BF16), rows, rows, rows,
            jax.ShapeDtypeStruct((n_rows, LANE), F32),
            jax.ShapeDtypeStruct((n_state, n_chan), F32),
            jax.ShapeDtypeStruct((2, n_chan), F32),
            jax.ShapeDtypeStruct((wout_rows, n_feat), BF16),
            jax.ShapeDtypeStruct((feat_rows, EARLY), feat_type(n_feat, n_seq, n_streams)),
        ],
        scratch_shapes=scratch,
        compiler_params=pltpu.CompilerParams(vmem_limit_bytes=63 * 2**20, **params),
        name="scan_all",
    )(
        bcs, spread, gather, raw, u, g, gate, d_gated, bias, skip, rates,
        ends, leads, totals, heads, tails, grads, normed_t,
    )


def finish_kernel(
    n_seq, n_wt, n_state,
    gated_t_ref, dgate_ref, dscan_ref, draw_ref, u_ref, conv_ref, grad_ref, normed_t_ref, win_ref,
    wout_ref, feat_ref, gated_ref, w_out_ref, x_ref, g_ref,
    gain_ref, dbc_ref, low_ref, wx_ref, wdt_ref, wconv_ref, bconv_ref, da_ref, a_ref, sums_ref,
    feat_out, wout_out, small_out, norm_out, out_out, gain_out,
    *scratch,
):
    scratch = list(scratch)
    take = lambda count: [scratch.pop(0) for _ in range(count)]
    seq, wt = lax.axis_index("seq"), lax.axis_index("wt")
    seq_bits, wt_bits = n_seq.bit_length() - 1, n_wt.bit_length() - 1
    seq_peer = lambda bit: (flip(seq, bit), wt)
    wt_peer = lambda bit: (seq, flip(wt, bit))
    n_chan, all_rows = gated_t_ref.shape
    parts = parts_of(n_chan, n_seq)
    ready = parts - 1
    half_seq = n_seq // 2
    here = n_wt * seq + wt
    mine = (seq % 2) * half_seq + seq // 2

    def summed_at(j):
        return (j % half_seq) * 2 + j // half_seq

    def device(flat):
        return flat // n_wt, flat % n_wt

    flat = n_seq * wt + mine
    owner, giver_block = device(flat), here % n_seq
    giver = (summed_at(giver_block), here // n_seq)
    elsewhere = flat != here
    per = n_seq // parts
    part_flat = [n_seq * wt + q * per + mine // parts for q in range(parts)]
    part_owner = [device(value) for value in part_flat]
    piece = mine % parts
    piece_giver = [
        (summed_at((giver_block % per) * parts + k), here // n_seq) for k in range(parts)
    ]
    piece_here = [n_wt * s + w == here for s, w in piece_giver]
    ahead, behind = (lax.rem(seq + 1, n_seq), wt), (lax.rem(seq + n_seq - 1, n_seq), wt)

    barrier = pltpu.get_barrier_semaphore()
    partners = [seq_peer(b) for b in range(seq_bits)]
    partners += [(seq, turn(wt, mask, wt_bits)) for mask in range(1, n_wt)]
    partners += [ahead, behind]
    for partner in partners:
        pl.semaphore_signal(barrier, inc=1, device_id=partner, device_id_type=MESH)

    arrivals = len(partners) + 2 * elsewhere.astype(jnp.int32)

    @pl.when(elsewhere)
    def _():
        for partner in (owner, giver):
            pl.semaphore_signal(barrier, inc=1, device_id=partner, device_id_type=MESH)

    if parts > 1:
        others = [(value != here, to) for value, to in zip(part_flat, part_owner)]
        others += [(jnp.logical_not(own), to) for own, to in zip(piece_here, piece_giver)]
        for away, to in others:
            arrivals = arrivals + away.astype(jnp.int32)

            @pl.when(away)
            def _():
                pl.semaphore_signal(barrier, inc=1, device_id=to, device_id_type=MESH)

    (
        gated_t, dgate, dscan, draw, normed_t, grads, win_rows, conv, d_conv, mix, first, half, land, fin,
        u_all, ddt, dbc, pack, rim_f, rim_s, fin_feat, fin_wout, fin_small, w_rows, gain_sum, small,
        piece_sems, send_sems, recv_sems,
    ) = take(29)
    n_wide = normed_t.shape[0] // WIDE
    wout_parts = take(n_wide) if ready else take(1) * n_wide
    feat_parts, norm_parts = take(4 if ready else 3), take(2)
    if not ready:
        inner = (slice(None),) * (seq_bits + 1)
        feat_parts += [feat_parts[0].at[inner + (slice(at, at + 256),)] for at in (0, 256)]
    copies = Copies(send_sems, recv_sems)
    part_chan = gated_t.shape[0]
    if not ready:
        u_all = gated_t
    n_feat = normed_t.shape[0]
    n_rows = all_rows // n_wt
    taps = wconv_ref.shape[0]
    steps = n_rows // SUB
    rim = (taps - 1) * SUB
    cols = 512

    def load(src, dst):
        return copies.local(src, dst)

    def grad_block(k):
        return load(grad_ref.at[:, :, k * cols : (k + 1) * cols], grads.at[k % 2])

    coming = {
        "draw": load(draw_ref, draw),
        "gated": load(gated_t_ref.at[ready * part_chan :], gated_t),
        0: grad_block(0),
        1: grad_block(1),
        "normed": load(normed_t_ref, normed_t),
        "dgate": load(dgate_ref, dgate),
        "conv": load(conv_ref.at[:, :, :cols], conv),
        "dscan": load(dscan_ref.at[:, :cols], dscan),
        "w_rows": load(
            win_ref.at[pl.ds(pl.multiple_of(seq * w_rows.shape[0], 16), w_rows.shape[0])], w_rows
        ),
    }

    ring, d_block = win_rows.shape[:2]

    def win_block(i):
        coming["win", i] = load(win_ref.at[i * d_block : (i + 1) * d_block], win_rows.at[i % ring])

    for k in range(cols // d_block):
        win_block(k)
    if ready:
        coming["wout"] = load(wout_ref, fin_wout.at[0])
        coming["feat"] = load(feat_ref, fin_feat.at[:, n_chan : n_chan + EARLY])
    pl.semaphore_wait(barrier, arrivals)

    rows_own = feat_out.shape[0]

    def own_rows(w):
        return pl.ds(pl.multiple_of(w * rows_own, 8), rows_own)

    delivered = []

    def to_wt(block_of, place):
        for mask in range(1, n_wt):
            peer = turn(wt, mask, wt_bits)
            delivered.append(copies.remote(block_of(peer), place, (seq, peer)).wait_recv)
        delivered.append(copies.local(block_of(wt), place).wait)

    def feat_done(at, cols):
        tile = math.gcd(w_rows.shape[0], 32)

        def body(i, carry):
            rows = pl.ds(pl.multiple_of(i * tile, tile), tile)
            done = fin_feat[rows, at : at + cols].astype(F32)
            product = w_rows[rows, at : at + cols].astype(F32) * done
            gain_sum[rows, :] += fold(product)
            return carry

        lax.fori_loop(0, w_rows.shape[0] // tile, body, 0)
        start = pl.multiple_of(((at // n_chan) * n_wt + wt) * n_chan + at % n_chan, LANE)
        to_wt(
            lambda w: fin_feat.at[own_rows(w), at : at + cols],
            feat_out.at[:, pl.ds(start, cols)],
        )

    moved = []

    def small_done():
        k, copies.count = copies.count, copies.count + 1
        away = pltpu.make_async_remote_copy(
            src_ref=fin_small, dst_ref=small_out, send_sem=send_sems.at[k],
            recv_sem=recv_sems.at[k], device_id=owner, device_id_type=MESH,
        )
        home = pltpu.make_async_copy(fin_small, small_out, send_sems.at[k])

        @pl.when(elsewhere)
        def _():
            away.start()

        @pl.when(jnp.logical_not(elsewhere))
        def _():
            home.start()

        def wait():
            @pl.when(elsewhere)
            def _():
                away.wait()

            @pl.when(jnp.logical_not(elsewhere))
            def _():
                home.wait()

        moved.append(wait)

    def wout_done(q, at, width, slot):
        place = fin_wout.at[q, :, at : at + width]
        target = wout_out.at[piece, :, at : at + width]
        away = pltpu.make_async_remote_copy(
            src_ref=place, dst_ref=target, send_sem=piece_sems.at[0, q, slot],
            recv_sem=piece_sems.at[1, piece, slot], device_id=part_owner[q], device_id_type=MESH,
        )
        home = pltpu.make_async_copy(place, target, piece_sems.at[0, q, slot])
        remote = part_flat[q] != here

        @pl.when(remote)
        def _():
            away.start()

        @pl.when(jnp.logical_not(remote))
        def _():
            home.start()

        def wait():
            @pl.when(remote)
            def _():
                away.wait_send()

            @pl.when(jnp.logical_not(remote))
            def _():
                home.wait()

        moved.append(wait)

    def wout_arrive(k, at, width, slot):
        target = wout_out.at[k, :, at : at + width]
        copy = pltpu.make_async_remote_copy(
            src_ref=target, dst_ref=target, send_sem=piece_sems.at[0, k, slot],
            recv_sem=piece_sems.at[1, k, slot], device_id=piece_giver[k], device_id_type=MESH,
        )

        @pl.when(jnp.logical_not(piece_here[k]))
        def _():
            copy.wait_recv()

    def wout_final(at, start, rows, total):
        columns = slice(at + start, at + start + total.shape[1])
        fin_wout[ready, rows, columns] = total.astype(BF16)

    def feat_final(at, start, rows, total):
        columns = slice(at + start, at + start + total.shape[1])
        fin_feat[rows, columns] = total.astype(fin_feat.dtype)

    def small_final(start, rows, total):
        fin_small[rows, start : start + total.shape[1]] = total.astype(BF16)

    wout_groups = [
        seq_group(
            copies, wout_parts[k], "chan", take, functools.partial(wout_final, k * WIDE), seq,
            seq_peer, functools.partial(wout_done, ready, k * WIDE, WIDE, k), lows[k],
        )
        for k, lows in zip(range(n_wide), [wout_lows(n_wide, True)] * n_wide)
    ]
    feat_groups = []
    for part, (at, _, low) in zip(feat_parts, feat_plan(n_chan, parts)):
        done = functools.partial(feat_done, at, part.shape[-1])
        feat_groups.append(
            seq_group(
                copies, part, "feat", take, functools.partial(feat_final, at), seq, seq_peer, done,
                low,
            )
        )
    gate_a, gate_b, conv_a, conv_b, conv_c = range(-ready, 5 - ready)
    small_group = seq_group(copies, small, "chan", take, small_final, seq, seq_peer, small_done)
    wide_groups = []
    for target in (norm_out, out_out):
        for k in range(n_feat // cols):

            def final(rows, total, target=target, k=k):
                target[rows, k * cols : (k + 1) * cols] = total

            order = tuple(range(wt_bits))
            job = Halving(
                copies, norm_parts[k % 2], list(reversed(order)), order, slice(0, cols),
                take(wt_bits), final, wt, wt_peer,
            )
            wide_groups.append(Group([job]))

    def wout(k):
        if not ready and k:
            take_until(k - 1)
            wout_groups[k - 1].release()
        for inner in range(WIDE // cols):
            block = k * (WIDE // cols) + inner
            coming[block].wait()
            right = grads[block % 2].reshape(all_rows, cols)
            lanes = slice(inner * cols, (inner + 1) * cols)
            tile = min(512, part_chan)
            rows, lead = wout_parts[k].shape[-2], len(wout_parts[k].shape) - 2
            within = (tile // rows).bit_length() - 1
            for m in range(0, part_chan, tile):
                value = jnp.dot(gated_t[m : m + tile, :], right, preferred_element_type=F32)
                index = tuple(
                    (m // rows >> (lead - 1 - q)) & 1 for q in range(lead - within)
                )
                wout_parts[k][index + (slice(None),) * (within + 1) + (lanes,)] = (
                    value.reshape((2,) * within + (rows, cols)).astype(BF16)
                )
            if block + 2 < n_feat // cols:
                coming[block + 2] = grad_block(block + 2)

    gain_sum[...] = jnp.zeros_like(gain_sum)
    coming["draw"].wait()
    for b in range(n_wt):
        at = slice(b * n_rows, (b + 1) * n_rows)
        mix[at, :] = jnp.dot(draw[at, :], wdt_ref[...], preferred_element_type=F32)
    width = LANE // n_wt
    mix[all_rows:, :] = dbc_ref[...]
    mixed = WtSum(copies, mix, first, half, land, fin, seq, wt, wt_bits)
    mixed.begin()
    coming["gated"].wait()

    def feat(k, right):
        if not ready and k == conv_b:
            take_until(first_feat + gate_a)
            feat_groups[gate_a].release()
        by_tiles(
            feat_parts[k], n_feat,
            lambda m: jnp.dot(normed_t[m, :], right, preferred_element_type=F32),
        )

    def low_pack():
        pack[LANE : 2 * LANE, :] = lax.dot_general(
            low_ref[...], draw[...], (((0,), (0,)), ((), ())), preferred_element_type=F32
        )
        mixed.end_send()
        coming["normed"].wait()
        coming["dgate"].wait()

    def early_feat():
        coming["w_rows"].wait()
        if ready:
            coming["feat"].wait()
            feat_done(n_chan, EARLY)
        mixed.copy.wait_recv()
        mixed_ready()

    tail_at = 2 * LANE + 3 * n_state

    def mixed_ready():
        ddt[...] = fin[:all_rows, :].astype(BF16)
        lane = lax.broadcasted_iota(jnp.int32, (n_rows, LANE), 1)
        for b in range(n_wt):
            part = fin[all_rows:, :]
            if b:
                part = pltpu.roll(part, LANE - b * width, 1)
            dbc[b * n_rows : (b + 1) * n_rows, :] = jnp.where(lane < width, part, 0.0).astype(BF16)
        coming["u"] = load(u_ref, u_all)

        pack[2 * LANE :, :] = jnp.zeros((LANE, n_chan), F32)
        pack[tail_at - n_state : tail_at, :] = da_ref[...] * (a_ref[...] * (1.0 / LOG2E))
        pack[tail_at + taps + 1 : tail_at + taps + 3, :] = sums_ref[...]

    def sums_of(total):
        return jnp.sum(total, 0, keepdims=True)

    chunk = lax.broadcasted_iota(jnp.int32, (SUB, cols), 0)
    rim_moves = []

    def conv_first(h):
        at = slice(h * cols, (h + 1) * cols)
        for b in range(n_wt):
            rows = slice(b * n_rows, (b + 1) * n_rows)
            d_in = lax.dot_general(
                ddt[rows, :], wx_ref[at, :LANE], (((1,), (1,)), ((), ())), preferred_element_type=F32
            )
            d_in = d_in + lax.dot_general(
                dbc[rows, : 2 * n_state], wx_ref[at, LANE:], (((1,), (1,)), ((), ())),
                preferred_element_type=F32,
            )
            d_conv[h, b, :n_rows, :] = d_in
        coming["conv"].wait()
        coming["dscan"].wait()

        def one(i, carry):
            b, j = i // (n_rows // 16), i % (n_rows // 16)
            rows = pl.ds(pl.multiple_of(j * 16, 16), 16)
            taken = [
                conv[b, pl.ds(pl.multiple_of(j * 16 + k * SUB, SUB), 16), :] for k in range(taps)
            ]
            out = bconv_ref[:, at]
            for k in range(taps):
                out = out + taken[k] * wconv_ref[k : k + 1, at]
            sig = jax.nn.sigmoid(out)
            from_scan = dscan[pl.ds(pl.multiple_of(i * 16, 16), 16), :].astype(F32)
            value = (d_conv[h, b, rows, :] + from_scan) * sig * (1.0 + out * (1.0 - sig))
            d_conv[h, b, rows, :] = value
            found = [value] + [value * piece for piece in taken]
            return tuple(c + f[:SUB] + f[SUB:] for c, f in zip(carry, found))

        zero = jnp.zeros((SUB, cols), F32)
        totals = lax.fori_loop(0, all_rows // 16, one, (zero,) * (taps + 1))
        pack[tail_at + taps : tail_at + taps + 1, at] = sums_of(totals[0])
        for k in range(taps):
            pack[tail_at + k : tail_at + k + 1, at] = sums_of(totals[k + 1])

        rim_f[...] = jnp.zeros_like(rim_f)
        for b in range(n_wt):
            for k in range(taps - 1):
                rim_f[b * (taps - 1) + k, :] = d_conv[h, b, k * SUB, :]
        rim_s[h, 0] = rim_f[...].astype(BF16)

        @pl.when(seq == n_seq - 1)
        def _():
            rim_s[h, 1] = jnp.zeros((16, cols), BF16)

        k, copies.count = copies.count, copies.count + 1
        move = pltpu.make_async_remote_copy(
            src_ref=rim_s.at[h, 0], dst_ref=rim_s.at[h, 1], send_sem=send_sems.at[k],
            recv_sem=recv_sems.at[k], device_id=behind, device_id_type=MESH,
        )
        rim_moves.append(move)

        @pl.when(seq > 0)
        def _():
            move.start()

        if h == 0:
            coming["conv"] = load(conv_ref.at[:, :, cols : 2 * cols], conv)
            coming["dscan"] = load(dscan_ref.at[:, cols : 2 * cols], dscan)

    def conv_second(h):
        at = slice(h * cols, (h + 1) * cols)

        @pl.when(seq < n_seq - 1)
        def _():
            rim_moves[h].wait_recv()

        landed = rim_s[h, 1].astype(F32)
        for b in range(n_wt):
            for k in range(taps - 1):
                turned = pltpu.roll(d_conv[h, b, k * SUB : (k + 1) * SUB, :], SUB - 1, 0)
                row = landed[b * (taps - 1) + k : b * (taps - 1) + k + 1, :]
                place = slice(n_rows + k * SUB, n_rows + (k + 1) * SUB)
                d_conv[h, b, place, :] = jnp.where(chunk == SUB - 1, row, turned)

        def one(i, carry):
            b, j = i // (n_rows // 16), i % (n_rows // 16)
            total = jnp.zeros((16, cols), F32)
            for k in range(taps):
                start = pl.multiple_of(j * 16 + (taps - 1 - k) * SUB, SUB)
                total = total + d_conv[h, b, pl.ds(start, 16), :] * wconv_ref[k : k + 1, at]
            draw[pl.ds(pl.multiple_of(i * 16, 16), 16), at] = total.astype(BF16)
            return carry

        lax.fori_loop(0, all_rows // 16, one, 0)

    def early_pieces():
        if ready:
            coming["wout"].wait()
            for k in range(n_wide):
                wout_done(0, k * WIDE, WIDE, k)

    def small_sums():
        coming["u"].wait()
        pack[:LANE, :] = lax.dot_general(
            ddt[...], u_all[...], (((0,), (0,)), ((), ())), preferred_element_type=F32
        )
        for_b = lax.dot_general(
            dbc[...], u_all[...], (((0,), (0,)), ((), ())), preferred_element_type=F32
        )
        pack[2 * LANE : 2 * LANE + 2 * n_state, :] = for_b[: 2 * n_state, :]
        coming["gated"] = load(gated_ref, u_all)
        tile = min(512, n_chan)
        for m in range(0, n_chan, tile):
            fill(small, m // small.shape[-2], pack[:, m : m + tile].T)

    per = cols // d_block
    n_norm = n_feat // cols

    def wide_part(k, block_of):
        part = norm_parts[k % 2]
        if k >= 2:
            take_until(len(seq_groups) + k - 2)
            wide_groups[k - 2].release()
        for b in range(n_wt):
            index = tuple((b >> (wt_bits - 1 - q)) & 1 for q in range(wt_bits))
            for lanes, value in block_of(slice(b * n_rows, (b + 1) * n_rows)):
                part[index + (slice(None), lanes)] = value.astype(BF16)

    def norm(k):
        def block_of(at):
            for part in range(per):
                rows_w = win_rows.at[(k * per + part) % ring]
                value = lax.dot_general(
                    draw[at, :], rows_w[:, :n_chan], (((1,), (1,)), ((), ())),
                    preferred_element_type=F32,
                )
                value = value + lax.dot_general(
                    dgate[at, :], rows_w[:, n_chan:], (((1,), (1,)), ((), ())),
                    preferred_element_type=F32,
                )
                yield slice(part * d_block, (part + 1) * d_block), value

        for part in range(per):
            coming["win", k * per + part].wait()
        wide_part(k, block_of)
        for part in range(per):
            if (k + 1) * per + part < per * n_norm:
                win_block((k + 1) * per + part)

    def out_block(k):
        coming["out", k] = load(w_out_ref.at[:, :, k * cols : (k + 1) * cols], grads.at[k % 2])

    def out(k):
        coming["out", k].wait()
        right = grads[k % 2].reshape(all_rows, cols)

        def block_of(at):
            yield slice(0, cols), jnp.dot(u_all[at, :], right, preferred_element_type=F32)

        wide_part(n_norm + k, block_of)
        if k + 2 < n_norm:
            out_block(k + 2)
        if k + 1 == n_norm:
            for at in range(n_norm):
                block = slice(at * cols, (at + 1) * cols)
                coming["x", at] = load(x_ref.at[:, block], dscan.at[at * n_rows : (at + 1) * n_rows])
                coming["g", at] = load(g_ref.at[:, block], grads.at[0, at])

    def last_of_wide():
        for at in range(n_norm):
            coming["x", at].wait()
            coming["g", at].wait()
        gain = jnp.concatenate([gain_ref[k].astype(F32)[0:1] for k in range(n_wt)], axis=1)
        to = lax.broadcasted_iota(jnp.int32, (n_rows, n_rows), 0)
        source = lax.broadcasted_iota(jnp.int32, (n_rows, n_rows), 1)
        order = (source == (to % steps) * SUB + to // steps).astype(F32)
        for target in (norm_out, out_out):
            for at in range(n_norm):
                block = slice(at * cols, (at + 1) * cols)
                target[:, block] = jnp.dot(
                    order, target[:, block], precision=lax.Precision.HIGHEST,
                    preferred_element_type=F32,
                )

        def one(i, carry):
            rows = pl.ds(pl.multiple_of(i * 16, 16), 16)
            x = jnp.concatenate(
                [
                    dscan[pl.ds(pl.multiple_of(at * n_rows + i * 16, 16), 16), :].astype(F32)
                    for at in range(n_norm)
                ],
                axis=1,
            )
            g = jnp.concatenate([grads[0, at, rows, :].astype(F32) for at in range(n_norm)], axis=1)
            out_out[rows, :] = out_out[rows, :] + x
            inv = lax.rsqrt(jnp.mean(x * x, axis=1, keepdims=True) + EPS)
            scaled = norm_out[rows, :] * gain
            along = jnp.mean(scaled * x, axis=1, keepdims=True)
            norm_out[rows, :] = g + inv * scaled - x * (inv * inv * inv) * along
            return carry

        lax.fori_loop(0, n_rows // 16, one, 0)

    def out_begin():
        coming["gated"].wait()
        out_block(0)
        out_block(1)

    seq_groups = wout_groups + feat_groups + [small_group]
    first_feat = n_wide
    works = [(1.3, functools.partial(wout, 0), [0])]
    works += [(1.5, functools.partial(mixed.middle, bit), []) for bit in range(1, wt_bits)]
    works += [(1.3, functools.partial(wout, k), [k]) for k in range(1, n_wide)]
    works += [
        (4.0, low_pack, []),
        (2.0, early_feat, []),
        (4.5, functools.partial(conv_first, 0), []),
        (4.5, functools.partial(conv_first, 1), []),
        (0.3, early_pieces, []),
        (2.5, lambda: feat(gate_b, dgate[:, cols:]), [first_feat + gate_b]),
        (2.5, functools.partial(conv_second, 0), []),
        (2.5, lambda: feat(conv_a, draw[:, :cols]), [first_feat + conv_a]),
        (2.5, functools.partial(conv_second, 1), []),
        (1.4, lambda: feat(conv_b, draw[:, cols : cols + 256]), [first_feat + conv_b]),
        (1.4, lambda: feat(conv_c, draw[:, cols + 256 :]), [first_feat + conv_c]),
        (4.0, small_sums, [len(seq_groups) - 1]),
    ]
    works += [(2.7, functools.partial(norm, k), [len(seq_groups) + k]) for k in range(n_norm)]
    if not ready:
        gate_first = (3.0, lambda: feat(gate_a, dgate[:, :cols]), [first_feat + gate_a])
        works.insert(len(works) - 14 - n_norm, gate_first)
    works += [(0.2, out_begin, [])]
    works += [(1.5, functools.partial(out, k), [len(seq_groups) + n_norm + k]) for k in range(n_norm)]
    clock, starts_at, ready_at = 5.0, [], {}
    for took, _, readied in works:
        starts_at.append(clock)
        clock += took
        for which in readied:
            ready_at[which] = clock
    all_groups = seq_groups + wide_groups
    entries = []
    for which, group in enumerate(all_groups):
        job = group.members[0]
        axis = "seq" if which < len(seq_groups) else "wt"
        rows = math.prod(job.source.shape[:-1])
        members = [(one.columns.stop - one.columns.start, one.order) for one in group.members]
        entries.append((ready_at[which], axis, rows * 2 / 2**20, members))
    moves = [(29.0, "seq", 1, 0.375), (60.0, "seq", 1, 0.375), (90.0, "seq", 1, 0.14)]
    actions = timetable(entries, moves)
    ended = max(time for time, which, _, _ in actions if which >= len(seq_groups))
    actions.append((ended, None, 0, 0))
    actions.sort(key=lambda action: action[0])

    def take_action(at=0):
        _, which, member, stage = actions.pop(at)
        if which is None:
            last_of_wide()
        else:
            all_groups[which].act(member, stage)

    def take_until(which):
        at = 0
        while at < len(actions):
            if actions[at][1] == which and actions[at][3] <= 1:
                take_action(at)
            else:
                at += 1

    for at, (_, work, _) in zip(starts_at, works):
        while actions and actions[0][0] <= at + 0.01:
            take_action()
        work()
    while actions:
        take_action()
    to_wt(lambda w: gain_sum.at[own_rows(w)], gain_out.at[wt])
    for wait in delivered:
        wait()
    for wait in moved:
        wait()
    for k in range(parts):
        for slot in range(n_wide):
            wout_arrive(k, slot * WIDE, WIDE, slot)
    for move in rim_moves:

        @pl.when(seq > 0)
        def _():
            move.wait_send()

    copies.finish()


def finish_all(
    gated_t, d_gate, d_scan_in, d_raw, inputs, conv, grads, normed_t, w_in, wout, feat, gated,
    w_out, x, g, gain, d_bc, dt_low, w_x, w_dt, w_conv, b_conv, d_rate, a_neg, sums,
):
    n_seq, n_wt = lax.axis_size("seq"), lax.axis_size("wt")
    seq_bits, wt_bits = n_seq.bit_length() - 1, n_wt.bit_length() - 1
    n_chan, all_rows = gated_t.shape
    n_feat, n_rows = normed_t.shape[0], all_rows // n_wt
    n_state, taps = a_neg.shape[0], w_conv.shape[0]
    cols = 512
    parts = parts_of(n_chan, n_seq)
    part_chan = n_chan // parts
    chan_rows, feat_rows, wout_rows = n_chan // n_seq, n_feat // n_seq, part_chan // n_seq
    size = (all_rows + n_rows) // 2
    small_cols, n_wide = 3 * LANE, n_feat // WIDE
    square = ((all_rows, n_chan), BF16)
    blocks = (2,) * seq_bits
    done_type = feat_type(n_feat, n_seq, n_wt)
    plan = feat_plan(n_chan, parts)
    scratch = [
        ((part_chan, all_rows), BF16), square, ((all_rows, cols), BF16), square,
        (normed_t.shape, BF16), ((2, n_wt, n_rows, cols), BF16), ((2, 256, 2 * n_chan), BF16),
        ((n_wt, conv.shape[1], cols), F32), ((2, n_wt, conv.shape[1], cols), F32),
        ((2 * size, LANE), F32), ((size, LANE), F32), ((wt_bits - 1, size, LANE), BF16),
        ((wt_bits - 1, size, LANE), BF16), ((2 * size, LANE), F32), square if parts > 1 else ((16, LANE), BF16), ((all_rows, LANE), BF16), ((all_rows, LANE), BF16),
        ((small_cols, n_chan), F32), ((16, cols), F32), ((2, 2, 16, cols), BF16),
        ((feat_rows, 2 * n_chan), done_type), ((parts, wout_rows, n_feat), BF16),
        ((chan_rows, small_cols), BF16), ((feat_rows, 2 * n_chan), BF16), ((feat_rows, LANE), F32),
        (blocks + (chan_rows, small_cols), BF16),
    ]
    scratch = [pltpu.VMEM(*item) for item in scratch]
    scratch += [pltpu.SemaphoreType.DMA((2, parts, n_wide))]
    scratch += [pltpu.SemaphoreType.DMA((180,))] * 2
    scratch += [pltpu.VMEM(blocks + (wout_rows, WIDE), BF16)] * (n_wide if parts > 1 else 1)
    scratch += [
        pltpu.VMEM(blocks + (feat_rows, width), BF16) for _, width, _ in plan[: 5 - parts % 2 * 2]
    ]
    scratch += [pltpu.VMEM((2,) * wt_bits + (n_rows, cols), BF16)] * 2
    for low in wout_lows(n_wide, True):
        scratch += seq_landings(seq_bits, wout_rows, [WIDE], low)
    for _, width, low in plan:
        scratch += seq_landings(seq_bits, feat_rows, [width], low)
    scratch += seq_landings(seq_bits, chan_rows, [small_cols])
    scratch += landings(wt_bits, n_rows, (cols,) * (2 * n_feat // cols))
    hbm = pl.BlockSpec(memory_space=pl.ANY)
    vmem = pl.BlockSpec(memory_space=pltpu.VMEM)
    return pl.pallas_call(
        functools.partial(finish_kernel, n_seq, n_wt, n_state),
        in_specs=[hbm] * 15 + [vmem] * 10,
        out_specs=[hbm, hbm, hbm, vmem, vmem, hbm],
        out_shape=[
            jax.ShapeDtypeStruct((feat_rows // n_wt, 2 * n_chan * n_wt), done_type),
            jax.ShapeDtypeStruct((parts, wout_rows, n_feat), BF16),
            jax.ShapeDtypeStruct((chan_rows, small_cols), BF16),
            jax.ShapeDtypeStruct((n_rows, n_feat), F32),
            jax.ShapeDtypeStruct((n_rows, n_feat), F32),
            jax.ShapeDtypeStruct((n_wt, feat_rows // n_wt, LANE), F32),
        ],
        scratch_shapes=scratch,
        compiler_params=pltpu.CompilerParams(
            collective_id=1, has_side_effects=True, vmem_limit_bytes=255 * 2**18
        ),
        name="finish_all",
    )(
        gated_t, d_gate, d_scan_in, d_raw, inputs, conv, grads, normed_t, w_in, wout, feat, gated,
        w_out.reshape(grads.shape), x, g, gain, d_bc, dt_low, w_x, w_dt, w_conv, b_conv, d_rate, a_neg, sums,
    )


class Gather:
    def __init__(self, copies, slots, seq, wt, bits):
        self.copies, self.slots, self.seq, self.wt, self.bits = copies, slots, seq, wt, bits
        self.arriving = {}

    def send(self, mask, src):
        slot = self.slots.at[turn(self.wt, mask, self.bits)]
        low = self.bits if mask == 0 else (mask & -mask).bit_length() - 1
        for bit in reversed(range(low)):
            peer = (self.seq, flip(self.wt, bit))
            self.arriving[mask | 1 << bit] = self.copies.remote(src, slot, peer)

    def arrive(self, mask):
        self.arriving[mask].wait_recv()
        self.send(mask, self.slots.at[turn(self.wt, mask, self.bits)])


def start_kernel(
    n_seq, n_wt,
    hidden_ref, grad_ref, gain_ref, starts_ref, win_ref, wout_ref, wconv_ref, bconv_ref, wx_ref,
    wdt_ref, spread_ref, bias_ref, rate_ref,
    normed_out, win_out, conv_out, gate_out, u_out, raw_out, low_out, bcs_out, dgated_out,
    dscan_out, grad_out, gain_out, end_out, lead_out, total_ref, head_ref, tail_ref,
    rows_s, grads_s, gain_s, starts_s, normed_s, win_s, wout_s, conv_s, gate_s, u_s, raw_s, low_s,
    bcs_s, dgated_s, dscan_s, mix_s, fin_s, first_s, half_s, land_s, rim_s, rim_in, normed_t,
    bcb, dec_in, drive_in, g_in, end_s, lead_s, run_s, span_s, own_span, gap_s, edge_send, edge_land, span_send,
    span_land,
    send_sems, recv_sems, join_send, join_recv,
):
    seq, wt = lax.axis_index("seq"), lax.axis_index("wt")
    bits = n_wt.bit_length() - 1
    n_rows, n_feat = hidden_ref.shape
    n_chan, shard = wout_ref.shape[0], win_ref.shape[0]
    taps = wconv_ref.shape[0]
    rim = (taps - 1) * SUB
    all_rows = n_wt * n_rows
    near_y, near_z = (flip(seq, 0), wt), (flip(seq, 1), wt)
    wt_peers = [(seq, turn(wt, mask, bits)) for mask in range(1, n_wt)]
    ahead, behind = (lax.rem(seq + 1, n_seq), wt), (lax.rem(seq + n_seq - 1, n_seq), wt)

    barrier = pltpu.get_barrier_semaphore()
    partners = wt_peers + [near_y, near_z, ahead, behind]
    for r in range(1, n_seq.bit_length() - 1):
        partners += [(lax.rem(seq + d, n_seq), wt) for d in (2**r, n_seq - 2**r)]
    for partner in partners:
        pl.semaphore_signal(barrier, inc=1, device_id=partner, device_id_type=MESH)
    pl.semaphore_wait(barrier, len(partners))

    copies = Copies(send_sems, recv_sems)
    part = shard // 4
    quarter = seq % 4

    def win_part(owner, which, at, rows, half):
        start = pl.multiple_of(owner * shard + which * part + at, 16)
        return win_s.at[pl.ds(start, rows), half * n_chan : (half + 1) * n_chan]

    def send_far(half):
        found = {}
        rows = pl.ds(pl.multiple_of(quarter * part, 16), part)
        for mask in range(2, n_wt):
            to = turn(wt, mask, bits)
            columns = pl.ds(pl.multiple_of((half * n_wt + to) * n_chan, LANE), n_chan)
            found[mask] = copies.remote(
                win_ref.at[rows, columns], win_part(wt, quarter, 0, part, half), (seq, to)
            )
        return found

    def send_near(half):
        to = flip(wt, 0)
        place = win_s.at[
            pl.ds(pl.multiple_of(wt * shard, 16), shard), half * n_chan : (half + 1) * n_chan
        ]
        columns = pl.ds(pl.multiple_of((half * n_wt + to) * n_chan, LANE), n_chan)
        own = pl.ds(pl.multiple_of((half * n_wt + wt) * n_chan, LANE), n_chan)
        return (
            copies.remote(win_ref.at[:, columns], place, (seq, to)),
            copies.local(win_ref.at[:, own], place),
        )

    def share_first(half, found):
        passed = {}
        for mask, copy in found.items():
            copy.wait_recv()
            block = win_part(turn(wt, mask, bits), quarter, 0, part, half)
            passed[mask] = (
                copies.remote(block, block, near_y), copies.remote(block, block, near_z)
            )
        return passed

    def share_second(half, passed):
        last = []
        for mask, (by_y, by_z) in passed.items():
            owner = turn(wt, mask, bits)
            by_z.wait_recv()
            block = win_part(owner, flip(quarter, 1), 0, part // 2, half)
            last.append(copies.remote(block, block, near_y))
            by_y.wait_recv()
            block = win_part(owner, flip(quarter, 0), part // 2, part // 2, half)
            last.append(copies.remote(block, block, near_z))
        return last

    def normalise(mask):
        at = turn(wt, mask, bits)
        gain = jnp.concatenate(
            [gain_s[k].astype(F32)[0:1] for k in range(n_wt)], axis=1
        )

        def body(i, carry):
            rows = pl.ds(pl.multiple_of(i * 16, 16), 16)
            x = rows_s[at, rows, :].astype(F32)
            inv = lax.rsqrt(jnp.mean(x * x, axis=1, keepdims=True) + EPS)
            place = pl.ds(pl.multiple_of(at * n_rows + i * 16, 16), 16)
            normed_s[place, :] = (x * inv * gain).astype(BF16)
            return carry

        lax.fori_loop(0, n_rows // 16, body, 0)

    far = send_far(0)
    rows = Gather(copies, rows_s, seq, wt, bits)
    gains = Gather(copies, gain_s, seq, wt, bits)
    starts = Gather(copies, starts_s, seq, wt, bits)
    own_copies = [
        copies.local(gain_ref, gain_s.at[wt]),
        copies.local(starts_ref, starts_s.at[wt]),
        copies.local(hidden_ref, rows_s.at[wt]),
    ]
    gains.send(0, gain_ref)
    rows.send(0, hidden_ref)
    near = send_near(0)
    starts.send(0, starts_ref)
    wout_copy = copies.local(wout_ref, wout_s)
    for mask in range(n_wt - 1, 0, -1):
        if mask in gains.arriving:
            gains.arrive(mask)
    for mask in range(1, n_wt):
        if mask not in (1, 2):
            gains.arriving[mask].wait_recv()
    for copy in own_copies:
        copy.wait()
    normalise(0)
    rows.arrive(1)
    normalise(1)
    passed = share_first(0, far)
    far = send_far(1)
    last = share_second(0, passed)
    near_gate = send_near(1)
    for mask in range(2, n_wt):
        rows.arrive(mask)
        if mask == 2:
            half_rows = n_rows // 2
            tops = Gather(copies, grads_s.at[:, :half_rows], seq, wt, bits)
            ends = Gather(copies, grads_s.at[:, half_rows:], seq, wt, bits)
            grad_copy = copies.local(grad_ref, grads_s.at[wt])
            tops.send(0, grad_ref.at[:half_rows])
        normalise(mask)
    results = [copies.local(gain_s, gain_out)]
    near[0].wait_recv()
    near[1].wait()
    for copy in last:
        copy.wait_recv()

    n_block, m_block = 256, 512

    def tiles(body):
        m_count = all_rows // m_block

        def one(i, carry):
            m = pl.multiple_of((i % m_count) * m_block, m_block)
            n = pl.multiple_of((i // m_count) * n_block, n_block)
            body(m, n)
            return carry

        lax.fori_loop(0, m_count * (n_chan // n_block), one, 0)

    def conv_tile(m, n):
        value = jnp.dot(
            normed_s[pl.ds(m, m_block), :], win_s[:, pl.ds(n, n_block)], preferred_element_type=F32
        )
        value = value.astype(BF16).astype(F32)
        for k in range(m_block // n_rows):
            conv_s[m // n_rows + k, rim:, pl.ds(n, n_block)] = value[k * n_rows : (k + 1) * n_rows]

    tiles(conv_tile)

    rim_s[...] = jnp.zeros_like(rim_s)
    for b in range(n_wt):
        for k in range(taps - 1):
            at = rim + n_rows - (taps - 1 - k) * SUB
            rim_s[b * (taps - 1) + k, :] = conv_s[b, at + SUB - 1, :]
    rim_s2 = rim_s[...].astype(BF16)
    rim_in[0] = rim_s2

    @pl.when(seq == 0)
    def _():
        rim_in[1] = jnp.zeros_like(rim_s2)

    k_rim, copies.count = copies.count, copies.count + 1
    rim_copy = pltpu.make_async_remote_copy(
        src_ref=rim_in.at[0], dst_ref=rim_in.at[1], send_sem=send_sems.at[k_rim],
        recv_sem=recv_sems.at[k_rim], device_id=ahead, device_id_type=MESH,
    )

    @pl.when(seq < n_seq - 1)
    def _():
        rim_copy.start()

    passed = share_first(1, far)

    def convolve(b, j):
        rows = pl.ds(pl.multiple_of(j * 16, 16), 16)
        total = bconv_ref[...] + conv_s[b, rows, :] * wconv_ref[0:1, :]
        for k in range(1, taps):
            at = pl.ds(pl.multiple_of(j * 16 + k * SUB, SUB), 16)
            total = total + conv_s[b, at, :] * wconv_ref[k : k + 1, :]
        place = pl.ds(pl.multiple_of(b * n_rows + j * 16, 16), 16)
        u_s[place, :] = (total * jax.nn.sigmoid(total)).astype(BF16)

    head = -(-(taps - 1) // 2)
    pairs = n_rows // 16

    def convolve_tail(i, carry):
        convolve(i // (pairs - head), head + i % (pairs - head))
        return carry

    lax.fori_loop(0, n_wt * (pairs - head), convolve_tail, 0)

    @pl.when(seq > 0)
    def _():
        rim_copy.wait_recv()

    rim_rows = rim_in[1].astype(F32)
    first = lax.broadcasted_iota(jnp.int32, (SUB, n_chan), 0) == 0
    for b in range(n_wt):
        for k in range(taps - 1):
            at = rim + n_rows - (taps - 1 - k) * SUB
            moved = pltpu.roll(conv_s[b, at : at + SUB, :], 1, 0)
            row = rim_rows[b * (taps - 1) + k : b * (taps - 1) + k + 1, :]
            conv_s[b, k * SUB : (k + 1) * SUB, :] = jnp.where(first, row, moved)
    lax.fori_loop(0, n_wt * head, lambda i, c: (convolve(i // head, i % head), c)[1], 0)
    results += [copies.local(conv_s, conv_out), copies.local(u_s, u_out)]

    packed = []
    for b in range(n_wt):
        block = u_s[b * n_rows : (b + 1) * n_rows, :]
        mix_s[b * n_rows : (b + 1) * n_rows, :] = jnp.dot(
            block, wx_ref[:, :LANE], preferred_element_type=F32
        )
        packed.append(jnp.dot(block, wx_ref[:, LANE:], preferred_element_type=F32))
    mix_s[all_rows:, :] = jnp.concatenate(packed, axis=1)
    mixed = WtSum(copies, mix_s, first_s, half_s, land_s, fin_s, seq, wt, bits)
    mixed.begin()
    last = share_second(1, passed)
    starts.arrive(2)

    def transpose(b):
        at = slice(b * n_rows, (b + 1) * n_rows)
        normed_t[:, at] = normed_s[at, :].T

    transpose(0)
    for bit in range(1, bits):
        mixed.middle(bit)
    ends.send(0, grad_ref.at[half_rows:])
    for b in range(1, n_wt):
        transpose(b)
    results.append(copies.local(normed_t, normed_out))
    mixed.end()

    low_s[...] = fin_s[:all_rows, :].astype(BF16)
    starts.arriving[1].wait_recv()
    starts.arriving[3].wait_recv()
    lane = lax.broadcasted_iota(jnp.int32, (n_rows, LANE), 1)
    width = LANE // n_wt
    for b in range(n_wt):
        moved = fin_s[all_rows:, :]
        if b:
            moved = pltpu.roll(moved, LANE - b * width, 1)
        bcs_s[b * n_rows : (b + 1) * n_rows, :] = (
            jnp.where(lane < width, moved, 0.0).astype(BF16) + starts_s[b]
        )

    def raw_tile(m, n):
        value = lax.dot_general(
            low_s[pl.ds(m, m_block), :], wdt_ref[pl.ds(n, n_block), :], (((1,), (1,)), ((), ())),
            preferred_element_type=F32,
        )
        raw_s[pl.ds(m, m_block), pl.ds(n, n_block)] = value.astype(BF16)

    tiles(raw_tile)
    results += [
        copies.local(low_s, low_out), copies.local(bcs_s, bcs_out), copies.local(raw_s, raw_out)
    ]

    near_gate[0].wait_recv()
    near_gate[1].wait()
    for copy in last:
        copy.wait_recv()
    results.append(copies.local(win_s, win_out))

    def gate_tile(m, n):
        value = jnp.dot(
            normed_s[pl.ds(m, m_block), :], win_s[:, pl.ds(n_chan + n, n_block)],
            preferred_element_type=F32,
        )
        gate_s[pl.ds(m, m_block), pl.ds(n, n_block)] = value.astype(BF16)

    tiles(gate_tile)
    results.append(copies.local(gate_s, gate_out))
    n_state = rate_ref.shape[0]
    width = dec_in.shape[1]
    steps = n_rows // SUB
    start_at = 2 * n_state * LANE

    def stream_of(i):
        base = wt + (i // 2) * (1 - 2 * bit_of(wt, 1)) * 2
        return base + (i % 2) * (1 - 2 * bit_of(wt, 0))

    def back(b):
        at = pl.ds(pl.multiple_of(b * n_rows, n_rows), n_rows)

        def one(i, carry):
            n = pl.ds(pl.multiple_of(i * n_block, n_block), n_block)
            d_gated = lax.dot_general(
                grads_s[b], wout_s[n, :], (((1,), (1,)), ((), ())), preferred_element_type=F32
            )
            gate = gate_s[at, n].astype(F32)
            dgated_s[at, n] = d_gated
            dscan_s[at, n] = (d_gated * gate * jax.nn.sigmoid(gate)).astype(BF16)
            return carry

        lax.fori_loop(0, n_chan // n_block, one, 0)

    def chunk_ends(b, part):
        columns = pl.ds(pl.multiple_of(part * width, width), width)

        def prepare(j, total):
            rows = pl.ds(pl.multiple_of(j * 16, 16), 16)
            at = pl.ds(pl.multiple_of(b * n_rows + j * 16, 16), 16)
            delta = softplus(raw_s[at, columns].astype(F32) + bias_ref[:, columns])
            held = jnp.where(wide(bcb[rows, start_at : start_at + LANE], width) > 0.5, RESET, delta)
            dec_in[rows, :] = held
            drive_in[rows, :] = delta * u_s[at, columns].astype(F32)
            g_in[rows, :] = dscan_s[at, columns].astype(F32)
            return total + held[:SUB] + held[SUB:]

        total = lax.fori_loop(0, steps // 2, prepare, jnp.zeros((SUB, width), F32))
        total_ref[b, :, columns] = total
        span = jnp.sum(total, 0, keepdims=True)
        span_s[b, :, columns] = span
        for first_n in range(0, n_state, 2):
            states = range(first_n, first_n + 2)

            def step(j, carry):
                rows = pl.ds(pl.multiple_of(j * SUB, SUB), SUB)
                held, drive, g = dec_in[rows, :], drive_in[rows, :], g_in[rows, :]
                running, products, passed = [], [], []
                for n, h, so_far, p in zip(states, *carry):
                    b_row = wide(bcb[rows, n * LANE : (n + 1) * LANE], width)
                    c_row = wide(bcb[rows, (n_state + n) * LANE : (n_state + n + 1) * LANE], width)
                    decay = jnp.exp2(held * rate_ref[n : n + 1, columns])
                    so_far = so_far * decay
                    running.append(decay * h + drive * b_row)
                    products.append(so_far)
                    passed.append(p + so_far * (g * c_row))
                return tuple(running), tuple(products), tuple(passed)

            zero = tuple(jnp.zeros((SUB, width), F32) for _ in states)
            one = tuple(jnp.ones((SUB, width), F32) for _ in states)
            carry = lax.fori_loop(0, steps, step, (zero, one, zero), unroll=4)
            for n, h, decay, p in zip(states, *carry):
                end = chunk_prefix(decay, h, False)[1]
                lead = chunk_prefix(decay, p, True)[1]
                end_s[b, n, :, columns], lead_s[b, n, :, columns] = end, lead
                run_s[0, b, n : n + 1, columns] = end[SUB - 1 :]
                run_s[1, b, n : n + 1, columns] = lead[:1]

    def ends_of(i, carry):
        b = stream_of(i)
        back(b)
        bcb[...] = jnp.dot(
            bcs_s[pl.ds(pl.multiple_of(b * n_rows, n_rows), n_rows), :], spread_ref[...],
            preferred_element_type=F32,
        )
        lax.fori_loop(0, n_chan // width, lambda part, c: (chunk_ends(b, part), c)[1], 0)
        return carry

    grad_copy.wait()
    tops.arrive(1)
    ends.arrive(1)
    wout_copy.wait()
    lax.fori_loop(0, 2, ends_of, 0)
    for mask in range(2, n_wt):
        tops.arrive(mask)
        ends.arrive(mask)
        ends_of(mask, 0)
    results.append(copies.local(grads_s, grad_out))
    results += [copies.local(dgated_s, dgated_out), copies.local(dscan_s, dscan_out)]
    results += [copies.local(end_s, end_out), copies.local(lead_s, lead_out)]
    join_rounds(
        n_seq, n_wt, seq, wt, rate_ref[...], head_ref, tail_ref, run_s, span_s, own_span, gap_s,
        edge_send, edge_land, span_send, span_land, join_send, join_recv,
    )
    for copy in results:
        copy.wait()

    @pl.when(seq < n_seq - 1)
    def _():
        rim_copy.wait_send()

    copies.finish()


def start_all(
    hidden, grad, gain, starts, w_in, w_out, w_conv, b_conv, w_x, w_dt, bias, rate_rows
):
    n_seq, n_wt = lax.axis_size("seq"), lax.axis_size("wt")
    n_rows, n_feat = hidden.shape
    n_chan, taps = w_out.shape[0], w_conv.shape[0]
    rows, rim = n_wt * n_rows, (taps - 1) * SUB
    shapes = [
        ((n_feat, rows), BF16), ((n_feat, 2 * n_chan), BF16), ((n_wt, rim + n_rows, n_chan), F32),
        ((rows, n_chan), BF16), ((rows, n_chan), BF16), ((rows, n_chan), BF16), ((rows, LANE), BF16),
        ((rows, LANE), BF16), ((rows, n_chan), F32), ((rows, n_chan), BF16),
        ((n_wt, n_rows, n_feat), BF16), ((n_wt,) + gain.shape, BF16),
        ((n_wt, rate_rows.shape[0], SUB, n_chan), F32),
        ((n_wt, rate_rows.shape[0], SUB, n_chan), F32), ((n_wt, SUB, n_chan), F32),
        ((n_wt,) + rate_rows.shape, F32), ((n_wt,) + rate_rows.shape, F32),
    ]
    normed, win, conv, gate, u, raw, low, bcs, dgated, dscan, grads, gains = shapes[:12]
    ends = shapes[12]
    n_state, rounds = rate_rows.shape[0], n_seq.bit_length() - 1
    count = (2 * n_state + 1) * LANE
    width = min(512, n_chan)
    spans, edges = (2 * n_wt, n_chan), (n_wt, n_state, n_chan)
    size = (rows + n_rows) // 2
    bits = n_wt.bit_length() - 1
    scratch = [
        grads, grads, gains, ((n_wt, n_rows, LANE), BF16), ((rows, n_feat), BF16), win, (w_out.shape, BF16), conv,
        gate, u, raw, low, bcs, dgated, dscan, ((2 * size, LANE), F32), ((2 * size, LANE), F32),
        ((size, LANE), F32), ((bits, size, LANE), BF16), ((bits, size, LANE), BF16),
        ((16, n_chan), F32),
        ((2, 16, n_chan), BF16), normed,
        ((n_rows, count), F32), ((n_rows, width), F32), ((n_rows, width), F32), ((n_rows, width), F32),
        ends, ends, ((2,) + edges, F32), ((n_wt, 1, n_chan), F32), (spans, F32), (spans, F32),
        ((2, 2) + edges, BF16),
        ((rounds, 2) + edges, BF16), ((rounds,) + spans, F32), ((rounds, 2) + spans, F32),
    ]
    hbm = pl.BlockSpec(memory_space=pl.ANY)
    vmem = pl.BlockSpec(memory_space=pltpu.VMEM)
    return pl.pallas_call(
        functools.partial(start_kernel, n_seq, n_wt),
        in_specs=[hbm] * 6 + [vmem] * 7,
        out_specs=[hbm] * (len(shapes) - 3) + [vmem] * 3,
        out_shape=[jax.ShapeDtypeStruct(*item) for item in shapes],
        scratch_shapes=[pltpu.VMEM(*item) for item in scratch]
        + [pltpu.SemaphoreType.DMA((90,))] * 2
        + [pltpu.SemaphoreType.DMA((rounds, 2, 2))] * 2,
        compiler_params=pltpu.CompilerParams(
            collective_id=2, has_side_effects=True, vmem_limit_bytes=4090 * 2**14
        ),
        name="start_all",
    )(
        hidden, grad, gain, starts, w_in, w_out, w_conv, b_conv, w_x, w_dt, spread_matrix(n_state),
        bias, rate_rows,
    )


def dot(left, right, left_dim=1, right_dim=0):
    return lax.dot_general(
        left, right, (((left_dim,), (right_dim,)), ((), ())), preferred_element_type=F32
    )


def to_chunks(rows):
    n_rows, width = rows.shape
    return rows.reshape(SUB, n_rows // SUB, width).swapaxes(0, 1).reshape(n_rows, width)


def per_device(
    hidden_in, doc_starts, norm_gain, in_weight, conv_weight, conv_bias, x_weight,
    dt_weight, dt_bias, a_log, d_skip, out_weight, grad_output,
):
    n_wt, n_seq = lax.axis_size("wt"), lax.axis_size("seq")
    seq_at = lax.axis_index("seq")
    n_chan = out_weight.shape[0]
    taps = conv_weight.shape[1]
    dt_rank = dt_weight.shape[1]
    n_state = a_log.shape[1]
    rows_own = hidden_in[0]
    n_rows, n_feat = rows_own.shape
    steps = n_rows // SUB

    w_conv = conv_weight.astype(F32)
    starts = jnp.pad(
        to_chunks(doc_starts[0].astype(BF16)[:, None]), ((0, 0), (2 * n_state, LANE - 2 * n_state - 1))
    )
    rates = (-LOG2E * jnp.exp(a_log.astype(F32))).T
    bias = dt_bias.astype(F32)[None]
    skip = d_skip.astype(F32)[None]
    (
        normed_t, w_in, padded, gate_in, inputs, dt_raw, dt_low, bcs, d_gated, d_scanned, grad_all, gains,
        ends, leads, totals, head, tail,
    ) = start_all(
        to_chunks(rows_own), to_chunks(grad_output[0]),
        jnp.broadcast_to(norm_gain[None], (16, norm_gain.shape[0])), starts, in_weight, out_weight,
        w_conv.T, conv_bias.astype(F32)[None], x_weight, dt_weight, bias,
        rates,
    )
    gain = gains[:, 0].reshape(n_feat).astype(F32)

    gated, gated_t, d_gate, d_scan_in, d_raw, d_bc, d_rate, sums, wout, feat = scan_all(
        bcs, dt_raw, inputs, d_scanned, gate_in, d_gated, bias, skip, rates,
        ends, leads, totals, head, tail, grad_all.reshape(n_wt * n_rows, n_feat), normed_t,
    )


    feat_grads, d_wout, small, input_grad, output, gain_parts = finish_all(
        gated_t, d_gate, d_scan_in, d_raw, inputs, padded, grad_all, normed_t, w_in, wout, feat,
        gated, out_weight, rows_own, grad_output[0], gains, d_bc, dt_low, x_weight, dt_weight, w_conv.T,
        conv_bias.astype(F32)[None], d_rate, rates, sums,
    )
    d_wout = d_wout.reshape(-1, n_feat).astype(F32)
    small = small.astype(F32)
    widths = (dt_rank, dt_rank, 2 * n_state, n_state, taps, 1, 1, 1)
    cuts, at = [], 0
    for piece in widths:
        cuts.append(small[:, at : at + piece])
        at += piece
    d_wx, d_wdt, d_wbc, d_loga, d_wconv, d_bconv, d_bdt, d_skips = cuts
    own = n_feat // (n_seq * n_wt)
    own_at = own * (n_wt * seq_at + lax.axis_index("wt"))
    gain_grad = jnp.sum(gain_parts, (0, 2)) / lax.dynamic_slice_in_dim(gain, own_at, own, 0)
    return (
        output[None],
        input_grad[None],
        gain_grad,
        feat_grads.astype(F32),
        d_wconv,
        d_bconv[:, 0],
        jnp.concatenate([d_wx, d_wbc], 1),
        d_wdt,
        d_bdt[:, 0],
        d_loga,
        d_skips[:, 0],
        d_wout,
    )


def solution(mesh):
    placed = (
        P("wt", "seq", None),
        P("wt", "seq"),
        P("wt"),
        P("wt", None),
        P("wt", None),
        P("wt"),
        P("wt", None),
        P("wt", None),
        P("wt"),
        P("wt", None),
        P("wt"),
        P("wt", None),
        P("wt", "seq", None),
    )
    every = ("seq", "wt")
    return jax.shard_map(
        per_device,
        mesh=mesh,
        in_specs=placed,
        out_specs=(
            P("wt", "seq", None),
            P("wt", "seq", None),
            P(every),
            P(every, None),
            P(every, None),
            P(every),
            P(every, None),
            P(every, None),
            P(every),
            P(every, None),
            P(every),
            P(every, None),
        ),
        check_vma=False,
    )
```

```python
import functools
import math

import jax
import jax.numpy as jnp
import ml_dtypes
import numpy as np
from jax import lax
from jax.experimental import pallas as pl
from jax.experimental.pallas import tpu as pltpu
from jax.sharding import PartitionSpec as P

EPS = 1e-05
LOG2E = 1.4426950408889634
RESET = 1e30
SUB = 8
LANE = 128
NBLK = 4
F32 = jnp.float32
BF16 = jnp.bfloat16
MESH = pl.DeviceIdType.MESH


def softplus(v):
    return jnp.maximum(v, 0.0) + jnp.log1p(jnp.exp(-jnp.abs(v)))


def wide(tile, width):
    return jnp.concatenate([tile] * (width // LANE), axis=1)


def fold(values):
    total = values[:, :LANE]
    for k in range(1, values.shape[1] // LANE):
        total = total + values[:, k * LANE : (k + 1) * LANE]
    return total


def chunk_prefix(decay, drive, reverse):
    chunk = lax.broadcasted_iota(jnp.int32, drive.shape, 0)
    for shift in (1, 2, 4):
        if reverse:
            other_decay = pltpu.roll(decay, SUB - shift, 0)
            other_drive = pltpu.roll(drive, SUB - shift, 0)
            inside = chunk < SUB - shift
        else:
            other_decay = pltpu.roll(decay, shift, 0)
            other_drive = pltpu.roll(drive, shift, 0)
            inside = chunk >= shift
        drive = jnp.where(inside, decay * other_drive + drive, drive)
        decay = jnp.where(inside, decay * other_decay, decay)
    return decay, drive


def spread_rows(bcs_ref, spread_ref, bcb):
    bcb[...] = jnp.dot(bcs_ref[...], spread_ref[...], preferred_element_type=F32)


def turn(index, mask, bits):
    for bit in range(bits):
        if mask >> bit & 1:
            index = flip(index, bit)
    return index


class Copies:
    def __init__(self, send_sems, recv_sems):
        self.send_sems, self.recv_sems = send_sems, recv_sems
        self.count, self.open = 0, []

    def remote(self, src, dst, peer):
        k, self.count = self.count, self.count + 1
        copy = pltpu.make_async_remote_copy(
            src_ref=src, dst_ref=dst, send_sem=self.send_sems.at[k],
            recv_sem=self.recv_sems.at[k], device_id=peer, device_id_type=MESH,
        )
        copy.start()
        self.open.append(copy)
        return copy

    def later(self, src_of, dst, peer):
        k, self.count = self.count, self.count + 1

        def make():
            return pltpu.make_async_remote_copy(
                src_ref=src_of(), dst_ref=dst, send_sem=self.send_sems.at[k],
                recv_sem=self.recv_sems.at[k], device_id=peer, device_id_type=MESH,
            )

        self.open.append(make)
        return make

    def local(self, src, dst):
        k, self.count = self.count, self.count + 1
        copy = pltpu.make_async_copy(src, dst, self.send_sems.at[k])
        copy.start()
        return copy

    def drop(self, copy):
        self.open = [other for other in self.open if other is not copy]

    def finish(self):
        for copy in self.open:
            (copy() if callable(copy) else copy).wait_send()


class WtSum:
    def __init__(self, copies, mix, first, half, land, total, seq, wt, bits):
        self.copies, self.mix, self.first, self.total = copies, mix, first, total
        self.half, self.land = half, land
        self.seq, self.wt, self.bits = seq, wt, bits
        size = mix.shape[0] // 2
        mine = bit_of(wt, 0)
        self.kept = pl.ds(pl.multiple_of(mine * size, 16), size)
        self.given = pl.ds(pl.multiple_of((1 - mine) * size, 16), size)

    def begin(self):
        peer = (self.seq, flip(self.wt, 0))
        self.copy = self.copies.remote(self.mix.at[self.given], self.first, peer)

    def so_far(self, bit):
        self.copy.wait_recv()
        if bit == 1:
            return self.mix[self.kept, :] + self.first[...]
        return self.half[bit - 2].astype(F32) + self.land[bit - 2].astype(F32)

    def middle(self, bit):
        self.half[bit - 1] = self.so_far(bit).astype(BF16)
        peer = (self.seq, flip(self.wt, bit))
        self.copy = self.copies.remote(self.half.at[bit - 1], self.land.at[bit - 1], peer)

    def end(self):
        self.end_send()
        self.copy.wait_recv()

    def end_send(self):
        self.total[self.kept, :] = self.so_far(self.bits)
        peer = (self.seq, flip(self.wt, 0))
        part = self.total.at[self.kept]
        self.copy = self.copies.remote(part, part, peer)


def flip(index, bit):
    return index + (1 - 2 * ((index // 2**bit) % 2)) * 2**bit


def bit_of(index, bit):
    return (index // 2**bit) % 2


def pick(left, bit, value):
    return tuple(value if b == bit else slice(None) for b in left)


def over_blocks(count, rows, body):
    tile = math.gcd(rows, 32)
    per_block = rows // tile

    def one(i, carry):
        block, row = i // per_block, (i % per_block) * tile
        index = tuple((block // 2 ** (count - 1 - k)) % 2 for k in range(count))
        body(index, pl.ds(pl.multiple_of(row, tile), tile))
        return carry

    lax.fori_loop(0, 2**count * per_block, one, 0)


class Halving:
    def __init__(self, copies, source, dims, order, columns, landing, final, me, peer):
        self.copies, self.source, self.dims, self.order = copies, source, dims, order
        self.columns, self.landing, self.final = columns, landing, final
        self.mine = {bit: bit_of(me, bit) for bit in order}
        self.theirs = {bit: 1 - value for bit, value in self.mine.items()}
        self.moves = [
            copies.later(functools.partial(self.block, stage), landing[stage], peer(bit))
            for stage, bit in enumerate(order)
        ]

    def left(self, stage):
        return [b for b in self.dims if b not in self.order[:stage]]

    def block(self, stage):
        bit = self.order[stage]
        other = pick(self.left(stage), bit, self.theirs[bit])
        if stage == 0:
            return self.source.at[other + (slice(None), self.columns)]
        return self.landing[stage - 1].at[other]

    def send(self, stage):
        self.moves[stage]().start()

    def add(self, stage):
        self.moves[stage]().wait_recv()
        mine = self.mine[self.order[stage]]
        left, after = self.left(stage), self.left(stage + 1)
        landed = self.landing[stage]

        def body(index, rows):
            at = iter(index)
            full = tuple(mine if b == self.order[stage] else next(at) for b in left)
            if stage == 0:
                kept = self.source[full + (rows, self.columns)]
            else:
                kept = self.landing[stage - 1][full + (rows, slice(None))]
            total = kept.astype(F32) + landed[index + (rows, slice(None))].astype(F32)
            if after:
                landed[index + (rows, slice(None))] = total.astype(BF16)
            else:
                self.final(rows, total)

        over_blocks(len(after), landed.shape[-2], body)


class Group:
    def __init__(self, members, done=None):
        self.members, self.done, self.stage = members, done, 0

    def launch(self):
        for job in self.members:
            job.send(0)

    def act(self, member, stage):
        job = self.members[member]
        if stage:
            job.add(stage - 1)
        if stage < len(job.order):
            job.send(stage)
        else:
            self.stage += 1
            if self.stage == len(self.members) and self.done:
                self.done()

    def advance(self, stage):
        stages = len(self.members[0].order)
        for job in self.members:
            job.add(stage)
            if stage + 1 < stages:
                job.send(stage + 1)
        if stage + 1 == stages and self.done:
            self.done()

    def release(self):
        for job in self.members:
            job.moves[0]().wait_send()
            job.copies.drop(job.moves[0])


def fill(target, at, value):
    rows, lead = target.shape[-2], len(target.shape) - 2
    inner = (value.shape[0] // rows).bit_length() - 1
    index = tuple((at // 2 ** (lead - 1 - k)) % 2 for k in range(lead - inner))
    target[index] = value.reshape((2,) * inner + (rows, value.shape[1])).astype(BF16)


def by_tiles(target, rows, value_of):
    tile = min(512, rows)

    def one(i, carry):
        m = pl.multiple_of(i * tile, tile)
        fill(target, i * (tile // target.shape[-2]), value_of(pl.ds(m, tile)))
        return carry

    lax.fori_loop(0, rows // tile, one, 0)


def seq_orders(width, seq_bits, low=None):
    low = width - LANE if low is None else low
    first = tuple(range(seq_bits))
    orders = ((0, low, first), (low, width - low, (1, 0) + first[2:]))
    return [item for item in orders if item[1]]


def timetable(groups, loads=()):
    rate, delay, turn_time, ahead = 23.3, 4.0, 1.0, 8.0
    jobs, free, clock, found = [], {}, 0.0, []
    for g, (ready, axis, size, members) in enumerate(groups):
        for m, (columns, order) in enumerate(members):
            jobs.append([ready, ready, g, m, 0, columns * size, axis, order])
    for ready, axis, bit, size in loads:
        jobs.append([ready, ready, -1, 0, 0, 2 * size, axis, (bit,)])
    while jobs:
        best = None
        for job in jobs:
            ready, made, g, m, stage, size, axis, order = job
            issue = max(clock, ready)
            if stage < len(order):
                bit = order[stage]
                link = (axis, min(bit, 1))
                issue = max(issue, free.get(link, 0.0) - ahead)
            key = (issue, -stage, made, g, m)
            if best is None or key < best[0]:
                best = (key, job)
        (issue, *_), job = best
        ready, made, g, m, stage, size, axis, order = job
        if g >= 0:
            found.append((issue, g, m, stage))
        clock = issue + (turn_time if stage else 0.1)
        if stage == len(order):
            jobs.remove(job)
            continue
        bit = order[stage]
        link = (axis, min(bit, 1))
        took = size / 2 ** (stage + 1) * rate
        if axis == "wt" and bit == 0:
            took = took / 6
        start = max(clock, free.get(link, 0.0))
        free[link] = end = start + took
        if bit > 1:
            start = max(start, free.get((axis, bit), 0.0))
            free[axis, bit] = end = start + 2 * took
        job[0], job[4] = end + delay, stage + 1
    return found


def seq_group(copies, source, name, take, final, seq, peer, done=None, low=None):
    seq_bits = len(source.shape) - 2
    dims = list(reversed(range(seq_bits)))
    if name == "chan":
        dims = [0] + dims[:-1]
    members = []
    for start, size, order in seq_orders(source.shape[-1], seq_bits, low):
        members.append(
            Halving(
                copies, source, dims, order, slice(start, start + size), take(seq_bits),
                functools.partial(final, start), seq, peer,
            )
        )
    return Group(members, done)


def landings(bits, rows, widths):
    return [
        pltpu.VMEM((2,) * (bits - 1 - stage) + (rows, width), BF16)
        for width in widths
        for stage in range(bits)
    ]


def seq_landings(seq_bits, rows, widths, low=None):
    found = []
    for width in widths:
        sizes = [size for _, size, _ in seq_orders(width, seq_bits, low)]
        found += landings(seq_bits, rows, sizes)
    return found


def wout_lows(n_wide, late):
    return [WIDE // 2 if late else 3 * WIDE // 4] + [7 * WIDE // 8 if late else WIDE // 2] * (n_wide - 1)


def feat_plan(n_chan, parts):
    half = n_chan // 2
    plan = [
        (n_chan + half, half, 3 * half // 4), (0, half, half), (half, half // 2, half // 2),
        (half + half // 2, half // 2, half // 4),
    ]
    return plan if parts > 1 else [(n_chan, half, None)] + plan


def feat_type(n_feat, n_seq, n_wt):
    return BF16 if n_feat // (n_seq * n_wt) % 16 == 0 else F32


def parts_of(n_chan, n_seq):
    return 2 if n_chan // n_seq >= 32 else 1


WIDE = 1024
EARLY = 512


def join_rounds(
    n_seq, n_streams, seq, wt, rate, head_ref, tail_ref, run_s, span_in, span_s, gap_s, send_s,
    land_s, span_send, span_land, send_sems, recv_sems,
):
    head_ref[...] = jnp.zeros_like(head_ref)
    tail_ref[...] = jnp.zeros_like(tail_ref)
    gap_s[...] = jnp.zeros_like(gap_s)
    for k in range(2 * n_streams):
        span_s[k : k + 1, :] = span_in[k % n_streams]
    started = []
    for r in range(n_seq.bit_length() - 1):
        d = 2**r
        if r > 1:
            for inside, copies in started[2 * r - 4 : 2 * r - 2]:

                @pl.when(inside)
                def _():
                    copies[0].wait_send()

        send_s[r % 2] = run_s[...].astype(BF16)
        span_send[r] = span_s[...]
        up = (seq + d < n_seq, lax.rem(seq + d, n_seq))
        down = (seq >= d, lax.rem(seq + n_seq - d, n_seq))
        for way, (inside, other) in enumerate((up, down)):
            copies = [
                pltpu.make_async_remote_copy(
                    src_ref=src, dst_ref=dst, send_sem=send_sems.at[r, way, k],
                    recv_sem=recv_sems.at[r, way, k], device_id=(other, wt), device_id_type=MESH,
                )
                for k, (src, dst) in enumerate(
                    ((send_s.at[r % 2, way], land_s.at[r, way]), (span_send.at[r], span_land.at[r, way]))
                )
            ]

            @pl.when(inside)
            def _():
                for copy in copies:
                    copy.start()

            started.append((inside, copies))
        for way, inside in ((0, down[0]), (1, up[0])):
            copies = started[-2 + way][1]
            out = (head_ref, tail_ref)[way]

            @pl.when(inside)
            def _():
                for copy in copies:
                    copy.wait_recv()
                for b in range(n_streams):
                    k = way * n_streams + b
                    landed = land_s[r, way, b].astype(F32)
                    span = span_land[r, way, k : k + 1, :]
                    gap, own = gap_s[k : k + 1, :], span_s[k : k + 1, :]
                    out[b] = out[b] + jnp.exp2(rate * gap) * landed
                    run_s[way, b] = run_s[way, b] + jnp.exp2(rate * own) * landed
                    gap_s[k : k + 1, :] = gap + span
                    span_s[k : k + 1, :] = own + span

    for at, (inside, copies) in enumerate(started):

        @pl.when(inside)
        def _():
            for copy in copies[at < len(started) - 4 :]:
                copy.wait_send()


def early_sums(n_seq, part, stream, width, grad_ref, normed_t_ref, wout_ref, feat_ref, scratch):
    gated_s, dgate_s, grads, normed_t = scratch[:4]
    feat_parts, scratch = scratch[4:6], scratch[6:]
    seq_bits = n_seq.bit_length() - 1
    count = grads.shape[1] // WIDE
    wout_parts, scratch = scratch[:count], scratch[count:]
    load_sems, send_sems, recv_sems = scratch[:3]
    scratch = scratch[3:]
    take = lambda k: [scratch.pop(0) for _ in range(k)]
    seq, wt = lax.axis_index("seq"), lax.axis_index("wt")
    copies = Copies(send_sems, recv_sems)
    peer = lambda bit: (flip(seq, bit), wt)

    def loads():
        return [
            pltpu.make_async_copy(grad_ref, grads, load_sems.at[0]),
            pltpu.make_async_copy(normed_t_ref, normed_t, load_sems.at[1]),
        ]

    def wout_final(at, start, rows, total):
        wout_ref[rows, at + start : at + start + total.shape[1]] = total.astype(BF16)

    def feat_final(at, start, rows, total):
        columns = slice(at + start, at + start + total.shape[1])
        feat_ref[rows, columns] = total.astype(feat_ref.dtype)

    lows = wout_lows(count, False)
    wouts = [
        seq_group(
            copies, wout_parts[k], "chan", take, functools.partial(wout_final, k * WIDE), seq, peer,
            low=lows[k],
        )
        for k in range(count)
    ]
    width = EARLY // 2
    feats = [
        seq_group(
            copies, feat_parts[k], "feat", take, functools.partial(feat_final, k * width), seq, peer
        )
        for k in range(2)
    ]
    groups = wouts + feats

    @pl.when((part == 0) & (stream == 0))
    def _():
        barrier = pltpu.get_barrier_semaphore()
        for bit in range(seq_bits):
            pl.semaphore_signal(barrier, inc=1, device_id=peer(bit), device_id_type=MESH)
        pl.semaphore_wait(barrier, seq_bits)
        for copy in loads():
            copy.start()

    def begin():
        for copy in loads():
            copy.wait()
        for k in range(count):
            for inner in range(0, WIDE, 512):
                at = k * WIDE + inner
                value = jnp.dot(
                    gated_s[...], grads[:, at : at + 512], preferred_element_type=F32
                )
                rows, lead = wout_parts[k].shape[-2], len(wout_parts[k].shape) - 2
                wout_parts[k][(slice(None),) * (lead + 1) + (slice(inner, inner + 512),)] = (
                    value.reshape((2,) * lead + (rows, 512)).astype(BF16)
                )

    def begin_feat():
        for k in range(2):
            at = slice(k * width, (k + 1) * width)
            by_tiles(
                feat_parts[k], normed_t.shape[0],
                lambda m: jnp.dot(normed_t[m, :], dgate_s[:, at], preferred_element_type=F32),
            )

    entries = []
    for which, group in enumerate(groups):
        rows = math.prod(group.members[0].source.shape[:-1])
        members = [(one.columns.stop - one.columns.start, one.order) for one in group.members]
        ready = 2.0 if which < count else 8.0
        entries.append((ready, "seq", rows * 2 / 2**20, members))
    times = [3.5, 9.0] + [9.0 + 2.9 * k for k in range(1, 15)]
    moments, last = {}, []
    for at, which, member, stage in timetable(entries):
        turns = [k for k, time in enumerate(times) if time >= at]
        moments.setdefault(turns[0] if turns else 16, []).append((which, member, stage))

    def moment(turn):
        if turn < 2:

            @pl.when((part == 1) & (stream == 0))
            def _():
                (begin, begin_feat)[turn]()

        for at in range(4):
            if at * 4 + turn in moments:

                @pl.when((part == 1) & (stream == at))
                def _():
                    for which, member, stage in moments[at * 4 + turn]:
                        groups[which].act(member, stage)

    def rest():
        for which, member, stage in moments.get(16, []):
            groups[which].act(member, stage)
        copies.finish()

    return moment, rest


def scan_kernel(
    n_state, n_seq, parts, bcs_ref, spread_ref, gather_ref, raw_ref, u_ref, g_ref, gate_ref, dgated_ref,
    bias_ref, skip_ref, a_ref, end_ref, lead_ref, total_ref, head_ref, tail_ref, grad_ref,
    normed_t_ref,
    gated_ref, gated_t_ref, dgate_ref, dscan_ref, draw_ref, dbc_ref, da_ref, sums_ref, wout_ref,
    feat_ref,
    bcb, acc_all, dec_in, delta_in, drive_in, g_in, y_sum, b_sum, d_sum, kept, decays, da_sum, row_sum, *scratch,
):
    n_rows, width = raw_ref.shape
    steps = n_rows // SUB
    part, stream = pl.program_id(0), pl.program_id(1)
    n_streams = pl.num_programs(1)
    acc = acc_all.at[stream]
    if parts > 1:
        early_moment, early_rest = early_sums(
            n_seq, part, stream, width, grad_ref, normed_t_ref, wout_ref, feat_ref, list(scratch)
        )
    start_at = 2 * n_state * LANE
    columns = pl.ds(pl.multiple_of(part * width, width), width)
    spread_rows(bcs_ref, spread_ref, bcb)

    @pl.when(part == 0)
    def _():
        acc_all[stream] = jnp.zeros(acc_all.shape[1:], F32)

    @pl.when(stream == 0)
    def _():
        da_sum[...] = jnp.zeros_like(da_sum)
        row_sum[...] = jnp.zeros_like(row_sum)

    def prepare(j, carry):
        rows = pl.ds(pl.multiple_of(j * 16, 16), 16)
        delta = softplus(raw_ref[rows, :].astype(F32) + bias_ref[...])
        starts = wide(bcb[rows, start_at : start_at + LANE], width)
        delta_in[rows, :] = delta
        dec_in[rows, :] = jnp.where(starts > 0.5, RESET, delta)
        drive_in[rows, :] = delta * u_ref[rows, :].astype(F32)
        g_in[rows, :] = g_ref[rows, :].astype(F32)
        return carry

    lax.fori_loop(0, steps // 2, prepare, 0)
    chunk = lax.broadcasted_iota(jnp.int32, (SUB, width), 0)
    total = total_ref[0]
    before, after = total, total
    for shift in (1, 2, 4):
        before = jnp.where(chunk >= shift, before + pltpu.roll(before, shift, 0), before)
        after = jnp.where(chunk < SUB - shift, after + pltpu.roll(after, SUB - shift, 0), after)
    before, after = pltpu.roll(before, 1, 0), pltpu.roll(after, SUB - 1, 0)

    for first in range(0, n_state, NBLK):
        if parts > 1:
            early_moment(first // NBLK)
        states = range(first, first + NBLK)
        entry, incoming = [], []
        for n in states:
            head, tail = head_ref[0, n : n + 1, :], tail_ref[0, n : n + 1, :]
            inner = pltpu.roll(end_ref[0, n], 1, 0) + jnp.exp2(before * a_ref[n : n + 1, :]) * head
            outer = pltpu.roll(lead_ref[0, n], SUB - 1, 0) + jnp.exp2(after * a_ref[n : n + 1, :]) * tail
            entry.append(jnp.where(chunk == 0, head, inner))
            incoming.append(jnp.where(chunk == SUB - 1, tail, outer))

        def forward(j, carry):
            rows = pl.ds(pl.multiple_of(j * SUB, SUB), SUB)
            held, drive, g = dec_in[rows, :], drive_in[rows, :], g_in[rows, :]
            running = []
            y = y_sum[rows, :] if first else None
            for k, (n, h) in enumerate(zip(states, carry)):
                b = wide(bcb[rows, n * LANE : (n + 1) * LANE], width)
                c_at = slice((n_state + n) * LANE, (n_state + n + 1) * LANE)
                c = wide(bcb[rows, c_at], width)
                decay = jnp.exp2(held * a_ref[n : n + 1, :])
                kept[k, rows, :] = h
                decays[k, rows, :] = decay
                h = decay * h + drive * b
                y = c * h if y is None else y + c * h
                acc[rows, c_at] += fold(h * g)
                running.append(h)
            y_sum[rows, :] = y
            return tuple(running)

        lax.fori_loop(0, steps, forward, tuple(entry), unroll=8)

        def backward(j, carry):
            rows = pl.ds(pl.multiple_of((steps - 1 - j) * SUB, SUB), SUB)
            delta, drive, g = delta_in[rows, :], drive_in[rows, :], g_in[rows, :]
            through = b_sum[rows, :] if first else None
            pulled = d_sum[rows, :] if first else None
            passed, da = [], []
            for k, (n, p, da_n) in enumerate(zip(states, carry[0], carry[1])):
                b_at = slice(n * LANE, (n + 1) * LANE)
                b = wide(bcb[rows, b_at], width)
                c = wide(bcb[rows, (n_state + n) * LANE : (n_state + n + 1) * LANE], width)
                adjoint = g * c + p
                p = decays[k, rows, :] * adjoint
                weighed = p * kept[k, rows, :]
                pulled = weighed * a_ref[n : n + 1, :] if pulled is None else pulled + weighed * a_ref[n : n + 1, :]
                through = adjoint * b if through is None else through + adjoint * b
                acc[rows, b_at] += fold(adjoint * drive)
                passed.append(p)
                da.append(da_n + weighed * delta)
            b_sum[rows, :] = through
            d_sum[rows, :] = pulled
            return tuple(passed), tuple(da)

        zero = tuple(jnp.zeros((SUB, width), F32) for _ in states)
        _, da = lax.fori_loop(0, steps, backward, (tuple(incoming), zero), unroll=8)
        for n, da_n in zip(states, da):
            da_sum[n] += da_n

    def finish(j, carry):
        bias_sum, skip_sum = carry
        rows = pl.ds(pl.multiple_of(j * 16, 16), 16)
        u, g, delta = u_ref[rows, :].astype(F32), g_in[rows, :], delta_in[rows, :]
        gate, d_gated = gate_ref[rows, :].astype(F32), dgated_ref[rows, :]
        scanned = (y_sum[rows, :] + skip_ref[...] * u).astype(BF16).astype(F32)
        sig = jax.nn.sigmoid(gate)
        gated_ref[rows, :] = (scanned * gate * sig).astype(BF16)
        d_gate = d_gated * scanned * sig * (1.0 + gate * (1.0 - sig))
        dgate_ref[rows, :] = d_gate.astype(BF16)
        through = b_sum[rows, :]
        dscan_ref[rows, :] = (delta * through + skip_ref[...] * g).astype(BF16)
        slope = jax.nn.sigmoid(raw_ref[rows, :].astype(F32) + bias_ref[...])
        d_pre = (d_sum[rows, :] * (1.0 / LOG2E) + u * through) * slope
        draw_ref[rows, :] = d_pre.astype(BF16)
        gu = g * u
        return bias_sum + d_pre[:SUB] + d_pre[SUB:], skip_sum + gu[:SUB] + gu[SUB:]

    zero = jnp.zeros((SUB, width), F32)
    bias_sum, skip_sum = lax.fori_loop(0, steps // 2, finish, (zero, zero))
    gated_t_ref[...] = gated_ref[...].T
    if parts > 1:
        gated_s, dgate_s = scratch[:2]

        @pl.when(part == 0)
        def _():
            at = pl.ds(pl.multiple_of(stream * n_rows, n_rows), n_rows)
            gated_s[:, at] = gated_t_ref[...]
            dgate_s[at, :] = dgate_ref[...]

    row_sum[0] += bias_sum
    row_sum[1] += skip_sum

    @pl.when(stream == n_streams - 1)
    def _():
        for n in range(n_state):
            da_ref[n : n + 1, columns] = jnp.sum(da_sum[n], 0, keepdims=True)
        for k in range(2):
            sums_ref[k : k + 1, columns] = jnp.sum(row_sum[k], 0, keepdims=True)


    last = part == pl.num_programs(0) - 1

    @pl.when(last)
    def _():
        found = jnp.dot(
            acc[...], gather_ref[...], precision=lax.Precision.HIGHEST, preferred_element_type=F32
        )

        @pl.when(stream == 0)
        def _():
            dbc_ref[...] = found

        @pl.when(stream > 0)
        def _():
            dbc_ref[...] += pltpu.roll(found, stream * 2 * n_state, 1)

    if parts > 1:

        @pl.when(last & (stream == n_streams - 1))
        def _():
            early_rest()


def spread_matrix(n_state):
    count = 2 * n_state + 1
    column = np.arange(count * LANE)[None, :] // LANE
    return jnp.asarray((np.arange(LANE)[:, None] == column).astype(ml_dtypes.bfloat16))


def gather_matrix(n_state):
    row = np.arange(2 * n_state * LANE)[:, None] // LANE
    return jnp.asarray((np.arange(LANE)[None, :] == row).astype(np.float32))


def scan_specs(n_streams, n_rows, n_chan, n_state, width):
    row = pl.BlockSpec((n_rows, width), lambda b, c: (b, c))
    thin = pl.BlockSpec((n_rows, LANE), lambda b, c: (b, 0))
    chan = pl.BlockSpec((1, width), lambda b, c: (0, c))
    rate = pl.BlockSpec((n_state, width), lambda b, c: (0, c))
    edge = pl.BlockSpec((1, n_state, SUB, width), lambda b, c: (b, 0, 0, c))
    total = pl.BlockSpec((1, SUB, width), lambda b, c: (b, 0, c))
    head = pl.BlockSpec((1, n_state, width), lambda b, c: (b, 0, c))
    return row, thin, chan, rate, edge, total, head


def whole(shape):
    return pl.BlockSpec(shape, lambda b, c: (0,) * len(shape))


def scan_all(
    bcs, raw, u, g, gate, d_gated, bias, skip, rates, ends, leads, totals, heads, tails, grads,
    normed_t,
):
    n_seq, n_streams = lax.axis_size("seq"), lax.axis_size("wt")
    n_rows, n_chan = raw.shape[0] // n_streams, raw.shape[1]
    n_state, n_feat = rates.shape[0], normed_t.shape[0]
    width = min(512, n_chan)
    parts = parts_of(n_chan, n_seq)
    seq_bits = n_seq.bit_length() - 1

    def swapped(spec):
        return pl.BlockSpec(spec.block_shape, lambda c, b: spec.index_map(b, c))

    row, thin, chan, rate, edge, total, head = map(
        swapped, scan_specs(n_streams, n_rows, n_chan, n_state, width)
    )
    count = (2 * n_state + 1) * LANE
    spread = spread_matrix(n_state)
    gather = gather_matrix(n_state)
    rows = jax.ShapeDtypeStruct(raw.shape, BF16)
    hbm = pl.BlockSpec(memory_space=pl.ANY)
    wout_rows, feat_rows = max(n_chan // parts // n_seq, 16), n_feat // n_seq
    scratch = [
        pltpu.VMEM((n_rows, count), F32),
        pltpu.VMEM((n_streams, n_rows, 2 * n_state * LANE), F32),
    ]
    scratch += [pltpu.VMEM((n_rows, width), F32)] * 7
    scratch += [pltpu.VMEM((NBLK, n_rows, width), F32)] * 2
    scratch += [pltpu.VMEM((n_state, SUB, width), F32), pltpu.VMEM((2, SUB, width), F32)]
    params = {}
    if parts > 1:
        blocks = (2,) * seq_bits
        n_wide = n_feat // WIDE
        scratch += [
            pltpu.VMEM((width, raw.shape[0]), BF16),
            pltpu.VMEM((raw.shape[0], width), BF16),
            pltpu.VMEM((raw.shape[0], n_feat), BF16),
            pltpu.VMEM(normed_t.shape, BF16),
        ]
        scratch += [pltpu.VMEM(blocks + (feat_rows, EARLY // 2), BF16)] * 2
        scratch += [pltpu.VMEM(blocks + (wout_rows, WIDE), BF16)] * n_wide
        scratch += [pltpu.SemaphoreType.DMA((2,))]
        scratch += [pltpu.SemaphoreType.DMA((2 * seq_bits * (n_wide + 2),))] * 2
        for low in wout_lows(n_wide, False):
            scratch += seq_landings(seq_bits, wout_rows, [WIDE], low)
        scratch += seq_landings(seq_bits, feat_rows, [EARLY // 2] * 2)
        params = dict(collective_id=4, has_side_effects=True)
    return pl.pallas_call(
        functools.partial(scan_kernel, n_state, n_seq, parts),
        grid=(n_chan // width, n_streams),
        in_specs=[
            thin, whole((LANE, count)), whole(gather.shape), row, row, row, row, row,
            chan, chan, rate, edge, edge, total, head, head, hbm, hbm,
        ],
        out_specs=[
            row, pl.BlockSpec((width, n_rows), lambda c, b: (c, b)), row, row, row,
            whole((n_rows, LANE)), whole((n_state, n_chan)), whole((2, n_chan)),
            whole((wout_rows, n_feat)), whole((feat_rows, EARLY)),
        ],
        out_shape=[
            rows, jax.ShapeDtypeStruct(raw.shape[::-1], BF16), rows, rows, rows,
            jax.ShapeDtypeStruct((n_rows, LANE), F32),
            jax.ShapeDtypeStruct((n_state, n_chan), F32),
            jax.ShapeDtypeStruct((2, n_chan), F32),
            jax.ShapeDtypeStruct((wout_rows, n_feat), BF16),
            jax.ShapeDtypeStruct((feat_rows, EARLY), feat_type(n_feat, n_seq, n_streams)),
        ],
        scratch_shapes=scratch,
        compiler_params=pltpu.CompilerParams(vmem_limit_bytes=63 * 2**20, **params),
        name="scan_all",
    )(
        bcs, spread, gather, raw, u, g, gate, d_gated, bias, skip, rates,
        ends, leads, totals, heads, tails, grads, normed_t,
    )


def finish_kernel(
    n_seq, n_wt, n_state,
    gated_t_ref, dgate_ref, dscan_ref, draw_ref, u_ref, conv_ref, grad_ref, normed_t_ref, win_ref,
    wout_ref, feat_ref, gated_ref, w_out_ref, x_ref, g_ref,
    gain_ref, dbc_ref, low_ref, wx_ref, wdt_ref, wconv_ref, bconv_ref, da_ref, a_ref, sums_ref,
    feat_out, wout_out, small_out, norm_out, out_out, gain_out,
    *scratch,
):
    scratch = list(scratch)
    take = lambda count: [scratch.pop(0) for _ in range(count)]
    seq, wt = lax.axis_index("seq"), lax.axis_index("wt")
    seq_bits, wt_bits = n_seq.bit_length() - 1, n_wt.bit_length() - 1
    seq_peer = lambda bit: (flip(seq, bit), wt)
    wt_peer = lambda bit: (seq, flip(wt, bit))
    n_chan, all_rows = gated_t_ref.shape
    parts = parts_of(n_chan, n_seq)
    ready = parts - 1
    half_seq = n_seq // 2
    here = n_wt * seq + wt
    mine = (seq % 2) * half_seq + seq // 2

    def summed_at(j):
        return (j % half_seq) * 2 + j // half_seq

    def device(flat):
        return flat // n_wt, flat % n_wt

    flat = n_seq * wt + mine
    owner, giver_block = device(flat), here % n_seq
    giver = (summed_at(giver_block), here // n_seq)
    elsewhere = flat != here
    per = n_seq // parts
    part_flat = [n_seq * wt + q * per + mine // parts for q in range(parts)]
    part_owner = [device(value) for value in part_flat]
    piece = mine % parts
    piece_giver = [
        (summed_at((giver_block % per) * parts + k), here // n_seq) for k in range(parts)
    ]
    piece_here = [n_wt * s + w == here for s, w in piece_giver]
    ahead, behind = (lax.rem(seq + 1, n_seq), wt), (lax.rem(seq + n_seq - 1, n_seq), wt)

    barrier = pltpu.get_barrier_semaphore()
    partners = [seq_peer(b) for b in range(seq_bits)]
    partners += [(seq, turn(wt, mask, wt_bits)) for mask in range(1, n_wt)]
    partners += [ahead, behind]
    for partner in partners:
        pl.semaphore_signal(barrier, inc=1, device_id=partner, device_id_type=MESH)

    arrivals = len(partners) + 2 * elsewhere.astype(jnp.int32)

    @pl.when(elsewhere)
    def _():
        for partner in (owner, giver):
            pl.semaphore_signal(barrier, inc=1, device_id=partner, device_id_type=MESH)

    if parts > 1:
        others = [(value != here, to) for value, to in zip(part_flat, part_owner)]
        others += [(jnp.logical_not(own), to) for own, to in zip(piece_here, piece_giver)]
        for away, to in others:
            arrivals = arrivals + away.astype(jnp.int32)

            @pl.when(away)
            def _():
                pl.semaphore_signal(barrier, inc=1, device_id=to, device_id_type=MESH)

    (
        gated_t, dgate, dscan, draw, normed_t, grads, win_rows, conv, d_conv, mix, first, half, land, fin,
        u_all, ddt, dbc, pack, rim_f, rim_s, fin_feat, fin_wout, fin_small, w_rows, gain_sum, small,
        piece_sems, send_sems, recv_sems,
    ) = take(29)
    n_wide = normed_t.shape[0] // WIDE
    wout_parts = take(n_wide) if ready else take(1) * n_wide
    feat_parts, norm_parts = take(4 if ready else 3), take(2)
    if not ready:
        inner = (slice(None),) * (seq_bits + 1)
        feat_parts += [feat_parts[0].at[inner + (slice(at, at + 256),)] for at in (0, 256)]
    copies = Copies(send_sems, recv_sems)
    part_chan = gated_t.shape[0]
    if not ready:
        u_all = gated_t
    n_feat = normed_t.shape[0]
    n_rows = all_rows // n_wt
    taps = wconv_ref.shape[0]
    steps = n_rows // SUB
    rim = (taps - 1) * SUB
    cols = 512

    def load(src, dst):
        return copies.local(src, dst)

    def grad_block(k):
        return load(grad_ref.at[:, :, k * cols : (k + 1) * cols], grads.at[k % 2])

    coming = {
        "draw": load(draw_ref, draw),
        "gated": load(gated_t_ref.at[ready * part_chan :], gated_t),
        0: grad_block(0),
        1: grad_block(1),
        "normed": load(normed_t_ref, normed_t),
        "dgate": load(dgate_ref, dgate),
        "conv": load(conv_ref.at[:, :, :cols], conv),
        "dscan": load(dscan_ref.at[:, :cols], dscan),
        "w_rows": load(
            win_ref.at[pl.ds(pl.multiple_of(seq * w_rows.shape[0], 16), w_rows.shape[0])], w_rows
        ),
    }

    ring, d_block = win_rows.shape[:2]

    def win_block(i):
        coming["win", i] = load(win_ref.at[i * d_block : (i + 1) * d_block], win_rows.at[i % ring])

    for k in range(cols // d_block):
        win_block(k)
    if ready:
        coming["wout"] = load(wout_ref, fin_wout.at[0])
        coming["feat"] = load(feat_ref, fin_feat.at[:, n_chan : n_chan + EARLY])
    pl.semaphore_wait(barrier, arrivals)

    rows_own = feat_out.shape[0]

    def own_rows(w):
        return pl.ds(pl.multiple_of(w * rows_own, 8), rows_own)

    delivered = []

    def to_wt(block_of, place):
        for mask in range(1, n_wt):
            peer = turn(wt, mask, wt_bits)
            delivered.append(copies.remote(block_of(peer), place, (seq, peer)).wait_recv)
        delivered.append(copies.local(block_of(wt), place).wait)

    def feat_done(at, cols):
        tile = math.gcd(w_rows.shape[0], 32)

        def body(i, carry):
            rows = pl.ds(pl.multiple_of(i * tile, tile), tile)
            done = fin_feat[rows, at : at + cols].astype(F32)
            product = w_rows[rows, at : at + cols].astype(F32) * done
            gain_sum[rows, :] += fold(product)
            return carry

        lax.fori_loop(0, w_rows.shape[0] // tile, body, 0)
        start = pl.multiple_of(((at // n_chan) * n_wt + wt) * n_chan + at % n_chan, LANE)
        to_wt(
            lambda w: fin_feat.at[own_rows(w), at : at + cols],
            feat_out.at[:, pl.ds(start, cols)],
        )

    moved = []

    def small_done():
        k, copies.count = copies.count, copies.count + 1
        away = pltpu.make_async_remote_copy(
            src_ref=fin_small, dst_ref=small_out, send_sem=send_sems.at[k],
            recv_sem=recv_sems.at[k], device_id=owner, device_id_type=MESH,
        )
        home = pltpu.make_async_copy(fin_small, small_out, send_sems.at[k])

        @pl.when(elsewhere)
        def _():
            away.start()

        @pl.when(jnp.logical_not(elsewhere))
        def _():
            home.start()

        def wait():
            @pl.when(elsewhere)
            def _():
                away.wait()

            @pl.when(jnp.logical_not(elsewhere))
            def _():
                home.wait()

        moved.append(wait)

    def wout_done(q, at, width, slot):
        place = fin_wout.at[q, :, at : at + width]
        target = wout_out.at[piece, :, at : at + width]
        away = pltpu.make_async_remote_copy(
            src_ref=place, dst_ref=target, send_sem=piece_sems.at[0, q, slot],
            recv_sem=piece_sems.at[1, piece, slot], device_id=part_owner[q], device_id_type=MESH,
        )
        home = pltpu.make_async_copy(place, target, piece_sems.at[0, q, slot])
        remote = part_flat[q] != here

        @pl.when(remote)
        def _():
            away.start()

        @pl.when(jnp.logical_not(remote))
        def _():
            home.start()

        def wait():
            @pl.when(remote)
            def _():
                away.wait_send()

            @pl.when(jnp.logical_not(remote))
            def _():
                home.wait()

        moved.append(wait)

    def wout_arrive(k, at, width, slot):
        target = wout_out.at[k, :, at : at + width]
        copy = pltpu.make_async_remote_copy(
            src_ref=target, dst_ref=target, send_sem=piece_sems.at[0, k, slot],
            recv_sem=piece_sems.at[1, k, slot], device_id=piece_giver[k], device_id_type=MESH,
        )

        @pl.when(jnp.logical_not(piece_here[k]))
        def _():
            copy.wait_recv()

    def wout_final(at, start, rows, total):
        columns = slice(at + start, at + start + total.shape[1])
        fin_wout[ready, rows, columns] = total.astype(BF16)

    def feat_final(at, start, rows, total):
        columns = slice(at + start, at + start + total.shape[1])
        fin_feat[rows, columns] = total.astype(fin_feat.dtype)

    def small_final(start, rows, total):
        fin_small[rows, start : start + total.shape[1]] = total.astype(BF16)

    wout_groups = [
        seq_group(
            copies, wout_parts[k], "chan", take, functools.partial(wout_final, k * WIDE), seq,
            seq_peer, functools.partial(wout_done, ready, k * WIDE, WIDE, k), lows[k],
        )
        for k, lows in zip(range(n_wide), [wout_lows(n_wide, True)] * n_wide)
    ]
    feat_groups = []
    for part, (at, _, low) in zip(feat_parts, feat_plan(n_chan, parts)):
        done = functools.partial(feat_done, at, part.shape[-1])
        feat_groups.append(
            seq_group(
                copies, part, "feat", take, functools.partial(feat_final, at), seq, seq_peer, done,
                low,
            )
        )
    gate_a, gate_b, conv_a, conv_b, conv_c = range(-ready, 5 - ready)
    small_group = seq_group(copies, small, "chan", take, small_final, seq, seq_peer, small_done)
    wide_groups = []
    for target in (norm_out, out_out):
        for k in range(n_feat // cols):

            def final(rows, total, target=target, k=k):
                target[rows, k * cols : (k + 1) * cols] = total

            order = tuple(range(wt_bits))
            job = Halving(
                copies, norm_parts[k % 2], list(reversed(order)), order, slice(0, cols),
                take(wt_bits), final, wt, wt_peer,
            )
            wide_groups.append(Group([job]))

    def wout(k):
        if not ready and k:
            take_until(k - 1)
            wout_groups[k - 1].release()
        for inner in range(WIDE // cols):
            block = k * (WIDE // cols) + inner
            coming[block].wait()
            right = grads[block % 2].reshape(all_rows, cols)
            lanes = slice(inner * cols, (inner + 1) * cols)
            tile = min(512, part_chan)
            rows, lead = wout_parts[k].shape[-2], len(wout_parts[k].shape) - 2
            within = (tile // rows).bit_length() - 1
            for m in range(0, part_chan, tile):
                value = jnp.dot(gated_t[m : m + tile, :], right, preferred_element_type=F32)
                index = tuple(
                    (m // rows >> (lead - 1 - q)) & 1 for q in range(lead - within)
                )
                wout_parts[k][index + (slice(None),) * (within + 1) + (lanes,)] = (
                    value.reshape((2,) * within + (rows, cols)).astype(BF16)
                )
            if block + 2 < n_feat // cols:
                coming[block + 2] = grad_block(block + 2)

    gain_sum[...] = jnp.zeros_like(gain_sum)
    coming["draw"].wait()
    for b in range(n_wt):
        at = slice(b * n_rows, (b + 1) * n_rows)
        mix[at, :] = jnp.dot(draw[at, :], wdt_ref[...], preferred_element_type=F32)
    width = LANE // n_wt
    mix[all_rows:, :] = dbc_ref[...]
    mixed = WtSum(copies, mix, first, half, land, fin, seq, wt, wt_bits)
    mixed.begin()
    coming["gated"].wait()

    def feat(k, right):
        if not ready and k == conv_b:
            take_until(first_feat + gate_a)
            feat_groups[gate_a].release()
        by_tiles(
            feat_parts[k], n_feat,
            lambda m: jnp.dot(normed_t[m, :], right, preferred_element_type=F32),
        )

    def low_pack():
        pack[LANE : 2 * LANE, :] = lax.dot_general(
            low_ref[...], draw[...], (((0,), (0,)), ((), ())), preferred_element_type=F32
        )
        mixed.end_send()
        coming["normed"].wait()
        coming["dgate"].wait()

    def early_feat():
        coming["w_rows"].wait()
        if ready:
            coming["feat"].wait()
            feat_done(n_chan, EARLY)
        mixed.copy.wait_recv()
        mixed_ready()

    tail_at = 2 * LANE + 3 * n_state

    def mixed_ready():
        ddt[...] = fin[:all_rows, :].astype(BF16)
        lane = lax.broadcasted_iota(jnp.int32, (n_rows, LANE), 1)
        for b in range(n_wt):
            part = fin[all_rows:, :]
            if b:
                part = pltpu.roll(part, LANE - b * width, 1)
            dbc[b * n_rows : (b + 1) * n_rows, :] = jnp.where(lane < width, part, 0.0).astype(BF16)
        coming["u"] = load(u_ref, u_all)

        pack[2 * LANE :, :] = jnp.zeros((LANE, n_chan), F32)
        pack[tail_at - n_state : tail_at, :] = da_ref[...] * (a_ref[...] * (1.0 / LOG2E))
        pack[tail_at + taps + 1 : tail_at + taps + 3, :] = sums_ref[...]

    def sums_of(total):
        return jnp.sum(total, 0, keepdims=True)

    chunk = lax.broadcasted_iota(jnp.int32, (SUB, cols), 0)
    rim_moves = []

    def conv_first(h):
        at = slice(h * cols, (h + 1) * cols)
        for b in range(n_wt):
            rows = slice(b * n_rows, (b + 1) * n_rows)
            d_in = lax.dot_general(
                ddt[rows, :], wx_ref[at, :LANE], (((1,), (1,)), ((), ())), preferred_element_type=F32
            )
            d_in = d_in + lax.dot_general(
                dbc[rows, : 2 * n_state], wx_ref[at, LANE:], (((1,), (1,)), ((), ())),
                preferred_element_type=F32,
            )
            d_conv[h, b, :n_rows, :] = d_in
        coming["conv"].wait()
        coming["dscan"].wait()

        def one(i, carry):
            b, j = i // (n_rows // 16), i % (n_rows // 16)
            rows = pl.ds(pl.multiple_of(j * 16, 16), 16)
            taken = [
                conv[b, pl.ds(pl.multiple_of(j * 16 + k * SUB, SUB), 16), :] for k in range(taps)
            ]
            out = bconv_ref[:, at]
            for k in range(taps):
                out = out + taken[k] * wconv_ref[k : k + 1, at]
            sig = jax.nn.sigmoid(out)
            from_scan = dscan[pl.ds(pl.multiple_of(i * 16, 16), 16), :].astype(F32)
            value = (d_conv[h, b, rows, :] + from_scan) * sig * (1.0 + out * (1.0 - sig))
            d_conv[h, b, rows, :] = value
            found = [value] + [value * piece for piece in taken]
            return tuple(c + f[:SUB] + f[SUB:] for c, f in zip(carry, found))

        zero = jnp.zeros((SUB, cols), F32)
        totals = lax.fori_loop(0, all_rows // 16, one, (zero,) * (taps + 1))
        pack[tail_at + taps : tail_at + taps + 1, at] = sums_of(totals[0])
        for k in range(taps):
            pack[tail_at + k : tail_at + k + 1, at] = sums_of(totals[k + 1])

        rim_f[...] = jnp.zeros_like(rim_f)
        for b in range(n_wt):
            for k in range(taps - 1):
                rim_f[b * (taps - 1) + k, :] = d_conv[h, b, k * SUB, :]
        rim_s[h, 0] = rim_f[...].astype(BF16)

        @pl.when(seq == n_seq - 1)
        def _():
            rim_s[h, 1] = jnp.zeros((16, cols), BF16)

        k, copies.count = copies.count, copies.count + 1
        move = pltpu.make_async_remote_copy(
            src_ref=rim_s.at[h, 0], dst_ref=rim_s.at[h, 1], send_sem=send_sems.at[k],
            recv_sem=recv_sems.at[k], device_id=behind, device_id_type=MESH,
        )
        rim_moves.append(move)

        @pl.when(seq > 0)
        def _():
            move.start()

        if h == 0:
            coming["conv"] = load(conv_ref.at[:, :, cols : 2 * cols], conv)
            coming["dscan"] = load(dscan_ref.at[:, cols : 2 * cols], dscan)

    def conv_second(h):
        at = slice(h * cols, (h + 1) * cols)

        @pl.when(seq < n_seq - 1)
        def _():
            rim_moves[h].wait_recv()

        landed = rim_s[h, 1].astype(F32)
        for b in range(n_wt):
            for k in range(taps - 1):
                turned = pltpu.roll(d_conv[h, b, k * SUB : (k + 1) * SUB, :], SUB - 1, 0)
                row = landed[b * (taps - 1) + k : b * (taps - 1) + k + 1, :]
                place = slice(n_rows + k * SUB, n_rows + (k + 1) * SUB)
                d_conv[h, b, place, :] = jnp.where(chunk == SUB - 1, row, turned)

        def one(i, carry):
            b, j = i // (n_rows // 16), i % (n_rows // 16)
            total = jnp.zeros((16, cols), F32)
            for k in range(taps):
                start = pl.multiple_of(j * 16 + (taps - 1 - k) * SUB, SUB)
                total = total + d_conv[h, b, pl.ds(start, 16), :] * wconv_ref[k : k + 1, at]
            draw[pl.ds(pl.multiple_of(i * 16, 16), 16), at] = total.astype(BF16)
            return carry

        lax.fori_loop(0, all_rows // 16, one, 0)

    def early_pieces():
        if ready:
            coming["wout"].wait()
            for k in range(n_wide):
                wout_done(0, k * WIDE, WIDE, k)

    def small_sums():
        coming["u"].wait()
        pack[:LANE, :] = lax.dot_general(
            ddt[...], u_all[...], (((0,), (0,)), ((), ())), preferred_element_type=F32
        )
        for_b = lax.dot_general(
            dbc[...], u_all[...], (((0,), (0,)), ((), ())), preferred_element_type=F32
        )
        pack[2 * LANE : 2 * LANE + 2 * n_state, :] = for_b[: 2 * n_state, :]
        coming["gated"] = load(gated_ref, u_all)
        tile = min(512, n_chan)
        for m in range(0, n_chan, tile):
            fill(small, m // small.shape[-2], pack[:, m : m + tile].T)

    per = cols // d_block
    n_norm = n_feat // cols

    def wide_part(k, block_of):
        part = norm_parts[k % 2]
        if k >= 2:
            take_until(len(seq_groups) + k - 2)
            wide_groups[k - 2].release()
        for b in range(n_wt):
            index = tuple((b >> (wt_bits - 1 - q)) & 1 for q in range(wt_bits))
            for lanes, value in block_of(slice(b * n_rows, (b + 1) * n_rows)):
                part[index + (slice(None), lanes)] = value.astype(BF16)

    def norm(k):
        def block_of(at):
            for part in range(per):
                rows_w = win_rows.at[(k * per + part) % ring]
                value = lax.dot_general(
                    draw[at, :], rows_w[:, :n_chan], (((1,), (1,)), ((), ())),
                    preferred_element_type=F32,
                )
                value = value + lax.dot_general(
                    dgate[at, :], rows_w[:, n_chan:], (((1,), (1,)), ((), ())),
                    preferred_element_type=F32,
                )
                yield slice(part * d_block, (part + 1) * d_block), value

        for part in range(per):
            coming["win", k * per + part].wait()
        wide_part(k, block_of)
        for part in range(per):
            if (k + 1) * per + part < per * n_norm:
                win_block((k + 1) * per + part)

    def out_block(k):
        coming["out", k] = load(w_out_ref.at[:, :, k * cols : (k + 1) * cols], grads.at[k % 2])

    def out(k):
        coming["out", k].wait()
        right = grads[k % 2].reshape(all_rows, cols)

        def block_of(at):
            yield slice(0, cols), jnp.dot(u_all[at, :], right, preferred_element_type=F32)

        wide_part(n_norm + k, block_of)
        if k + 2 < n_norm:
            out_block(k + 2)
        if k + 1 == n_norm:
            for at in range(n_norm):
                block = slice(at * cols, (at + 1) * cols)
                coming["x", at] = load(x_ref.at[:, block], dscan.at[at * n_rows : (at + 1) * n_rows])
                coming["g", at] = load(g_ref.at[:, block], grads.at[0, at])

    def last_of_wide():
        for at in range(n_norm):
            coming["x", at].wait()
            coming["g", at].wait()
        gain = jnp.concatenate([gain_ref[k].astype(F32)[0:1] for k in range(n_wt)], axis=1)
        to = lax.broadcasted_iota(jnp.int32, (n_rows, n_rows), 0)
        source = lax.broadcasted_iota(jnp.int32, (n_rows, n_rows), 1)
        order = (source == (to % steps) * SUB + to // steps).astype(F32)
        for target in (norm_out, out_out):
            for at in range(n_norm):
                block = slice(at * cols, (at + 1) * cols)
                target[:, block] = jnp.dot(
                    order, target[:, block], precision=lax.Precision.HIGHEST,
                    preferred_element_type=F32,
                )

        def one(i, carry):
            rows = pl.ds(pl.multiple_of(i * 16, 16), 16)
            x = jnp.concatenate(
                [
                    dscan[pl.ds(pl.multiple_of(at * n_rows + i * 16, 16), 16), :].astype(F32)
                    for at in range(n_norm)
                ],
                axis=1,
            )
            g = jnp.concatenate([grads[0, at, rows, :].astype(F32) for at in range(n_norm)], axis=1)
            out_out[rows, :] = out_out[rows, :] + x
            inv = lax.rsqrt(jnp.mean(x * x, axis=1, keepdims=True) + EPS)
            scaled = norm_out[rows, :] * gain
            along = jnp.mean(scaled * x, axis=1, keepdims=True)
            norm_out[rows, :] = g + inv * scaled - x * (inv * inv * inv) * along
            return carry

        lax.fori_loop(0, n_rows // 16, one, 0)

    def out_begin():
        coming["gated"].wait()
        out_block(0)
        out_block(1)

    seq_groups = wout_groups + feat_groups + [small_group]
    first_feat = n_wide
    works = [(1.3, functools.partial(wout, 0), [0])]
    works += [(1.5, functools.partial(mixed.middle, bit), []) for bit in range(1, wt_bits)]
    works += [(1.3, functools.partial(wout, k), [k]) for k in range(1, n_wide)]
    works += [
        (4.0, low_pack, []),
        (2.0, early_feat, []),
        (4.5, functools.partial(conv_first, 0), []),
        (4.5, functools.partial(conv_first, 1), []),
        (0.3, early_pieces, []),
        (2.5, lambda: feat(gate_b, dgate[:, cols:]), [first_feat + gate_b]),
        (2.5, functools.partial(conv_second, 0), []),
        (2.5, lambda: feat(conv_a, draw[:, :cols]), [first_feat + conv_a]),
        (2.5, functools.partial(conv_second, 1), []),
        (1.4, lambda: feat(conv_b, draw[:, cols : cols + 256]), [first_feat + conv_b]),
        (1.4, lambda: feat(conv_c, draw[:, cols + 256 :]), [first_feat + conv_c]),
        (4.0, small_sums, [len(seq_groups) - 1]),
    ]
    works += [(2.7, functools.partial(norm, k), [len(seq_groups) + k]) for k in range(n_norm)]
    if not ready:
        gate_first = (3.0, lambda: feat(gate_a, dgate[:, :cols]), [first_feat + gate_a])
        works.insert(len(works) - 14 - n_norm, gate_first)
    works += [(0.2, out_begin, [])]
    works += [(1.5, functools.partial(out, k), [len(seq_groups) + n_norm + k]) for k in range(n_norm)]
    clock, starts_at, ready_at = 5.0, [], {}
    for took, _, readied in works:
        starts_at.append(clock)
        clock += took
        for which in readied:
            ready_at[which] = clock
    all_groups = seq_groups + wide_groups
    entries = []
    for which, group in enumerate(all_groups):
        job = group.members[0]
        axis = "seq" if which < len(seq_groups) else "wt"
        rows = math.prod(job.source.shape[:-1])
        members = [(one.columns.stop - one.columns.start, one.order) for one in group.members]
        entries.append((ready_at[which], axis, rows * 2 / 2**20, members))
    moves = [(29.0, "seq", 1, 0.375), (60.0, "seq", 1, 0.375), (90.0, "seq", 1, 0.14)]
    actions = timetable(entries, moves)
    ended = max(time for time, which, _, _ in actions if which >= len(seq_groups))
    actions.append((ended, None, 0, 0))
    actions.sort(key=lambda action: action[0])

    def take_action(at=0):
        _, which, member, stage = actions.pop(at)
        if which is None:
            last_of_wide()
        else:
            all_groups[which].act(member, stage)

    def take_until(which):
        at = 0
        while at < len(actions):
            if actions[at][1] == which and actions[at][3] <= 1:
                take_action(at)
            else:
                at += 1

    for at, (_, work, _) in zip(starts_at, works):
        while actions and actions[0][0] <= at + 0.01:
            take_action()
        work()
    while actions:
        take_action()
    to_wt(lambda w: gain_sum.at[own_rows(w)], gain_out.at[wt])
    for wait in delivered:
        wait()
    for wait in moved:
        wait()
    for k in range(parts):
        for slot in range(n_wide):
            wout_arrive(k, slot * WIDE, WIDE, slot)
    for move in rim_moves:

        @pl.when(seq > 0)
        def _():
            move.wait_send()

    copies.finish()


def finish_all(
    gated_t, d_gate, d_scan_in, d_raw, inputs, conv, grads, normed_t, w_in, wout, feat, gated,
    w_out, x, g, gain, d_bc, dt_low, w_x, w_dt, w_conv, b_conv, d_rate, a_neg, sums,
):
    n_seq, n_wt = lax.axis_size("seq"), lax.axis_size("wt")
    seq_bits, wt_bits = n_seq.bit_length() - 1, n_wt.bit_length() - 1
    n_chan, all_rows = gated_t.shape
    n_feat, n_rows = normed_t.shape[0], all_rows // n_wt
    n_state, taps = a_neg.shape[0], w_conv.shape[0]
    cols = 512
    parts = parts_of(n_chan, n_seq)
    part_chan = n_chan // parts
    chan_rows, feat_rows, wout_rows = n_chan // n_seq, n_feat // n_seq, part_chan // n_seq
    size = (all_rows + n_rows) // 2
    small_cols, n_wide = 3 * LANE, n_feat // WIDE
    square = ((all_rows, n_chan), BF16)
    blocks = (2,) * seq_bits
    done_type = feat_type(n_feat, n_seq, n_wt)
    plan = feat_plan(n_chan, parts)
    scratch = [
        ((part_chan, all_rows), BF16), square, ((all_rows, cols), BF16), square,
        (normed_t.shape, BF16), ((2, n_wt, n_rows, cols), BF16), ((2, 256, 2 * n_chan), BF16),
        ((n_wt, conv.shape[1], cols), F32), ((2, n_wt, conv.shape[1], cols), F32),
        ((2 * size, LANE), F32), ((size, LANE), F32), ((wt_bits - 1, size, LANE), BF16),
        ((wt_bits - 1, size, LANE), BF16), ((2 * size, LANE), F32), square if parts > 1 else ((16, LANE), BF16), ((all_rows, LANE), BF16), ((all_rows, LANE), BF16),
        ((small_cols, n_chan), F32), ((16, cols), F32), ((2, 2, 16, cols), BF16),
        ((feat_rows, 2 * n_chan), done_type), ((parts, wout_rows, n_feat), BF16),
        ((chan_rows, small_cols), BF16), ((feat_rows, 2 * n_chan), BF16), ((feat_rows, LANE), F32),
        (blocks + (chan_rows, small_cols), BF16),
    ]
    scratch = [pltpu.VMEM(*item) for item in scratch]
    scratch += [pltpu.SemaphoreType.DMA((2, parts, n_wide))]
    scratch += [pltpu.SemaphoreType.DMA((180,))] * 2
    scratch += [pltpu.VMEM(blocks + (wout_rows, WIDE), BF16)] * (n_wide if parts > 1 else 1)
    scratch += [
        pltpu.VMEM(blocks + (feat_rows, width), BF16) for _, width, _ in plan[: 5 - parts % 2 * 2]
    ]
    scratch += [pltpu.VMEM((2,) * wt_bits + (n_rows, cols), BF16)] * 2
    for low in wout_lows(n_wide, True):
        scratch += seq_landings(seq_bits, wout_rows, [WIDE], low)
    for _, width, low in plan:
        scratch += seq_landings(seq_bits, feat_rows, [width], low)
    scratch += seq_landings(seq_bits, chan_rows, [small_cols])
    scratch += landings(wt_bits, n_rows, (cols,) * (2 * n_feat // cols))
    hbm = pl.BlockSpec(memory_space=pl.ANY)
    vmem = pl.BlockSpec(memory_space=pltpu.VMEM)
    return pl.pallas_call(
        functools.partial(finish_kernel, n_seq, n_wt, n_state),
        in_specs=[hbm] * 15 + [vmem] * 10,
        out_specs=[hbm, hbm, hbm, vmem, vmem, hbm],
        out_shape=[
            jax.ShapeDtypeStruct((feat_rows // n_wt, 2 * n_chan * n_wt), done_type),
            jax.ShapeDtypeStruct((parts, wout_rows, n_feat), BF16),
            jax.ShapeDtypeStruct((chan_rows, small_cols), BF16),
            jax.ShapeDtypeStruct((n_rows, n_feat), F32),
            jax.ShapeDtypeStruct((n_rows, n_feat), F32),
            jax.ShapeDtypeStruct((n_wt, feat_rows // n_wt, LANE), F32),
        ],
        scratch_shapes=scratch,
        compiler_params=pltpu.CompilerParams(
            collective_id=1, has_side_effects=True, vmem_limit_bytes=255 * 2**18
        ),
        name="finish_all",
    )(
        gated_t, d_gate, d_scan_in, d_raw, inputs, conv, grads, normed_t, w_in, wout, feat, gated,
        w_out.reshape(grads.shape), x, g, gain, d_bc, dt_low, w_x, w_dt, w_conv, b_conv, d_rate, a_neg, sums,
    )


class Gather:
    def __init__(self, copies, slots, seq, wt, bits):
        self.copies, self.slots, self.seq, self.wt, self.bits = copies, slots, seq, wt, bits
        self.arriving = {}

    def send(self, mask, src):
        slot = self.slots.at[turn(self.wt, mask, self.bits)]
        low = self.bits if mask == 0 else (mask & -mask).bit_length() - 1
        for bit in reversed(range(low)):
            peer = (self.seq, flip(self.wt, bit))
            self.arriving[mask | 1 << bit] = self.copies.remote(src, slot, peer)

    def arrive(self, mask):
        self.arriving[mask].wait_recv()
        self.send(mask, self.slots.at[turn(self.wt, mask, self.bits)])


def start_kernel(
    n_seq, n_wt,
    hidden_ref, grad_ref, gain_ref, starts_ref, win_ref, wout_ref, wconv_ref, bconv_ref, wx_ref,
    wdt_ref, spread_ref, bias_ref, rate_ref,
    normed_out, win_out, conv_out, gate_out, u_out, raw_out, low_out, bcs_out, dgated_out,
    dscan_out, grad_out, gain_out, end_out, lead_out, total_ref, head_ref, tail_ref,
    rows_s, grads_s, gain_s, starts_s, normed_s, win_s, wout_s, conv_s, gate_s, u_s, raw_s, low_s,
    bcs_s, dgated_s, dscan_s, mix_s, fin_s, first_s, half_s, land_s, rim_s, rim_in, normed_t,
    bcb, dec_in, drive_in, g_in, end_s, lead_s, run_s, span_s, own_span, gap_s, edge_send, edge_land, span_send,
    span_land,
    send_sems, recv_sems, join_send, join_recv,
):
    seq, wt = lax.axis_index("seq"), lax.axis_index("wt")
    bits = n_wt.bit_length() - 1
    n_rows, n_feat = hidden_ref.shape
    n_chan, shard = wout_ref.shape[0], win_ref.shape[0]
    taps = wconv_ref.shape[0]
    rim = (taps - 1) * SUB
    all_rows = n_wt * n_rows
    near_y, near_z = (flip(seq, 0), wt), (flip(seq, 1), wt)
    wt_peers = [(seq, turn(wt, mask, bits)) for mask in range(1, n_wt)]
    ahead, behind = (lax.rem(seq + 1, n_seq), wt), (lax.rem(seq + n_seq - 1, n_seq), wt)

    barrier = pltpu.get_barrier_semaphore()
    partners = wt_peers + [near_y, near_z, ahead, behind]
    for r in range(1, n_seq.bit_length() - 1):
        partners += [(lax.rem(seq + d, n_seq), wt) for d in (2**r, n_seq - 2**r)]
    for partner in partners:
        pl.semaphore_signal(barrier, inc=1, device_id=partner, device_id_type=MESH)
    pl.semaphore_wait(barrier, len(partners))

    copies = Copies(send_sems, recv_sems)
    part = shard // 4
    quarter = seq % 4

    def win_part(owner, which, at, rows, half):
        start = pl.multiple_of(owner * shard + which * part + at, 16)
        return win_s.at[pl.ds(start, rows), half * n_chan : (half + 1) * n_chan]

    def send_far(half):
        found = {}
        rows = pl.ds(pl.multiple_of(quarter * part, 16), part)
        for mask in range(2, n_wt):
            to = turn(wt, mask, bits)
            columns = pl.ds(pl.multiple_of((half * n_wt + to) * n_chan, LANE), n_chan)
            found[mask] = copies.remote(
                win_ref.at[rows, columns], win_part(wt, quarter, 0, part, half), (seq, to)
            )
        return found

    def send_near(half):
        to = flip(wt, 0)
        place = win_s.at[
            pl.ds(pl.multiple_of(wt * shard, 16), shard), half * n_chan : (half + 1) * n_chan
        ]
        columns = pl.ds(pl.multiple_of((half * n_wt + to) * n_chan, LANE), n_chan)
        own = pl.ds(pl.multiple_of((half * n_wt + wt) * n_chan, LANE), n_chan)
        return (
            copies.remote(win_ref.at[:, columns], place, (seq, to)),
            copies.local(win_ref.at[:, own], place),
        )

    def share_first(half, found):
        passed = {}
        for mask, copy in found.items():
            copy.wait_recv()
            block = win_part(turn(wt, mask, bits), quarter, 0, part, half)
            passed[mask] = (
                copies.remote(block, block, near_y), copies.remote(block, block, near_z)
            )
        return passed

    def share_second(half, passed):
        last = []
        for mask, (by_y, by_z) in passed.items():
            owner = turn(wt, mask, bits)
            by_z.wait_recv()
            block = win_part(owner, flip(quarter, 1), 0, part // 2, half)
            last.append(copies.remote(block, block, near_y))
            by_y.wait_recv()
            block = win_part(owner, flip(quarter, 0), part // 2, part // 2, half)
            last.append(copies.remote(block, block, near_z))
        return last

    def normalise(mask):
        at = turn(wt, mask, bits)
        gain = jnp.concatenate(
            [gain_s[k].astype(F32)[0:1] for k in range(n_wt)], axis=1
        )

        def body(i, carry):
            rows = pl.ds(pl.multiple_of(i * 16, 16), 16)
            x = rows_s[at, rows, :].astype(F32)
            inv = lax.rsqrt(jnp.mean(x * x, axis=1, keepdims=True) + EPS)
            place = pl.ds(pl.multiple_of(at * n_rows + i * 16, 16), 16)
            normed_s[place, :] = (x * inv * gain).astype(BF16)
            return carry

        lax.fori_loop(0, n_rows // 16, body, 0)

    far = send_far(0)
    rows = Gather(copies, rows_s, seq, wt, bits)
    gains = Gather(copies, gain_s, seq, wt, bits)
    starts = Gather(copies, starts_s, seq, wt, bits)
    own_copies = [
        copies.local(gain_ref, gain_s.at[wt]),
        copies.local(starts_ref, starts_s.at[wt]),
        copies.local(hidden_ref, rows_s.at[wt]),
    ]
    gains.send(0, gain_ref)
    rows.send(0, hidden_ref)
    near = send_near(0)
    starts.send(0, starts_ref)
    wout_copy = copies.local(wout_ref, wout_s)
    for mask in range(n_wt - 1, 0, -1):
        if mask in gains.arriving:
            gains.arrive(mask)
    for mask in range(1, n_wt):
        if mask not in (1, 2):
            gains.arriving[mask].wait_recv()
    for copy in own_copies:
        copy.wait()
    normalise(0)
    rows.arrive(1)
    normalise(1)
    passed = share_first(0, far)
    far = send_far(1)
    last = share_second(0, passed)
    near_gate = send_near(1)
    for mask in range(2, n_wt):
        rows.arrive(mask)
        if mask == 2:
            half_rows = n_rows // 2
            tops = Gather(copies, grads_s.at[:, :half_rows], seq, wt, bits)
            ends = Gather(copies, grads_s.at[:, half_rows:], seq, wt, bits)
            grad_copy = copies.local(grad_ref, grads_s.at[wt])
            tops.send(0, grad_ref.at[:half_rows])
        normalise(mask)
    results = [copies.local(gain_s, gain_out)]
    near[0].wait_recv()
    near[1].wait()
    for copy in last:
        copy.wait_recv()

    n_block, m_block = 256, 512

    def tiles(body):
        m_count = all_rows // m_block

        def one(i, carry):
            m = pl.multiple_of((i % m_count) * m_block, m_block)
            n = pl.multiple_of((i // m_count) * n_block, n_block)
            body(m, n)
            return carry

        lax.fori_loop(0, m_count * (n_chan // n_block), one, 0)

    def conv_tile(m, n):
        value = jnp.dot(
            normed_s[pl.ds(m, m_block), :], win_s[:, pl.ds(n, n_block)], preferred_element_type=F32
        )
        value = value.astype(BF16).astype(F32)
        for k in range(m_block // n_rows):
            conv_s[m // n_rows + k, rim:, pl.ds(n, n_block)] = value[k * n_rows : (k + 1) * n_rows]

    tiles(conv_tile)

    rim_s[...] = jnp.zeros_like(rim_s)
    for b in range(n_wt):
        for k in range(taps - 1):
            at = rim + n_rows - (taps - 1 - k) * SUB
            rim_s[b * (taps - 1) + k, :] = conv_s[b, at + SUB - 1, :]
    rim_s2 = rim_s[...].astype(BF16)
    rim_in[0] = rim_s2

    @pl.when(seq == 0)
    def _():
        rim_in[1] = jnp.zeros_like(rim_s2)

    k_rim, copies.count = copies.count, copies.count + 1
    rim_copy = pltpu.make_async_remote_copy(
        src_ref=rim_in.at[0], dst_ref=rim_in.at[1], send_sem=send_sems.at[k_rim],
        recv_sem=recv_sems.at[k_rim], device_id=ahead, device_id_type=MESH,
    )

    @pl.when(seq < n_seq - 1)
    def _():
        rim_copy.start()

    passed = share_first(1, far)

    def convolve(b, j):
        rows = pl.ds(pl.multiple_of(j * 16, 16), 16)
        total = bconv_ref[...] + conv_s[b, rows, :] * wconv_ref[0:1, :]
        for k in range(1, taps):
            at = pl.ds(pl.multiple_of(j * 16 + k * SUB, SUB), 16)
            total = total + conv_s[b, at, :] * wconv_ref[k : k + 1, :]
        place = pl.ds(pl.multiple_of(b * n_rows + j * 16, 16), 16)
        u_s[place, :] = (total * jax.nn.sigmoid(total)).astype(BF16)

    head = -(-(taps - 1) // 2)
    pairs = n_rows // 16

    def convolve_tail(i, carry):
        convolve(i // (pairs - head), head + i % (pairs - head))
        return carry

    lax.fori_loop(0, n_wt * (pairs - head), convolve_tail, 0)

    @pl.when(seq > 0)
    def _():
        rim_copy.wait_recv()

    rim_rows = rim_in[1].astype(F32)
    first = lax.broadcasted_iota(jnp.int32, (SUB, n_chan), 0) == 0
    for b in range(n_wt):
        for k in range(taps - 1):
            at = rim + n_rows - (taps - 1 - k) * SUB
            moved = pltpu.roll(conv_s[b, at : at + SUB, :], 1, 0)
            row = rim_rows[b * (taps - 1) + k : b * (taps - 1) + k + 1, :]
            conv_s[b, k * SUB : (k + 1) * SUB, :] = jnp.where(first, row, moved)
    lax.fori_loop(0, n_wt * head, lambda i, c: (convolve(i // head, i % head), c)[1], 0)
    results += [copies.local(conv_s, conv_out), copies.local(u_s, u_out)]

    packed = []
    for b in range(n_wt):
        block = u_s[b * n_rows : (b + 1) * n_rows, :]
        mix_s[b * n_rows : (b + 1) * n_rows, :] = jnp.dot(
            block, wx_ref[:, :LANE], preferred_element_type=F32
        )
        packed.append(jnp.dot(block, wx_ref[:, LANE:], preferred_element_type=F32))
    mix_s[all_rows:, :] = jnp.concatenate(packed, axis=1)
    mixed = WtSum(copies, mix_s, first_s, half_s, land_s, fin_s, seq, wt, bits)
    mixed.begin()
    last = share_second(1, passed)
    starts.arrive(2)

    def transpose(b):
        at = slice(b * n_rows, (b + 1) * n_rows)
        normed_t[:, at] = normed_s[at, :].T

    transpose(0)
    for bit in range(1, bits):
        mixed.middle(bit)
    ends.send(0, grad_ref.at[half_rows:])
    for b in range(1, n_wt):
        transpose(b)
    results.append(copies.local(normed_t, normed_out))
    mixed.end()

    low_s[...] = fin_s[:all_rows, :].astype(BF16)
    starts.arriving[1].wait_recv()
    starts.arriving[3].wait_recv()
    lane = lax.broadcasted_iota(jnp.int32, (n_rows, LANE), 1)
    width = LANE // n_wt
    for b in range(n_wt):
        moved = fin_s[all_rows:, :]
        if b:
            moved = pltpu.roll(moved, LANE - b * width, 1)
        bcs_s[b * n_rows : (b + 1) * n_rows, :] = (
            jnp.where(lane < width, moved, 0.0).astype(BF16) + starts_s[b]
        )

    def raw_tile(m, n):
        value = lax.dot_general(
            low_s[pl.ds(m, m_block), :], wdt_ref[pl.ds(n, n_block), :], (((1,), (1,)), ((), ())),
            preferred_element_type=F32,
        )
        raw_s[pl.ds(m, m_block), pl.ds(n, n_block)] = value.astype(BF16)

    tiles(raw_tile)
    results += [
        copies.local(low_s, low_out), copies.local(bcs_s, bcs_out), copies.local(raw_s, raw_out)
    ]

    near_gate[0].wait_recv()
    near_gate[1].wait()
    for copy in last:
        copy.wait_recv()
    results.append(copies.local(win_s, win_out))

    def gate_tile(m, n):
        value = jnp.dot(
            normed_s[pl.ds(m, m_block), :], win_s[:, pl.ds(n_chan + n, n_block)],
            preferred_element_type=F32,
        )
        gate_s[pl.ds(m, m_block), pl.ds(n, n_block)] = value.astype(BF16)

    tiles(gate_tile)
    results.append(copies.local(gate_s, gate_out))
    n_state = rate_ref.shape[0]
    width = dec_in.shape[1]
    steps = n_rows // SUB
    start_at = 2 * n_state * LANE

    def stream_of(i):
        base = wt + (i // 2) * (1 - 2 * bit_of(wt, 1)) * 2
        return base + (i % 2) * (1 - 2 * bit_of(wt, 0))

    def back(b):
        at = pl.ds(pl.multiple_of(b * n_rows, n_rows), n_rows)

        def one(i, carry):
            n = pl.ds(pl.multiple_of(i * n_block, n_block), n_block)
            d_gated = lax.dot_general(
                grads_s[b], wout_s[n, :], (((1,), (1,)), ((), ())), preferred_element_type=F32
            )
            gate = gate_s[at, n].astype(F32)
            dgated_s[at, n] = d_gated
            dscan_s[at, n] = (d_gated * gate * jax.nn.sigmoid(gate)).astype(BF16)
            return carry

        lax.fori_loop(0, n_chan // n_block, one, 0)

    def chunk_ends(b, part):
        columns = pl.ds(pl.multiple_of(part * width, width), width)

        def prepare(j, total):
            rows = pl.ds(pl.multiple_of(j * 16, 16), 16)
            at = pl.ds(pl.multiple_of(b * n_rows + j * 16, 16), 16)
            delta = softplus(raw_s[at, columns].astype(F32) + bias_ref[:, columns])
            held = jnp.where(wide(bcb[rows, start_at : start_at + LANE], width) > 0.5, RESET, delta)
            dec_in[rows, :] = held
            drive_in[rows, :] = delta * u_s[at, columns].astype(F32)
            g_in[rows, :] = dscan_s[at, columns].astype(F32)
            return total + held[:SUB] + held[SUB:]

        total = lax.fori_loop(0, steps // 2, prepare, jnp.zeros((SUB, width), F32))
        total_ref[b, :, columns] = total
        span = jnp.sum(total, 0, keepdims=True)
        span_s[b, :, columns] = span
        for first_n in range(0, n_state, 2):
            states = range(first_n, first_n + 2)

            def step(j, carry):
                rows = pl.ds(pl.multiple_of(j * SUB, SUB), SUB)
                held, drive, g = dec_in[rows, :], drive_in[rows, :], g_in[rows, :]
                running, products, passed = [], [], []
                for n, h, so_far, p in zip(states, *carry):
                    b_row = wide(bcb[rows, n * LANE : (n + 1) * LANE], width)
                    c_row = wide(bcb[rows, (n_state + n) * LANE : (n_state + n + 1) * LANE], width)
                    decay = jnp.exp2(held * rate_ref[n : n + 1, columns])
                    so_far = so_far * decay
                    running.append(decay * h + drive * b_row)
                    products.append(so_far)
                    passed.append(p + so_far * (g * c_row))
                return tuple(running), tuple(products), tuple(passed)

            zero = tuple(jnp.zeros((SUB, width), F32) for _ in states)
            one = tuple(jnp.ones((SUB, width), F32) for _ in states)
            carry = lax.fori_loop(0, steps, step, (zero, one, zero), unroll=8)
            for n, h, decay, p in zip(states, *carry):
                end = chunk_prefix(decay, h, False)[1]
                lead = chunk_prefix(decay, p, True)[1]
                end_s[b, n, :, columns], lead_s[b, n, :, columns] = end, lead
                run_s[0, b, n : n + 1, columns] = end[SUB - 1 :]
                run_s[1, b, n : n + 1, columns] = lead[:1]

    def ends_of(i, carry):
        b = stream_of(i)
        back(b)
        bcb[...] = jnp.dot(
            bcs_s[pl.ds(pl.multiple_of(b * n_rows, n_rows), n_rows), :], spread_ref[...],
            preferred_element_type=F32,
        )
        lax.fori_loop(0, n_chan // width, lambda part, c: (chunk_ends(b, part), c)[1], 0)
        return carry

    grad_copy.wait()
    tops.arrive(1)
    ends.arrive(1)
    wout_copy.wait()
    lax.fori_loop(0, 2, ends_of, 0)
    for mask in range(2, n_wt):
        tops.arrive(mask)
        ends.arrive(mask)
        ends_of(mask, 0)
    results.append(copies.local(grads_s, grad_out))
    results += [copies.local(dgated_s, dgated_out), copies.local(dscan_s, dscan_out)]
    results += [copies.local(end_s, end_out), copies.local(lead_s, lead_out)]
    join_rounds(
        n_seq, n_wt, seq, wt, rate_ref[...], head_ref, tail_ref, run_s, span_s, own_span, gap_s,
        edge_send, edge_land, span_send, span_land, join_send, join_recv,
    )
    for copy in results:
        copy.wait()

    @pl.when(seq < n_seq - 1)
    def _():
        rim_copy.wait_send()

    copies.finish()


def start_all(
    hidden, grad, gain, starts, w_in, w_out, w_conv, b_conv, w_x, w_dt, bias, rate_rows
):
    n_seq, n_wt = lax.axis_size("seq"), lax.axis_size("wt")
    n_rows, n_feat = hidden.shape
    n_chan, taps = w_out.shape[0], w_conv.shape[0]
    rows, rim = n_wt * n_rows, (taps - 1) * SUB
    shapes = [
        ((n_feat, rows), BF16), ((n_feat, 2 * n_chan), BF16), ((n_wt, rim + n_rows, n_chan), F32),
        ((rows, n_chan), BF16), ((rows, n_chan), BF16), ((rows, n_chan), BF16), ((rows, LANE), BF16),
        ((rows, LANE), BF16), ((rows, n_chan), F32), ((rows, n_chan), BF16),
        ((n_wt, n_rows, n_feat), BF16), ((n_wt,) + gain.shape, BF16),
        ((n_wt, rate_rows.shape[0], SUB, n_chan), F32),
        ((n_wt, rate_rows.shape[0], SUB, n_chan), F32), ((n_wt, SUB, n_chan), F32),
        ((n_wt,) + rate_rows.shape, F32), ((n_wt,) + rate_rows.shape, F32),
    ]
    normed, win, conv, gate, u, raw, low, bcs, dgated, dscan, grads, gains = shapes[:12]
    ends = shapes[12]
    n_state, rounds = rate_rows.shape[0], n_seq.bit_length() - 1
    count = (2 * n_state + 1) * LANE
    width = min(512, n_chan)
    spans, edges = (2 * n_wt, n_chan), (n_wt, n_state, n_chan)
    size = (rows + n_rows) // 2
    bits = n_wt.bit_length() - 1
    scratch = [
        grads, grads, gains, ((n_wt, n_rows, LANE), BF16), ((rows, n_feat), BF16), win, (w_out.shape, BF16), conv,
        gate, u, raw, low, bcs, dgated, dscan, ((2 * size, LANE), F32), ((2 * size, LANE), F32),
        ((size, LANE), F32), ((bits, size, LANE), BF16), ((bits, size, LANE), BF16),
        ((16, n_chan), F32),
        ((2, 16, n_chan), BF16), normed,
        ((n_rows, count), F32), ((n_rows, width), F32), ((n_rows, width), F32), ((n_rows, width), F32),
        ends, ends, ((2,) + edges, F32), ((n_wt, 1, n_chan), F32), (spans, F32), (spans, F32),
        ((2, 2) + edges, BF16),
        ((rounds, 2) + edges, BF16), ((rounds,) + spans, F32), ((rounds, 2) + spans, F32),
    ]
    hbm = pl.BlockSpec(memory_space=pl.ANY)
    vmem = pl.BlockSpec(memory_space=pltpu.VMEM)
    return pl.pallas_call(
        functools.partial(start_kernel, n_seq, n_wt),
        in_specs=[hbm] * 6 + [vmem] * 7,
        out_specs=[hbm] * (len(shapes) - 3) + [vmem] * 3,
        out_shape=[jax.ShapeDtypeStruct(*item) for item in shapes],
        scratch_shapes=[pltpu.VMEM(*item) for item in scratch]
        + [pltpu.SemaphoreType.DMA((90,))] * 2
        + [pltpu.SemaphoreType.DMA((rounds, 2, 2))] * 2,
        compiler_params=pltpu.CompilerParams(
            collective_id=2, has_side_effects=True, vmem_limit_bytes=4090 * 2**14
        ),
        name="start_all",
    )(
        hidden, grad, gain, starts, w_in, w_out, w_conv, b_conv, w_x, w_dt, spread_matrix(n_state),
        bias, rate_rows,
    )


def dot(left, right, left_dim=1, right_dim=0):
    return lax.dot_general(
        left, right, (((left_dim,), (right_dim,)), ((), ())), preferred_element_type=F32
    )


def to_chunks(rows):
    n_rows, width = rows.shape
    return rows.reshape(SUB, n_rows // SUB, width).swapaxes(0, 1).reshape(n_rows, width)


def per_device(
    hidden_in, doc_starts, norm_gain, in_weight, conv_weight, conv_bias, x_weight,
    dt_weight, dt_bias, a_log, d_skip, out_weight, grad_output,
):
    n_wt, n_seq = lax.axis_size("wt"), lax.axis_size("seq")
    seq_at = lax.axis_index("seq")
    n_chan = out_weight.shape[0]
    taps = conv_weight.shape[1]
    dt_rank = dt_weight.shape[1]
    n_state = a_log.shape[1]
    rows_own = hidden_in[0]
    n_rows, n_feat = rows_own.shape
    steps = n_rows // SUB

    w_conv = conv_weight.astype(F32)
    starts = jnp.pad(
        to_chunks(doc_starts[0].astype(BF16)[:, None]), ((0, 0), (2 * n_state, LANE - 2 * n_state - 1))
    )
    rates = (-LOG2E * jnp.exp(a_log.astype(F32))).T
    bias = dt_bias.astype(F32)[None]
    skip = d_skip.astype(F32)[None]
    (
        normed_t, w_in, padded, gate_in, inputs, dt_raw, dt_low, bcs, d_gated, d_scanned, grad_all, gains,
        ends, leads, totals, head, tail,
    ) = start_all(
        to_chunks(rows_own), to_chunks(grad_output[0]),
        jnp.broadcast_to(norm_gain[None], (16, norm_gain.shape[0])), starts, in_weight, out_weight,
        w_conv.T, conv_bias.astype(F32)[None], x_weight, dt_weight, bias,
        rates,
    )
    gain = gains[:, 0].reshape(n_feat).astype(F32)

    gated, gated_t, d_gate, d_scan_in, d_raw, d_bc, d_rate, sums, wout, feat = scan_all(
        bcs, dt_raw, inputs, d_scanned, gate_in, d_gated, bias, skip, rates,
        ends, leads, totals, head, tail, grad_all.reshape(n_wt * n_rows, n_feat), normed_t,
    )


    feat_grads, d_wout, small, input_grad, output, gain_parts = finish_all(
        gated_t, d_gate, d_scan_in, d_raw, inputs, padded, grad_all, normed_t, w_in, wout, feat,
        gated, out_weight, rows_own, grad_output[0], gains, d_bc, dt_low, x_weight, dt_weight, w_conv.T,
        conv_bias.astype(F32)[None], d_rate, rates, sums,
    )
    d_wout = d_wout.reshape(-1, n_feat).astype(F32)
    small = small.astype(F32)
    widths = (dt_rank, dt_rank, 2 * n_state, n_state, taps, 1, 1, 1)
    cuts, at = [], 0
    for piece in widths:
        cuts.append(small[:, at : at + piece])
        at += piece
    d_wx, d_wdt, d_wbc, d_loga, d_wconv, d_bconv, d_bdt, d_skips = cuts
    own = n_feat // (n_seq * n_wt)
    own_at = own * (n_wt * seq_at + lax.axis_index("wt"))
    gain_grad = jnp.sum(gain_parts, (0, 2)) / lax.dynamic_slice_in_dim(gain, own_at, own, 0)
    return (
        output[None],
        input_grad[None],
        gain_grad,
        feat_grads.astype(F32),
        d_wconv,
        d_bconv[:, 0],
        jnp.concatenate([d_wx, d_wbc], 1),
        d_wdt,
        d_bdt[:, 0],
        d_loga,
        d_skips[:, 0],
        d_wout,
    )


def solution(mesh):
    placed = (
        P("wt", "seq", None),
        P("wt", "seq"),
        P("wt"),
        P("wt", None),
        P("wt", None),
        P("wt"),
        P("wt", None),
        P("wt", None),
        P("wt"),
        P("wt", None),
        P("wt"),
        P("wt", None),
        P("wt", "seq", None),
    )
    every = ("seq", "wt")
    return jax.shard_map(
        per_device,
        mesh=mesh,
        in_specs=placed,
        out_specs=(
            P("wt", "seq", None),
            P("wt", "seq", None),
            P(every),
            P(every, None),
            P(every, None),
            P(every),
            P(every, None),
            P(every, None),
            P(every),
            P(every, None),
            P(every),
            P(every, None),
        ),
        check_vma=False,
    )
```

```python
import functools
import math

import jax
import jax.numpy as jnp
import ml_dtypes
import numpy as np
from jax import lax
from jax.experimental import pallas as pl
from jax.experimental.pallas import tpu as pltpu
from jax.sharding import PartitionSpec as P

EPS = 1e-05
LOG2E = 1.4426950408889634
RESET = 1e30
SUB = 8
LANE = 128
NBLK = 4
F32 = jnp.float32
BF16 = jnp.bfloat16
MESH = pl.DeviceIdType.MESH


def softplus(v):
    return jnp.maximum(v, 0.0) + jnp.log1p(jnp.exp(-jnp.abs(v)))


def wide(tile, width):
    return jnp.concatenate([tile] * (width // LANE), axis=1)


def fold(values):
    total = values[:, :LANE]
    for k in range(1, values.shape[1] // LANE):
        total = total + values[:, k * LANE : (k + 1) * LANE]
    return total


def chunk_prefix(decay, drive, reverse):
    chunk = lax.broadcasted_iota(jnp.int32, drive.shape, 0)
    for shift in (1, 2, 4):
        if reverse:
            other_decay = pltpu.roll(decay, SUB - shift, 0)
            other_drive = pltpu.roll(drive, SUB - shift, 0)
            inside = chunk < SUB - shift
        else:
            other_decay = pltpu.roll(decay, shift, 0)
            other_drive = pltpu.roll(drive, shift, 0)
            inside = chunk >= shift
        drive = jnp.where(inside, decay * other_drive + drive, drive)
        decay = jnp.where(inside, decay * other_decay, decay)
    return decay, drive


def spread_rows(bcs_ref, spread_ref, bcb):
    bcb[...] = jnp.dot(bcs_ref[...], spread_ref[...], preferred_element_type=F32)


def turn(index, mask, bits):
    for bit in range(bits):
        if mask >> bit & 1:
            index = flip(index, bit)
    return index


class Copies:
    def __init__(self, send_sems, recv_sems):
        self.send_sems, self.recv_sems = send_sems, recv_sems
        self.count, self.open = 0, []

    def remote(self, src, dst, peer):
        k, self.count = self.count, self.count + 1
        copy = pltpu.make_async_remote_copy(
            src_ref=src, dst_ref=dst, send_sem=self.send_sems.at[k],
            recv_sem=self.recv_sems.at[k], device_id=peer, device_id_type=MESH,
        )
        copy.start()
        self.open.append(copy)
        return copy

    def later(self, src_of, dst, peer):
        k, self.count = self.count, self.count + 1

        def make():
            return pltpu.make_async_remote_copy(
                src_ref=src_of(), dst_ref=dst, send_sem=self.send_sems.at[k],
                recv_sem=self.recv_sems.at[k], device_id=peer, device_id_type=MESH,
            )

        self.open.append(make)
        return make

    def local(self, src, dst):
        k, self.count = self.count, self.count + 1
        copy = pltpu.make_async_copy(src, dst, self.send_sems.at[k])
        copy.start()
        return copy

    def drop(self, copy):
        self.open = [other for other in self.open if other is not copy]

    def finish(self):
        for copy in self.open:
            (copy() if callable(copy) else copy).wait_send()


class WtSum:
    def __init__(self, copies, mix, first, half, land, total, seq, wt, bits):
        self.copies, self.mix, self.first, self.total = copies, mix, first, total
        self.half, self.land = half, land
        self.seq, self.wt, self.bits = seq, wt, bits
        size = mix.shape[0] // 2
        mine = bit_of(wt, 0)
        self.kept = pl.ds(pl.multiple_of(mine * size, 16), size)
        self.given = pl.ds(pl.multiple_of((1 - mine) * size, 16), size)

    def begin(self):
        peer = (self.seq, flip(self.wt, 0))
        self.copy = self.copies.remote(self.mix.at[self.given], self.first, peer)

    def so_far(self, bit):
        self.copy.wait_recv()
        if bit == 1:
            return self.mix[self.kept, :] + self.first[...]
        return self.half[bit - 2].astype(F32) + self.land[bit - 2].astype(F32)

    def middle(self, bit):
        self.half[bit - 1] = self.so_far(bit).astype(BF16)
        peer = (self.seq, flip(self.wt, bit))
        self.copy = self.copies.remote(self.half.at[bit - 1], self.land.at[bit - 1], peer)

    def end(self):
        self.end_send()
        self.copy.wait_recv()

    def end_send(self):
        self.total[self.kept, :] = self.so_far(self.bits)
        peer = (self.seq, flip(self.wt, 0))
        part = self.total.at[self.kept]
        self.copy = self.copies.remote(part, part, peer)


def flip(index, bit):
    return index + (1 - 2 * ((index // 2**bit) % 2)) * 2**bit


def bit_of(index, bit):
    return (index // 2**bit) % 2


def pick(left, bit, value):
    return tuple(value if b == bit else slice(None) for b in left)


def over_blocks(count, rows, body):
    tile = math.gcd(rows, 32)
    per_block = rows // tile

    def one(i, carry):
        block, row = i // per_block, (i % per_block) * tile
        index = tuple((block // 2 ** (count - 1 - k)) % 2 for k in range(count))
        body(index, pl.ds(pl.multiple_of(row, tile), tile))
        return carry

    lax.fori_loop(0, 2**count * per_block, one, 0)


class Halving:
    def __init__(self, copies, source, dims, order, columns, landing, final, me, peer):
        self.copies, self.source, self.dims, self.order = copies, source, dims, order
        self.columns, self.landing, self.final = columns, landing, final
        self.mine = {bit: bit_of(me, bit) for bit in order}
        self.theirs = {bit: 1 - value for bit, value in self.mine.items()}
        self.moves = [
            copies.later(functools.partial(self.block, stage), landing[stage], peer(bit))
            for stage, bit in enumerate(order)
        ]

    def left(self, stage):
        return [b for b in self.dims if b not in self.order[:stage]]

    def block(self, stage):
        bit = self.order[stage]
        other = pick(self.left(stage), bit, self.theirs[bit])
        if stage == 0:
            return self.source.at[other + (slice(None), self.columns)]
        return self.landing[stage - 1].at[other]

    def send(self, stage):
        self.moves[stage]().start()

    def add(self, stage):
        self.moves[stage]().wait_recv()
        mine = self.mine[self.order[stage]]
        left, after = self.left(stage), self.left(stage + 1)
        landed = self.landing[stage]

        def body(index, rows):
            at = iter(index)
            full = tuple(mine if b == self.order[stage] else next(at) for b in left)
            if stage == 0:
                kept = self.source[full + (rows, self.columns)]
            else:
                kept = self.landing[stage - 1][full + (rows, slice(None))]
            total = kept.astype(F32) + landed[index + (rows, slice(None))].astype(F32)
            if after:
                landed[index + (rows, slice(None))] = total.astype(BF16)
            else:
                self.final(rows, total)

        over_blocks(len(after), landed.shape[-2], body)


class Group:
    def __init__(self, members, done=None):
        self.members, self.done, self.stage = members, done, 0

    def launch(self):
        for job in self.members:
            job.send(0)

    def act(self, member, stage):
        job = self.members[member]
        if stage:
            job.add(stage - 1)
        if stage < len(job.order):
            job.send(stage)
        else:
            self.stage += 1
            if self.stage == len(self.members) and self.done:
                self.done()

    def advance(self, stage):
        stages = len(self.members[0].order)
        for job in self.members:
            job.add(stage)
            if stage + 1 < stages:
                job.send(stage + 1)
        if stage + 1 == stages and self.done:
            self.done()

    def release(self):
        for job in self.members:
            job.moves[0]().wait_send()
            job.copies.drop(job.moves[0])


def fill(target, at, value):
    rows, lead = target.shape[-2], len(target.shape) - 2
    inner = (value.shape[0] // rows).bit_length() - 1
    index = tuple((at // 2 ** (lead - 1 - k)) % 2 for k in range(lead - inner))
    target[index] = value.reshape((2,) * inner + (rows, value.shape[1])).astype(BF16)


def by_tiles(target, rows, value_of):
    tile = min(512, rows)

    def one(i, carry):
        m = pl.multiple_of(i * tile, tile)
        fill(target, i * (tile // target.shape[-2]), value_of(pl.ds(m, tile)))
        return carry

    lax.fori_loop(0, rows // tile, one, 0)


def seq_orders(width, seq_bits, low=None):
    low = width - LANE if low is None else low
    first = tuple(range(seq_bits))
    orders = ((0, low, first), (low, width - low, (1, 0) + first[2:]))
    return [item for item in orders if item[1]]


def timetable(groups, loads=()):
    rate, delay, turn_time, ahead = 23.3, 4.0, 1.0, 8.0
    jobs, free, clock, found = [], {}, 0.0, []
    for g, (ready, axis, size, members) in enumerate(groups):
        for m, (columns, order) in enumerate(members):
            jobs.append([ready, ready, g, m, 0, columns * size, axis, order])
    for ready, axis, bit, size in loads:
        jobs.append([ready, ready, -1, 0, 0, 2 * size, axis, (bit,)])
    while jobs:
        best = None
        for job in jobs:
            ready, made, g, m, stage, size, axis, order = job
            issue = max(clock, ready)
            if stage < len(order):
                bit = order[stage]
                link = (axis, min(bit, 1))
                issue = max(issue, free.get(link, 0.0) - ahead)
            key = (issue, -stage, made, g, m)
            if best is None or key < best[0]:
                best = (key, job)
        (issue, *_), job = best
        ready, made, g, m, stage, size, axis, order = job
        if g >= 0:
            found.append((issue, g, m, stage))
        clock = issue + (turn_time if stage else 0.1)
        if stage == len(order):
            jobs.remove(job)
            continue
        bit = order[stage]
        link = (axis, min(bit, 1))
        took = size / 2 ** (stage + 1) * rate
        if axis == "wt" and bit == 0:
            took = took / 6
        start = max(clock, free.get(link, 0.0))
        free[link] = end = start + took
        if bit > 1:
            start = max(start, free.get((axis, bit), 0.0))
            free[axis, bit] = end = start + 2 * took
        job[0], job[4] = end + delay, stage + 1
    return found


def seq_group(copies, source, name, take, final, seq, peer, done=None, low=None):
    seq_bits = len(source.shape) - 2
    dims = list(reversed(range(seq_bits)))
    if name == "chan":
        dims = [0] + dims[:-1]
    members = []
    for start, size, order in seq_orders(source.shape[-1], seq_bits, low):
        members.append(
            Halving(
                copies, source, dims, order, slice(start, start + size), take(seq_bits),
                functools.partial(final, start), seq, peer,
            )
        )
    return Group(members, done)


def landings(bits, rows, widths):
    return [
        pltpu.VMEM((2,) * (bits - 1 - stage) + (rows, width), BF16)
        for width in widths
        for stage in range(bits)
    ]


def seq_landings(seq_bits, rows, widths, low=None):
    found = []
    for width in widths:
        sizes = [size for _, size, _ in seq_orders(width, seq_bits, low)]
        found += landings(seq_bits, rows, sizes)
    return found


def wout_lows(n_wide, late):
    return [WIDE // 2 if late else 3 * WIDE // 4] + [7 * WIDE // 8 if late else WIDE // 2] * (n_wide - 1)


def feat_plan(n_chan, parts):
    half = n_chan // 2
    plan = [
        (n_chan + half, half, 3 * half // 4), (0, half, half), (half, half // 2, half // 2),
        (half + half // 2, half // 2, half // 4),
    ]
    return plan if parts > 1 else [(n_chan, half, None)] + plan


def feat_type(n_feat, n_seq, n_wt):
    return BF16 if n_feat // (n_seq * n_wt) % 16 == 0 else F32


def parts_of(n_chan, n_seq):
    return 2 if n_chan // n_seq >= 32 else 1


WIDE = 1024
EARLY = 512


def join_rounds(
    n_seq, n_streams, seq, wt, rate, head_ref, tail_ref, run_s, span_in, span_s, gap_s, send_s,
    land_s, span_send, span_land, send_sems, recv_sems,
):
    head_ref[...] = jnp.zeros_like(head_ref)
    tail_ref[...] = jnp.zeros_like(tail_ref)
    gap_s[...] = jnp.zeros_like(gap_s)
    for k in range(2 * n_streams):
        span_s[k : k + 1, :] = span_in[k % n_streams]
    started = []
    for r in range(n_seq.bit_length() - 1):
        d = 2**r
        if r > 1:
            for inside, copies in started[2 * r - 4 : 2 * r - 2]:

                @pl.when(inside)
                def _():
                    copies[0].wait_send()

        send_s[r % 2] = run_s[...].astype(BF16)
        span_send[r] = span_s[...]
        up = (seq + d < n_seq, lax.rem(seq + d, n_seq))
        down = (seq >= d, lax.rem(seq + n_seq - d, n_seq))
        for way, (inside, other) in enumerate((up, down)):
            copies = [
                pltpu.make_async_remote_copy(
                    src_ref=src, dst_ref=dst, send_sem=send_sems.at[r, way, k],
                    recv_sem=recv_sems.at[r, way, k], device_id=(other, wt), device_id_type=MESH,
                )
                for k, (src, dst) in enumerate(
                    ((send_s.at[r % 2, way], land_s.at[r, way]), (span_send.at[r], span_land.at[r, way]))
                )
            ]

            @pl.when(inside)
            def _():
                for copy in copies:
                    copy.start()

            started.append((inside, copies))
        for way, inside in ((0, down[0]), (1, up[0])):
            copies = started[-2 + way][1]
            out = (head_ref, tail_ref)[way]

            @pl.when(inside)
            def _():
                for copy in copies:
                    copy.wait_recv()
                for b in range(n_streams):
                    k = way * n_streams + b
                    landed = land_s[r, way, b].astype(F32)
                    span = span_land[r, way, k : k + 1, :]
                    gap, own = gap_s[k : k + 1, :], span_s[k : k + 1, :]
                    out[b] = out[b] + jnp.exp2(rate * gap) * landed
                    run_s[way, b] = run_s[way, b] + jnp.exp2(rate * own) * landed
                    gap_s[k : k + 1, :] = gap + span
                    span_s[k : k + 1, :] = own + span

    for at, (inside, copies) in enumerate(started):

        @pl.when(inside)
        def _():
            for copy in copies[at < len(started) - 4 :]:
                copy.wait_send()


def early_sums(n_seq, part, stream, width, grad_ref, normed_t_ref, wout_ref, feat_ref, scratch):
    gated_s, dgate_s, grads, normed_t = scratch[:4]
    feat_parts, scratch = scratch[4:6], scratch[6:]
    seq_bits = n_seq.bit_length() - 1
    count = grads.shape[1] // WIDE
    wout_parts, scratch = scratch[:count], scratch[count:]
    load_sems, send_sems, recv_sems = scratch[:3]
    scratch = scratch[3:]
    take = lambda k: [scratch.pop(0) for _ in range(k)]
    seq, wt = lax.axis_index("seq"), lax.axis_index("wt")
    copies = Copies(send_sems, recv_sems)
    peer = lambda bit: (flip(seq, bit), wt)

    def loads():
        return [
            pltpu.make_async_copy(grad_ref, grads, load_sems.at[0]),
            pltpu.make_async_copy(normed_t_ref, normed_t, load_sems.at[1]),
        ]

    def wout_final(at, start, rows, total):
        wout_ref[rows, at + start : at + start + total.shape[1]] = total.astype(BF16)

    def feat_final(at, start, rows, total):
        columns = slice(at + start, at + start + total.shape[1])
        feat_ref[rows, columns] = total.astype(feat_ref.dtype)

    lows = wout_lows(count, False)
    wouts = [
        seq_group(
            copies, wout_parts[k], "chan", take, functools.partial(wout_final, k * WIDE), seq, peer,
            low=lows[k],
        )
        for k in range(count)
    ]
    width = EARLY // 2
    feats = [
        seq_group(
            copies, feat_parts[k], "feat", take, functools.partial(feat_final, k * width), seq, peer
        )
        for k in range(2)
    ]
    groups = wouts + feats

    @pl.when((part == 0) & (stream == 0))
    def _():
        barrier = pltpu.get_barrier_semaphore()
        for bit in range(seq_bits):
            pl.semaphore_signal(barrier, inc=1, device_id=peer(bit), device_id_type=MESH)
        pl.semaphore_wait(barrier, seq_bits)
        for copy in loads():
            copy.start()

    def begin():
        for copy in loads():
            copy.wait()
        for k in range(count):
            for inner in range(0, WIDE, 512):
                at = k * WIDE + inner
                value = jnp.dot(
                    gated_s[...], grads[:, at : at + 512], preferred_element_type=F32
                )
                rows, lead = wout_parts[k].shape[-2], len(wout_parts[k].shape) - 2
                wout_parts[k][(slice(None),) * (lead + 1) + (slice(inner, inner + 512),)] = (
                    value.reshape((2,) * lead + (rows, 512)).astype(BF16)
                )

    def begin_feat():
        for k in range(2):
            at = slice(k * width, (k + 1) * width)
            by_tiles(
                feat_parts[k], normed_t.shape[0],
                lambda m: jnp.dot(normed_t[m, :], dgate_s[:, at], preferred_element_type=F32),
            )

    entries = []
    for which, group in enumerate(groups):
        rows = math.prod(group.members[0].source.shape[:-1])
        members = [(one.columns.stop - one.columns.start, one.order) for one in group.members]
        ready = 2.0 if which < count else 8.0
        entries.append((ready, "seq", rows * 2 / 2**20, members))
    times = [3.5, 9.0] + [9.0 + 2.9 * k for k in range(1, 15)]
    moments, last = {}, []
    for at, which, member, stage in timetable(entries):
        turns = [k for k, time in enumerate(times) if time >= at]
        moments.setdefault(turns[0] if turns else 16, []).append((which, member, stage))

    def moment(turn):
        if turn < 2:

            @pl.when((part == 1) & (stream == 0))
            def _():
                (begin, begin_feat)[turn]()

        for at in range(4):
            if at * 4 + turn in moments:

                @pl.when((part == 1) & (stream == at))
                def _():
                    for which, member, stage in moments[at * 4 + turn]:
                        groups[which].act(member, stage)

    def rest():
        for which, member, stage in moments.get(16, []):
            groups[which].act(member, stage)
        copies.finish()

    return moment, rest


def scan_kernel(
    n_state, n_seq, parts, bcs_ref, spread_ref, gather_ref, raw_ref, u_ref, g_ref, gate_ref, dgated_ref,
    bias_ref, skip_ref, a_ref, end_ref, lead_ref, total_ref, head_ref, tail_ref, grad_ref,
    normed_t_ref,
    gated_ref, gated_t_ref, dgate_ref, dscan_ref, draw_ref, dbc_ref, da_ref, sums_ref, wout_ref,
    feat_ref,
    bcb, acc_all, dec_in, delta_in, drive_in, g_in, y_sum, b_sum, d_sum, kept, decays, da_sum, row_sum, *scratch,
):
    n_rows, width = raw_ref.shape
    steps = n_rows // SUB
    part, stream = pl.program_id(0), pl.program_id(1)
    n_streams = pl.num_programs(1)
    acc = acc_all.at[stream]
    if parts > 1:
        early_moment, early_rest = early_sums(
            n_seq, part, stream, width, grad_ref, normed_t_ref, wout_ref, feat_ref, list(scratch)
        )
    start_at = 2 * n_state * LANE
    columns = pl.ds(pl.multiple_of(part * width, width), width)
    spread_rows(bcs_ref, spread_ref, bcb)

    @pl.when(part == 0)
    def _():
        acc_all[stream] = jnp.zeros(acc_all.shape[1:], F32)

    @pl.when(stream == 0)
    def _():
        da_sum[...] = jnp.zeros_like(da_sum)
        row_sum[...] = jnp.zeros_like(row_sum)

    def prepare(j, carry):
        rows = pl.ds(pl.multiple_of(j * 16, 16), 16)
        delta = softplus(raw_ref[rows, :].astype(F32) + bias_ref[...])
        starts = wide(bcb[rows, start_at : start_at + LANE], width)
        delta_in[rows, :] = delta
        dec_in[rows, :] = jnp.where(starts > 0.5, RESET, delta)
        drive_in[rows, :] = delta * u_ref[rows, :].astype(F32)
        g_in[rows, :] = g_ref[rows, :].astype(F32)
        return carry

    lax.fori_loop(0, steps // 2, prepare, 0, unroll=2)
    chunk = lax.broadcasted_iota(jnp.int32, (SUB, width), 0)
    total = total_ref[0]
    before, after = total, total
    for shift in (1, 2, 4):
        before = jnp.where(chunk >= shift, before + pltpu.roll(before, shift, 0), before)
        after = jnp.where(chunk < SUB - shift, after + pltpu.roll(after, SUB - shift, 0), after)
    before, after = pltpu.roll(before, 1, 0), pltpu.roll(after, SUB - 1, 0)

    for first in range(0, n_state, NBLK):
        if parts > 1:
            early_moment(first // NBLK)
        states = range(first, first + NBLK)
        entry, incoming = [], []
        for n in states:
            head, tail = head_ref[0, n : n + 1, :], tail_ref[0, n : n + 1, :]
            inner = pltpu.roll(end_ref[0, n], 1, 0) + jnp.exp2(before * a_ref[n : n + 1, :]) * head
            outer = pltpu.roll(lead_ref[0, n], SUB - 1, 0) + jnp.exp2(after * a_ref[n : n + 1, :]) * tail
            entry.append(jnp.where(chunk == 0, head, inner))
            incoming.append(jnp.where(chunk == SUB - 1, tail, outer))

        def forward(j, carry):
            rows = pl.ds(pl.multiple_of(j * SUB, SUB), SUB)
            held, drive, g = dec_in[rows, :], drive_in[rows, :], g_in[rows, :]
            running = []
            y = y_sum[rows, :] if first else None
            for k, (n, h) in enumerate(zip(states, carry)):
                b = wide(bcb[rows, n * LANE : (n + 1) * LANE], width)
                c_at = slice((n_state + n) * LANE, (n_state + n + 1) * LANE)
                c = wide(bcb[rows, c_at], width)
                decay = jnp.exp2(held * a_ref[n : n + 1, :])
                kept[k, rows, :] = h
                decays[k, rows, :] = decay
                h = decay * h + drive * b
                y = c * h if y is None else y + c * h
                acc[rows, c_at] += fold(h * g)
                running.append(h)
            y_sum[rows, :] = y
            return tuple(running)

        lax.fori_loop(0, steps, forward, tuple(entry), unroll=8)

        def backward(j, carry):
            rows = pl.ds(pl.multiple_of((steps - 1 - j) * SUB, SUB), SUB)
            delta, drive, g = delta_in[rows, :], drive_in[rows, :], g_in[rows, :]
            through = b_sum[rows, :] if first else None
            pulled = d_sum[rows, :] if first else None
            passed, da = [], []
            for k, (n, p, da_n) in enumerate(zip(states, carry[0], carry[1])):
                b_at = slice(n * LANE, (n + 1) * LANE)
                b = wide(bcb[rows, b_at], width)
                c = wide(bcb[rows, (n_state + n) * LANE : (n_state + n + 1) * LANE], width)
                adjoint = g * c + p
                p = decays[k, rows, :] * adjoint
                weighed = p * kept[k, rows, :]
                pulled = weighed * a_ref[n : n + 1, :] if pulled is None else pulled + weighed * a_ref[n : n + 1, :]
                through = adjoint * b if through is None else through + adjoint * b
                acc[rows, b_at] += fold(adjoint * drive)
                passed.append(p)
                da.append(da_n + weighed * delta)
            b_sum[rows, :] = through
            d_sum[rows, :] = pulled
            return tuple(passed), tuple(da)

        zero = tuple(jnp.zeros((SUB, width), F32) for _ in states)
        _, da = lax.fori_loop(0, steps, backward, (tuple(incoming), zero), unroll=8)
        for n, da_n in zip(states, da):
            da_sum[n] += da_n

    def finish(j, carry):
        bias_sum, skip_sum = carry
        rows = pl.ds(pl.multiple_of(j * 16, 16), 16)
        u, g, delta = u_ref[rows, :].astype(F32), g_in[rows, :], delta_in[rows, :]
        gate, d_gated = gate_ref[rows, :].astype(F32), dgated_ref[rows, :]
        scanned = (y_sum[rows, :] + skip_ref[...] * u).astype(BF16).astype(F32)
        sig = jax.nn.sigmoid(gate)
        gated_ref[rows, :] = (scanned * gate * sig).astype(BF16)
        d_gate = d_gated * scanned * sig * (1.0 + gate * (1.0 - sig))
        dgate_ref[rows, :] = d_gate.astype(BF16)
        through = b_sum[rows, :]
        dscan_ref[rows, :] = (delta * through + skip_ref[...] * g).astype(BF16)
        slope = jax.nn.sigmoid(raw_ref[rows, :].astype(F32) + bias_ref[...])
        d_pre = (d_sum[rows, :] * (1.0 / LOG2E) + u * through) * slope
        draw_ref[rows, :] = d_pre.astype(BF16)
        gu = g * u
        return bias_sum + d_pre[:SUB] + d_pre[SUB:], skip_sum + gu[:SUB] + gu[SUB:]

    zero = jnp.zeros((SUB, width), F32)
    bias_sum, skip_sum = lax.fori_loop(0, steps // 2, finish, (zero, zero), unroll=2)
    gated_t_ref[...] = gated_ref[...].T
    if parts > 1:
        gated_s, dgate_s = scratch[:2]

        @pl.when(part == 0)
        def _():
            at = pl.ds(pl.multiple_of(stream * n_rows, n_rows), n_rows)
            gated_s[:, at] = gated_t_ref[...]
            dgate_s[at, :] = dgate_ref[...]

    row_sum[0] += bias_sum
    row_sum[1] += skip_sum

    @pl.when(stream == n_streams - 1)
    def _():
        for n in range(n_state):
            da_ref[n : n + 1, columns] = jnp.sum(da_sum[n], 0, keepdims=True)
        for k in range(2):
            sums_ref[k : k + 1, columns] = jnp.sum(row_sum[k], 0, keepdims=True)


    last = part == pl.num_programs(0) - 1

    @pl.when(last)
    def _():
        found = jnp.dot(
            acc[...], gather_ref[...], precision=lax.Precision.HIGHEST, preferred_element_type=F32
        )

        @pl.when(stream == 0)
        def _():
            dbc_ref[...] = found

        @pl.when(stream > 0)
        def _():
            dbc_ref[...] += pltpu.roll(found, stream * 2 * n_state, 1)

    if parts > 1:

        @pl.when(last & (stream == n_streams - 1))
        def _():
            early_rest()


def spread_matrix(n_state):
    count = 2 * n_state + 1
    column = np.arange(count * LANE)[None, :] // LANE
    return jnp.asarray((np.arange(LANE)[:, None] == column).astype(ml_dtypes.bfloat16))


def gather_matrix(n_state):
    row = np.arange(2 * n_state * LANE)[:, None] // LANE
    return jnp.asarray((np.arange(LANE)[None, :] == row).astype(np.float32))


def scan_specs(n_streams, n_rows, n_chan, n_state, width):
    row = pl.BlockSpec((n_rows, width), lambda b, c: (b, c))
    thin = pl.BlockSpec((n_rows, LANE), lambda b, c: (b, 0))
    chan = pl.BlockSpec((1, width), lambda b, c: (0, c))
    rate = pl.BlockSpec((n_state, width), lambda b, c: (0, c))
    edge = pl.BlockSpec((1, n_state, SUB, width), lambda b, c: (b, 0, 0, c))
    total = pl.BlockSpec((1, SUB, width), lambda b, c: (b, 0, c))
    head = pl.BlockSpec((1, n_state, width), lambda b, c: (b, 0, c))
    return row, thin, chan, rate, edge, total, head


def whole(shape):
    return pl.BlockSpec(shape, lambda b, c: (0,) * len(shape))


def scan_all(
    bcs, raw, u, g, gate, d_gated, bias, skip, rates, ends, leads, totals, heads, tails, grads,
    normed_t,
):
    n_seq, n_streams = lax.axis_size("seq"), lax.axis_size("wt")
    n_rows, n_chan = raw.shape[0] // n_streams, raw.shape[1]
    n_state, n_feat = rates.shape[0], normed_t.shape[0]
    width = min(512, n_chan)
    parts = parts_of(n_chan, n_seq)
    seq_bits = n_seq.bit_length() - 1

    def swapped(spec):
        return pl.BlockSpec(spec.block_shape, lambda c, b: spec.index_map(b, c))

    row, thin, chan, rate, edge, total, head = map(
        swapped, scan_specs(n_streams, n_rows, n_chan, n_state, width)
    )
    count = (2 * n_state + 1) * LANE
    spread = spread_matrix(n_state)
    gather = gather_matrix(n_state)
    rows = jax.ShapeDtypeStruct(raw.shape, BF16)
    hbm = pl.BlockSpec(memory_space=pl.ANY)
    wout_rows, feat_rows = max(n_chan // parts // n_seq, 16), n_feat // n_seq
    scratch = [
        pltpu.VMEM((n_rows, count), F32),
        pltpu.VMEM((n_streams, n_rows, 2 * n_state * LANE), F32),
    ]
    scratch += [pltpu.VMEM((n_rows, width), F32)] * 7
    scratch += [pltpu.VMEM((NBLK, n_rows, width), F32)] * 2
    scratch += [pltpu.VMEM((n_state, SUB, width), F32), pltpu.VMEM((2, SUB, width), F32)]
    params = {}
    if parts > 1:
        blocks = (2,) * seq_bits
        n_wide = n_feat // WIDE
        scratch += [
            pltpu.VMEM((width, raw.shape[0]), BF16),
            pltpu.VMEM((raw.shape[0], width), BF16),
            pltpu.VMEM((raw.shape[0], n_feat), BF16),
            pltpu.VMEM(normed_t.shape, BF16),
        ]
        scratch += [pltpu.VMEM(blocks + (feat_rows, EARLY // 2), BF16)] * 2
        scratch += [pltpu.VMEM(blocks + (wout_rows, WIDE), BF16)] * n_wide
        scratch += [pltpu.SemaphoreType.DMA((2,))]
        scratch += [pltpu.SemaphoreType.DMA((2 * seq_bits * (n_wide + 2),))] * 2
        for low in wout_lows(n_wide, False):
            scratch += seq_landings(seq_bits, wout_rows, [WIDE], low)
        scratch += seq_landings(seq_bits, feat_rows, [EARLY // 2] * 2)
        params = dict(collective_id=4, has_side_effects=True)
    return pl.pallas_call(
        functools.partial(scan_kernel, n_state, n_seq, parts),
        grid=(n_chan // width, n_streams),
        in_specs=[
            thin, whole((LANE, count)), whole(gather.shape), row, row, row, row, row,
            chan, chan, rate, edge, edge, total, head, head, hbm, hbm,
        ],
        out_specs=[
            row, pl.BlockSpec((width, n_rows), lambda c, b: (c, b)), row, row, row,
            whole((n_rows, LANE)), whole((n_state, n_chan)), whole((2, n_chan)),
            whole((wout_rows, n_feat)), whole((feat_rows, EARLY)),
        ],
        out_shape=[
            rows, jax.ShapeDtypeStruct(raw.shape[::-1], BF16), rows, rows, rows,
            jax.ShapeDtypeStruct((n_rows, LANE), F32),
            jax.ShapeDtypeStruct((n_state, n_chan), F32),
            jax.ShapeDtypeStruct((2, n_chan), F32),
            jax.ShapeDtypeStruct((wout_rows, n_feat), BF16),
            jax.ShapeDtypeStruct((feat_rows, EARLY), feat_type(n_feat, n_seq, n_streams)),
        ],
        scratch_shapes=scratch,
        compiler_params=pltpu.CompilerParams(vmem_limit_bytes=63 * 2**20, **params),
        name="scan_all",
    )(
        bcs, spread, gather, raw, u, g, gate, d_gated, bias, skip, rates,
        ends, leads, totals, heads, tails, grads, normed_t,
    )


def finish_kernel(
    n_seq, n_wt, n_state,
    gated_t_ref, dgate_ref, dscan_ref, draw_ref, u_ref, conv_ref, grad_ref, normed_t_ref, win_ref,
    wout_ref, feat_ref, gated_ref, w_out_ref, x_ref, g_ref,
    gain_ref, dbc_ref, low_ref, wx_ref, wdt_ref, wconv_ref, bconv_ref, da_ref, a_ref, sums_ref,
    feat_out, wout_out, small_out, norm_out, out_out, gain_out,
    *scratch,
):
    scratch = list(scratch)
    take = lambda count: [scratch.pop(0) for _ in range(count)]
    seq, wt = lax.axis_index("seq"), lax.axis_index("wt")
    seq_bits, wt_bits = n_seq.bit_length() - 1, n_wt.bit_length() - 1
    seq_peer = lambda bit: (flip(seq, bit), wt)
    wt_peer = lambda bit: (seq, flip(wt, bit))
    n_chan, all_rows = gated_t_ref.shape
    parts = parts_of(n_chan, n_seq)
    ready = parts - 1
    half_seq = n_seq // 2
    here = n_wt * seq + wt
    mine = (seq % 2) * half_seq + seq // 2

    def summed_at(j):
        return (j % half_seq) * 2 + j // half_seq

    def device(flat):
        return flat // n_wt, flat % n_wt

    flat = n_seq * wt + mine
    owner, giver_block = device(flat), here % n_seq
    giver = (summed_at(giver_block), here // n_seq)
    elsewhere = flat != here
    per = n_seq // parts
    part_flat = [n_seq * wt + q * per + mine // parts for q in range(parts)]
    part_owner = [device(value) for value in part_flat]
    piece = mine % parts
    piece_giver = [
        (summed_at((giver_block % per) * parts + k), here // n_seq) for k in range(parts)
    ]
    piece_here = [n_wt * s + w == here for s, w in piece_giver]
    ahead, behind = (lax.rem(seq + 1, n_seq), wt), (lax.rem(seq + n_seq - 1, n_seq), wt)

    barrier = pltpu.get_barrier_semaphore()
    partners = [seq_peer(b) for b in range(seq_bits)]
    partners += [(seq, turn(wt, mask, wt_bits)) for mask in range(1, n_wt)]
    partners += [ahead, behind]
    for partner in partners:
        pl.semaphore_signal(barrier, inc=1, device_id=partner, device_id_type=MESH)

    arrivals = len(partners) + 2 * elsewhere.astype(jnp.int32)

    @pl.when(elsewhere)
    def _():
        for partner in (owner, giver):
            pl.semaphore_signal(barrier, inc=1, device_id=partner, device_id_type=MESH)

    if parts > 1:
        others = [(value != here, to) for value, to in zip(part_flat, part_owner)]
        others += [(jnp.logical_not(own), to) for own, to in zip(piece_here, piece_giver)]
        for away, to in others:
            arrivals = arrivals + away.astype(jnp.int32)

            @pl.when(away)
            def _():
                pl.semaphore_signal(barrier, inc=1, device_id=to, device_id_type=MESH)

    (
        gated_t, dgate, dscan, draw, normed_t, grads, win_rows, conv, d_conv, mix, first, half, land, fin,
        u_all, ddt, dbc, pack, rim_f, rim_s, fin_feat, fin_wout, fin_small, w_rows, gain_sum, small,
        piece_sems, send_sems, recv_sems,
    ) = take(29)
    n_wide = normed_t.shape[0] // WIDE
    wout_parts = take(n_wide) if ready else take(1) * n_wide
    feat_parts, norm_parts = take(4 if ready else 3), take(2)
    if not ready:
        inner = (slice(None),) * (seq_bits + 1)
        feat_parts += [feat_parts[0].at[inner + (slice(at, at + 256),)] for at in (0, 256)]
    copies = Copies(send_sems, recv_sems)
    part_chan = gated_t.shape[0]
    if not ready:
        u_all = gated_t
    n_feat = normed_t.shape[0]
    n_rows = all_rows // n_wt
    taps = wconv_ref.shape[0]
    steps = n_rows // SUB
    rim = (taps - 1) * SUB
    cols = 512

    def load(src, dst):
        return copies.local(src, dst)

    def grad_block(k):
        return load(grad_ref.at[:, :, k * cols : (k + 1) * cols], grads.at[k % 2])

    coming = {
        "draw": load(draw_ref, draw),
        "gated": load(gated_t_ref.at[ready * part_chan :], gated_t),
        0: grad_block(0),
        1: grad_block(1),
        "normed": load(normed_t_ref, normed_t),
        "dgate": load(dgate_ref, dgate),
        "conv": load(conv_ref.at[:, :, :cols], conv),
        "dscan": load(dscan_ref.at[:, :cols], dscan),
        "w_rows": load(
            win_ref.at[pl.ds(pl.multiple_of(seq * w_rows.shape[0], 16), w_rows.shape[0])], w_rows
        ),
    }

    ring, d_block = win_rows.shape[:2]

    def win_block(i):
        coming["win", i] = load(win_ref.at[i * d_block : (i + 1) * d_block], win_rows.at[i % ring])

    for k in range(cols // d_block):
        win_block(k)
    if ready:
        coming["wout"] = load(wout_ref, fin_wout.at[0])
        coming["feat"] = load(feat_ref, fin_feat.at[:, n_chan : n_chan + EARLY])
    pl.semaphore_wait(barrier, arrivals)

    rows_own = feat_out.shape[0]

    def own_rows(w):
        return pl.ds(pl.multiple_of(w * rows_own, 8), rows_own)

    delivered = []

    def to_wt(block_of, place):
        for mask in range(1, n_wt):
            peer = turn(wt, mask, wt_bits)
            delivered.append(copies.remote(block_of(peer), place, (seq, peer)).wait_recv)
        delivered.append(copies.local(block_of(wt), place).wait)

    def feat_done(at, cols):
        tile = math.gcd(w_rows.shape[0], 32)

        def body(i, carry):
            rows = pl.ds(pl.multiple_of(i * tile, tile), tile)
            done = fin_feat[rows, at : at + cols].astype(F32)
            product = w_rows[rows, at : at + cols].astype(F32) * done
            gain_sum[rows, :] += fold(product)
            return carry

        lax.fori_loop(0, w_rows.shape[0] // tile, body, 0)
        start = pl.multiple_of(((at // n_chan) * n_wt + wt) * n_chan + at % n_chan, LANE)
        to_wt(
            lambda w: fin_feat.at[own_rows(w), at : at + cols],
            feat_out.at[:, pl.ds(start, cols)],
        )

    moved = []

    def small_done():
        k, copies.count = copies.count, copies.count + 1
        away = pltpu.make_async_remote_copy(
            src_ref=fin_small, dst_ref=small_out, send_sem=send_sems.at[k],
            recv_sem=recv_sems.at[k], device_id=owner, device_id_type=MESH,
        )
        home = pltpu.make_async_copy(fin_small, small_out, send_sems.at[k])

        @pl.when(elsewhere)
        def _():
            away.start()

        @pl.when(jnp.logical_not(elsewhere))
        def _():
            home.start()

        def wait():
            @pl.when(elsewhere)
            def _():
                away.wait()

            @pl.when(jnp.logical_not(elsewhere))
            def _():
                home.wait()

        moved.append(wait)

    def wout_done(q, at, width, slot):
        place = fin_wout.at[q, :, at : at + width]
        target = wout_out.at[piece, :, at : at + width]
        away = pltpu.make_async_remote_copy(
            src_ref=place, dst_ref=target, send_sem=piece_sems.at[0, q, slot],
            recv_sem=piece_sems.at[1, piece, slot], device_id=part_owner[q], device_id_type=MESH,
        )
        home = pltpu.make_async_copy(place, target, piece_sems.at[0, q, slot])
        remote = part_flat[q] != here

        @pl.when(remote)
        def _():
            away.start()

        @pl.when(jnp.logical_not(remote))
        def _():
            home.start()

        def wait():
            @pl.when(remote)
            def _():
                away.wait_send()

            @pl.when(jnp.logical_not(remote))
            def _():
                home.wait()

        moved.append(wait)

    def wout_arrive(k, at, width, slot):
        target = wout_out.at[k, :, at : at + width]
        copy = pltpu.make_async_remote_copy(
            src_ref=target, dst_ref=target, send_sem=piece_sems.at[0, k, slot],
            recv_sem=piece_sems.at[1, k, slot], device_id=piece_giver[k], device_id_type=MESH,
        )

        @pl.when(jnp.logical_not(piece_here[k]))
        def _():
            copy.wait_recv()

    def wout_final(at, start, rows, total):
        columns = slice(at + start, at + start + total.shape[1])
        fin_wout[ready, rows, columns] = total.astype(BF16)

    def feat_final(at, start, rows, total):
        columns = slice(at + start, at + start + total.shape[1])
        fin_feat[rows, columns] = total.astype(fin_feat.dtype)

    def small_final(start, rows, total):
        fin_small[rows, start : start + total.shape[1]] = total.astype(BF16)

    wout_groups = [
        seq_group(
            copies, wout_parts[k], "chan", take, functools.partial(wout_final, k * WIDE), seq,
            seq_peer, functools.partial(wout_done, ready, k * WIDE, WIDE, k), lows[k],
        )
        for k, lows in zip(range(n_wide), [wout_lows(n_wide, True)] * n_wide)
    ]
    feat_groups = []
    for part, (at, _, low) in zip(feat_parts, feat_plan(n_chan, parts)):
        done = functools.partial(feat_done, at, part.shape[-1])
        feat_groups.append(
            seq_group(
                copies, part, "feat", take, functools.partial(feat_final, at), seq, seq_peer, done,
                low,
            )
        )
    gate_a, gate_b, conv_a, conv_b, conv_c = range(-ready, 5 - ready)
    small_group = seq_group(copies, small, "chan", take, small_final, seq, seq_peer, small_done)
    wide_groups = []
    for target in (norm_out, out_out):
        for k in range(n_feat // cols):

            def final(rows, total, target=target, k=k):
                target[rows, k * cols : (k + 1) * cols] = total

            order = tuple(range(wt_bits))
            job = Halving(
                copies, norm_parts[k % 2], list(reversed(order)), order, slice(0, cols),
                take(wt_bits), final, wt, wt_peer,
            )
            wide_groups.append(Group([job]))

    def wout(k):
        if not ready and k:
            take_until(k - 1)
            wout_groups[k - 1].release()
        for inner in range(WIDE // cols):
            block = k * (WIDE // cols) + inner
            coming[block].wait()
            right = grads[block % 2].reshape(all_rows, cols)
            lanes = slice(inner * cols, (inner + 1) * cols)
            tile = min(512, part_chan)
            rows, lead = wout_parts[k].shape[-2], len(wout_parts[k].shape) - 2
            within = (tile // rows).bit_length() - 1
            for m in range(0, part_chan, tile):
                value = jnp.dot(gated_t[m : m + tile, :], right, preferred_element_type=F32)
                index = tuple(
                    (m // rows >> (lead - 1 - q)) & 1 for q in range(lead - within)
                )
                wout_parts[k][index + (slice(None),) * (within + 1) + (lanes,)] = (
                    value.reshape((2,) * within + (rows, cols)).astype(BF16)
                )
            if block + 2 < n_feat // cols:
                coming[block + 2] = grad_block(block + 2)

    gain_sum[...] = jnp.zeros_like(gain_sum)
    coming["draw"].wait()
    for b in range(n_wt):
        at = slice(b * n_rows, (b + 1) * n_rows)
        mix[at, :] = jnp.dot(draw[at, :], wdt_ref[...], preferred_element_type=F32)
    width = LANE // n_wt
    mix[all_rows:, :] = dbc_ref[...]
    mixed = WtSum(copies, mix, first, half, land, fin, seq, wt, wt_bits)
    mixed.begin()
    coming["gated"].wait()

    def feat(k, right):
        if not ready and k == conv_b:
            take_until(first_feat + gate_a)
            feat_groups[gate_a].release()
        by_tiles(
            feat_parts[k], n_feat,
            lambda m: jnp.dot(normed_t[m, :], right, preferred_element_type=F32),
        )

    def low_pack():
        pack[LANE : 2 * LANE, :] = lax.dot_general(
            low_ref[...], draw[...], (((0,), (0,)), ((), ())), preferred_element_type=F32
        )
        mixed.end_send()
        coming["normed"].wait()
        coming["dgate"].wait()

    def early_feat():
        coming["w_rows"].wait()
        if ready:
            coming["feat"].wait()
            feat_done(n_chan, EARLY)
        mixed.copy.wait_recv()
        mixed_ready()

    tail_at = 2 * LANE + 3 * n_state

    def mixed_ready():
        ddt[...] = fin[:all_rows, :].astype(BF16)
        lane = lax.broadcasted_iota(jnp.int32, (n_rows, LANE), 1)
        for b in range(n_wt):
            part = fin[all_rows:, :]
            if b:
                part = pltpu.roll(part, LANE - b * width, 1)
            dbc[b * n_rows : (b + 1) * n_rows, :] = jnp.where(lane < width, part, 0.0).astype(BF16)
        coming["u"] = load(u_ref, u_all)

        pack[2 * LANE :, :] = jnp.zeros((LANE, n_chan), F32)
        pack[tail_at - n_state : tail_at, :] = da_ref[...] * (a_ref[...] * (1.0 / LOG2E))
        pack[tail_at + taps + 1 : tail_at + taps + 3, :] = sums_ref[...]

    def sums_of(total):
        return jnp.sum(total, 0, keepdims=True)

    chunk = lax.broadcasted_iota(jnp.int32, (SUB, cols), 0)
    rim_moves = []

    def conv_first(h):
        at = slice(h * cols, (h + 1) * cols)
        for b in range(n_wt):
            rows = slice(b * n_rows, (b + 1) * n_rows)
            d_in = lax.dot_general(
                ddt[rows, :], wx_ref[at, :LANE], (((1,), (1,)), ((), ())), preferred_element_type=F32
            )
            d_in = d_in + lax.dot_general(
                dbc[rows, : 2 * n_state], wx_ref[at, LANE:], (((1,), (1,)), ((), ())),
                preferred_element_type=F32,
            )
            d_conv[h, b, :n_rows, :] = d_in
        coming["conv"].wait()
        coming["dscan"].wait()

        def one(i, carry):
            b, j = i // (n_rows // 16), i % (n_rows // 16)
            rows = pl.ds(pl.multiple_of(j * 16, 16), 16)
            taken = [
                conv[b, pl.ds(pl.multiple_of(j * 16 + k * SUB, SUB), 16), :] for k in range(taps)
            ]
            out = bconv_ref[:, at]
            for k in range(taps):
                out = out + taken[k] * wconv_ref[k : k + 1, at]
            sig = jax.nn.sigmoid(out)
            from_scan = dscan[pl.ds(pl.multiple_of(i * 16, 16), 16), :].astype(F32)
            value = (d_conv[h, b, rows, :] + from_scan) * sig * (1.0 + out * (1.0 - sig))
            d_conv[h, b, rows, :] = value
            found = [value] + [value * piece for piece in taken]
            return tuple(c + f[:SUB] + f[SUB:] for c, f in zip(carry, found))

        zero = jnp.zeros((SUB, cols), F32)
        totals = lax.fori_loop(0, all_rows // 16, one, (zero,) * (taps + 1))
        pack[tail_at + taps : tail_at + taps + 1, at] = sums_of(totals[0])
        for k in range(taps):
            pack[tail_at + k : tail_at + k + 1, at] = sums_of(totals[k + 1])

        rim_f[...] = jnp.zeros_like(rim_f)
        for b in range(n_wt):
            for k in range(taps - 1):
                rim_f[b * (taps - 1) + k, :] = d_conv[h, b, k * SUB, :]
        rim_s[h, 0] = rim_f[...].astype(BF16)

        @pl.when(seq == n_seq - 1)
        def _():
            rim_s[h, 1] = jnp.zeros((16, cols), BF16)

        k, copies.count = copies.count, copies.count + 1
        move = pltpu.make_async_remote_copy(
            src_ref=rim_s.at[h, 0], dst_ref=rim_s.at[h, 1], send_sem=send_sems.at[k],
            recv_sem=recv_sems.at[k], device_id=behind, device_id_type=MESH,
        )
        rim_moves.append(move)

        @pl.when(seq > 0)
        def _():
            move.start()

        if h == 0:
            coming["conv"] = load(conv_ref.at[:, :, cols : 2 * cols], conv)
            coming["dscan"] = load(dscan_ref.at[:, cols : 2 * cols], dscan)

    def conv_second(h):
        at = slice(h * cols, (h + 1) * cols)

        @pl.when(seq < n_seq - 1)
        def _():
            rim_moves[h].wait_recv()

        landed = rim_s[h, 1].astype(F32)
        for b in range(n_wt):
            for k in range(taps - 1):
                turned = pltpu.roll(d_conv[h, b, k * SUB : (k + 1) * SUB, :], SUB - 1, 0)
                row = landed[b * (taps - 1) + k : b * (taps - 1) + k + 1, :]
                place = slice(n_rows + k * SUB, n_rows + (k + 1) * SUB)
                d_conv[h, b, place, :] = jnp.where(chunk == SUB - 1, row, turned)

        def one(i, carry):
            b, j = i // (n_rows // 16), i % (n_rows // 16)
            total = jnp.zeros((16, cols), F32)
            for k in range(taps):
                start = pl.multiple_of(j * 16 + (taps - 1 - k) * SUB, SUB)
                total = total + d_conv[h, b, pl.ds(start, 16), :] * wconv_ref[k : k + 1, at]
            draw[pl.ds(pl.multiple_of(i * 16, 16), 16), at] = total.astype(BF16)
            return carry

        lax.fori_loop(0, all_rows // 16, one, 0)

    def early_pieces():
        if ready:
            coming["wout"].wait()
            for k in range(n_wide):
                wout_done(0, k * WIDE, WIDE, k)

    def small_sums():
        coming["u"].wait()
        pack[:LANE, :] = lax.dot_general(
            ddt[...], u_all[...], (((0,), (0,)), ((), ())), preferred_element_type=F32
        )
        for_b = lax.dot_general(
            dbc[...], u_all[...], (((0,), (0,)), ((), ())), preferred_element_type=F32
        )
        pack[2 * LANE : 2 * LANE + 2 * n_state, :] = for_b[: 2 * n_state, :]
        coming["gated"] = load(gated_ref, u_all)
        tile = min(512, n_chan)
        for m in range(0, n_chan, tile):
            fill(small, m // small.shape[-2], pack[:, m : m + tile].T)

    per = cols // d_block
    n_norm = n_feat // cols

    def wide_part(k, block_of):
        part = norm_parts[k % 2]
        if k >= 2:
            take_until(len(seq_groups) + k - 2)
            wide_groups[k - 2].release()
        for b in range(n_wt):
            index = tuple((b >> (wt_bits - 1 - q)) & 1 for q in range(wt_bits))
            for lanes, value in block_of(slice(b * n_rows, (b + 1) * n_rows)):
                part[index + (slice(None), lanes)] = value.astype(BF16)

    def norm(k):
        def block_of(at):
            for part in range(per):
                rows_w = win_rows.at[(k * per + part) % ring]
                value = lax.dot_general(
                    draw[at, :], rows_w[:, :n_chan], (((1,), (1,)), ((), ())),
                    preferred_element_type=F32,
                )
                value = value + lax.dot_general(
                    dgate[at, :], rows_w[:, n_chan:], (((1,), (1,)), ((), ())),
                    preferred_element_type=F32,
                )
                yield slice(part * d_block, (part + 1) * d_block), value

        for part in range(per):
            coming["win", k * per + part].wait()
        wide_part(k, block_of)
        for part in range(per):
            if (k + 1) * per + part < per * n_norm:
                win_block((k + 1) * per + part)

    def out_block(k):
        coming["out", k] = load(w_out_ref.at[:, :, k * cols : (k + 1) * cols], grads.at[k % 2])

    def out(k):
        coming["out", k].wait()
        right = grads[k % 2].reshape(all_rows, cols)

        def block_of(at):
            yield slice(0, cols), jnp.dot(u_all[at, :], right, preferred_element_type=F32)

        wide_part(n_norm + k, block_of)
        if k + 2 < n_norm:
            out_block(k + 2)
        if k + 1 == n_norm:
            for at in range(n_norm):
                block = slice(at * cols, (at + 1) * cols)
                coming["x", at] = load(x_ref.at[:, block], dscan.at[at * n_rows : (at + 1) * n_rows])
                coming["g", at] = load(g_ref.at[:, block], grads.at[0, at])

    def last_of_wide():
        for at in range(n_norm):
            coming["x", at].wait()
            coming["g", at].wait()
        gain = jnp.concatenate([gain_ref[k].astype(F32)[0:1] for k in range(n_wt)], axis=1)
        to = lax.broadcasted_iota(jnp.int32, (n_rows, n_rows), 0)
        source = lax.broadcasted_iota(jnp.int32, (n_rows, n_rows), 1)
        order = (source == (to % steps) * SUB + to // steps).astype(F32)
        for target in (norm_out, out_out):
            for at in range(n_norm):
                block = slice(at * cols, (at + 1) * cols)
                target[:, block] = jnp.dot(
                    order, target[:, block], precision=lax.Precision.HIGHEST,
                    preferred_element_type=F32,
                )

        def one(i, carry):
            rows = pl.ds(pl.multiple_of(i * 16, 16), 16)
            x = jnp.concatenate(
                [
                    dscan[pl.ds(pl.multiple_of(at * n_rows + i * 16, 16), 16), :].astype(F32)
                    for at in range(n_norm)
                ],
                axis=1,
            )
            g = jnp.concatenate([grads[0, at, rows, :].astype(F32) for at in range(n_norm)], axis=1)
            out_out[rows, :] = out_out[rows, :] + x
            inv = lax.rsqrt(jnp.mean(x * x, axis=1, keepdims=True) + EPS)
            scaled = norm_out[rows, :] * gain
            along = jnp.mean(scaled * x, axis=1, keepdims=True)
            norm_out[rows, :] = g + inv * scaled - x * (inv * inv * inv) * along
            return carry

        lax.fori_loop(0, n_rows // 16, one, 0)

    def out_begin():
        coming["gated"].wait()
        out_block(0)
        out_block(1)

    seq_groups = wout_groups + feat_groups + [small_group]
    first_feat = n_wide
    works = [(1.3, functools.partial(wout, 0), [0])]
    works += [(1.5, functools.partial(mixed.middle, bit), []) for bit in range(1, wt_bits)]
    works += [(1.3, functools.partial(wout, k), [k]) for k in range(1, n_wide)]
    works += [
        (4.0, low_pack, []),
        (2.0, early_feat, []),
        (4.5, functools.partial(conv_first, 0), []),
        (4.5, functools.partial(conv_first, 1), []),
        (0.3, early_pieces, []),
        (2.5, lambda: feat(gate_b, dgate[:, cols:]), [first_feat + gate_b]),
        (2.5, functools.partial(conv_second, 0), []),
        (2.5, lambda: feat(conv_a, draw[:, :cols]), [first_feat + conv_a]),
        (2.5, functools.partial(conv_second, 1), []),
        (1.4, lambda: feat(conv_b, draw[:, cols : cols + 256]), [first_feat + conv_b]),
        (1.4, lambda: feat(conv_c, draw[:, cols + 256 :]), [first_feat + conv_c]),
        (4.0, small_sums, [len(seq_groups) - 1]),
    ]
    works += [(2.7, functools.partial(norm, k), [len(seq_groups) + k]) for k in range(n_norm)]
    if not ready:
        gate_first = (3.0, lambda: feat(gate_a, dgate[:, :cols]), [first_feat + gate_a])
        works.insert(len(works) - 14 - n_norm, gate_first)
    works += [(0.2, out_begin, [])]
    works += [(1.5, functools.partial(out, k), [len(seq_groups) + n_norm + k]) for k in range(n_norm)]
    clock, starts_at, ready_at = 5.0, [], {}
    for took, _, readied in works:
        starts_at.append(clock)
        clock += took
        for which in readied:
            ready_at[which] = clock
    all_groups = seq_groups + wide_groups
    entries = []
    for which, group in enumerate(all_groups):
        job = group.members[0]
        axis = "seq" if which < len(seq_groups) else "wt"
        rows = math.prod(job.source.shape[:-1])
        members = [(one.columns.stop - one.columns.start, one.order) for one in group.members]
        entries.append((ready_at[which], axis, rows * 2 / 2**20, members))
    moves = [(29.0, "seq", 1, 0.375), (60.0, "seq", 1, 0.375), (90.0, "seq", 1, 0.14)]
    actions = timetable(entries, moves)
    ended = max(time for time, which, _, _ in actions if which >= len(seq_groups))
    actions.append((ended, None, 0, 0))
    actions.sort(key=lambda action: action[0])

    def take_action(at=0):
        _, which, member, stage = actions.pop(at)
        if which is None:
            last_of_wide()
        else:
            all_groups[which].act(member, stage)

    def take_until(which):
        at = 0
        while at < len(actions):
            if actions[at][1] == which and actions[at][3] <= 1:
                take_action(at)
            else:
                at += 1

    for at, (_, work, _) in zip(starts_at, works):
        while actions and actions[0][0] <= at + 0.01:
            take_action()
        work()
    while actions:
        take_action()
    to_wt(lambda w: gain_sum.at[own_rows(w)], gain_out.at[wt])
    for wait in delivered:
        wait()
    for wait in moved:
        wait()
    for k in range(parts):
        for slot in range(n_wide):
            wout_arrive(k, slot * WIDE, WIDE, slot)
    for move in rim_moves:

        @pl.when(seq > 0)
        def _():
            move.wait_send()

    copies.finish()


def finish_all(
    gated_t, d_gate, d_scan_in, d_raw, inputs, conv, grads, normed_t, w_in, wout, feat, gated,
    w_out, x, g, gain, d_bc, dt_low, w_x, w_dt, w_conv, b_conv, d_rate, a_neg, sums,
):
    n_seq, n_wt = lax.axis_size("seq"), lax.axis_size("wt")
    seq_bits, wt_bits = n_seq.bit_length() - 1, n_wt.bit_length() - 1
    n_chan, all_rows = gated_t.shape
    n_feat, n_rows = normed_t.shape[0], all_rows // n_wt
    n_state, taps = a_neg.shape[0], w_conv.shape[0]
    cols = 512
    parts = parts_of(n_chan, n_seq)
    part_chan = n_chan // parts
    chan_rows, feat_rows, wout_rows = n_chan // n_seq, n_feat // n_seq, part_chan // n_seq
    size = (all_rows + n_rows) // 2
    small_cols, n_wide = 3 * LANE, n_feat // WIDE
    square = ((all_rows, n_chan), BF16)
    blocks = (2,) * seq_bits
    done_type = feat_type(n_feat, n_seq, n_wt)
    plan = feat_plan(n_chan, parts)
    scratch = [
        ((part_chan, all_rows), BF16), square, ((all_rows, cols), BF16), square,
        (normed_t.shape, BF16), ((2, n_wt, n_rows, cols), BF16), ((2, 256, 2 * n_chan), BF16),
        ((n_wt, conv.shape[1], cols), F32), ((2, n_wt, conv.shape[1], cols), F32),
        ((2 * size, LANE), F32), ((size, LANE), F32), ((wt_bits - 1, size, LANE), BF16),
        ((wt_bits - 1, size, LANE), BF16), ((2 * size, LANE), F32), square if parts > 1 else ((16, LANE), BF16), ((all_rows, LANE), BF16), ((all_rows, LANE), BF16),
        ((small_cols, n_chan), F32), ((16, cols), F32), ((2, 2, 16, cols), BF16),
        ((feat_rows, 2 * n_chan), done_type), ((parts, wout_rows, n_feat), BF16),
        ((chan_rows, small_cols), BF16), ((feat_rows, 2 * n_chan), BF16), ((feat_rows, LANE), F32),
        (blocks + (chan_rows, small_cols), BF16),
    ]
    scratch = [pltpu.VMEM(*item) for item in scratch]
    scratch += [pltpu.SemaphoreType.DMA((2, parts, n_wide))]
    scratch += [pltpu.SemaphoreType.DMA((180,))] * 2
    scratch += [pltpu.VMEM(blocks + (wout_rows, WIDE), BF16)] * (n_wide if parts > 1 else 1)
    scratch += [
        pltpu.VMEM(blocks + (feat_rows, width), BF16) for _, width, _ in plan[: 5 - parts % 2 * 2]
    ]
    scratch += [pltpu.VMEM((2,) * wt_bits + (n_rows, cols), BF16)] * 2
    for low in wout_lows(n_wide, True):
        scratch += seq_landings(seq_bits, wout_rows, [WIDE], low)
    for _, width, low in plan:
        scratch += seq_landings(seq_bits, feat_rows, [width], low)
    scratch += seq_landings(seq_bits, chan_rows, [small_cols])
    scratch += landings(wt_bits, n_rows, (cols,) * (2 * n_feat // cols))
    hbm = pl.BlockSpec(memory_space=pl.ANY)
    vmem = pl.BlockSpec(memory_space=pltpu.VMEM)
    return pl.pallas_call(
        functools.partial(finish_kernel, n_seq, n_wt, n_state),
        in_specs=[hbm] * 15 + [vmem] * 10,
        out_specs=[hbm, hbm, hbm, vmem, vmem, hbm],
        out_shape=[
            jax.ShapeDtypeStruct((feat_rows // n_wt, 2 * n_chan * n_wt), done_type),
            jax.ShapeDtypeStruct((parts, wout_rows, n_feat), BF16),
            jax.ShapeDtypeStruct((chan_rows, small_cols), BF16),
            jax.ShapeDtypeStruct((n_rows, n_feat), F32),
            jax.ShapeDtypeStruct((n_rows, n_feat), F32),
            jax.ShapeDtypeStruct((n_wt, feat_rows // n_wt, LANE), F32),
        ],
        scratch_shapes=scratch,
        compiler_params=pltpu.CompilerParams(
            collective_id=1, has_side_effects=True, vmem_limit_bytes=255 * 2**18
        ),
        name="finish_all",
    )(
        gated_t, d_gate, d_scan_in, d_raw, inputs, conv, grads, normed_t, w_in, wout, feat, gated,
        w_out.reshape(grads.shape), x, g, gain, d_bc, dt_low, w_x, w_dt, w_conv, b_conv, d_rate, a_neg, sums,
    )


class Gather:
    def __init__(self, copies, slots, seq, wt, bits):
        self.copies, self.slots, self.seq, self.wt, self.bits = copies, slots, seq, wt, bits
        self.arriving = {}

    def send(self, mask, src):
        slot = self.slots.at[turn(self.wt, mask, self.bits)]
        low = self.bits if mask == 0 else (mask & -mask).bit_length() - 1
        for bit in reversed(range(low)):
            peer = (self.seq, flip(self.wt, bit))
            self.arriving[mask | 1 << bit] = self.copies.remote(src, slot, peer)

    def arrive(self, mask):
        self.arriving[mask].wait_recv()
        self.send(mask, self.slots.at[turn(self.wt, mask, self.bits)])


def start_kernel(
    n_seq, n_wt,
    hidden_ref, grad_ref, gain_ref, starts_ref, win_ref, wout_ref, wconv_ref, bconv_ref, wx_ref,
    wdt_ref, spread_ref, bias_ref, rate_ref,
    normed_out, win_out, conv_out, gate_out, u_out, raw_out, low_out, bcs_out, dgated_out,
    dscan_out, grad_out, gain_out, end_out, lead_out, total_ref, head_ref, tail_ref,
    rows_s, grads_s, gain_s, starts_s, normed_s, win_s, wout_s, conv_s, gate_s, u_s, raw_s, low_s,
    bcs_s, dgated_s, dscan_s, mix_s, fin_s, first_s, half_s, land_s, rim_s, rim_in, normed_t,
    bcb, dec_in, drive_in, g_in, end_s, lead_s, run_s, span_s, own_span, gap_s, edge_send, edge_land, span_send,
    span_land,
    send_sems, recv_sems, join_send, join_recv,
):
    seq, wt = lax.axis_index("seq"), lax.axis_index("wt")
    bits = n_wt.bit_length() - 1
    n_rows, n_feat = hidden_ref.shape
    n_chan, shard = wout_ref.shape[0], win_ref.shape[0]
    taps = wconv_ref.shape[0]
    rim = (taps - 1) * SUB
    all_rows = n_wt * n_rows
    near_y, near_z = (flip(seq, 0), wt), (flip(seq, 1), wt)
    wt_peers = [(seq, turn(wt, mask, bits)) for mask in range(1, n_wt)]
    ahead, behind = (lax.rem(seq + 1, n_seq), wt), (lax.rem(seq + n_seq - 1, n_seq), wt)

    barrier = pltpu.get_barrier_semaphore()
    partners = wt_peers + [near_y, near_z, ahead, behind]
    for r in range(1, n_seq.bit_length() - 1):
        partners += [(lax.rem(seq + d, n_seq), wt) for d in (2**r, n_seq - 2**r)]
    for partner in partners:
        pl.semaphore_signal(barrier, inc=1, device_id=partner, device_id_type=MESH)
    pl.semaphore_wait(barrier, len(partners))

    copies = Copies(send_sems, recv_sems)
    part = shard // 4
    quarter = seq % 4

    def win_part(owner, which, at, rows, half):
        start = pl.multiple_of(owner * shard + which * part + at, 16)
        return win_s.at[pl.ds(start, rows), half * n_chan : (half + 1) * n_chan]

    def send_far(half):
        found = {}
        rows = pl.ds(pl.multiple_of(quarter * part, 16), part)
        for mask in range(2, n_wt):
            to = turn(wt, mask, bits)
            columns = pl.ds(pl.multiple_of((half * n_wt + to) * n_chan, LANE), n_chan)
            found[mask] = copies.remote(
                win_ref.at[rows, columns], win_part(wt, quarter, 0, part, half), (seq, to)
            )
        return found

    def send_near(half):
        to = flip(wt, 0)
        place = win_s.at[
            pl.ds(pl.multiple_of(wt * shard, 16), shard), half * n_chan : (half + 1) * n_chan
        ]
        columns = pl.ds(pl.multiple_of((half * n_wt + to) * n_chan, LANE), n_chan)
        own = pl.ds(pl.multiple_of((half * n_wt + wt) * n_chan, LANE), n_chan)
        return (
            copies.remote(win_ref.at[:, columns], place, (seq, to)),
            copies.local(win_ref.at[:, own], place),
        )

    def share_first(half, found):
        passed = {}
        for mask, copy in found.items():
            copy.wait_recv()
            block = win_part(turn(wt, mask, bits), quarter, 0, part, half)
            passed[mask] = (
                copies.remote(block, block, near_y), copies.remote(block, block, near_z)
            )
        return passed

    def share_second(half, passed):
        last = []
        for mask, (by_y, by_z) in passed.items():
            owner = turn(wt, mask, bits)
            by_z.wait_recv()
            block = win_part(owner, flip(quarter, 1), 0, part // 2, half)
            last.append(copies.remote(block, block, near_y))
            by_y.wait_recv()
            block = win_part(owner, flip(quarter, 0), part // 2, part // 2, half)
            last.append(copies.remote(block, block, near_z))
        return last

    def normalise(mask):
        at = turn(wt, mask, bits)
        gain = jnp.concatenate(
            [gain_s[k].astype(F32)[0:1] for k in range(n_wt)], axis=1
        )

        def body(i, carry):
            rows = pl.ds(pl.multiple_of(i * 16, 16), 16)
            x = rows_s[at, rows, :].astype(F32)
            inv = lax.rsqrt(jnp.mean(x * x, axis=1, keepdims=True) + EPS)
            place = pl.ds(pl.multiple_of(at * n_rows + i * 16, 16), 16)
            normed_s[place, :] = (x * inv * gain).astype(BF16)
            return carry

        lax.fori_loop(0, n_rows // 16, body, 0, unroll=2)

    far = send_far(0)
    rows = Gather(copies, rows_s, seq, wt, bits)
    gains = Gather(copies, gain_s, seq, wt, bits)
    starts = Gather(copies, starts_s, seq, wt, bits)
    own_copies = [
        copies.local(gain_ref, gain_s.at[wt]),
        copies.local(starts_ref, starts_s.at[wt]),
        copies.local(hidden_ref, rows_s.at[wt]),
    ]
    gains.send(0, gain_ref)
    rows.send(0, hidden_ref)
    near = send_near(0)
    starts.send(0, starts_ref)
    wout_copy = copies.local(wout_ref, wout_s)
    for mask in range(n_wt - 1, 0, -1):
        if mask in gains.arriving:
            gains.arrive(mask)
    for mask in range(1, n_wt):
        if mask not in (1, 2):
            gains.arriving[mask].wait_recv()
    for copy in own_copies:
        copy.wait()
    normalise(0)
    rows.arrive(1)
    normalise(1)
    passed = share_first(0, far)
    far = send_far(1)
    last = share_second(0, passed)
    near_gate = send_near(1)
    for mask in range(2, n_wt):
        rows.arrive(mask)
        if mask == 2:
            half_rows = n_rows // 2
            tops = Gather(copies, grads_s.at[:, :half_rows], seq, wt, bits)
            ends = Gather(copies, grads_s.at[:, half_rows:], seq, wt, bits)
            grad_copy = copies.local(grad_ref, grads_s.at[wt])
            tops.send(0, grad_ref.at[:half_rows])
        normalise(mask)
    results = [copies.local(gain_s, gain_out)]
    near[0].wait_recv()
    near[1].wait()
    for copy in last:
        copy.wait_recv()

    n_block, m_block = 256, 512

    def tiles(body):
        m_count = all_rows // m_block

        def one(i, carry):
            m = pl.multiple_of((i % m_count) * m_block, m_block)
            n = pl.multiple_of((i // m_count) * n_block, n_block)
            body(m, n)
            return carry

        lax.fori_loop(0, m_count * (n_chan // n_block), one, 0)

    def conv_tile(m, n):
        value = jnp.dot(
            normed_s[pl.ds(m, m_block), :], win_s[:, pl.ds(n, n_block)], preferred_element_type=F32
        )
        value = value.astype(BF16).astype(F32)
        for k in range(m_block // n_rows):
            conv_s[m // n_rows + k, rim:, pl.ds(n, n_block)] = value[k * n_rows : (k + 1) * n_rows]

    tiles(conv_tile)

    rim_s[...] = jnp.zeros_like(rim_s)
    for b in range(n_wt):
        for k in range(taps - 1):
            at = rim + n_rows - (taps - 1 - k) * SUB
            rim_s[b * (taps - 1) + k, :] = conv_s[b, at + SUB - 1, :]
    rim_s2 = rim_s[...].astype(BF16)
    rim_in[0] = rim_s2

    @pl.when(seq == 0)
    def _():
        rim_in[1] = jnp.zeros_like(rim_s2)

    k_rim, copies.count = copies.count, copies.count + 1
    rim_copy = pltpu.make_async_remote_copy(
        src_ref=rim_in.at[0], dst_ref=rim_in.at[1], send_sem=send_sems.at[k_rim],
        recv_sem=recv_sems.at[k_rim], device_id=ahead, device_id_type=MESH,
    )

    @pl.when(seq < n_seq - 1)
    def _():
        rim_copy.start()

    passed = share_first(1, far)

    def convolve(b, j):
        rows = pl.ds(pl.multiple_of(j * 16, 16), 16)
        total = bconv_ref[...] + conv_s[b, rows, :] * wconv_ref[0:1, :]
        for k in range(1, taps):
            at = pl.ds(pl.multiple_of(j * 16 + k * SUB, SUB), 16)
            total = total + conv_s[b, at, :] * wconv_ref[k : k + 1, :]
        place = pl.ds(pl.multiple_of(b * n_rows + j * 16, 16), 16)
        u_s[place, :] = (total * jax.nn.sigmoid(total)).astype(BF16)

    head = -(-(taps - 1) // 2)
    pairs = n_rows // 16

    def convolve_tail(i, carry):
        convolve(i // (pairs - head), head + i % (pairs - head))
        return carry

    lax.fori_loop(0, n_wt * (pairs - head), convolve_tail, 0, unroll=2)

    @pl.when(seq > 0)
    def _():
        rim_copy.wait_recv()

    rim_rows = rim_in[1].astype(F32)
    first = lax.broadcasted_iota(jnp.int32, (SUB, n_chan), 0) == 0
    for b in range(n_wt):
        for k in range(taps - 1):
            at = rim + n_rows - (taps - 1 - k) * SUB
            moved = pltpu.roll(conv_s[b, at : at + SUB, :], 1, 0)
            row = rim_rows[b * (taps - 1) + k : b * (taps - 1) + k + 1, :]
            conv_s[b, k * SUB : (k + 1) * SUB, :] = jnp.where(first, row, moved)
    lax.fori_loop(0, n_wt * head, lambda i, c: (convolve(i // head, i % head), c)[1], 0)
    results += [copies.local(conv_s, conv_out), copies.local(u_s, u_out)]

    packed = []
    for b in range(n_wt):
        block = u_s[b * n_rows : (b + 1) * n_rows, :]
        mix_s[b * n_rows : (b + 1) * n_rows, :] = jnp.dot(
            block, wx_ref[:, :LANE], preferred_element_type=F32
        )
        packed.append(jnp.dot(block, wx_ref[:, LANE:], preferred_element_type=F32))
    mix_s[all_rows:, :] = jnp.concatenate(packed, axis=1)
    mixed = WtSum(copies, mix_s, first_s, half_s, land_s, fin_s, seq, wt, bits)
    mixed.begin()
    last = share_second(1, passed)
    starts.arrive(2)

    def transpose(b):
        at = slice(b * n_rows, (b + 1) * n_rows)
        normed_t[:, at] = normed_s[at, :].T

    transpose(0)
    for bit in range(1, bits):
        mixed.middle(bit)
    ends.send(0, grad_ref.at[half_rows:])
    for b in range(1, n_wt):
        transpose(b)
    results.append(copies.local(normed_t, normed_out))
    mixed.end()

    low_s[...] = fin_s[:all_rows, :].astype(BF16)
    starts.arriving[1].wait_recv()
    starts.arriving[3].wait_recv()
    lane = lax.broadcasted_iota(jnp.int32, (n_rows, LANE), 1)
    width = LANE // n_wt
    for b in range(n_wt):
        moved = fin_s[all_rows:, :]
        if b:
            moved = pltpu.roll(moved, LANE - b * width, 1)
        bcs_s[b * n_rows : (b + 1) * n_rows, :] = (
            jnp.where(lane < width, moved, 0.0).astype(BF16) + starts_s[b]
        )

    def raw_tile(m, n):
        value = lax.dot_general(
            low_s[pl.ds(m, m_block), :], wdt_ref[pl.ds(n, n_block), :], (((1,), (1,)), ((), ())),
            preferred_element_type=F32,
        )
        raw_s[pl.ds(m, m_block), pl.ds(n, n_block)] = value.astype(BF16)

    tiles(raw_tile)
    results += [
        copies.local(low_s, low_out), copies.local(bcs_s, bcs_out), copies.local(raw_s, raw_out)
    ]

    near_gate[0].wait_recv()
    near_gate[1].wait()
    for copy in last:
        copy.wait_recv()
    results.append(copies.local(win_s, win_out))

    def gate_tile(m, n):
        value = jnp.dot(
            normed_s[pl.ds(m, m_block), :], win_s[:, pl.ds(n_chan + n, n_block)],
            preferred_element_type=F32,
        )
        gate_s[pl.ds(m, m_block), pl.ds(n, n_block)] = value.astype(BF16)

    tiles(gate_tile)
    results.append(copies.local(gate_s, gate_out))
    n_state = rate_ref.shape[0]
    width = dec_in.shape[1]
    steps = n_rows // SUB
    start_at = 2 * n_state * LANE

    def stream_of(i):
        base = wt + (i // 2) * (1 - 2 * bit_of(wt, 1)) * 2
        return base + (i % 2) * (1 - 2 * bit_of(wt, 0))

    def back(b):
        at = pl.ds(pl.multiple_of(b * n_rows, n_rows), n_rows)

        def one(i, carry):
            n = pl.ds(pl.multiple_of(i * n_block, n_block), n_block)
            d_gated = lax.dot_general(
                grads_s[b], wout_s[n, :], (((1,), (1,)), ((), ())), preferred_element_type=F32
            )
            gate = gate_s[at, n].astype(F32)
            dgated_s[at, n] = d_gated
            dscan_s[at, n] = (d_gated * gate * jax.nn.sigmoid(gate)).astype(BF16)
            return carry

        lax.fori_loop(0, n_chan // n_block, one, 0)

    def chunk_ends(b, part):
        columns = pl.ds(pl.multiple_of(part * width, width), width)

        def prepare(j, total):
            rows = pl.ds(pl.multiple_of(j * 16, 16), 16)
            at = pl.ds(pl.multiple_of(b * n_rows + j * 16, 16), 16)
            delta = softplus(raw_s[at, columns].astype(F32) + bias_ref[:, columns])
            held = jnp.where(wide(bcb[rows, start_at : start_at + LANE], width) > 0.5, RESET, delta)
            dec_in[rows, :] = held
            drive_in[rows, :] = delta * u_s[at, columns].astype(F32)
            g_in[rows, :] = dscan_s[at, columns].astype(F32)
            return total + held[:SUB] + held[SUB:]

        total = lax.fori_loop(0, steps // 2, prepare, jnp.zeros((SUB, width), F32), unroll=2)
        total_ref[b, :, columns] = total
        span = jnp.sum(total, 0, keepdims=True)
        span_s[b, :, columns] = span
        for first_n in range(0, n_state, 2):
            states = range(first_n, first_n + 2)

            def step(j, carry):
                rows = pl.ds(pl.multiple_of(j * SUB, SUB), SUB)
                held, drive, g = dec_in[rows, :], drive_in[rows, :], g_in[rows, :]
                running, products, passed = [], [], []
                for n, h, so_far, p in zip(states, *carry):
                    b_row = wide(bcb[rows, n * LANE : (n + 1) * LANE], width)
                    c_row = wide(bcb[rows, (n_state + n) * LANE : (n_state + n + 1) * LANE], width)
                    decay = jnp.exp2(held * rate_ref[n : n + 1, columns])
                    so_far = so_far * decay
                    running.append(decay * h + drive * b_row)
                    products.append(so_far)
                    passed.append(p + so_far * (g * c_row))
                return tuple(running), tuple(products), tuple(passed)

            zero = tuple(jnp.zeros((SUB, width), F32) for _ in states)
            one = tuple(jnp.ones((SUB, width), F32) for _ in states)
            carry = lax.fori_loop(0, steps, step, (zero, one, zero), unroll=8)
            for n, h, decay, p in zip(states, *carry):
                end = chunk_prefix(decay, h, False)[1]
                lead = chunk_prefix(decay, p, True)[1]
                end_s[b, n, :, columns], lead_s[b, n, :, columns] = end, lead
                run_s[0, b, n : n + 1, columns] = end[SUB - 1 :]
                run_s[1, b, n : n + 1, columns] = lead[:1]

    def ends_of(i, carry):
        b = stream_of(i)
        back(b)
        bcb[...] = jnp.dot(
            bcs_s[pl.ds(pl.multiple_of(b * n_rows, n_rows), n_rows), :], spread_ref[...],
            preferred_element_type=F32,
        )
        lax.fori_loop(0, n_chan // width, lambda part, c: (chunk_ends(b, part), c)[1], 0)
        return carry

    grad_copy.wait()
    tops.arrive(1)
    ends.arrive(1)
    wout_copy.wait()
    lax.fori_loop(0, 2, ends_of, 0)
    for mask in range(2, n_wt):
        tops.arrive(mask)
        ends.arrive(mask)
        ends_of(mask, 0)
    results.append(copies.local(grads_s, grad_out))
    results += [copies.local(dgated_s, dgated_out), copies.local(dscan_s, dscan_out)]
    results += [copies.local(end_s, end_out), copies.local(lead_s, lead_out)]
    join_rounds(
        n_seq, n_wt, seq, wt, rate_ref[...], head_ref, tail_ref, run_s, span_s, own_span, gap_s,
        edge_send, edge_land, span_send, span_land, join_send, join_recv,
    )
    for copy in results:
        copy.wait()

    @pl.when(seq < n_seq - 1)
    def _():
        rim_copy.wait_send()

    copies.finish()


def start_all(
    hidden, grad, gain, starts, w_in, w_out, w_conv, b_conv, w_x, w_dt, bias, rate_rows
):
    n_seq, n_wt = lax.axis_size("seq"), lax.axis_size("wt")
    n_rows, n_feat = hidden.shape
    n_chan, taps = w_out.shape[0], w_conv.shape[0]
    rows, rim = n_wt * n_rows, (taps - 1) * SUB
    shapes = [
        ((n_feat, rows), BF16), ((n_feat, 2 * n_chan), BF16), ((n_wt, rim + n_rows, n_chan), F32),
        ((rows, n_chan), BF16), ((rows, n_chan), BF16), ((rows, n_chan), BF16), ((rows, LANE), BF16),
        ((rows, LANE), BF16), ((rows, n_chan), F32), ((rows, n_chan), BF16),
        ((n_wt, n_rows, n_feat), BF16), ((n_wt,) + gain.shape, BF16),
        ((n_wt, rate_rows.shape[0], SUB, n_chan), F32),
        ((n_wt, rate_rows.shape[0], SUB, n_chan), F32), ((n_wt, SUB, n_chan), F32),
        ((n_wt,) + rate_rows.shape, F32), ((n_wt,) + rate_rows.shape, F32),
    ]
    normed, win, conv, gate, u, raw, low, bcs, dgated, dscan, grads, gains = shapes[:12]
    ends = shapes[12]
    n_state, rounds = rate_rows.shape[0], n_seq.bit_length() - 1
    count = (2 * n_state + 1) * LANE
    width = min(512, n_chan)
    spans, edges = (2 * n_wt, n_chan), (n_wt, n_state, n_chan)
    size = (rows + n_rows) // 2
    bits = n_wt.bit_length() - 1
    scratch = [
        grads, grads, gains, ((n_wt, n_rows, LANE), BF16), ((rows, n_feat), BF16), win, (w_out.shape, BF16), conv,
        gate, u, raw, low, bcs, dgated, dscan, ((2 * size, LANE), F32), ((2 * size, LANE), F32),
        ((size, LANE), F32), ((bits, size, LANE), BF16), ((bits, size, LANE), BF16),
        ((16, n_chan), F32),
        ((2, 16, n_chan), BF16), normed,
        ((n_rows, count), F32), ((n_rows, width), F32), ((n_rows, width), F32), ((n_rows, width), F32),
        ends, ends, ((2,) + edges, F32), ((n_wt, 1, n_chan), F32), (spans, F32), (spans, F32),
        ((2, 2) + edges, BF16),
        ((rounds, 2) + edges, BF16), ((rounds,) + spans, F32), ((rounds, 2) + spans, F32),
    ]
    hbm = pl.BlockSpec(memory_space=pl.ANY)
    vmem = pl.BlockSpec(memory_space=pltpu.VMEM)
    return pl.pallas_call(
        functools.partial(start_kernel, n_seq, n_wt),
        in_specs=[hbm] * 6 + [vmem] * 7,
        out_specs=[hbm] * (len(shapes) - 3) + [vmem] * 3,
        out_shape=[jax.ShapeDtypeStruct(*item) for item in shapes],
        scratch_shapes=[pltpu.VMEM(*item) for item in scratch]
        + [pltpu.SemaphoreType.DMA((90,))] * 2
        + [pltpu.SemaphoreType.DMA((rounds, 2, 2))] * 2,
        compiler_params=pltpu.CompilerParams(
            collective_id=2, has_side_effects=True, vmem_limit_bytes=4090 * 2**14
        ),
        name="start_all",
    )(
        hidden, grad, gain, starts, w_in, w_out, w_conv, b_conv, w_x, w_dt, spread_matrix(n_state),
        bias, rate_rows,
    )


def dot(left, right, left_dim=1, right_dim=0):
    return lax.dot_general(
        left, right, (((left_dim,), (right_dim,)), ((), ())), preferred_element_type=F32
    )


def to_chunks(rows):
    n_rows, width = rows.shape
    return rows.reshape(SUB, n_rows // SUB, width).swapaxes(0, 1).reshape(n_rows, width)


def per_device(
    hidden_in, doc_starts, norm_gain, in_weight, conv_weight, conv_bias, x_weight,
    dt_weight, dt_bias, a_log, d_skip, out_weight, grad_output,
):
    n_wt, n_seq = lax.axis_size("wt"), lax.axis_size("seq")
    seq_at = lax.axis_index("seq")
    n_chan = out_weight.shape[0]
    taps = conv_weight.shape[1]
    dt_rank = dt_weight.shape[1]
    n_state = a_log.shape[1]
    rows_own = hidden_in[0]
    n_rows, n_feat = rows_own.shape
    steps = n_rows // SUB

    w_conv = conv_weight.astype(F32)
    starts = jnp.pad(
        to_chunks(doc_starts[0].astype(BF16)[:, None]), ((0, 0), (2 * n_state, LANE - 2 * n_state - 1))
    )
    rates = (-LOG2E * jnp.exp(a_log.astype(F32))).T
    bias = dt_bias.astype(F32)[None]
    skip = d_skip.astype(F32)[None]
    (
        normed_t, w_in, padded, gate_in, inputs, dt_raw, dt_low, bcs, d_gated, d_scanned, grad_all, gains,
        ends, leads, totals, head, tail,
    ) = start_all(
        to_chunks(rows_own), to_chunks(grad_output[0]),
        jnp.broadcast_to(norm_gain[None], (16, norm_gain.shape[0])), starts, in_weight, out_weight,
        w_conv.T, conv_bias.astype(F32)[None], x_weight, dt_weight, bias,
        rates,
    )
    gain = gains[:, 0].reshape(n_feat).astype(F32)

    gated, gated_t, d_gate, d_scan_in, d_raw, d_bc, d_rate, sums, wout, feat = scan_all(
        bcs, dt_raw, inputs, d_scanned, gate_in, d_gated, bias, skip, rates,
        ends, leads, totals, head, tail, grad_all.reshape(n_wt * n_rows, n_feat), normed_t,
    )


    feat_grads, d_wout, small, input_grad, output, gain_parts = finish_all(
        gated_t, d_gate, d_scan_in, d_raw, inputs, padded, grad_all, normed_t, w_in, wout, feat,
        gated, out_weight, rows_own, grad_output[0], gains, d_bc, dt_low, x_weight, dt_weight, w_conv.T,
        conv_bias.astype(F32)[None], d_rate, rates, sums,
    )
    d_wout = d_wout.reshape(-1, n_feat).astype(F32)
    small = small.astype(F32)
    widths = (dt_rank, dt_rank, 2 * n_state, n_state, taps, 1, 1, 1)
    cuts, at = [], 0
    for piece in widths:
        cuts.append(small[:, at : at + piece])
        at += piece
    d_wx, d_wdt, d_wbc, d_loga, d_wconv, d_bconv, d_bdt, d_skips = cuts
    own = n_feat // (n_seq * n_wt)
    own_at = own * (n_wt * seq_at + lax.axis_index("wt"))
    gain_grad = jnp.sum(gain_parts, (0, 2)) / lax.dynamic_slice_in_dim(gain, own_at, own, 0)
    return (
        output[None],
        input_grad[None],
        gain_grad,
        feat_grads.astype(F32),
        d_wconv,
        d_bconv[:, 0],
        jnp.concatenate([d_wx, d_wbc], 1),
        d_wdt,
        d_bdt[:, 0],
        d_loga,
        d_skips[:, 0],
        d_wout,
    )


def solution(mesh):
    placed = (
        P("wt", "seq", None),
        P("wt", "seq"),
        P("wt"),
        P("wt", None),
        P("wt", None),
        P("wt"),
        P("wt", None),
        P("wt", None),
        P("wt"),
        P("wt", None),
        P("wt"),
        P("wt", None),
        P("wt", "seq", None),
    )
    every = ("seq", "wt")
    return jax.shard_map(
        per_device,
        mesh=mesh,
        in_specs=placed,
        out_specs=(
            P("wt", "seq", None),
            P("wt", "seq", None),
            P(every),
            P(every, None),
            P(every, None),
            P(every),
            P(every, None),
            P(every, None),
            P(every),
            P(every, None),
            P(every),
            P(every, None),
        ),
        check_vma=False,
    )
```
